32 devices in a mesh: ctx: 8 (over z, x), mp: 4 (over y, core).
Axes of the slice: x: 2, y: 2, z: 4, core: 2. Of those that a mesh axis runs over, the one named last changes fastest.
Arguments:
- query_rows: bfloat16 [1024, 2048], P('ctx', 'mp'), may hold values from -51 to 51
- key_rows: bfloat16 [1024, 2048], P('ctx', 'mp'), may hold values from -4 to 4
- value_rows: bfloat16 [1024, 2048], P('ctx', 'mp'), may hold values from -6 to 6
- inputs: bfloat16 [1024, 2048], P('ctx', 'mp'), may hold values from -3 to 3
- out_weight: bfloat16 [2048, 2048], P('mp'), may hold values from -0.125 to 0.125
- kernel: float32 [31, 2048], P(None, 'mp'), may hold values from -1 to 1
- cotangent: bfloat16 [1024, 2048], P('ctx', 'mp'), may hold values from -6 to 6
Outputs:
- output: bfloat16 [1024, 2048], P('ctx', 'mp')
- grad_input: bfloat16 [1024, 2048], P('ctx', 'mp')
- grad_query: bfloat16 [1024, 2048], P('ctx', 'mp')
- grad_key: bfloat16 [1024, 2048], P('ctx', 'mp')
- grad_value: bfloat16 [1024, 2048], P('ctx', 'mp')
The draws below stay inside these ranges and needn't reach their ends.
All inputs are finite; a program needn't handle non-finite values.
Results may differ from the reference program's by a relative error of at most 0.024.
Values may be sent and summed in bfloat16 or wider, within the bound.
No kernel may reach another device: no remote copies, remote signals or barrier semaphores. Data moves between devices by JAX's collectives and lax.ppermute only.
A program may use at most 64 MiB of HBM per device.

```python
import math
import jax
import jax.numpy as jnp
from jax import lax

D = 2048
HEADS = 16
HDIM = 128
KS = 31
LOOK = 2
FR_DEV = 128
FRAMES = 1024


def band_pair(key):
    base_key = jax.random.fold_in(key, 11)
    first_key = jax.random.fold_in(base_key, 1)
    second_key = jax.random.fold_in(base_key, 2)
    key_vals = jnp.clip(jax.random.normal(first_key, (FRAMES, D), jnp.float32), -4.0, 4.0)
    query_vals = jnp.clip(3.0 * jax.random.normal(second_key, (FRAMES, D), jnp.float32), -12.0, 12.0)
    return (query_vals, key_vals)


def draw_query_rows(key, part):
    return band_pair(key)[0].astype(jnp.bfloat16)


def draw_key_rows(key, part):
    return band_pair(key)[1].astype(jnp.bfloat16)


def block_levels(own_key, shape, shards, least, top_value):
    gain = 1.0
    for axis_at, blocks in shards:
        draws = jax.random.uniform(jax.random.fold_in(jax.random.fold_in(own_key, 6), axis_at), (blocks,), jnp.float32, least / len(shards), top_value / len(shards))
        gain = gain * jnp.repeat(jnp.exp(draws), shape[axis_at] // blocks).reshape((-1,) + (1,) * (len(shape) - 1 - axis_at))
    return gain


def scatter_about(own_key, extent, spread, reach, cuts=(), held_as=jnp.bfloat16):
    entries = jax.random.normal(own_key, extent, jnp.float32) * spread
    if len(cuts) > 0:
        entries = block_levels(own_key, extent, cuts, -0.22, 0.18) * entries
    return jnp.clip(entries, min=-reach, max=reach).astype(held_as)


def setup_inputs(seed: int = 0) -> dict:
    streams_of = jax.random.split(jax.random.key(seed), 8)
    return {
        "query_rows": draw_query_rows(jax.random.fold_in(streams_of[7], 71), 0),
        "key_rows": draw_key_rows(jax.random.fold_in(streams_of[7], 71), 0),
        "value_rows": scatter_about(streams_of[2], (FRAMES, D), 1.0, 6.0, ((0, 8), (1, 4))),
        "inputs": scatter_about(streams_of[3], (FRAMES, D), 0.5, 3.0, ((0, 8), (1, 4))),
        "out_weight": scatter_about(streams_of[4], (D, D), D ** -0.5, 0.125, ((0, 4),)),
        "kernel": scatter_about(streams_of[5], (KS, D), KS ** -0.5, 1.0, ((1, 4),), jnp.float32),
        "cotangent": scatter_about(streams_of[6], (FRAMES, D), 1.0, 6.0, ((0, 8), (1, 4))),
    }


def split_heads(values_in):
    return values_in.astype(jnp.float32).reshape(values_in.shape[0], HEADS, HDIM)

def take_rows(values_in, row_start, length):
    return lax.dynamic_slice_in_dim(values_in, row_start, length, 0)

def reference(query_rows, key_rows, value_rows, inputs, out_weight, kernel, cotangent):
    score_scale = 1.0 / math.sqrt(HDIM)
    window_len = (2 * LOOK + 1) * FR_DEV
    margin = LOOK * FR_DEV
    blocks = FRAMES // FR_DEV

    def padded(values_in):
        return jnp.pad(values_in, ((margin, margin), (0, 0)))
    key_pad = padded(key_rows)
    value_pad = padded(value_rows)
    query_pad = padded(query_rows)

    def window_mask(block_index):
        owners = jnp.arange(window_len, dtype=jnp.int32) // FR_DEV - LOOK + block_index
        return (owners >= 0) & (owners < blocks)

    def forward_block(block_index):
        row_start = (block_index * FR_DEV).astype(jnp.int32)
        query_block = split_heads(take_rows(query_rows, row_start, FR_DEV))
        key_win = split_heads(take_rows(key_pad, row_start, window_len))
        value_win = split_heads(take_rows(value_pad, row_start, window_len))
        scores = jnp.einsum('qhd,khd->hqk', query_block, key_win) * score_scale
        scores = jnp.where(window_mask(block_index)[None, None, :], scores, -jnp.inf)
        row_max = lax.optimization_barrier(jnp.max(scores, axis=2))
        log_total = row_max + jnp.log(lax.optimization_barrier(jnp.sum(jnp.exp(scores - row_max[:, :, None]), axis=2)))
        probs_low = jnp.exp(scores - log_total[:, :, None]).astype(jnp.bfloat16)
        attended = jnp.einsum('hqk,khd->qhd', probs_low.astype(jnp.float32), value_win).astype(jnp.bfloat16)
        return (attended.reshape(FR_DEV, D), log_total)
    attended, log_parts = lax.map(forward_block, jnp.arange(blocks, dtype=jnp.int32))
    attended = attended.reshape(FRAMES, D)
    log_total = jnp.transpose(log_parts, (1, 0, 2)).reshape(HEADS, FRAMES)
    mixed = jnp.dot(attended, out_weight, preferred_element_type=jnp.float32)
    hidden = (inputs.astype(jnp.float32) + mixed).astype(jnp.bfloat16)
    half_kernel = KS // 2
    hidden_pad = jnp.pad(hidden.astype(jnp.float32), ((half_kernel, half_kernel), (0, 0)))
    conv_out = jnp.zeros((FRAMES, D), jnp.float32)
    for tap_index in range(KS):
        conv_out = conv_out + kernel[tap_index][None, :] * hidden_pad[tap_index:tap_index + FRAMES]
    conv_gate = jax.nn.sigmoid(conv_out)
    output = (hidden.astype(jnp.float32) + conv_out * conv_gate).astype(jnp.bfloat16)
    grad_conv = (cotangent.astype(jnp.float32) * (conv_gate + conv_out * conv_gate * (1.0 - conv_gate))).astype(jnp.bfloat16)
    grad_pad = jnp.pad(grad_conv.astype(jnp.float32), ((half_kernel, half_kernel), (0, 0)))
    grad_hidden = cotangent.astype(jnp.float32)
    for tap_index in range(KS):
        first_row = 2 * half_kernel - tap_index
        grad_hidden = grad_hidden + kernel[tap_index][None, :] * grad_pad[first_row:first_row + FRAMES]
    grad_input = grad_hidden.astype(jnp.bfloat16)
    upstream = jnp.dot(grad_input, out_weight.T, preferred_element_type=jnp.float32).astype(jnp.bfloat16)
    row_delta = lax.optimization_barrier(jnp.sum(split_heads(upstream) * split_heads(attended), axis=2)).T
    up_pad = padded(upstream)
    lse_pad = jnp.pad(log_total, ((0, 0), (margin, margin)))
    delta_pad = jnp.pad(row_delta, ((0, 0), (margin, margin)))

    def query_grad(block_index):
        row_start = (block_index * FR_DEV).astype(jnp.int32)
        query_block = split_heads(take_rows(query_rows, row_start, FR_DEV))
        up_block = split_heads(take_rows(upstream, row_start, FR_DEV))
        key_win = split_heads(take_rows(key_pad, row_start, window_len))
        value_win = split_heads(take_rows(value_pad, row_start, window_len))
        lse_block = lax.dynamic_slice_in_dim(log_total, row_start, FR_DEV, 1)
        delta_block = lax.dynamic_slice_in_dim(row_delta, row_start, FR_DEV, 1)
        scores = jnp.einsum('qhd,khd->hqk', query_block, key_win) * score_scale
        scores = jnp.where(window_mask(block_index)[None, None, :], scores, -jnp.inf)
        probs = jnp.exp(scores - lse_block[:, :, None])
        grad_dots = jnp.einsum('qhd,khd->hqk', up_block, value_win)
        grad_scores = (probs * (grad_dots - delta_block[:, :, None]) * score_scale).astype(jnp.bfloat16)
        result = jnp.einsum('hqk,khd->qhd', grad_scores.astype(jnp.float32), key_win)
        return result.astype(jnp.bfloat16).reshape(FR_DEV, D)

    def key_grad(block_index):
        row_start = (block_index * FR_DEV).astype(jnp.int32)
        key_block = split_heads(take_rows(key_rows, row_start, FR_DEV))
        value_block = split_heads(take_rows(value_rows, row_start, FR_DEV))
        query_win = split_heads(take_rows(query_pad, row_start, window_len))
        up_win = split_heads(take_rows(up_pad, row_start, window_len))
        lse_win = lax.dynamic_slice_in_dim(lse_pad, row_start, window_len, 1)
        delta_win = lax.dynamic_slice_in_dim(delta_pad, row_start, window_len, 1)
        valid = window_mask(block_index)[None, :, None]
        scores = jnp.einsum('qhd,khd->hqk', query_win, key_block) * score_scale
        probs = jnp.where(valid, jnp.exp(scores - lse_win[:, :, None]), 0.0)
        grad_value = jnp.einsum('hqk,qhd->khd', probs.astype(jnp.bfloat16).astype(jnp.float32), up_win)
        grad_dots = jnp.einsum('qhd,khd->hqk', up_win, value_block)
        grad_scores = (probs * (grad_dots - delta_win[:, :, None]) * score_scale).astype(jnp.bfloat16)
        grad_key = jnp.einsum('hqk,qhd->khd', grad_scores.astype(jnp.float32), query_win)
        return (grad_key.astype(jnp.bfloat16).reshape(FR_DEV, D), grad_value.astype(jnp.bfloat16).reshape(FR_DEV, D))
    grad_query = lax.map(query_grad, jnp.arange(blocks, dtype=jnp.int32)).reshape(FRAMES, D)
    grad_key, grad_value = lax.map(key_grad, jnp.arange(blocks, dtype=jnp.int32))
    return (output, grad_input, grad_query, grad_key.reshape(FRAMES, D), grad_value.reshape(FRAMES, D))
```

```python
import functools
import math

import jax
import jax.numpy as jnp
from jax import lax
from jax.experimental import pallas as pl
from jax.experimental.pallas import tpu as pltpu
from jax.sharding import PartitionSpec as P

HDIM = 128
F32 = jnp.float32
BF16 = jnp.bfloat16
HALO = 16
NT = (((1,), (1,)), ((), ()))
NN = (((1,), (0,)), ((), ()))


def dot_nt(a, b):
    return lax.dot_general(a, b, NT, preferred_element_type=F32)


def dot_nn(a, b):
    return lax.dot_general(a, b, NN, preferred_element_type=F32)


def pair_swap(block, axis, bit):
    return lax.ppermute(block, axis, [(i, i ^ bit) for i in range(lax.axis_size(axis))])


def ring_routes(count):
    rise = [(i, i + 2) for i in range(0, count - 2, 2)] + [(count - 2, count - 1)]
    fall = [(i, i - 2) for i in range(count - 1, 2, -2)] + [(1, 0)]
    route = rise + fall
    return route, [(b, a) for a, b in route]


def ring(block, way):
    return lax.ppermute(block, "ctx", ring_routes(lax.axis_size("ctx"))[way])


def kernel_call(body, outs, args, flops, name):
    smem = pl.BlockSpec(memory_space=pltpu.SMEM)
    vmem = pl.BlockSpec(memory_space=pltpu.VMEM)
    nbytes = sum(math.prod(a.shape) * a.dtype.itemsize for a in list(args) + list(outs))
    return pl.pallas_call(
        body,
        out_shape=outs,
        in_specs=[smem] + [vmem] * (len(args) - 1),
        out_specs=tuple(vmem for _ in outs),
        compiler_params=pltpu.CompilerParams(vmem_limit_bytes=24 * 1024 * 1024),
        cost_estimate=pl.CostEstimate(flops=flops, bytes_accessed=nbytes, transcendentals=0),
        name=name,
    )(*args)


def shaped(shape, dtype):
    return jax.ShapeDtypeStruct(shape, dtype)


def off_bias(flag):
    return jnp.where(flag > 0, jnp.float32(0.0), jnp.float32(-jnp.inf))


def head_cols(h):
    return slice(h * HDIM, (h + 1) * HDIM)


def window_scores(scale, flags, q, kvs, cols):
    frames = q.shape[0]
    biases = (None, None, off_bias(flags[1]), off_bias(flags[2]), off_bias(flags[1]))
    keys = jnp.concatenate([kv[0:frames, cols] for kv in kvs], axis=0)
    scores = dot_nt(q[:, cols], keys) * scale
    parts = []
    for b, bias in enumerate(biases):
        part = scores[:, b * frames : (b + 1) * frames]
        parts.append(part if bias is None else part + bias)
    return jnp.concatenate(parts, axis=1), keys


def forward_body(scale, flags, q, own, near, first, second, relay, weight, att, lse, send, keep):
    frames, width = q.shape
    kvs = (own, near, first, second, relay)
    lane = lax.broadcasted_iota(jnp.int32, (frames, HDIM), 1)
    lse_tile = jnp.zeros((frames, HDIM), F32)
    for h in range(width // HDIM):
        cols = head_cols(h)
        scores, _ = window_scores(scale, flags, q, kvs, cols)
        row_max = jnp.max(scores, axis=1, keepdims=True)
        log_total = row_max + jnp.log(jnp.sum(jnp.exp(scores - row_max), axis=1, keepdims=True))
        probs_low = jnp.exp(scores - log_total).astype(BF16)
        values = jnp.concatenate([kv[frames : 2 * frames, cols] for kv in kvs], axis=0)
        att[:, cols] = dot_nn(probs_low, values).astype(BF16)
        lse_tile = jnp.where(lane == h, log_total, lse_tile)
    lse[...] = lse_tile
    place = flags[3]
    attended = att[...]

    def share(target):
        block = weight[:, pl.ds(pl.multiple_of(target * width, 128), width)]
        return dot_nn(attended, block).astype(BF16)

    send[:, 0:width] = share(place ^ 3)
    send[:, width : 2 * width] = share(place ^ 1)
    keep[:, 0:width] = share(place ^ 2)
    keep[:, width : 2 * width] = share(place)


def hidden_body(flags, inputs, keep, core, across, cot, hidden, rims):
    frames, width = inputs.shape
    mine = slice(width, 2 * width)
    total = inputs[...].astype(F32) + keep[:, mine].astype(F32) + core[:, mine].astype(F32)
    hidden[...] = (total + across[...].astype(F32)).astype(BF16)
    wide = 2 * HALO
    rims[0:wide, :] = hidden[0:wide, :]
    rims[wide : 2 * wide, :] = hidden[frames - wide : frames, :]
    rims[2 * wide : 2 * wide + HALO, :] = cot[0:HALO, :]
    rims[2 * wide + HALO : 3 * wide, :] = cot[frames - HALO : frames, :]


def shifted_sum(load, taps_of, rows, lanes):
    total = None
    for b in range(8):
        part = None
        reach = rows if b == 0 else rows + 8
        for a in range(4):
            tap = taps_of(8 * a + b)
            if tap is None:
                continue
            term = tap * load(8 * a, reach)
            part = term if part is None else part + term
        if b:
            part = pltpu.roll(part, reach - b, 0)[0:rows]
        total = part if total is None else total + part
    return total


def conv_body(flags, hidden, rim_near, rim_first, cot, taps, output, grad_input, padded, grads):
    frames, width = hidden.shape
    wide = 2 * HALO
    count = taps.shape[0]
    even = flags[0] > 0
    have = jnp.where(flags[1] > 0, jnp.float32(1.0), jnp.float32(0.0))
    low_ok = jnp.where(even, have, jnp.float32(1.0))
    high_ok = jnp.where(even, jnp.float32(1.0), have)

    def low_of(rows):
        return jnp.where(even, rim_first[rows, :].astype(F32), rim_near[rows, :].astype(F32)) * low_ok

    def high_of(rows):
        return jnp.where(even, rim_near[rows, :].astype(F32), rim_first[rows, :].astype(F32)) * high_ok

    padded[0:wide, :] = low_of(slice(wide, 2 * wide))
    padded[wide : wide + frames, :] = hidden[...].astype(F32)
    padded[wide + frames : 2 * wide + frames, :] = high_of(slice(0, wide))
    cot_low = low_of(slice(2 * wide + HALO, 3 * wide))
    cot_high = high_of(slice(2 * wide, 2 * wide + HALO))
    for c in range(0, width, 128):
        cols = slice(c, c + 128)

        def tap_at(j):
            return taps[j : j + 1, cols] if 0 <= j < count else None

        conv = shifted_sum(
            lambda at, rows: padded[at : at + rows, cols],
            lambda s: tap_at(s - 1),
            frames + 2 * HALO,
            cols,
        )
        gate = 1.0 / (1.0 + jnp.exp(-conv))
        mid = slice(HALO, HALO + frames)
        own = padded[wide : wide + frames, cols]
        output[:, cols] = (own + conv[mid] * gate[mid]).astype(BF16)
        slope = gate + conv * gate * (1.0 - gate)
        own_cot = cot[:, cols].astype(F32)
        cots = jnp.concatenate([cot_low[:, cols], own_cot, cot_high[:, cols]], axis=0)
        grads[0 : frames + 2 * HALO, cols] = (cots * slope).astype(BF16).astype(F32)
        back = shifted_sum(
            lambda at, rows: grads[at : at + rows, cols],
            lambda s: tap_at(count - s) if s else None,
            frames,
            cols,
        )
        grad_input[:, cols] = (own_cot + back).astype(BF16)


def term_rows(rows):
    width = rows[0].shape[1]
    at = lax.broadcasted_iota(jnp.int32, (16, width), 0)
    block = jnp.zeros((16, width), F32)
    for r, row in enumerate(rows):
        rest = row
        for k in range(3):
            term = rest.astype(BF16).astype(F32)
            rest = rest - term
            block = jnp.where(at == 3 * r + k, term, block)
    return block.astype(BF16)


def upstream_body(flags, own, core, across, cross, weight, att, lse, message, delta):
    frames, width = own.shape
    place = flags[3]
    total = None
    for flip, block in ((0, own), (1, core), (2, across), (3, cross)):
        at = pl.ds(pl.multiple_of((place ^ flip) * width, 128), width)
        part = dot_nt(block[...], weight[:, at])
        total = part if total is None else total + part
    up = total.astype(BF16)
    message[0:frames, :] = up
    lane = lax.broadcasted_iota(jnp.int32, (frames, HDIM), 1)
    tile = jnp.zeros((frames, HDIM), F32)
    for h in range(width // HDIM):
        cols = head_cols(h)
        product = up[:, cols].astype(F32) * att[:, cols].astype(F32)
        tile = jnp.where(lane == h, jnp.sum(product, axis=1, keepdims=True), tile)
    delta[...] = tile
    lse_rows = lse[...].T
    delta_rows = tile.T
    for h in range(width // HDIM):
        message[frames : frames + 16, head_cols(h)] = term_rows(
            [lse_rows[h : h + 1, :], delta_rows[h : h + 1, :]]
        )


def query_grad_body(scale, flags, q, own, near, first, second, relay, message, lse, delta, grad_query):
    frames, width = q.shape
    kvs = (own, near, first, second, relay)
    for h in range(width // HDIM):
        cols = head_cols(h)
        scores, keys = window_scores(scale, flags, q, kvs, cols)
        probs = jnp.exp(scores - lse[:, h : h + 1])
        values = jnp.concatenate([kv[frames : 2 * frames, cols] for kv in kvs], axis=0)
        dots = dot_nt(message[0:frames, cols], values)
        grads = (probs * (dots - delta[:, h : h + 1]) * scale).astype(BF16)
        grad_query[:, cols] = dot_nn(grads, keys).astype(BF16)


def key_grad_body(scale, flags, own, *refs):
    queries, messages, (grad_key, grad_value) = refs[0:5], refs[5:10], refs[10:12]
    frames, width = queries[0].shape
    biases = (None, None, off_bias(flags[1]), off_bias(flags[2]), off_bias(flags[1]))
    for h in range(width // HDIM):
        cols = head_cols(h)
        asks = jnp.concatenate([q[:, cols] for q in queries], axis=0)
        ups = jnp.concatenate([m[0:frames, cols] for m in messages], axis=0)
        scores = dot_nt(own[0:frames, cols], asks) * scale
        dots = dot_nt(own[frames : 2 * frames, cols], ups)
        probs_low, grads = [], []
        for b, bias in enumerate(biases):
            at = slice(b * frames, (b + 1) * frames)
            terms = messages[b][frames : frames + 16, cols].astype(F32)
            log_total = terms[0:1] + terms[1:2] + terms[2:3]
            row_delta = terms[3:4] + terms[4:5] + terms[5:6]
            part = scores[:, at] if bias is None else scores[:, at] + bias
            probs = jnp.exp(part - log_total)
            probs_low.append(probs.astype(BF16))
            grads.append((probs * (dots[:, at] - row_delta) * scale).astype(BF16))
        grad_value[:, cols] = dot_nn(jnp.concatenate(probs_low, axis=1), ups).astype(BF16)
        grad_key[:, cols] = dot_nn(jnp.concatenate(grads, axis=1), asks).astype(BF16)


def per_device(query_rows, key_rows, value_rows, inputs, out_weight, kernel, cotangent):
    frames, width = query_rows.shape
    whole = out_weight.shape[1]
    scale = 1.0 / math.sqrt(HDIM)
    block, count = lax.axis_index("ctx"), lax.axis_size("ctx")
    even = block % 2 == 0
    lower, upper = block >= 2, block < count - 2
    flags = jnp.stack(
        [even, jnp.where(even, lower, upper), jnp.where(even, upper, lower), lax.axis_index("mp")]
    ).astype(jnp.int32)
    tile = shaped((frames, width), BF16)
    half = shaped((frames, 2 * width), BF16)
    side = shaped((frames, HDIM), F32)

    kv = jnp.concatenate([key_rows, value_rows], axis=0)
    kv_second = ring(kv, 1)
    kv_first = ring(kv, 0)
    kv_near = pair_swap(kv, "ctx", 1)
    kv_relay = pair_swap(kv_second, "ctx", 1)
    window = (kv, kv_near, kv_first, kv_second, kv_relay)

    att, lse, send, keep = kernel_call(
        functools.partial(forward_body, scale),
        (tile, side, half, half),
        (flags, query_rows, *window, out_weight),
        2 * frames * width * (10 * frames + whole),
        "forward",
    )
    core = pair_swap(send, "mp", 1)
    outgoing = keep[:, 0:width] + core[:, 0:width]
    outgoing, query_late = lax.optimization_barrier((outgoing, query_rows))
    across = pair_swap(outgoing, "mp", 2)
    q_second = ring(query_late, 1)
    q_first = ring(query_late, 0)

    hidden, rims = kernel_call(
        hidden_body,
        (tile, shaped((6 * HALO, width), BF16)),
        (flags, inputs, keep, core, across, cotangent),
        4 * frames * width,
        "hidden",
    )
    rim_near = pair_swap(rims, "ctx", 1)
    rim_first = ring(rim_near, 0)

    output, grad_input = pl.pallas_call(
        conv_body,
        out_shape=(tile, tile),
        in_specs=[pl.BlockSpec(memory_space=pltpu.SMEM)]
        + [pl.BlockSpec(memory_space=pltpu.VMEM)] * 5,
        out_specs=(pl.BlockSpec(memory_space=pltpu.VMEM),) * 2,
        scratch_shapes=[
            pltpu.VMEM((frames + 4 * HALO, width), F32),
            pltpu.VMEM((frames + 2 * HALO, width), F32),
        ],
        compiler_params=pltpu.CompilerParams(vmem_limit_bytes=24 * 1024 * 1024),
        cost_estimate=pl.CostEstimate(
            flops=130 * frames * width, bytes_accessed=10 * frames * width, transcendentals=0
        ),
        name="conv",
    )(flags, hidden, rim_near, rim_first, cotangent, kernel)

    grad_input, query_last, second_last = lax.optimization_barrier(
        (grad_input, query_rows, q_second)
    )
    gi_across = pair_swap(grad_input, "mp", 2)
    gi_core = pair_swap(grad_input, "mp", 1)
    q_near = pair_swap(query_last, "ctx", 1)
    q_relay = pair_swap(second_last, "ctx", 1)
    gi_cross = pair_swap(gi_across, "mp", 1)

    message, delta = kernel_call(
        upstream_body,
        (shaped((frames + 16, width), BF16), side),
        (flags, grad_input, gi_core, gi_across, gi_cross, out_weight, att, lse),
        2 * frames * width * whole,
        "upstream",
    )
    m_second = ring(message, 1)
    m_first = ring(message, 0)
    m_near = pair_swap(message, "ctx", 1)
    m_relay = pair_swap(m_second, "ctx", 1)

    (grad_query,) = kernel_call(
        functools.partial(query_grad_body, scale),
        (tile,),
        (flags, query_rows, *window, message, lse, delta),
        30 * frames * frames * width,
        "query_grad",
    )
    grad_key, grad_value = kernel_call(
        functools.partial(key_grad_body, scale),
        (tile, tile),
        (flags, kv, query_rows, q_near, q_first, q_second, q_relay)
        + (message, m_near, m_first, m_second, m_relay),
        40 * frames * frames * width,
        "key_grad",
    )
    return (output, grad_input, grad_query, grad_key, grad_value)


def solution(mesh):
    rows = P("ctx", "mp")
    return jax.shard_map(
        per_device,
        mesh=mesh,
        in_specs=(rows, rows, rows, rows, P("mp", None), P(None, "mp"), rows),
        out_specs=(rows,) * 5,
        check_vma=False,
    )
```

```python
import functools
import math

import jax
import jax.numpy as jnp
from jax import lax
from jax.experimental import pallas as pl
from jax.experimental.pallas import tpu as pltpu
from jax.sharding import PartitionSpec as P

HDIM = 128
F32 = jnp.float32
BF16 = jnp.bfloat16
HALO = 16
NT = (((1,), (1,)), ((), ()))
NN = (((1,), (0,)), ((), ()))


def dot_nt(a, b):
    return lax.dot_general(a, b, NT, preferred_element_type=F32)


def dot_nn(a, b):
    return lax.dot_general(a, b, NN, preferred_element_type=F32)


def pair_swap(block, axis, bit):
    return lax.ppermute(block, axis, [(i, i ^ bit) for i in range(lax.axis_size(axis))])


def ring_routes(count):
    rise = [(i, i + 2) for i in range(0, count - 2, 2)] + [(count - 2, count - 1)]
    fall = [(i, i - 2) for i in range(count - 1, 2, -2)] + [(1, 0)]
    route = rise + fall
    return route, [(b, a) for a, b in route]


def ring(block, way):
    return lax.ppermute(block, "ctx", ring_routes(lax.axis_size("ctx"))[way])


def inner_swap(block):
    return lax.ppermute(block, "ctx", [(i, i ^ 1) for i in range(2, lax.axis_size("ctx") - 2)])


def window_of(block):
    second = ring(block, 1)
    first = ring(block, 0)
    near = inner_swap(block)
    return near, first, second, pair_swap(second, "ctx", 1)


SMEM = pl.BlockSpec(memory_space=pltpu.SMEM)
VMEM = pl.BlockSpec(memory_space=pltpu.VMEM)
ANY = pl.BlockSpec(memory_space=pl.ANY)
HBM = pl.BlockSpec(memory_space=pltpu.HBM)


def kernel_call(body, outs, args, flops, name, spaces=None, scratch=(), mib=24, out_space=VMEM):
    nbytes = sum(math.prod(a.shape) * a.dtype.itemsize for a in list(args) + list(outs))
    return pl.pallas_call(
        body,
        out_shape=outs,
        in_specs=spaces or [SMEM] + [VMEM] * (len(args) - 1),
        out_specs=tuple(out_space for _ in outs),
        scratch_shapes=scratch,
        compiler_params=pltpu.CompilerParams(vmem_limit_bytes=mib * 1024 * 1024),
        cost_estimate=pl.CostEstimate(flops=flops, bytes_accessed=nbytes, transcendentals=0),
        name=name,
    )(*args)


def shaped(shape, dtype):
    return jax.ShapeDtypeStruct(shape, dtype)


def off_bias(flag):
    return jnp.where(flag > 0, jnp.float32(0.0), jnp.float32(-jnp.inf))


def head_cols(h):
    return slice(h * HDIM, (h + 1) * HDIM)


def pack_body(key, value, packed, sems):
    frames = key.shape[0]
    copies = [
        pltpu.make_async_copy(key, packed.at[pl.ds(0, frames)], sems.at[0]),
        pltpu.make_async_copy(value, packed.at[pl.ds(frames, frames)], sems.at[1]),
    ]
    for copy in copies:
        copy.start()
    for copy in copies:
        copy.wait()


def stacked(kvs, rows, cols):
    return jnp.concatenate([kv[rows, cols] for kv in kvs], axis=0)


def fetch_body(weight, seen, fetched, sem):
    copy = pltpu.make_async_copy(weight, fetched, sem)
    copy.start()
    copy.wait()


def forward_body(scale, flags, q, own, near, first, second, sums, tops, totals):
    frames, width = q.shape
    kvs = (near, own, first, second)
    lane = lax.broadcasted_iota(jnp.int32, (frames, HDIM), 1)
    top_tile = jnp.zeros((frames, HDIM), F32)
    total_tile = jnp.zeros((frames, HDIM), F32)
    bias = off_bias(flags[1])
    for h in range(width // HDIM):
        cols = head_cols(h)
        scores = dot_nt(q[:, cols], stacked(kvs, slice(0, frames), cols)) * scale
        scores = jnp.concatenate([scores[:, 0:frames] + bias, scores[:, frames:]], axis=1)
        top = jnp.max(scores, axis=1, keepdims=True)
        probs = jnp.exp(scores - top)
        sums[:, cols] = dot_nn(probs.astype(BF16), stacked(kvs, slice(frames, 2 * frames), cols))
        top_tile = jnp.where(lane == h, top, top_tile)
        total_tile = jnp.where(lane == h, jnp.sum(probs, axis=1, keepdims=True), total_tile)
    tops[...] = top_tile
    totals[...] = total_tile


def project_body(scale, flags, q, relay, sums, tops, totals, weight, att, lse, send, keep, q_message):
    frames, width = q.shape
    lane = lax.broadcasted_iota(jnp.int32, (frames, HDIM), 1)
    lse_tile = jnp.zeros((frames, HDIM), F32)
    bias = off_bias(flags[2])
    for h in range(width // HDIM):
        cols = head_cols(h)
        scores = dot_nt(q[:, cols], relay[0:frames, cols]) * scale + bias
        old_top = tops[:, h : h + 1]
        top = jnp.maximum(old_top, jnp.max(scores, axis=1, keepdims=True))
        shrink = jnp.exp(old_top - top)
        probs = jnp.exp(scores - top)
        total = totals[:, h : h + 1] * shrink + jnp.sum(probs, axis=1, keepdims=True)
        summed = sums[:, cols] * shrink + dot_nn(probs.astype(BF16), relay[frames : 2 * frames, cols])
        att[:, cols] = (summed / total).astype(BF16)
        lse_tile = jnp.where(lane == h, top + jnp.log(total), lse_tile)
    lse[...] = lse_tile
    place = flags[3]
    attended = att[...]

    def share(target):
        block = weight[:, pl.ds(pl.multiple_of(target * width, 128), width)]
        return dot_nn(attended, block).astype(BF16)

    send[:, 0:width] = share(place ^ 3)
    send[:, width : 2 * width] = share(place ^ 1)
    keep[:, 0:width] = share(place ^ 2)
    keep[:, width : 2 * width] = share(place)
    q_message[0:frames, :] = q[...]
    put_terms(q_message, lse_tile)


def term_rows(row):
    width = row.shape[1]
    at = lax.broadcasted_iota(jnp.int32, (16, width), 0)
    block = jnp.zeros((16, width), F32)
    rest = row
    for k in range(3):
        term = rest.astype(BF16).astype(F32)
        rest = rest - term
        block = jnp.where(at == k, term, block)
    return block.astype(BF16)


def put_terms(message, tile):
    frames = tile.shape[0]
    rows = tile.T
    for h in range(message.shape[1] // HDIM):
        message[frames : frames + 16, head_cols(h)] = term_rows(rows[h : h + 1, :])


def terms_of(message, frames, cols):
    terms = message[frames : frames + 16, cols].astype(F32)
    return terms[0:1] + terms[1:2] + terms[2:3]


def hidden_body(flags, inputs, keep, core, across, cot, seen_a, seen_b, hidden, rims):
    frames, width = inputs.shape
    mine = slice(width, 2 * width)
    total = inputs[...].astype(F32) + keep[:, mine].astype(F32) + core[:, mine].astype(F32)
    hidden[...] = (total + across[...].astype(F32)).astype(BF16)
    wide = 2 * HALO
    rims[0:wide, :] = hidden[0:wide, :]
    rims[wide : 2 * wide, :] = hidden[frames - wide : frames, :]
    rims[2 * wide : 2 * wide + HALO, :] = cot[0:HALO, :]
    rims[2 * wide + HALO : 3 * wide, :] = cot[frames - HALO : frames, :]


def shifted_sum(load, taps_of, rows):
    total = None
    for b in range(8):
        part = None
        reach = rows if b == 0 else rows + 8
        for a in range(4):
            tap = taps_of(8 * a + b)
            if tap is None:
                continue
            term = tap * load(8 * a, reach)
            part = term if part is None else part + term
        if b:
            part = pltpu.roll(part, reach - b, 0)[0:rows]
        total = part if total is None else total + part
    return total


def silu_parts(conv, cots):
    gate = 1.0 / (1.0 + jnp.exp(-conv))
    grad = cots * (gate + conv * gate * (1.0 - gate))
    return conv * gate, grad.astype(BF16).astype(F32)


def taps_forward(taps, cols):
    count = taps.shape[0]
    return lambda s: taps[s - 1 : s, cols] if 1 <= s <= count else None


def taps_backward(taps, cols):
    count = taps.shape[0]
    return lambda s: taps[count - s : count - s + 1, cols] if 1 <= s <= count else None


def conv_inner_body(hidden, cot, taps, rows_out, edge_conv, part_grad, padded, grads):
    frames, width = hidden.shape
    wide = 2 * HALO
    padded[0:wide, :] = jnp.zeros((wide, width), F32)
    padded[wide : wide + frames, :] = hidden[...].astype(F32)
    padded[wide + frames : 2 * wide + frames, :] = jnp.zeros((wide, width), F32)
    grads[0:wide, :] = jnp.zeros((wide, width), F32)
    grads[frames : frames + wide, :] = jnp.zeros((wide, width), F32)
    inner = slice(HALO, frames - HALO)
    for c in range(0, width, 128):
        cols = slice(c, c + 128)
        conv = shifted_sum(
            lambda at, rows: padded[at : at + rows, cols], taps_forward(taps, cols), frames + wide
        )
        edge_conv[0:wide, cols] = conv[0:wide]
        edge_conv[wide : 2 * wide, cols] = conv[frames : frames + wide]
        cots = cot[:, cols].astype(F32)
        silu, grad = silu_parts(conv[wide:frames], cots[inner])
        rows_out[inner, cols] = (hidden[inner, cols].astype(F32) + silu).astype(BF16)
        grads[wide:frames, cols] = grad
        back = shifted_sum(
            lambda at, rows: grads[at : at + rows, cols], taps_backward(taps, cols), frames
        )
        part_grad[:, cols] = cots + back


def conv_edge_body(
    flags, hidden, rim_near, rim_first, cot, taps, rows_in, edge_conv, part_grad,
    output, grad_input, grad_copy, padded, grads,
):
    frames, width = hidden.shape
    wide = 2 * HALO
    even = flags[0] > 0
    have = jnp.where(flags[2] > 0, jnp.float32(1.0), jnp.float32(0.0))
    low_ok = jnp.where(even, have, jnp.float32(1.0))
    high_ok = jnp.where(even, jnp.float32(1.0), have)

    def low_of(rows):
        return jnp.where(even, rim_first[rows, :].astype(F32), rim_near[rows, :].astype(F32)) * low_ok

    def high_of(rows):
        return jnp.where(even, rim_near[rows, :].astype(F32), rim_first[rows, :].astype(F32)) * high_ok

    padded[0:wide, :] = low_of(slice(wide, 2 * wide))
    padded[wide : 2 * wide, :] = jnp.zeros((wide, width), F32)
    padded[2 * wide : 3 * wide, :] = high_of(slice(0, wide))
    grads[wide : 2 * wide, :] = jnp.zeros((wide, width), F32)
    cot_low = low_of(slice(2 * wide + HALO, 3 * wide))
    cot_high = high_of(slice(2 * wide, 2 * wide + HALO))
    low, high = slice(0, HALO), slice(frames - HALO, frames)
    inner = slice(HALO, frames - HALO)
    output[inner, :] = rows_in[inner, :]
    for c in range(0, width, 128):
        cols = slice(c, c + 128)
        conv = edge_conv[:, cols] + shifted_sum(
            lambda at, rows: padded[at : at + rows, cols], taps_forward(taps, cols), 2 * wide
        )
        cots = jnp.concatenate(
            [cot_low[:, cols], cot[low, cols].astype(F32), cot[high, cols].astype(F32), cot_high[:, cols]],
            axis=0,
        )
        silu, grad = silu_parts(conv, cots)
        output[low, cols] = (hidden[low, cols].astype(F32) + silu[HALO:wide]).astype(BF16)
        output[high, cols] = (hidden[high, cols].astype(F32) + silu[wide : wide + HALO]).astype(BF16)
        grads[0:wide, cols] = grad[0:wide]
        grads[2 * wide : 3 * wide, cols] = grad[wide : 2 * wide]
        back = shifted_sum(
            lambda at, rows: grads[at : at + rows, cols], taps_backward(taps, cols), 2 * wide
        )
        part = part_grad[:, cols]
        total = jnp.concatenate(
            [part[0:wide] + back[0:wide], part[wide : frames - wide], part[frames - wide :] + back[wide:]],
            axis=0,
        ).astype(BF16)
        grad_input[:, cols] = total
        grad_copy[:, cols] = total


def upstream_body(flags, own, core, across, cross, weight, att, seen_a, seen_b, message, delta):
    frames, width = own.shape
    place = flags[3]
    total = None
    for flip, block in ((0, own), (1, core), (2, across), (3, cross)):
        at = pl.ds(pl.multiple_of((place ^ flip) * width, 128), width)
        part = dot_nt(block[...], weight[:, at])
        total = part if total is None else total + part
    up = total.astype(BF16)
    message[0:frames, :] = up
    lane = lax.broadcasted_iota(jnp.int32, (frames, HDIM), 1)
    tile = jnp.zeros((frames, HDIM), F32)
    for h in range(width // HDIM):
        cols = head_cols(h)
        product = up[:, cols].astype(F32) * att[:, cols].astype(F32)
        tile = jnp.where(lane == h, jnp.sum(product, axis=1, keepdims=True), tile)
    delta[...] = tile
    put_terms(message, tile)


def query_grad_body(scale, flags, q, own, near, first, second, relay, message, lse, delta, grad_query):
    frames, width = q.shape
    kvs = (near, relay, own, first, second)
    biases = (off_bias(flags[1]), off_bias(flags[2]))
    for h in range(width // HDIM):
        cols = head_cols(h)
        keys = stacked(kvs, slice(0, frames), cols)
        scores = dot_nt(q[:, cols], keys) * scale - lse[:, h : h + 1]
        scores = jnp.concatenate(
            [scores[:, 0:frames] + biases[0], scores[:, frames : 2 * frames] + biases[1]]
            + [scores[:, 2 * frames :]],
            axis=1,
        )
        dots = dot_nt(message[0:frames, cols], stacked(kvs, slice(frames, 2 * frames), cols))
        grads = (jnp.exp(scores) * (dots - delta[:, h : h + 1]) * scale).astype(BF16)
        grad_query[:, cols] = dot_nn(grads, keys).astype(BF16)


def key_terms(scale, own, queries, messages, biases, cols):
    frames = own.shape[0] // 2
    asks = stacked(queries, slice(0, frames), cols)
    ups = stacked(messages, slice(0, frames), cols)
    scores = dot_nt(own[0:frames, cols], asks) * scale
    dots = dot_nt(own[frames : 2 * frames, cols], ups)
    probs_low, grads = [], []
    for b, bias in enumerate(biases):
        at = slice(b * frames, (b + 1) * frames)
        part = scores[:, at] - terms_of(queries[b], frames, cols)
        probs = jnp.exp(part if bias is None else part + bias)
        probs_low.append(probs.astype(BF16))
        grads.append((probs * (dots[:, at] - terms_of(messages[b], frames, cols)) * scale).astype(BF16))
    key_part = dot_nn(jnp.concatenate(grads, axis=1), asks)
    return key_part, dot_nn(jnp.concatenate(probs_low, axis=1), ups)


def key_part_body(scale, flags, own, *refs):
    queries, messages, (key_part, value_part) = refs[0:4], refs[4:8], refs[8:10]
    biases = (None, off_bias(flags[1]), None, None)
    for h in range(own.shape[1] // HDIM):
        cols = head_cols(h)
        key_part[:, cols], value_part[:, cols] = key_terms(scale, own, queries, messages, biases, cols)


def key_grad_body(scale, flags, own, query, message, key_part, value_part, grad_key, grad_value):
    biases = (off_bias(flags[2]),)
    for h in range(own.shape[1] // HDIM):
        cols = head_cols(h)
        keys, values = key_terms(scale, own, (query,), (message,), biases, cols)
        grad_key[:, cols] = (key_part[:, cols] + keys).astype(BF16)
        grad_value[:, cols] = (value_part[:, cols] + values).astype(BF16)


def per_device(query_rows, key_rows, value_rows, inputs, out_weight, kernel, cotangent):
    frames, width = query_rows.shape
    whole = out_weight.shape[1]
    wide = 2 * HALO
    scale = 1.0 / math.sqrt(HDIM)
    block, count = lax.axis_index("ctx"), lax.axis_size("ctx")
    even = block % 2 == 0
    lower, upper = block >= 2, block < count - 2
    flags = jnp.stack(
        [even, lower & upper, jnp.where(even, lower, upper), lax.axis_index("mp")]
    ).astype(jnp.int32)
    tile = shaped((frames, width), BF16)
    tile32 = shaped((frames, width), F32)
    half = shaped((frames, 2 * width), BF16)
    side = shaped((frames, HDIM), F32)
    noted = shaped((frames + 16, width), BF16)
    square = frames * frames * width

    (kv,) = kernel_call(
        pack_body, (shaped((2 * frames, width), BF16),), (key_rows, value_rows), 0, "pack",
        [HBM] * 2, [pltpu.SemaphoreType.DMA((2,))], 60, HBM,
    )
    near, first, second, relay = window_of(kv)
    (weight,) = kernel_call(
        fetch_body, (shaped(out_weight.shape, BF16),), (out_weight, second), 0, "fetch",
        [HBM, ANY], [pltpu.SemaphoreType.DMA(())],
    )
    sums, tops, totals = kernel_call(
        functools.partial(forward_body, scale),
        (tile32, side, side),
        (flags, query_rows, kv, near, first, second),
        16 * square, "forward",
    )
    att, lse, send, keep, q_own = kernel_call(
        functools.partial(project_body, scale),
        (tile, side, half, half, noted),
        (flags, query_rows, relay, sums, tops, totals, weight),
        4 * square + 2 * frames * width * whole, "project",
    )

    core = pair_swap(send, "mp", 1)
    across = pair_swap(keep[:, 0:width] + core[:, 0:width], "mp", 2)
    q_second = ring(q_own, 1)
    q_first = ring(q_own, 0)
    hidden, rims = kernel_call(
        hidden_body,
        (tile, shaped((3 * wide, width), BF16)),
        (flags, inputs, keep, core, across, cotangent, q_second, q_first),
        4 * frames * width, "hidden", [SMEM] + [VMEM] * 5 + [ANY] * 2,
    )

    rim_near = pair_swap(rims, "ctx", 1)
    rows_out, edge_conv, part_grad = kernel_call(
        conv_inner_body,
        (tile, shaped((2 * wide, width), F32), tile32),
        (hidden, cotangent, kernel),
        140 * frames * width, "conv_inner", [VMEM] * 3,
        [pltpu.VMEM((frames + 2 * wide, width), F32), pltpu.VMEM((frames + wide, width), F32)],
    )
    rim_first = ring(rim_near, 0)
    output, grad_input, grad_copy = kernel_call(
        conv_edge_body,
        (tile, tile, tile),
        (flags, hidden, rim_near, rim_first, cotangent, kernel, rows_out, edge_conv, part_grad),
        70 * frames * width, "conv_edge", None,
        [pltpu.VMEM((3 * wide, width), F32), pltpu.VMEM((3 * wide, width), F32)],
    )

    gi_across = pair_swap(grad_copy, "mp", 2)
    gi_core = pair_swap(grad_copy, "mp", 1)
    q_near = inner_swap(q_own)
    q_relay = pair_swap(q_second, "ctx", 1)
    gi_cross = pair_swap(gi_across, "mp", 1)
    message, delta = kernel_call(
        upstream_body,
        (noted, side),
        (flags, grad_copy, gi_core, gi_across, gi_cross, weight, att, q_near, q_relay),
        2 * frames * width * whole, "upstream", [SMEM] + [VMEM] * 6 + [ANY] * 2,
    )

    m_near, m_first, m_second, m_relay = window_of(message)
    (grad_query,) = kernel_call(
        functools.partial(query_grad_body, scale),
        (tile,),
        (flags, query_rows, kv, near, first, second, relay, message, lse, delta),
        30 * square, "query_grad",
    )
    key_part, value_part = kernel_call(
        functools.partial(key_part_body, scale),
        (tile32, tile32),
        (flags, kv, q_own, q_near, q_first, q_second, message, m_near, m_first, m_second),
        32 * square, "key_part",
    )
    grad_key, grad_value = kernel_call(
        functools.partial(key_grad_body, scale),
        (tile, tile),
        (flags, kv, q_relay, m_relay, key_part, value_part),
        8 * square, "key_grad",
    )
    return (output, grad_input, grad_query, grad_key, grad_value)


def solution(mesh):
    rows = P("ctx", "mp")
    return jax.shard_map(
        per_device,
        mesh=mesh,
        in_specs=(rows, rows, rows, rows, P("mp", None), P(None, "mp"), rows),
        out_specs=(rows,) * 5,
        check_vma=False,
    )
```

```python
import functools
import math

import jax
import jax.numpy as jnp
from jax import lax
from jax.experimental import pallas as pl
from jax.experimental.pallas import tpu as pltpu
from jax.sharding import PartitionSpec as P

HDIM = 128
F32 = jnp.float32
BF16 = jnp.bfloat16
HALO = 16
NT = (((1,), (1,)), ((), ()))
NN = (((1,), (0,)), ((), ()))


def dot_nt(a, b):
    return lax.dot_general(a, b, NT, preferred_element_type=F32)


def dot_nn(a, b):
    return lax.dot_general(a, b, NN, preferred_element_type=F32)


def pair_swap(block, axis, bit):
    return lax.ppermute(block, axis, [(i, i ^ bit) for i in range(lax.axis_size(axis))])


def ring_routes(count):
    rise = [(i, i + 2) for i in range(0, count - 2, 2)] + [(count - 2, count - 1)]
    fall = [(i, i - 2) for i in range(count - 1, 2, -2)] + [(1, 0)]
    route = rise + fall
    return route, [(b, a) for a, b in route]


def ring(block, way):
    return lax.ppermute(block, "ctx", ring_routes(lax.axis_size("ctx"))[way])


def total_swap(block, partner_of):
    count, places = lax.axis_size("ctx"), lax.axis_size("mp")
    route = []
    for i in range(count):
        other = partner_of(i, count)
        for m in range(places):
            target = i * places + (m ^ 1) if other is None else other * places + m
            route.append((i * places + m, target))
    return lax.ppermute(block, ("ctx", "mp"), route)


def inner_swap(block):
    return total_swap(block, lambda i, count: i ^ 1 if 2 <= i < count - 2 else None)


def outer_swap(block):
    return total_swap(block, lambda i, count: ((i + 1) ^ 1) - 1 if 0 < i < count - 1 else None)


def window_of(block):
    second = ring(block, 1)
    first = ring(block, 0)
    near = inner_swap(block)
    return near, first, second, pair_swap(second, "ctx", 1)


SMEM = pl.BlockSpec(memory_space=pltpu.SMEM)
VMEM = pl.BlockSpec(memory_space=pltpu.VMEM)
ANY = pl.BlockSpec(memory_space=pl.ANY)
HBM = pl.BlockSpec(memory_space=pltpu.HBM)


def kernel_call(body, outs, args, flops, name, spaces=None, scratch=(), mib=24, out_space=VMEM):
    nbytes = sum(math.prod(a.shape) * a.dtype.itemsize for a in list(args) + list(outs))
    return pl.pallas_call(
        body,
        out_shape=outs,
        in_specs=spaces or [SMEM] + [VMEM] * (len(args) - 1),
        out_specs=tuple(out_space for _ in outs),
        scratch_shapes=scratch,
        compiler_params=pltpu.CompilerParams(vmem_limit_bytes=mib * 1024 * 1024),
        cost_estimate=pl.CostEstimate(flops=flops, bytes_accessed=nbytes, transcendentals=0),
        name=name,
    )(*args)


def shaped(shape, dtype):
    return jax.ShapeDtypeStruct(shape, dtype)


def off_bias(flag):
    return jnp.where(flag > 0, jnp.float32(0.0), jnp.float32(-jnp.inf))


def head_cols(h):
    return slice(h * HDIM, (h + 1) * HDIM)


def stacked(kvs, rows, cols):
    return jnp.concatenate([kv[rows, cols] for kv in kvs], axis=0)


def fetch_body(weight, seen, fetched, sem):
    copy = pltpu.make_async_copy(weight, fetched, sem)
    copy.start()
    copy.wait()


def forward_body(scale, flags, q, own, near, first, second, sums, tops, totals):
    frames, width = q.shape
    kvs = (near, own, first, second)
    lane = lax.broadcasted_iota(jnp.int32, (frames, HDIM), 1)
    top_tile = jnp.zeros((frames, HDIM), F32)
    total_tile = jnp.zeros((frames, HDIM), F32)
    bias = off_bias(flags[1])
    for h in range(width // HDIM):
        cols = head_cols(h)
        scores = dot_nt(q[:, cols], stacked(kvs, slice(0, frames), cols)) * scale
        scores = jnp.concatenate([scores[:, 0:frames] + bias, scores[:, frames:]], axis=1)
        top = jnp.max(scores, axis=1, keepdims=True)
        probs = jnp.exp(scores - top)
        sums[:, cols] = dot_nn(probs.astype(BF16), stacked(kvs, slice(frames, 2 * frames), cols))
        top_tile = jnp.where(lane == h, top, top_tile)
        total_tile = jnp.where(lane == h, jnp.sum(probs, axis=1, keepdims=True), total_tile)
    tops[...] = top_tile
    totals[...] = total_tile


def project_body(scale, flags, q, relay, sums, tops, totals, weight, att, lse, send, keep, q_message):
    frames, width = q.shape
    lane = lax.broadcasted_iota(jnp.int32, (frames, HDIM), 1)
    lse_tile = jnp.zeros((frames, HDIM), F32)
    bias = off_bias(flags[2])
    for h in range(width // HDIM):
        cols = head_cols(h)
        scores = dot_nt(q[:, cols], relay[0:frames, cols]) * scale + bias
        old_top = tops[:, h : h + 1]
        top = jnp.maximum(old_top, jnp.max(scores, axis=1, keepdims=True))
        shrink = jnp.exp(old_top - top)
        probs = jnp.exp(scores - top)
        total = totals[:, h : h + 1] * shrink + jnp.sum(probs, axis=1, keepdims=True)
        summed = sums[:, cols] * shrink + dot_nn(probs.astype(BF16), relay[frames : 2 * frames, cols])
        att[:, cols] = (summed / total).astype(BF16)
        lse_tile = jnp.where(lane == h, top + jnp.log(total), lse_tile)
    lse[...] = lse_tile
    place = flags[3]
    attended = att[...]

    def share(target):
        block = weight[:, pl.ds(pl.multiple_of(target * width, 128), width)]
        return dot_nn(attended, block).astype(BF16)

    send[:, 0:width] = share(place ^ 3)
    send[:, width : 2 * width] = share(place ^ 1)
    keep[:, 0:width] = share(place ^ 2)
    keep[:, width : 2 * width] = share(place)
    q_message[0:frames, :] = q[...]
    put_terms(q_message, lse_tile)


def term_rows(row):
    width = row.shape[1]
    at = lax.broadcasted_iota(jnp.int32, (16, width), 0)
    block = jnp.zeros((16, width), F32)
    rest = row
    for k in range(3):
        term = rest.astype(BF16).astype(F32)
        rest = rest - term
        block = jnp.where(at == k, term, block)
    return block.astype(BF16)


def put_terms(message, tile):
    frames = tile.shape[0]
    rows = tile.T
    for h in range(message.shape[1] // HDIM):
        message[frames : frames + 16, head_cols(h)] = term_rows(rows[h : h + 1, :])


def terms_of(message, frames, cols):
    terms = message[frames : frames + 16, cols].astype(F32)
    return terms[0:1] + terms[1:2] + terms[2:3]


def hidden_body(flags, inputs, keep, core, across, cot, seen_a, seen_b, hidden, rim_near, rim_far):
    frames, width = inputs.shape
    wide = 2 * HALO
    mine = slice(width, 2 * width)
    total = inputs[...].astype(F32) + keep[:, mine].astype(F32) + core[:, mine].astype(F32)
    total = (total + across[...].astype(F32)).astype(BF16)
    hidden[...] = total
    even = flags[0] > 0
    for at, first, last in (
        (slice(0, wide), total[0:wide], total[frames - wide :]),
        (slice(wide, wide + HALO), cot[0:HALO, :], cot[frames - HALO : frames, :]),
    ):
        first, last = first.astype(F32), last.astype(F32)
        rim_near[at, :] = jnp.where(even, last, first).astype(BF16)
        rim_far[at, :] = jnp.where(even, first, last).astype(BF16)


def shifted_sum(load, taps_of, rows):
    total = None
    for b in range(8):
        part = None
        reach = rows if b == 0 else rows + 8
        for a in range(4):
            tap = taps_of(8 * a + b)
            if tap is None:
                continue
            term = tap * load(8 * a, reach)
            part = term if part is None else part + term
        if b:
            part = pltpu.roll(part, reach - b, 0)[0:rows]
        total = part if total is None else total + part
    return total


def silu_parts(conv, cots):
    gate = 1.0 / (1.0 + jnp.exp(-conv))
    grad = cots * (gate + conv * gate * (1.0 - gate))
    return conv * gate, grad.astype(BF16).astype(F32)


def taps_forward(taps, cols):
    count = taps.shape[0]
    return lambda s: taps[s - 1 : s, cols] if 1 <= s <= count else None


def taps_backward(taps, cols):
    count = taps.shape[0]
    return lambda s: taps[count - s : count - s + 1, cols] if 1 <= s <= count else None


def conv_inner_body(hidden, cot, taps, rows_out, edge_conv, part_grad, padded, grads):
    frames, width = hidden.shape
    wide = 2 * HALO
    padded[0:wide, :] = jnp.zeros((wide, width), F32)
    padded[wide : wide + frames, :] = hidden[...].astype(F32)
    padded[wide + frames : 2 * wide + frames, :] = jnp.zeros((wide, width), F32)
    grads[0:wide, :] = jnp.zeros((wide, width), F32)
    grads[frames : frames + wide, :] = jnp.zeros((wide, width), F32)
    inner = slice(HALO, frames - HALO)
    for c in range(0, width, 128):
        cols = slice(c, c + 128)
        conv = shifted_sum(
            lambda at, rows: padded[at : at + rows, cols], taps_forward(taps, cols), frames + wide
        )
        edge_conv[0:wide, cols] = conv[0:wide]
        edge_conv[wide : 2 * wide, cols] = conv[frames : frames + wide]
        cots = cot[:, cols].astype(F32)
        silu, grad = silu_parts(conv[wide:frames], cots[inner])
        rows_out[inner, cols] = (hidden[inner, cols].astype(F32) + silu).astype(BF16)
        grads[wide:frames, cols] = grad
        back = shifted_sum(
            lambda at, rows: grads[at : at + rows, cols], taps_backward(taps, cols), frames
        )
        part_grad[:, cols] = cots + back


def conv_edge_body(
    flags, hidden, rim_near, rim_far, cot, taps, rows_in, edge_conv, part_grad,
    output, grad_input, padded, grads,
):
    frames, width = hidden.shape
    wide = 2 * HALO
    even = flags[0] > 0
    have = jnp.where(flags[2] > 0, jnp.float32(1.0), jnp.float32(0.0))
    low_ok = jnp.where(even, have, jnp.float32(1.0))
    high_ok = jnp.where(even, jnp.float32(1.0), have)
    rims, cots_of = slice(0, wide), slice(wide, wide + HALO)

    def low_of(rows):
        return jnp.where(even, rim_far[rows, :].astype(F32), rim_near[rows, :].astype(F32)) * low_ok

    def high_of(rows):
        return jnp.where(even, rim_near[rows, :].astype(F32), rim_far[rows, :].astype(F32)) * high_ok

    padded[0:wide, :] = low_of(rims)
    padded[wide : 2 * wide, :] = jnp.zeros((wide, width), F32)
    padded[2 * wide : 3 * wide, :] = high_of(rims)
    grads[wide : 2 * wide, :] = jnp.zeros((wide, width), F32)
    cot_low, cot_high = low_of(cots_of), high_of(cots_of)
    low, high = slice(0, HALO), slice(frames - HALO, frames)
    inner = slice(HALO, frames - HALO)
    output[inner, :] = rows_in[inner, :]
    for c in range(0, width, 128):
        cols = slice(c, c + 128)
        conv = edge_conv[:, cols] + shifted_sum(
            lambda at, rows: padded[at : at + rows, cols], taps_forward(taps, cols), 2 * wide
        )
        cots = jnp.concatenate(
            [cot_low[:, cols], cot[low, cols].astype(F32), cot[high, cols].astype(F32), cot_high[:, cols]],
            axis=0,
        )
        silu, grad = silu_parts(conv, cots)
        output[low, cols] = (hidden[low, cols].astype(F32) + silu[HALO:wide]).astype(BF16)
        output[high, cols] = (hidden[high, cols].astype(F32) + silu[wide : wide + HALO]).astype(BF16)
        grads[0:wide, cols] = grad[0:wide]
        grads[2 * wide : 3 * wide, cols] = grad[wide : 2 * wide]
        back = shifted_sum(
            lambda at, rows: grads[at : at + rows, cols], taps_backward(taps, cols), 2 * wide
        )
        part = part_grad[:, cols]
        grad_input[:, cols] = jnp.concatenate(
            [part[0:wide] + back[0:wide], part[wide : frames - wide], part[frames - wide :] + back[wide:]],
            axis=0,
        ).astype(BF16)


def upstream_part(flags, weight, pieces):
    width = weight.shape[0]
    total = None
    for flip, block in pieces:
        at = pl.ds(pl.multiple_of((flags[3] ^ flip) * width, 128), width)
        part = dot_nt(block[...], weight[:, at])
        total = part if total is None else total + part
    return total


def upstream_chip_body(flags, own, core, weight, partial):
    partial[...] = upstream_part(flags, weight, ((0, own), (1, core)))


def upstream_body(flags, across, cross, weight, att, partial, seen_a, seen_b, message, delta):
    frames, width = across.shape
    total = partial[...] + upstream_part(flags, weight, ((2, across), (3, cross)))
    up = total.astype(BF16)
    message[0:frames, :] = up
    lane = lax.broadcasted_iota(jnp.int32, (frames, HDIM), 1)
    tile = jnp.zeros((frames, HDIM), F32)
    for h in range(width // HDIM):
        cols = head_cols(h)
        product = up[:, cols].astype(F32) * att[:, cols].astype(F32)
        tile = jnp.where(lane == h, jnp.sum(product, axis=1, keepdims=True), tile)
    delta[...] = tile
    put_terms(message, tile)


def query_grad_body(
    scale, flags, q, own, near, first, second, relay, message, lse, delta, output_here, grad_here,
    output, grad_input, grad_query, held, sems,
):
    writes = [
        pltpu.make_async_copy(output_here, output, sems.at[0]),
        pltpu.make_async_copy(grad_here, grad_input, sems.at[1]),
    ]
    for write in writes:
        write.start()
    frames, width = q.shape
    kvs = (near, relay, own, first, second)
    biases = (off_bias(flags[1]), off_bias(flags[2]))
    for h in range(width // HDIM):
        cols = head_cols(h)
        keys = stacked(kvs, slice(0, frames), cols)
        scores = dot_nt(q[:, cols], keys) * scale - lse[:, h : h + 1]
        scores = jnp.concatenate(
            [scores[:, 0:frames] + biases[0], scores[:, frames : 2 * frames] + biases[1]]
            + [scores[:, 2 * frames :]],
            axis=1,
        )
        dots = dot_nt(message[0:frames, cols], stacked(kvs, slice(frames, 2 * frames), cols))
        grads = (jnp.exp(scores) * (dots - delta[:, h : h + 1]) * scale).astype(BF16)
        held[:, cols] = dot_nn(grads, keys).astype(BF16)
    writes.append(pltpu.make_async_copy(held, grad_query, sems.at[2]))
    writes[2].start()
    for write in writes:
        write.wait()


def key_probs(scale, own, queries, biases, cols):
    frames = own.shape[0] // 2
    scores = dot_nt(own[0:frames, cols], stacked(queries, slice(0, frames), cols)) * scale
    parts = []
    for b, bias in enumerate(biases):
        part = scores[:, b * frames : (b + 1) * frames] - terms_of(queries[b], frames, cols)
        parts.append(jnp.exp(part if bias is None else part + bias))
    return jnp.concatenate(parts, axis=1)


def value_terms(probs, messages, cols):
    frames = probs.shape[0]
    return dot_nn(probs.astype(BF16), stacked(messages, slice(0, frames), cols))


def key_terms(scale, own, probs, queries, messages, cols):
    frames = own.shape[0] // 2
    dots = dot_nt(own[frames : 2 * frames, cols], stacked(messages, slice(0, frames), cols))
    deltas = jnp.concatenate([terms_of(m, frames, cols) for m in messages], axis=1)
    grads = (probs * (dots - deltas) * scale).astype(BF16)
    return dot_nn(grads, stacked(queries, slice(0, frames), cols))


def key_part_body(scale, flags, own, *refs):
    queries, late_query, messages, (key_part, value_part, late) = refs[0:4], refs[4], refs[5:9], refs[9:12]
    biases = (None, off_bias(flags[1]), None, None)
    for h in range(own.shape[1] // HDIM):
        cols = head_cols(h)
        probs = key_probs(scale, own, queries, biases, cols)
        value_part[:, cols] = value_terms(probs, messages, cols)
        key_part[:, cols] = key_terms(scale, own, probs, queries, messages, cols)
        late[:, cols] = key_probs(scale, own, (late_query,), (off_bias(flags[2]),), cols)


def key_grad_body(
    scale, own, query, message, late, key_part, value_part, grad_key, grad_value, held_key, held_value, sems
):
    heads = [head_cols(h) for h in range(own.shape[1] // HDIM)]
    for cols in heads:
        held_value[:, cols] = (value_part[:, cols] + value_terms(late[:, cols], (message,), cols)).astype(BF16)
    value_write = pltpu.make_async_copy(held_value, grad_value, sems.at[0])
    value_write.start()
    for cols in heads:
        keys = key_terms(scale, own, late[:, cols], (query,), (message,), cols)
        held_key[:, cols] = (key_part[:, cols] + keys).astype(BF16)
    key_write = pltpu.make_async_copy(held_key, grad_key, sems.at[1])
    key_write.start()
    value_write.wait()
    key_write.wait()


def per_device(query_rows, key_rows, value_rows, inputs, out_weight, kernel, cotangent):
    frames, width = query_rows.shape
    whole = out_weight.shape[1]
    wide = 2 * HALO
    scale = 1.0 / math.sqrt(HDIM)
    block, count = lax.axis_index("ctx"), lax.axis_size("ctx")
    even = block % 2 == 0
    lower, upper = block >= 2, block < count - 2
    flags = jnp.stack(
        [even, lower & upper, jnp.where(even, lower, upper), lax.axis_index("mp")]
    ).astype(jnp.int32)
    tile = shaped((frames, width), BF16)
    tile32 = shaped((frames, width), F32)
    half = shaped((frames, 2 * width), BF16)
    side = shaped((frames, HDIM), F32)
    rim = shaped((wide + HALO, width), BF16)
    noted = shaped((frames + 16, width), BF16)
    square = frames * frames * width

    zero = jnp.zeros((), BF16)
    kv = lax.pad(key_rows, zero, ((0, frames, 0), (0, 0, 0))) + lax.pad(
        value_rows, zero, ((frames, 0, 0), (0, 0, 0))
    )
    near, first, second, relay = window_of(kv)
    (weight,) = kernel_call(
        fetch_body, (shaped(out_weight.shape, BF16),), (out_weight, second), 0, "fetch",
        [HBM, ANY], [pltpu.SemaphoreType.DMA(())],
    )
    sums, tops, totals = kernel_call(
        functools.partial(forward_body, scale),
        (tile32, side, side),
        (flags, query_rows, kv, near, first, second),
        16 * square, "forward",
    )
    att, lse, send, keep, q_own = kernel_call(
        functools.partial(project_body, scale),
        (tile, side, half, half, noted),
        (flags, query_rows, relay, sums, tops, totals, weight),
        4 * square + 2 * frames * width * whole, "project",
    )

    core = pair_swap(send, "mp", 1)
    across = pair_swap(keep[:, 0:width] + core[:, 0:width], "mp", 2)
    q_second = ring(q_own, 1)
    q_first = ring(q_own, 0)
    hidden, rim_up, rim_down = kernel_call(
        hidden_body,
        (tile, rim, rim),
        (flags, inputs, keep, core, across, cotangent, q_second, q_first),
        4 * frames * width, "hidden", [SMEM] + [VMEM] * 5 + [ANY] * 2,
    )

    rim_far = outer_swap(rim_down)
    rim_near = pair_swap(rim_up, "ctx", 1)
    rows_out, edge_conv, part_grad = kernel_call(
        conv_inner_body,
        (tile, shaped((2 * wide, width), F32), tile32),
        (hidden, cotangent, kernel),
        140 * frames * width, "conv_inner", [VMEM] * 3,
        [pltpu.VMEM((frames + 2 * wide, width), F32), pltpu.VMEM((frames + wide, width), F32)],
    )
    output_here, grad_here = kernel_call(
        conv_edge_body,
        (tile, tile),
        (flags, hidden, rim_near, rim_far, cotangent, kernel, rows_out, edge_conv, part_grad),
        70 * frames * width, "conv_edge", None,
        [pltpu.VMEM((3 * wide, width), F32), pltpu.VMEM((3 * wide, width), F32)],
    )

    gi_across = pair_swap(grad_here, "mp", 2)
    gi_core = pair_swap(grad_here, "mp", 1)
    q_near = inner_swap(q_own)
    q_relay = pair_swap(q_second, "ctx", 1)
    gi_cross = pair_swap(gi_across, "mp", 1)
    (partial,) = kernel_call(
        upstream_chip_body, (tile32,), (flags, grad_here, gi_core, weight),
        frames * width * whole, "upstream_chip",
    )
    message, delta = kernel_call(
        upstream_body,
        (noted, side),
        (flags, gi_across, gi_cross, weight, att, partial, q_near, q_relay),
        frames * width * whole, "upstream", [SMEM] + [VMEM] * 5 + [ANY] * 2,
    )

    m_near, m_first, m_second, m_relay = window_of(message)
    output, grad_input, grad_query = kernel_call(
        functools.partial(query_grad_body, scale),
        (tile, tile, tile),
        (flags, query_rows, kv, near, first, second, relay, message, lse, delta)
        + (output_here, grad_here),
        30 * square, "query_grad", None,
        [pltpu.VMEM((frames, width), BF16), pltpu.SemaphoreType.DMA((3,))], 24, HBM,
    )
    key_part, value_part, late = kernel_call(
        functools.partial(key_part_body, scale),
        (tile32, tile32, tile32),
        (flags, kv, q_own, q_near, q_first, q_second, q_relay, message, m_near, m_first, m_second),
        34 * square, "key_part",
    )
    grad_key, grad_value = kernel_call(
        functools.partial(key_grad_body, scale),
        (tile, tile),
        (kv, q_relay, m_relay, late, key_part, value_part),
        6 * square, "key_grad", [VMEM] * 6,
        [pltpu.VMEM((frames, width), BF16)] * 2 + [pltpu.SemaphoreType.DMA((2,))], 24, HBM,
    )
    return (output, grad_input, grad_query, grad_key, grad_value)


def solution(mesh):
    rows = P("ctx", "mp")
    return jax.shard_map(
        per_device,
        mesh=mesh,
        in_specs=(rows, rows, rows, rows, P("mp", None), P(None, "mp"), rows),
        out_specs=(rows,) * 5,
        check_vma=False,
    )
```

```python
import functools
import math

import jax
import jax.numpy as jnp
from jax import lax
from jax.experimental import pallas as pl
from jax.experimental.pallas import tpu as pltpu
from jax.sharding import PartitionSpec as P

HDIM = 128
F32 = jnp.float32
BF16 = jnp.bfloat16
HALO = 16
NT = (((1,), (1,)), ((), ()))
NN = (((1,), (0,)), ((), ()))


def dot_nt(a, b):
    return lax.dot_general(a, b, NT, preferred_element_type=F32)


def dot_nn(a, b):
    return lax.dot_general(a, b, NN, preferred_element_type=F32)


def pair_swap(block, axis, bit):
    return lax.ppermute(block, axis, [(i, i ^ bit) for i in range(lax.axis_size(axis))])


def ring_routes(count):
    rise = [(i, i + 2) for i in range(0, count - 2, 2)] + [(count - 2, count - 1)]
    fall = [(i, i - 2) for i in range(count - 1, 2, -2)] + [(1, 0)]
    route = rise + fall
    return route, [(b, a) for a, b in route]


def ring(block, way):
    return lax.ppermute(block, "ctx", ring_routes(lax.axis_size("ctx"))[way])


def total_swap(block, partner_of):
    count, places = lax.axis_size("ctx"), lax.axis_size("mp")
    route = []
    for i in range(count):
        other = partner_of(i, count)
        for m in range(places):
            target = i * places + (m ^ 1) if other is None else other * places + m
            route.append((i * places + m, target))
    return lax.ppermute(block, ("ctx", "mp"), route)


def inner_swap(block):
    return total_swap(block, lambda i, count: i ^ 1 if 2 <= i < count - 2 else None)


def outer_swap(block):
    return total_swap(block, lambda i, count: ((i + 1) ^ 1) - 1 if 0 < i < count - 1 else None)


def window_of(block):
    second = ring(block, 1)
    first = ring(block, 0)
    near = inner_swap(block)
    return near, first, second, pair_swap(second, "ctx", 1)


SMEM = pl.BlockSpec(memory_space=pltpu.SMEM)
VMEM = pl.BlockSpec(memory_space=pltpu.VMEM)
ANY = pl.BlockSpec(memory_space=pl.ANY)
HBM = pl.BlockSpec(memory_space=pltpu.HBM)


def kernel_call(body, outs, args, micros, name, spaces=None, scratch=(), mib=24, out_space=VMEM):
    return pl.pallas_call(
        body,
        out_shape=outs,
        in_specs=spaces or [SMEM] + [VMEM] * (len(args) - 1),
        out_specs=tuple(out_space for _ in outs),
        scratch_shapes=scratch,
        compiler_params=pltpu.CompilerParams(vmem_limit_bytes=mib * 1024 * 1024),
        cost_estimate=pl.CostEstimate(
            flops=0, bytes_accessed=int(micros * 3.69e6), transcendentals=0
        ),
        name=name,
    )(*args)


def shaped(shape, dtype):
    return jax.ShapeDtypeStruct(shape, dtype)


def off_bias(flag):
    return jnp.where(flag > 0, jnp.float32(0.0), jnp.float32(-jnp.inf))


def head_cols(h):
    return slice(h * HDIM, (h + 1) * HDIM)


def stacked(blocks, rows, cols):
    return jnp.concatenate([block[rows, cols] for block in blocks], axis=0)


def hold_body(block, seen, held):
    held[...] = block[...]


def forward_body(scale, flags, q, own, near, first, second, sums, tops, totals):
    frames, width = q.shape
    lane = lax.broadcasted_iota(jnp.int32, (frames, HDIM), 1)
    top_tile = jnp.zeros((frames, HDIM), F32)
    total_tile = jnp.zeros((frames, HDIM), F32)
    bias = off_bias(flags[1])
    blocks = (near, own, first, second)
    for h in range(width // HDIM):
        cols = head_cols(h)
        scores = dot_nt(q[:, cols], stacked(blocks, slice(0, frames), cols)) * scale
        scores = jnp.concatenate([scores[:, 0:frames] + bias, scores[:, frames:]], axis=1)
        top = jnp.max(scores, axis=1, keepdims=True)
        probs = jnp.exp(scores - top)
        sums[:, cols] = dot_nn(probs.astype(BF16), stacked(blocks, slice(frames, 2 * frames), cols))
        top_tile = jnp.where(lane == h, top, top_tile)
        total_tile = jnp.where(lane == h, jnp.sum(probs, axis=1, keepdims=True), total_tile)
    tops[...] = top_tile
    totals[...] = total_tile


def share_of(attended, weight, target):
    width = weight.shape[0]
    block = weight[:, pl.ds(pl.multiple_of(target * width, 128), width)]
    return dot_nn(attended, block).astype(BF16)


def project_body(
    scale, flags, q, relay, sums, tops, totals, weight, att, lse, send, keep
):
    frames, width = q.shape
    lane = lax.broadcasted_iota(jnp.int32, (frames, HDIM), 1)
    lse_tile = jnp.zeros((frames, HDIM), F32)
    bias = off_bias(flags[2])
    for h in range(width // HDIM):
        cols = head_cols(h)
        scores = dot_nt(q[:, cols], relay[0:frames, cols]) * scale + bias
        old_top = tops[:, h : h + 1]
        top = jnp.maximum(old_top, jnp.max(scores, axis=1, keepdims=True))
        shrink = jnp.exp(old_top - top)
        probs = jnp.exp(scores - top)
        total = totals[:, h : h + 1] * shrink + jnp.sum(probs, axis=1, keepdims=True)
        summed = sums[:, cols] * shrink + dot_nn(probs.astype(BF16), relay[frames : 2 * frames, cols])
        att[:, cols] = (summed / total).astype(BF16)
        lse_tile = jnp.where(lane == h, top + jnp.log(total), lse_tile)
    lse[...] = lse_tile
    attended = att[...]
    send[...] = share_of(attended, weight, flags[3] ^ 3)
    keep[...] = share_of(attended, weight, flags[3] ^ 2)


def join_body(keep, core, q, q_second, outgoing, q_copy, second_copy):
    outgoing[...] = (keep[...].astype(F32) + core[...].astype(F32)).astype(BF16)
    q_copy[...] = q[...]
    second_copy[...] = q_second[...]


def project_own_body(flags, att, weight, seen_a, seen_b, send, keep):
    attended = att[...]
    send[...] = share_of(attended, weight, flags[3] ^ 1)
    keep[...] = share_of(attended, weight, flags[3])


def term_rows(rows):
    width = rows[0].shape[1]
    at = lax.broadcasted_iota(jnp.int32, (16, width), 0)
    block = jnp.zeros((16, width), F32)
    for r, rest in enumerate(rows):
        for k in range(3):
            term = rest.astype(BF16).astype(F32)
            rest = rest - term
            block = jnp.where(at == 3 * r + k, term, block)
    return block.astype(BF16)


def put_terms(message, tiles):
    frames = tiles[0].shape[0]
    turned = [tile.T for tile in tiles]
    for h in range(message.shape[1] // HDIM):
        message[frames : frames + 16, head_cols(h)] = term_rows([t[h : h + 1, :] for t in turned])


def terms_of(message, frames, which, cols):
    terms = message[frames : frames + 16, cols].astype(F32)
    return terms[3 * which : 3 * which + 1] + terms[3 * which + 1 : 3 * which + 2] + terms[3 * which + 2 : 3 * which + 3]


def hidden_body(flags, inputs, keep, core, across, cot, seen_a, seen_b, hidden, rim_near, rim_far):
    frames, width = inputs.shape
    wide = 2 * HALO
    total = inputs[...].astype(F32) + keep[...].astype(F32) + core[...].astype(F32)
    total = (total + across[...].astype(F32)).astype(BF16)
    hidden[...] = total
    even = flags[0] > 0
    for at, first, last in (
        (slice(0, wide), total[0:wide], total[frames - wide :]),
        (slice(wide, wide + HALO), cot[0:HALO, :], cot[frames - HALO : frames, :]),
    ):
        first, last = first.astype(F32), last.astype(F32)
        rim_near[at, :] = jnp.where(even, last, first).astype(BF16)
        rim_far[at, :] = jnp.where(even, first, last).astype(BF16)


def shifted_sum(load, taps_of, rows):
    total = None
    for b in range(8):
        part = None
        reach = rows if b == 0 else rows + 8
        for a in range(4):
            tap = taps_of(8 * a + b)
            if tap is None:
                continue
            term = tap * load(8 * a, reach)
            part = term if part is None else part + term
        if b:
            part = pltpu.roll(part, reach - b, 0)[0:rows]
        total = part if total is None else total + part
    return total


def silu_parts(conv, cots):
    gate = 1.0 / (1.0 + jnp.exp(-conv))
    grad = cots * (gate + conv * gate * (1.0 - gate))
    return conv * gate, grad.astype(BF16).astype(F32)


def taps_forward(taps, cols):
    count = taps.shape[0]
    return lambda s: taps[s - 1 : s, cols] if 1 <= s <= count else None


def taps_backward(taps, cols):
    count = taps.shape[0]
    return lambda s: taps[count - s : count - s + 1, cols] if 1 <= s <= count else None


def conv_inner_body(hidden, cot, taps, rows_out, edge_conv, part_grad, padded, grads):
    frames, width = hidden.shape
    wide = 2 * HALO
    padded[0:wide, :] = jnp.zeros((wide, width), F32)
    padded[wide : wide + frames, :] = hidden[...].astype(F32)
    padded[wide + frames : 2 * wide + frames, :] = jnp.zeros((wide, width), F32)
    grads[0:wide, :] = jnp.zeros((wide, width), F32)
    grads[frames : frames + wide, :] = jnp.zeros((wide, width), F32)
    inner = slice(HALO, frames - HALO)
    for c in range(0, width, 128):
        cols = slice(c, c + 128)
        conv = shifted_sum(
            lambda at, rows: padded[at : at + rows, cols], taps_forward(taps, cols), frames + wide
        )
        edge_conv[0:wide, cols] = conv[0:wide]
        edge_conv[wide : 2 * wide, cols] = conv[frames : frames + wide]
        cots = cot[:, cols].astype(F32)
        silu, grad = silu_parts(conv[wide:frames], cots[inner])
        rows_out[inner, cols] = (hidden[inner, cols].astype(F32) + silu).astype(BF16)
        grads[wide:frames, cols] = grad
        back = shifted_sum(
            lambda at, rows: grads[at : at + rows, cols], taps_backward(taps, cols), frames
        )
        part_grad[:, cols] = cots + back


def conv_edge_body(
    flags, hidden, rim_near, rim_far, cot, taps, rows_in, edge_conv, part_grad,
    output, grad_input, padded, grads,
):
    frames, width = hidden.shape
    wide = 2 * HALO
    even = flags[0] > 0
    have = jnp.where(flags[2] > 0, jnp.float32(1.0), jnp.float32(0.0))
    low_ok = jnp.where(even, have, jnp.float32(1.0))
    high_ok = jnp.where(even, jnp.float32(1.0), have)
    rims, cots_of = slice(0, wide), slice(wide, wide + HALO)

    def low_of(rows):
        return jnp.where(even, rim_far[rows, :].astype(F32), rim_near[rows, :].astype(F32)) * low_ok

    def high_of(rows):
        return jnp.where(even, rim_near[rows, :].astype(F32), rim_far[rows, :].astype(F32)) * high_ok

    padded[0:wide, :] = low_of(rims)
    padded[wide : 2 * wide, :] = jnp.zeros((wide, width), F32)
    padded[2 * wide : 3 * wide, :] = high_of(rims)
    grads[wide : 2 * wide, :] = jnp.zeros((wide, width), F32)
    cot_low, cot_high = low_of(cots_of), high_of(cots_of)
    low, high = slice(0, HALO), slice(frames - HALO, frames)
    inner = slice(HALO, frames - HALO)
    output[inner, :] = rows_in[inner, :]
    for c in range(0, width, 128):
        cols = slice(c, c + 128)
        conv = edge_conv[:, cols] + shifted_sum(
            lambda at, rows: padded[at : at + rows, cols], taps_forward(taps, cols), 2 * wide
        )
        cots = jnp.concatenate(
            [cot_low[:, cols], cot[low, cols].astype(F32), cot[high, cols].astype(F32), cot_high[:, cols]],
            axis=0,
        )
        silu, grad = silu_parts(conv, cots)
        output[low, cols] = (hidden[low, cols].astype(F32) + silu[HALO:wide]).astype(BF16)
        output[high, cols] = (hidden[high, cols].astype(F32) + silu[wide : wide + HALO]).astype(BF16)
        grads[0:wide, cols] = grad[0:wide]
        grads[2 * wide : 3 * wide, cols] = grad[wide : 2 * wide]
        back = shifted_sum(
            lambda at, rows: grads[at : at + rows, cols], taps_backward(taps, cols), 2 * wide
        )
        part = part_grad[:, cols]
        grad_input[:, cols] = jnp.concatenate(
            [part[0:wide] + back[0:wide], part[wide : frames - wide], part[frames - wide :] + back[wide:]],
            axis=0,
        ).astype(BF16)


def upstream_part(flags, weight, pieces):
    width = weight.shape[0]
    total = None
    for flip, block in pieces:
        at = pl.ds(pl.multiple_of((flags[3] ^ flip) * width, 128), width)
        part = dot_nt(block[...], weight[:, at])
        total = part if total is None else total + part
    return total


def upstream_chip_body(flags, own, core, weight, partial):
    partial[...] = upstream_part(flags, weight, ((0, own), (1, core)))


def upstream_across_body(flags, across, weight, before, partial):
    partial[...] = before[...] + upstream_part(flags, weight, ((2, across),))


def upstream_body(flags, cross, weight, att, lse, partial, message, delta):
    frames, width = cross.shape
    total = partial[...] + upstream_part(flags, weight, ((3, cross),))
    up = total.astype(BF16)
    message[0:frames, :] = up
    lane = lax.broadcasted_iota(jnp.int32, (frames, HDIM), 1)
    tile = jnp.zeros((frames, HDIM), F32)
    for h in range(width // HDIM):
        cols = head_cols(h)
        product = up[:, cols].astype(F32) * att[:, cols].astype(F32)
        tile = jnp.where(lane == h, jnp.sum(product, axis=1, keepdims=True), tile)
    delta[...] = tile
    put_terms(message, [lse[...], tile])


def query_grad_body(
    scale, flags, q, own, near, first, second, relay, message, lse, delta, output_here, grad_here,
    output, grad_input, grad_query, held, sems,
):
    writes = [
        pltpu.make_async_copy(output_here, output, sems.at[0]),
        pltpu.make_async_copy(grad_here, grad_input, sems.at[1]),
    ]
    for write in writes:
        write.start()
    frames, width = q.shape
    near_bias, relay_bias = off_bias(flags[1]), off_bias(flags[2])
    blocks = (near, own, first, second, relay)
    for h in range(width // HDIM):
        cols = head_cols(h)
        keys = stacked(blocks, slice(0, frames), cols)
        scores = dot_nt(q[:, cols], keys) * scale - lse[:, h : h + 1]
        scores = jnp.concatenate(
            [scores[:, 0:frames] + near_bias, scores[:, frames : 4 * frames]]
            + [scores[:, 4 * frames :] + relay_bias],
            axis=1,
        )
        dots = dot_nt(message[0:frames, cols], stacked(blocks, slice(frames, 2 * frames), cols))
        grads = (jnp.exp(scores) * (dots - delta[:, h : h + 1]) * scale).astype(BF16)
        held[:, cols] = dot_nn(grads, keys).astype(BF16)
    writes.append(pltpu.make_async_copy(held, grad_query, sems.at[2]))
    writes[2].start()
    for write in writes:
        write.wait()


def key_probs(scale, own, queries, messages, biases, cols):
    frames = own.shape[0] // 2
    scores = dot_nt(own[0:frames, cols], stacked(queries, slice(0, frames), cols)) * scale
    parts = []
    for b, bias in enumerate(biases):
        part = scores[:, b * frames : (b + 1) * frames] - terms_of(messages[b], frames, 0, cols)
        parts.append(jnp.exp(part if bias is None else part + bias))
    return jnp.concatenate(parts, axis=1)


def value_terms(probs, messages, cols):
    frames = probs.shape[0]
    return dot_nn(probs.astype(BF16), stacked(messages, slice(0, frames), cols))


def key_terms(scale, own, probs, queries, messages, cols):
    frames = own.shape[0] // 2
    dots = dot_nt(own[frames : 2 * frames, cols], stacked(messages, slice(0, frames), cols))
    deltas = jnp.concatenate([terms_of(m, frames, 1, cols) for m in messages], axis=1)
    grads = (probs * (dots - deltas) * scale).astype(BF16)
    return dot_nn(grads, stacked(queries, slice(0, frames), cols))


def key_part_body(scale, flags, own, *refs):
    queries, late_query, messages, (key_part, value_part, late) = refs[0:4], refs[4], refs[5:9], refs[9:12]
    frames = own.shape[0] // 2
    biases = (None, off_bias(flags[1]), None, None)
    late_bias = off_bias(flags[2])
    for h in range(own.shape[1] // HDIM):
        cols = head_cols(h)
        probs = key_probs(scale, own, queries, messages, biases, cols)
        value_part[:, cols] = value_terms(probs, messages, cols)
        key_part[:, cols] = key_terms(scale, own, probs, queries, messages, cols)
        late[:, cols] = dot_nt(own[0:frames, cols], late_query[:, cols]) * scale + late_bias


def key_grad_body(
    scale, own, query, message, late, key_part, value_part, grad_key, grad_value, held_key, held_value, sems
):
    frames = own.shape[0] // 2
    heads = [head_cols(h) for h in range(own.shape[1] // HDIM)]
    probs = [jnp.exp(late[:, cols] - terms_of(message, frames, 0, cols)) for cols in heads]
    for cols, prob in zip(heads, probs):
        held_value[:, cols] = (value_part[:, cols] + value_terms(prob, (message,), cols)).astype(BF16)
    value_write = pltpu.make_async_copy(held_value, grad_value, sems.at[0])
    value_write.start()
    for cols, prob in zip(heads, probs):
        keys = key_terms(scale, own, prob, (query,), (message,), cols)
        held_key[:, cols] = (key_part[:, cols] + keys).astype(BF16)
    key_write = pltpu.make_async_copy(held_key, grad_key, sems.at[1])
    key_write.start()
    value_write.wait()
    key_write.wait()


def per_device(query_rows, key_rows, value_rows, inputs, out_weight, kernel, cotangent):
    frames, width = query_rows.shape
    wide = 2 * HALO
    scale = 1.0 / math.sqrt(HDIM)
    block, count = lax.axis_index("ctx"), lax.axis_size("ctx")
    even = block % 2 == 0
    lower, upper = block >= 2, block < count - 2
    flags = jnp.stack(
        [even, lower & upper, jnp.where(even, lower, upper), lax.axis_index("mp")]
    ).astype(jnp.int32)
    tile = shaped((frames, width), BF16)
    tile32 = shaped((frames, width), F32)
    side = shaped((frames, HDIM), F32)
    rim = shaped((wide + HALO, width), BF16)
    noted = shaped((frames + 16, width), BF16)

    zero = jnp.zeros((), BF16)
    kv = lax.pad(key_rows, zero, ((0, frames, 0), (0, 0, 0))) + lax.pad(
        value_rows, zero, ((frames, 0, 0), (0, 0, 0))
    )
    near, first, second, relay = window_of(kv)
    (q_early,) = kernel_call(hold_body, (tile,), (query_rows, second), 0.3, "hold", [VMEM, ANY])
    q_second = ring(q_early, 1)
    q_first = ring(q_early, 0)
    sums, tops, totals = kernel_call(
        functools.partial(forward_body, scale),
        (tile32, side, side),
        (flags, q_early, kv, near, first, second),
        1.7, "forward",
    )
    att, lse, send, keep = kernel_call(
        functools.partial(project_body, scale),
        (tile, side, tile, tile),
        (flags, q_early, relay, sums, tops, totals, out_weight),
        1.8, "project",
    )

    core = pair_swap(send, "mp", 1)
    own_send, own_keep = kernel_call(
        project_own_body, (tile, tile), (flags, att, out_weight, q_second, q_first), 0.9,
        "project_own", [SMEM] + [VMEM] * 2 + [ANY] * 2,
    )
    outgoing, q_own, q_handed = kernel_call(
        join_body, (tile, tile, tile), (keep, core, q_early, q_second), 0.3, "join", [VMEM] * 4
    )
    across = pair_swap(outgoing, "mp", 2)
    own_core = pair_swap(own_send, "mp", 1)
    q_near = inner_swap(q_own)
    q_relay = pair_swap(q_handed, "ctx", 1)
    hidden, rim_up, rim_down = kernel_call(
        hidden_body,
        (tile, rim, rim),
        (flags, inputs, own_keep, own_core, across, cotangent, q_near, q_relay),
        0.6, "hidden", [SMEM] + [VMEM] * 5 + [ANY] * 2,
    )

    rim_far = outer_swap(rim_down)
    rim_near = pair_swap(rim_up, "ctx", 1)
    rows_out, edge_conv, part_grad = kernel_call(
        conv_inner_body,
        (tile, shaped((2 * wide, width), F32), tile32),
        (hidden, cotangent, kernel),
        1.6, "conv_inner", [VMEM] * 3,
        [pltpu.VMEM((frames + 2 * wide, width), F32), pltpu.VMEM((frames + wide, width), F32)],
    )
    output_here, grad_here = kernel_call(
        conv_edge_body,
        (tile, tile),
        (flags, hidden, rim_near, rim_far, cotangent, kernel, rows_out, edge_conv, part_grad),
        1.3, "conv_edge", None,
        [pltpu.VMEM((3 * wide, width), F32), pltpu.VMEM((3 * wide, width), F32)],
    )

    gi_across = pair_swap(grad_here, "mp", 2)
    gi_core = pair_swap(grad_here, "mp", 1)
    gi_cross = pair_swap(gi_across, "mp", 1)
    (partial,) = kernel_call(
        upstream_chip_body, (tile32,), (flags, grad_here, gi_core, out_weight), 1.0, "upstream_chip"
    )
    (partial,) = kernel_call(
        upstream_across_body, (tile32,), (flags, gi_across, out_weight, partial), 0.6, "upstream_across"
    )
    message, delta = kernel_call(
        upstream_body,
        (noted, side),
        (flags, gi_cross, out_weight, att, lse, partial),
        0.9, "upstream",
    )

    m_near, m_first, m_second, m_relay = window_of(message)
    output, grad_input, grad_query = kernel_call(
        functools.partial(query_grad_body, scale),
        (tile, tile, tile),
        (flags, q_own, kv, near, first, second, relay)
        + (message, lse, delta, output_here, grad_here),
        2.3, "query_grad", None,
        [pltpu.VMEM((frames, width), BF16), pltpu.SemaphoreType.DMA((3,))], 24, HBM,
    )
    key_part, value_part, late = kernel_call(
        functools.partial(key_part_body, scale),
        (tile32, tile32, tile32),
        (flags, kv, q_own, q_near, q_first, q_second, q_relay, message, m_near, m_first, m_second),
        2.2, "key_part",
    )
    grad_key, grad_value = kernel_call(
        functools.partial(key_grad_body, scale),
        (tile, tile),
        (kv, q_relay, m_relay, late, key_part, value_part),
        1.5, "key_grad", [VMEM] * 6,
        [pltpu.VMEM((frames, width), BF16)] * 2 + [pltpu.SemaphoreType.DMA((2,))], 24, HBM,
    )
    return (output, grad_input, grad_query, grad_key, grad_value)


def solution(mesh):
    rows = P("ctx", "mp")
    return jax.shard_map(
        per_device,
        mesh=mesh,
        in_specs=(rows, rows, rows, rows, P("mp", None), P(None, "mp"), rows),
        out_specs=(rows,) * 5,
        check_vma=False,
    )
```

```python
import functools
import math

import jax
import jax.numpy as jnp
from jax import lax
from jax.experimental import pallas as pl
from jax.experimental.pallas import tpu as pltpu
from jax.sharding import PartitionSpec as P

HDIM = 128
F32 = jnp.float32
BF16 = jnp.bfloat16
HALO = 16
NT = (((1,), (1,)), ((), ()))
NN = (((1,), (0,)), ((), ()))


def dot_nt(a, b):
    return lax.dot_general(a, b, NT, preferred_element_type=F32)


def dot_nn(a, b):
    return lax.dot_general(a, b, NN, preferred_element_type=F32)


def pair_swap(block, axis, bit):
    return lax.ppermute(block, axis, [(i, i ^ bit) for i in range(lax.axis_size(axis))])


def ring_routes(count):
    rise = [(i, i + 2) for i in range(0, count - 2, 2)] + [(count - 2, count - 1)]
    fall = [(i, i - 2) for i in range(count - 1, 2, -2)] + [(1, 0)]
    route = rise + fall
    return route, [(b, a) for a, b in route]


def ring(block, way):
    return lax.ppermute(block, "ctx", ring_routes(lax.axis_size("ctx"))[way])


def total_swap(block, partner_of):
    count, places = lax.axis_size("ctx"), lax.axis_size("mp")
    route = []
    for i in range(count):
        other = partner_of(i, count)
        for m in range(places):
            target = i * places + (m ^ 1) if other is None else other * places + m
            route.append((i * places + m, target))
    return lax.ppermute(block, ("ctx", "mp"), route)


def inner_swap(block):
    return total_swap(block, lambda i, count: i ^ 1 if 2 <= i < count - 2 else None)


def outer_swap(block):
    return total_swap(block, lambda i, count: ((i + 1) ^ 1) - 1 if 0 < i < count - 1 else None)


def window_of(block):
    second = ring(block, 1)
    first = ring(block, 0)
    near = inner_swap(block)
    return near, first, second, pair_swap(second, "ctx", 1)


VMEM = pl.BlockSpec(memory_space=pltpu.VMEM)
ANY = pl.BlockSpec(memory_space=pl.ANY)
HBM = pl.BlockSpec(memory_space=pltpu.HBM)


def kernel_call(body, outs, args, micros, name, unread=0, scratch=(), out_space=VMEM):
    return pl.pallas_call(
        body,
        out_shape=outs,
        in_specs=[VMEM] * (len(args) - unread) + [ANY] * unread,
        out_specs=tuple(out_space for _ in outs),
        scratch_shapes=scratch,
        compiler_params=pltpu.CompilerParams(vmem_limit_bytes=24 * 1024 * 1024),
        cost_estimate=pl.CostEstimate(
            flops=0, bytes_accessed=int(micros * 3.69e6), transcendentals=0
        ),
        name=name,
    )(*args)


def shaped(shape, dtype):
    return jax.ShapeDtypeStruct(shape, dtype)


def is_even():
    return lax.axis_index("ctx") % 2 == 0


def near_swapped():
    block = lax.axis_index("ctx")
    return (block >= 2) & (block < lax.axis_size("ctx") - 2)


def far_there():
    block = lax.axis_index("ctx")
    return jnp.where(is_even(), block >= 2, block < lax.axis_size("ctx") - 2)


def bias_of(there):
    return jnp.where(there, jnp.float32(0.0), jnp.float32(-jnp.inf))


def columns(width):
    return [slice(c, c + HDIM) for c in range(0, width, HDIM)]


def stacked(blocks, rows, cols):
    return jnp.concatenate([block[rows, cols] for block in blocks], axis=0)


def with_ones(values):
    return jnp.concatenate([values, jnp.ones_like(values)], axis=1)


def by_block(scores, biases, stats=None):
    parts = []
    for b, bias in enumerate(biases):
        part = scores[:, b * HDIM : (b + 1) * HDIM]
        if stats is not None:
            part = part - stats[b]
        parts.append(part if bias is None else part + bias)
    return jnp.concatenate(parts, axis=1)


def tile_of(wide):
    lane = lax.broadcasted_iota(jnp.int32, (wide[0].shape[0], HDIM), 1)
    tile = jnp.zeros((wide[0].shape[0], HDIM), F32)
    for h, part in enumerate(wide):
        tile = jnp.where(lane == h, part, tile)
    return tile


def term_rows(rows):
    at = lax.broadcasted_iota(jnp.int32, (16, rows[0].shape[1]), 0)
    block = jnp.zeros((16, rows[0].shape[1]), F32)
    for r, rest in enumerate(rows):
        for k in range(3):
            term = rest.astype(BF16).astype(F32)
            rest = rest - term
            block = jnp.where(at == 3 * r + k, term, block)
    return block.astype(BF16)


def stat_rows(message, frames, which, cols):
    terms = message[frames : frames + 16, cols].astype(F32)
    at = 3 * which
    return terms[at : at + 1] + terms[at + 1 : at + 2] + terms[at + 2 : at + 3]


def weight_columns(weight, flip):
    width = weight.shape[0]
    at = (lax.axis_index("mp") ^ flip) * width
    return weight[:, pl.ds(pl.multiple_of(at, 128), width)]


def hold_body(block, seen, held):
    held[...] = block[...]


def forward_body(scale, q, own, near, first, second, sums, tops, totals):
    frames, width = q.shape
    heads = columns(width)
    blocks = (near, own, first, second)
    biases = (bias_of(near_swapped()), None, None, None)
    keys, values = slice(0, frames), slice(frames, 2 * frames)
    scores = [dot_nt(q[:, c], stacked(blocks, keys, c)) * scale for c in heads]
    scores = [by_block(s, biases) for s in scores]
    top = [jnp.max(s, axis=1, keepdims=True) for s in scores]
    probs = [jnp.exp(s - t).astype(BF16) for s, t in zip(scores, top)]
    summed = [dot_nn(p, with_ones(stacked(blocks, values, c))) for p, c in zip(probs, heads)]
    for c, t, s in zip(heads, top, summed):
        tops[:, c] = jnp.broadcast_to(t, (frames, HDIM))
        sums[:, c] = s[:, 0:HDIM]
        totals[:, c] = s[:, HDIM:]


def project_body(scale, q, relay, sums, tops, totals, weight, att, lse, send, keep):
    frames, width = q.shape
    heads = columns(width)
    bias = bias_of(far_there())
    scores = [dot_nt(q[:, c], relay[0:frames, c]) * scale + bias for c in heads]
    before = [tops[:, c] for c in heads]
    top = [jnp.maximum(b, jnp.max(s, axis=1, keepdims=True)) for b, s in zip(before, scores)]
    shrink = [jnp.exp(b - t) for b, t in zip(before, top)]
    probs = [jnp.exp(s - t).astype(BF16) for s, t in zip(scores, top)]
    late = [dot_nn(p, with_ones(relay[frames : 2 * frames, c])) for p, c in zip(probs, heads)]
    total = [totals[:, c] * k + s[:, HDIM:] for c, k, s in zip(heads, shrink, late)]
    summed = [sums[:, c] * k + s[:, 0:HDIM] for c, k, s in zip(heads, shrink, late)]
    attended = jnp.concatenate([(s * (1.0 / t)).astype(BF16) for s, t in zip(summed, total)], axis=1)
    sent = dot_nn(attended, weight_columns(weight, 3)).astype(BF16)
    kept = dot_nn(attended, weight_columns(weight, 2)).astype(BF16)
    logs = [t + jnp.log(n) for t, n in zip(top, total)]
    att[...] = attended
    send[...] = sent
    keep[...] = kept
    for c, part in zip(heads, logs):
        lse[:, c] = part


def project_own_body(att, weight, seen_a, seen_b, send, keep):
    sent = dot_nn(att[...], weight_columns(weight, 1)).astype(BF16)
    kept = dot_nn(att[...], weight_columns(weight, 0)).astype(BF16)
    send[...] = sent
    keep[...] = kept


def join_body(keep, core, q, outgoing, q_copy):
    outgoing[...] = (keep[...].astype(F32) + core[...].astype(F32)).astype(BF16)
    q_copy[...] = q[...]


def hidden_body(inputs, keep, core, across, cot, hidden, rim_near, rim_far):
    frames, width = inputs.shape
    wide = 2 * HALO
    total = inputs[...].astype(F32) + keep[...].astype(F32) + core[...].astype(F32)
    total = (total + across[...].astype(F32)).astype(BF16)
    even = is_even()
    for at, first, last in (
        (slice(0, wide), total[0:wide], total[frames - wide :]),
        (slice(wide, wide + HALO), cot[0:HALO, :], cot[frames - HALO : frames, :]),
    ):
        first, last = first.astype(F32), last.astype(F32)
        rim_near[at, :] = jnp.where(even, last, first).astype(BF16)
        rim_far[at, :] = jnp.where(even, first, last).astype(BF16)
    hidden[...] = total


def shifted_sum(rows, taps_of, count):
    total = None
    for b in range(8):
        part = None
        reach = count if b == 0 else count + 8
        for a in range(4):
            tap = taps_of(8 * a + b)
            if tap is None:
                continue
            term = tap * rows[8 * a : 8 * a + reach]
            part = term if part is None else part + term
        if b:
            part = pltpu.roll(part, reach - b, 0)[0:count]
        total = part if total is None else total + part
    return total


def silu_parts(conv, cots):
    gate = 1.0 / (1.0 + jnp.exp(-conv))
    grad = cots * (gate + conv * gate * (1.0 - gate))
    return conv * gate, grad.astype(BF16).astype(F32)


def taps_forward(taps, cols):
    count = taps.shape[0]
    return lambda s: taps[s - 1 : s, cols] if 1 <= s <= count else None


def taps_backward(taps, cols):
    count = taps.shape[0]
    return lambda s: taps[count - s : count - s + 1, cols] if 1 <= s <= count else None


def conv_inner_body(hidden, cot, taps, seen, rows_out, edge_conv, part_grad):
    frames, width = hidden.shape
    wide = 2 * HALO
    inner = slice(HALO, frames - HALO)
    none = jnp.zeros((wide, HDIM), F32)
    for cols in columns(width):
        own = hidden[:, cols].astype(F32)
        cots = cot[:, cols].astype(F32)
        conv = shifted_sum(
            jnp.concatenate([none, own, none], axis=0), taps_forward(taps, cols), frames + wide
        )
        silu, grad = silu_parts(conv[wide:frames], cots[inner])
        back = shifted_sum(
            jnp.concatenate([none, grad, none], axis=0), taps_backward(taps, cols), frames
        )
        edge_conv[0:wide, cols] = conv[0:wide]
        edge_conv[wide : 2 * wide, cols] = conv[frames : frames + wide]
        rows_out[inner, cols] = (own[inner] + silu).astype(BF16)
        part_grad[:, cols] = cots + back


def conv_edge_body(
    hidden, rim_near, rim_far, cot, taps, rows_in, edge_conv, part_grad, q_second,
    output, grad_input, second_copy,
):
    frames, width = hidden.shape
    wide = 2 * HALO
    even, far = is_even(), far_there()
    rims, cots_of = slice(0, wide), slice(wide, wide + HALO)
    low, high = slice(0, HALO), slice(frames - HALO, frames)
    inner = slice(HALO, frames - HALO)
    none = jnp.zeros((wide, HDIM), F32)

    def sides(rows, cols):
        near = rim_near[rows, cols].astype(F32)
        beyond = jnp.where(far, rim_far[rows, cols].astype(F32), 0.0)
        return jnp.where(even, beyond, near), jnp.where(even, near, beyond)

    for cols in columns(width):
        row_low, row_high = sides(rims, cols)
        cot_low, cot_high = sides(cots_of, cols)
        conv = edge_conv[:, cols] + shifted_sum(
            jnp.concatenate([row_low, none, row_high], axis=0), taps_forward(taps, cols), 2 * wide
        )
        cots = jnp.concatenate(
            [cot_low, cot[low, cols].astype(F32), cot[high, cols].astype(F32), cot_high], axis=0
        )
        silu, grad = silu_parts(conv, cots)
        back = shifted_sum(
            jnp.concatenate([grad[0:wide], none, grad[wide:]], axis=0), taps_backward(taps, cols), 2 * wide
        )
        part = part_grad[:, cols]
        grad_input[:, cols] = jnp.concatenate(
            [part[0:wide] + back[0:wide], part[wide : frames - wide], part[frames - wide :] + back[wide:]],
            axis=0,
        ).astype(BF16)
        output[low, cols] = (hidden[low, cols].astype(F32) + silu[HALO:wide]).astype(BF16)
        output[inner, cols] = rows_in[inner, cols]
        output[high, cols] = (hidden[high, cols].astype(F32) + silu[wide : wide + HALO]).astype(BF16)
    second_copy[...] = q_second[...]


def upstream_chip_body(own, core, weight, partial):
    partial[...] = dot_nt(own[...], weight_columns(weight, 0)) + dot_nt(core[...], weight_columns(weight, 1))


def upstream_across_body(across, weight, before, partial):
    partial[...] = before[...] + dot_nt(across[...], weight_columns(weight, 2))


def upstream_body(cross, weight, att, lse, partial, seen, message, delta):
    frames, width = cross.shape
    heads = columns(width)
    up = (partial[...] + dot_nt(cross[...], weight_columns(weight, 3))).astype(BF16)
    products = [up[:, c].astype(F32) * att[:, c].astype(F32) for c in heads]
    deltas = [jnp.broadcast_to(jnp.sum(p, axis=1, keepdims=True), (frames, HDIM)) for p in products]
    lse_rows = tile_of([lse[:, c] for c in heads]).T
    delta_rows = tile_of(deltas).T
    terms = [term_rows([lse_rows[h : h + 1], delta_rows[h : h + 1]]) for h in range(len(heads))]
    message[0:frames, :] = up
    message[frames : frames + 16, :] = jnp.concatenate(terms, axis=1)
    for c, part in zip(heads, deltas):
        delta[:, c] = part


def query_grad_body(
    scale, q, own, near, first, second, relay, message, lse, delta, output_here, grad_here,
    output, grad_input, grad_query, held, sems,
):
    writes = [
        pltpu.make_async_copy(output_here, output, sems.at[0]),
        pltpu.make_async_copy(grad_here, grad_input, sems.at[1]),
    ]
    for write in writes:
        write.start()
    frames, width = q.shape
    heads = columns(width)
    blocks = (near, own, first, second, relay)
    biases = (bias_of(near_swapped()), None, None, None, bias_of(far_there()))
    above, below = slice(0, frames), slice(frames, 2 * frames)
    keys = [stacked(blocks, above, c) for c in heads]
    scores = [dot_nt(q[:, c], k) * scale for c, k in zip(heads, keys)]
    dots = [dot_nt(message[0:frames, c], stacked(blocks, below, c)) for c in heads]
    probs = [jnp.exp(by_block(s, biases, [lse[:, c]] * 5)) for c, s in zip(heads, scores)]
    drops = [by_block(d, (None,) * 5, [delta[:, c]] * 5) for c, d in zip(heads, dots)]
    grads = [(p * d * scale).astype(BF16) for p, d in zip(probs, drops)]
    held[...] = jnp.concatenate([dot_nn(g, k).astype(BF16) for g, k in zip(grads, keys)], axis=1)
    writes.append(pltpu.make_async_copy(held, grad_query, sems.at[2]))
    writes[2].start()
    for write in writes:
        write.wait()


def key_part_body(scale, own, *refs):
    queries, late_query, messages, (key_part, value_part, late) = refs[0:4], refs[4], refs[5:9], refs[9:12]
    frames = own.shape[0] // 2
    heads = columns(own.shape[1])
    above, below = slice(0, frames), slice(frames, 2 * frames)
    biases = (None, bias_of(near_swapped()), None, None)
    asks = [stacked(queries, above, c) for c in heads]
    ups = [stacked(messages, above, c) for c in heads]
    scores = [dot_nt(own[above, c], a) * scale for c, a in zip(heads, asks)]
    dots = [dot_nt(own[below, c], u) for c, u in zip(heads, ups)]
    last = [dot_nt(own[above, c], late_query[:, c]) * scale + bias_of(far_there()) for c in heads]
    logs = [[stat_rows(m, frames, 0, c) for m in messages] for c in heads]
    deltas = [[stat_rows(m, frames, 1, c) for m in messages] for c in heads]
    probs = [jnp.exp(by_block(s, biases, n)) for s, n in zip(scores, logs)]
    drops = [by_block(d, (None,) * 4, n) for d, n in zip(dots, deltas)]
    grads = [(p * d * scale).astype(BF16) for p, d in zip(probs, drops)]
    value_sums = [dot_nn(p.astype(BF16), u) for p, u in zip(probs, ups)]
    key_sums = [dot_nn(g, a) for g, a in zip(grads, asks)]
    for c, k, v, s in zip(heads, key_sums, value_sums, last):
        key_part[:, c] = k
        value_part[:, c] = v
        late[:, c] = s


def key_grad_body(
    scale, own, query, message, late, key_part, value_part, grad_key, grad_value, held_key, held_value, sems
):
    frames = own.shape[0] // 2
    heads = columns(own.shape[1])
    above, below = slice(0, frames), slice(frames, 2 * frames)
    ups = [message[above, c] for c in heads]
    probs = [jnp.exp(late[:, c] - stat_rows(message, frames, 0, c)) for c in heads]
    dots = [dot_nt(own[below, c], u) for c, u in zip(heads, ups)]
    values = [value_part[:, c] + dot_nn(p.astype(BF16), u) for c, p, u in zip(heads, probs, ups)]
    held_value[...] = jnp.concatenate([v.astype(BF16) for v in values], axis=1)
    value_write = pltpu.make_async_copy(held_value, grad_value, sems.at[0])
    value_write.start()
    drops = [d - stat_rows(message, frames, 1, c) for c, d in zip(heads, dots)]
    grads = [(p * d * scale).astype(BF16) for p, d in zip(probs, drops)]
    keys = [key_part[:, c] + dot_nn(g, query[:, c]) for c, g in zip(heads, grads)]
    held_key[...] = jnp.concatenate([k.astype(BF16) for k in keys], axis=1)
    key_write = pltpu.make_async_copy(held_key, grad_key, sems.at[1])
    key_write.start()
    value_write.wait()
    key_write.wait()


def per_device(query_rows, key_rows, value_rows, inputs, out_weight, kernel, cotangent):
    frames, width = query_rows.shape
    wide = 2 * HALO
    scale = 1.0 / math.sqrt(HDIM)
    tile = shaped((frames, width), BF16)
    tile32 = shaped((frames, width), F32)
    rim = shaped((wide + HALO, width), BF16)
    noted = shaped((frames + 16, width), BF16)

    zero = jnp.zeros((), BF16)
    kv = lax.pad(key_rows, zero, ((0, frames, 0), (0, 0, 0))) + lax.pad(
        value_rows, zero, ((frames, 0, 0), (0, 0, 0))
    )
    near, first, second, relay = window_of(kv)
    (q_early,) = kernel_call(hold_body, (tile,), (query_rows, second), 0.1, "hold", 1)
    q_second = ring(q_early, 1)
    q_first = ring(q_early, 0)
    sums, tops, totals = kernel_call(
        functools.partial(forward_body, scale),
        (tile32, tile32, tile32),
        (q_early, kv, near, first, second),
        1.0, "forward",
    )
    att, lse, send, keep = kernel_call(
        functools.partial(project_body, scale),
        (tile, tile32, tile, tile),
        (q_early, relay, sums, tops, totals, out_weight),
        1.0, "project",
    )

    core = pair_swap(send, "mp", 1)
    own_send, own_keep = kernel_call(
        project_own_body, (tile, tile), (att, out_weight, q_second, q_first), 0.4, "project_own", 2
    )
    outgoing, q_own = kernel_call(join_body, (tile, tile), (keep, core, q_early), 0.1, "join")
    across = pair_swap(outgoing, "mp", 2)
    own_core = pair_swap(own_send, "mp", 1)
    q_near = inner_swap(q_own)
    hidden, rim_up, rim_down = kernel_call(
        hidden_body,
        (tile, rim, rim),
        (inputs, own_keep, own_core, across, cotangent),
        0.2, "hidden",
    )

    rim_far = outer_swap(rim_down)
    rim_near = pair_swap(rim_up, "ctx", 1)
    rows_out, edge_conv, part_grad = kernel_call(
        conv_inner_body,
        (tile, shaped((2 * wide, width), F32), tile32),
        (hidden, cotangent, kernel, q_near),
        1.6, "conv_inner", 1,
    )
    output_here, grad_here, q_handed = kernel_call(
        conv_edge_body,
        (tile, tile, tile),
        (hidden, rim_near, rim_far, cotangent, kernel, rows_out, edge_conv, part_grad, q_second),
        0.8, "conv_edge",
    )

    gi_across = pair_swap(grad_here, "mp", 2)
    gi_core = pair_swap(grad_here, "mp", 1)
    q_relay = pair_swap(q_handed, "ctx", 1)
    (partial,) = kernel_call(
        upstream_chip_body, (tile32,), (grad_here, gi_core, out_weight), 0.5, "upstream_chip"
    )
    (turned,) = kernel_call(hold_body, (tile,), (gi_across, partial), 0.1, "turn", 1)
    gi_cross = pair_swap(turned, "mp", 1)
    (partial,) = kernel_call(
        upstream_across_body, (tile32,), (turned, out_weight, partial), 0.4, "upstream_across"
    )
    message, delta = kernel_call(
        upstream_body,
        (noted, tile32),
        (gi_cross, out_weight, att, lse, partial, q_relay),
        0.5, "upstream", 1,
    )

    m_near, m_first, m_second, m_relay = window_of(message)
    output, grad_input, grad_query = kernel_call(
        functools.partial(query_grad_body, scale),
        (tile, tile, tile),
        (q_own, kv, near, first, second, relay, message, lse, delta, output_here, grad_here),
        1.8, "query_grad", 0,
        [pltpu.VMEM((frames, width), BF16), pltpu.SemaphoreType.DMA((3,))], HBM,
    )
    key_part, value_part, late = kernel_call(
        functools.partial(key_part_body, scale),
        (tile32, tile32, tile32),
        (kv, q_own, q_near, q_first, q_second, q_relay, message, m_near, m_first, m_second),
        1.5, "key_part",
    )
    grad_key, grad_value = kernel_call(
        functools.partial(key_grad_body, scale),
        (tile, tile),
        (kv, q_relay, m_relay, late, key_part, value_part),
        1.0, "key_grad", 0,
        [pltpu.VMEM((frames, width), BF16)] * 2 + [pltpu.SemaphoreType.DMA((2,))], HBM,
    )
    return (output, grad_input, grad_query, grad_key, grad_value)


def solution(mesh):
    rows = P("ctx", "mp")
    return jax.shard_map(
        per_device,
        mesh=mesh,
        in_specs=(rows, rows, rows, rows, P("mp", None), P(None, "mp"), rows),
        out_specs=(rows,) * 5,
        check_vma=False,
    )
```

```python
import functools
import math

import jax
import jax.numpy as jnp
from jax import lax
from jax.experimental import pallas as pl
from jax.experimental.pallas import tpu as pltpu
from jax.sharding import PartitionSpec as P

HDIM = 128
F32 = jnp.float32
BF16 = jnp.bfloat16
HALO = 16
NT = (((1,), (1,)), ((), ()))
NN = (((1,), (0,)), ((), ()))


def dot_nt(a, b):
    return lax.dot_general(a, b, NT, preferred_element_type=F32)


def dot_nn(a, b):
    return lax.dot_general(a, b, NN, preferred_element_type=F32)


def pair_swap(block, axis, bit):
    return lax.ppermute(block, axis, [(i, i ^ bit) for i in range(lax.axis_size(axis))])


def ring_routes(count):
    rise = [(i, i + 2) for i in range(0, count - 2, 2)] + [(count - 2, count - 1)]
    fall = [(i, i - 2) for i in range(count - 1, 2, -2)] + [(1, 0)]
    route = rise + fall
    return route, [(b, a) for a, b in route]


def ring(block, way):
    return lax.ppermute(block, "ctx", ring_routes(lax.axis_size("ctx"))[way])


def total_swap(block, partner_of):
    count, places = lax.axis_size("ctx"), lax.axis_size("mp")
    route = []
    for i in range(count):
        other = partner_of(i, count)
        for m in range(places):
            target = i * places + (m ^ 1) if other is None else other * places + m
            route.append((i * places + m, target))
    return lax.ppermute(block, ("ctx", "mp"), route)


def inner_swap(block):
    return total_swap(block, lambda i, count: i ^ 1 if 2 <= i < count - 2 else None)


def outer_swap(block):
    return total_swap(block, lambda i, count: ((i + 1) ^ 1) - 1 if 0 < i < count - 1 else None)


def window_of(block):
    second = ring(block, 1)
    first = ring(block, 0)
    near = inner_swap(block)
    return near, first, second, pair_swap(second, "ctx", 1)


VMEM = pl.BlockSpec(memory_space=pltpu.VMEM)
ANY = pl.BlockSpec(memory_space=pl.ANY)
HBM = pl.BlockSpec(memory_space=pltpu.HBM)


def kernel_call(body, outs, args, micros, name, unread=0, scratch=(), out_space=VMEM):
    return pl.pallas_call(
        body,
        out_shape=outs,
        in_specs=[VMEM] * (len(args) - unread) + [ANY] * unread,
        out_specs=tuple(out_space for _ in outs),
        scratch_shapes=scratch,
        compiler_params=pltpu.CompilerParams(vmem_limit_bytes=24 * 1024 * 1024),
        cost_estimate=pl.CostEstimate(
            flops=0, bytes_accessed=int(micros * 3.69e6), transcendentals=0
        ),
        name=name,
    )(*args)


def shaped(shape, dtype):
    return jax.ShapeDtypeStruct(shape, dtype)


def is_even():
    return lax.axis_index("ctx") % 2 == 0


def near_swapped():
    block = lax.axis_index("ctx")
    return (block >= 2) & (block < lax.axis_size("ctx") - 2)


def far_there():
    block = lax.axis_index("ctx")
    return jnp.where(is_even(), block >= 2, block < lax.axis_size("ctx") - 2)


def bias_of(there):
    return jnp.where(there, jnp.float32(0.0), jnp.float32(-jnp.inf))


def columns(width):
    return [slice(c, c + HDIM) for c in range(0, width, HDIM)]


def stacked(blocks, rows, cols):
    return jnp.concatenate([block[rows, cols] for block in blocks], axis=0)


def with_ones(values):
    return jnp.concatenate([values, jnp.ones_like(values)], axis=1)


def by_block(scores, biases, stats=None):
    parts = []
    for b, bias in enumerate(biases):
        part = scores[:, b * HDIM : (b + 1) * HDIM]
        if stats is not None:
            part = part - stats[b]
        parts.append(part if bias is None else part + bias)
    return jnp.concatenate(parts, axis=1)


def tile_of(wide):
    lane = lax.broadcasted_iota(jnp.int32, (wide[0].shape[0], HDIM), 1)
    tile = jnp.zeros((wide[0].shape[0], HDIM), F32)
    for h, part in enumerate(wide):
        tile = jnp.where(lane == h, part, tile)
    return tile


def term_rows(rows):
    at = lax.broadcasted_iota(jnp.int32, (16, rows[0].shape[1]), 0)
    block = jnp.zeros((16, rows[0].shape[1]), F32)
    for r, rest in enumerate(rows):
        for k in range(3):
            term = rest.astype(BF16).astype(F32)
            rest = rest - term
            block = jnp.where(at == 3 * r + k, term, block)
    return block.astype(BF16)


def stat_rows(message, frames, which, cols):
    terms = message[frames : frames + 16, cols].astype(F32)
    at = 3 * which
    return terms[at : at + 1] + terms[at + 1 : at + 2] + terms[at + 2 : at + 3]


def weight_columns(weight, flip):
    width = weight.shape[0]
    at = (lax.axis_index("mp") ^ flip) * width
    return weight[:, pl.ds(pl.multiple_of(at, 128), width)]


def hold_body(block, seen, held):
    held[...] = block[...]


def split_body(joined, seen, *parts):
    frames = parts[0].shape[0]
    for k, part in enumerate(parts):
        part[...] = joined[k * frames : (k + 1) * frames, :]


def forward_body(scale, q, *refs):
    frames, width = q.shape
    heads = columns(width)
    keys, values, (sums, tops, totals) = refs[0:4], refs[4:8], refs[8:11]
    biases = (None, bias_of(near_swapped()), None, None)
    every = slice(0, frames)
    scores = [dot_nt(q[:, c], stacked(keys, every, c)) * scale for c in heads]
    scores = [by_block(s, biases) for s in scores]
    top = [jnp.max(s, axis=1, keepdims=True) for s in scores]
    probs = [jnp.exp(s - t).astype(BF16) for s, t in zip(scores, top)]
    summed = [dot_nn(p, with_ones(stacked(values, every, c))) for p, c in zip(probs, heads)]
    for c, t, s in zip(heads, top, summed):
        tops[:, c] = jnp.broadcast_to(t, (frames, HDIM))
        sums[:, c] = s[:, 0:HDIM]
        totals[:, c] = s[:, HDIM:]


def project_body(scale, q, relay_key, relay_value, sums, tops, totals, weight, att, lse, send, keep):
    frames, width = q.shape
    heads = columns(width)
    bias = bias_of(far_there())
    scores = [dot_nt(q[:, c], relay_key[:, c]) * scale + bias for c in heads]
    before = [tops[:, c] for c in heads]
    top = [jnp.maximum(b, jnp.max(s, axis=1, keepdims=True)) for b, s in zip(before, scores)]
    shrink = [jnp.exp(b - t) for b, t in zip(before, top)]
    probs = [jnp.exp(s - t).astype(BF16) for s, t in zip(scores, top)]
    late = [dot_nn(p, with_ones(relay_value[:, c])) for p, c in zip(probs, heads)]
    total = [totals[:, c] * k + s[:, HDIM:] for c, k, s in zip(heads, shrink, late)]
    summed = [sums[:, c] * k + s[:, 0:HDIM] for c, k, s in zip(heads, shrink, late)]
    attended = jnp.concatenate([(s * (1.0 / t)).astype(BF16) for s, t in zip(summed, total)], axis=1)
    sent = dot_nn(attended, weight_columns(weight, 3)).astype(BF16)
    kept = dot_nn(attended, weight_columns(weight, 2)).astype(BF16)
    logs = [t + jnp.log(n) for t, n in zip(top, total)]
    att[...] = attended
    send[...] = sent
    keep[...] = kept
    for c, part in zip(heads, logs):
        lse[:, c] = part


def project_own_body(att, weight, seen_a, seen_b, send, keep):
    sent = dot_nn(att[...], weight_columns(weight, 1)).astype(BF16)
    kept = dot_nn(att[...], weight_columns(weight, 0)).astype(BF16)
    send[...] = sent
    keep[...] = kept


def join_body(keep, core, q, outgoing, q_copy):
    outgoing[...] = (keep[...].astype(F32) + core[...].astype(F32)).astype(BF16)
    q_copy[...] = q[...]


def hidden_body(inputs, keep, core, across, cot, hidden, rim_near, rim_far):
    frames, width = inputs.shape
    wide = 2 * HALO
    total = inputs[...].astype(F32) + keep[...].astype(F32) + core[...].astype(F32)
    total = (total + across[...].astype(F32)).astype(BF16)
    even = is_even()
    for at, first, last in (
        (slice(0, wide), total[0:wide], total[frames - wide :]),
        (slice(wide, wide + HALO), cot[0:HALO, :], cot[frames - HALO : frames, :]),
    ):
        first, last = first.astype(F32), last.astype(F32)
        rim_near[at, :] = jnp.where(even, last, first).astype(BF16)
        rim_far[at, :] = jnp.where(even, first, last).astype(BF16)
    hidden[...] = total


def shifted_sum(rows, taps_of, count):
    total = None
    for b in range(8):
        part = None
        reach = count if b == 0 else count + 8
        for a in range(4):
            tap = taps_of(8 * a + b)
            if tap is None:
                continue
            term = tap * rows[8 * a : 8 * a + reach]
            part = term if part is None else part + term
        if b:
            part = pltpu.roll(part, reach - b, 0)[0:count]
        total = part if total is None else total + part
    return total


def silu_parts(conv, cots):
    gate = 1.0 / (1.0 + jnp.exp(-conv))
    grad = cots * (gate + conv * gate * (1.0 - gate))
    return conv * gate, grad.astype(BF16).astype(F32)


def taps_forward(taps, cols):
    count = taps.shape[0]
    return lambda s: taps[s - 1 : s, cols] if 1 <= s <= count else None


def taps_backward(taps, cols):
    count = taps.shape[0]
    return lambda s: taps[count - s : count - s + 1, cols] if 1 <= s <= count else None


def conv_inner_body(hidden, cot, taps, seen, rows_out, edge_conv, part_grad):
    frames, width = hidden.shape
    wide = 2 * HALO
    inner = slice(HALO, frames - HALO)
    none = jnp.zeros((wide, HDIM), F32)
    for cols in columns(width):
        own = hidden[:, cols].astype(F32)
        cots = cot[:, cols].astype(F32)
        conv = shifted_sum(
            jnp.concatenate([none, own, none], axis=0), taps_forward(taps, cols), frames + wide
        )
        silu, grad = silu_parts(conv[wide:frames], cots[inner])
        back = shifted_sum(
            jnp.concatenate([none, grad, none], axis=0), taps_backward(taps, cols), frames
        )
        edge_conv[0:wide, cols] = conv[0:wide]
        edge_conv[wide : 2 * wide, cols] = conv[frames : frames + wide]
        rows_out[inner, cols] = (own[inner] + silu).astype(BF16)
        part_grad[:, cols] = cots + back


def conv_edge_body(
    hidden, rim_near, rim_far, cot, taps, rows_in, edge_conv, part_grad, q_second,
    output, grad_input, second_copy,
):
    frames, width = hidden.shape
    wide = 2 * HALO
    even, far = is_even(), far_there()
    rims, cots_of = slice(0, wide), slice(wide, wide + HALO)
    low, high = slice(0, HALO), slice(frames - HALO, frames)
    inner = slice(HALO, frames - HALO)
    none = jnp.zeros((wide, HDIM), F32)

    def sides(rows, cols):
        near = rim_near[rows, cols].astype(F32)
        beyond = jnp.where(far, rim_far[rows, cols].astype(F32), 0.0)
        return jnp.where(even, beyond, near), jnp.where(even, near, beyond)

    for cols in columns(width):
        row_low, row_high = sides(rims, cols)
        cot_low, cot_high = sides(cots_of, cols)
        conv = edge_conv[:, cols] + shifted_sum(
            jnp.concatenate([row_low, none, row_high], axis=0), taps_forward(taps, cols), 2 * wide
        )
        cots = jnp.concatenate(
            [cot_low, cot[low, cols].astype(F32), cot[high, cols].astype(F32), cot_high], axis=0
        )
        silu, grad = silu_parts(conv, cots)
        back = shifted_sum(
            jnp.concatenate([grad[0:wide], none, grad[wide:]], axis=0), taps_backward(taps, cols), 2 * wide
        )
        part = part_grad[:, cols]
        grad_input[:, cols] = jnp.concatenate(
            [part[0:wide] + back[0:wide], part[wide : frames - wide], part[frames - wide :] + back[wide:]],
            axis=0,
        ).astype(BF16)
        output[low, cols] = (hidden[low, cols].astype(F32) + silu[HALO:wide]).astype(BF16)
        output[inner, cols] = rows_in[inner, cols]
        output[high, cols] = (hidden[high, cols].astype(F32) + silu[wide : wide + HALO]).astype(BF16)
    second_copy[...] = q_second[...]


def upstream_chip_body(own, core, weight, partial):
    partial[...] = dot_nt(own[...], weight_columns(weight, 0)) + dot_nt(core[...], weight_columns(weight, 1))


def upstream_across_body(across, weight, before, partial):
    partial[...] = before[...] + dot_nt(across[...], weight_columns(weight, 2))


def upstream_body(cross, weight, att, lse, partial, seen, message, delta):
    frames, width = cross.shape
    heads = columns(width)
    up = (partial[...] + dot_nt(cross[...], weight_columns(weight, 3))).astype(BF16)
    products = [up[:, c].astype(F32) * att[:, c].astype(F32) for c in heads]
    deltas = [jnp.broadcast_to(jnp.sum(p, axis=1, keepdims=True), (frames, HDIM)) for p in products]
    lse_rows = tile_of([lse[:, c] for c in heads]).T
    delta_rows = tile_of(deltas).T
    terms = [term_rows([lse_rows[h : h + 1], delta_rows[h : h + 1]]) for h in range(len(heads))]
    message[0:frames, :] = up
    message[frames : frames + 16, :] = jnp.concatenate(terms, axis=1)
    for c, part in zip(heads, deltas):
        delta[:, c] = part


def query_grad_body(
    scale, q, message, lse, delta, output_here, grad_here, *refs
):
    keys_of, values_of, (output, grad_input, grad_query, held, sems) = refs[0:5], refs[5:10], refs[10:15]
    writes = [
        pltpu.make_async_copy(output_here, output, sems.at[0]),
        pltpu.make_async_copy(grad_here, grad_input, sems.at[1]),
    ]
    for write in writes:
        write.start()
    frames, width = q.shape
    heads = columns(width)
    biases = (None, bias_of(near_swapped()), None, None, bias_of(far_there()))
    every = slice(0, frames)
    keys = [stacked(keys_of, every, c) for c in heads]
    scores = [dot_nt(q[:, c], k) * scale for c, k in zip(heads, keys)]
    dots = [dot_nt(message[0:frames, c], stacked(values_of, every, c)) for c in heads]
    probs = [jnp.exp(by_block(s, biases, [lse[:, c]] * 5)) for c, s in zip(heads, scores)]
    drops = [by_block(d, (None,) * 5, [delta[:, c]] * 5) for c, d in zip(heads, dots)]
    grads = [(p * d * scale).astype(BF16) for p, d in zip(probs, drops)]
    held[...] = jnp.concatenate([dot_nn(g, k).astype(BF16) for g, k in zip(grads, keys)], axis=1)
    writes.append(pltpu.make_async_copy(held, grad_query, sems.at[2]))
    writes[2].start()
    for write in writes:
        write.wait()


def key_part_body(scale, key, value, *refs):
    queries, late_query, messages, (key_part, value_part, late) = refs[0:4], refs[4], refs[5:9], refs[9:12]
    frames, width = key.shape
    heads = columns(width)
    every = slice(0, frames)
    biases = (None, bias_of(near_swapped()), None, None)
    asks = [stacked(queries, every, c) for c in heads]
    ups = [stacked(messages, every, c) for c in heads]
    scores = [dot_nt(key[:, c], a) * scale for c, a in zip(heads, asks)]
    dots = [dot_nt(value[:, c], u) for c, u in zip(heads, ups)]
    last = [dot_nt(key[:, c], late_query[:, c]) * scale + bias_of(far_there()) for c in heads]
    logs = [[stat_rows(m, frames, 0, c) for m in messages] for c in heads]
    deltas = [[stat_rows(m, frames, 1, c) for m in messages] for c in heads]
    probs = [jnp.exp(by_block(s, biases, n)) for s, n in zip(scores, logs)]
    drops = [by_block(d, (None,) * 4, n) for d, n in zip(dots, deltas)]
    grads = [(p * d * scale).astype(BF16) for p, d in zip(probs, drops)]
    value_sums = [dot_nn(p.astype(BF16), u) for p, u in zip(probs, ups)]
    key_sums = [dot_nn(g, a) for g, a in zip(grads, asks)]
    for c, k, v, s in zip(heads, key_sums, value_sums, last):
        key_part[:, c] = k
        value_part[:, c] = v
        late[:, c] = s


def key_grad_body(
    scale, value, query, message, late, key_part, value_part, grad_key, grad_value, held_key, held_value, sems
):
    frames, width = value.shape
    heads = columns(width)
    ups = [message[0:frames, c] for c in heads]
    probs = [jnp.exp(late[:, c] - stat_rows(message, frames, 0, c)) for c in heads]
    dots = [dot_nt(value[:, c], u) for c, u in zip(heads, ups)]
    values = [value_part[:, c] + dot_nn(p.astype(BF16), u) for c, p, u in zip(heads, probs, ups)]
    held_value[...] = jnp.concatenate([v.astype(BF16) for v in values], axis=1)
    value_write = pltpu.make_async_copy(held_value, grad_value, sems.at[0])
    value_write.start()
    drops = [d - stat_rows(message, frames, 1, c) for c, d in zip(heads, dots)]
    grads = [(p * d * scale).astype(BF16) for p, d in zip(probs, drops)]
    keys = [key_part[:, c] + dot_nn(g, query[:, c]) for c, g in zip(heads, grads)]
    held_key[...] = jnp.concatenate([k.astype(BF16) for k in keys], axis=1)
    key_write = pltpu.make_async_copy(held_key, grad_key, sems.at[1])
    key_write.start()
    value_write.wait()
    key_write.wait()


def per_device(query_rows, key_rows, value_rows, inputs, out_weight, kernel, cotangent):
    frames, width = query_rows.shape
    wide = 2 * HALO
    scale = 1.0 / math.sqrt(HDIM)
    tile = shaped((frames, width), BF16)
    tile32 = shaped((frames, width), F32)
    rim = shaped((wide + HALO, width), BF16)
    noted = shaped((frames + 16, width), BF16)

    keys = (key_rows, *window_of(key_rows))
    values = (value_rows, *window_of(value_rows))
    zero = jnp.zeros((), BF16)
    joined = sum(
        lax.pad(rows, zero, ((k * frames, (2 - k) * frames, 0), (0, 0, 0)))
        for k, rows in enumerate((query_rows, key_rows, value_rows))
    )
    q_early, key, value = kernel_call(
        split_body, (tile, tile, tile), (joined, values[3]), 0.1, "split", 1
    )
    keys, values = (key, *keys[1:]), (value, *values[1:])
    q_second = ring(q_early, 1)
    q_first = ring(q_early, 0)
    sums, tops, totals = kernel_call(
        functools.partial(forward_body, scale),
        (tile32, tile32, tile32),
        (q_early, *keys[0:4], *values[0:4]),
        1.0, "forward",
    )
    att, lse, send, keep = kernel_call(
        functools.partial(project_body, scale),
        (tile, tile32, tile, tile),
        (q_early, keys[4], values[4], sums, tops, totals, out_weight),
        1.0, "project",
    )

    core = pair_swap(send, "mp", 1)
    own_send, own_keep = kernel_call(
        project_own_body, (tile, tile), (att, out_weight, q_second, q_first), 0.4, "project_own", 2
    )
    outgoing, q_own = kernel_call(join_body, (tile, tile), (keep, core, q_early), 0.1, "join")
    across = pair_swap(outgoing, "mp", 2)
    own_core = pair_swap(own_send, "mp", 1)
    q_near = inner_swap(q_own)
    hidden, rim_up, rim_down = kernel_call(
        hidden_body,
        (tile, rim, rim),
        (inputs, own_keep, own_core, across, cotangent),
        0.2, "hidden",
    )

    rim_far = outer_swap(rim_down)
    rim_near = pair_swap(rim_up, "ctx", 1)
    rows_out, edge_conv, part_grad = kernel_call(
        conv_inner_body,
        (tile, shaped((2 * wide, width), F32), tile32),
        (hidden, cotangent, kernel, q_near),
        1.6, "conv_inner", 1,
    )
    output_here, grad_here, q_handed = kernel_call(
        conv_edge_body,
        (tile, tile, tile),
        (hidden, rim_near, rim_far, cotangent, kernel, rows_out, edge_conv, part_grad, q_second),
        0.8, "conv_edge",
    )

    gi_across = pair_swap(grad_here, "mp", 2)
    gi_core = pair_swap(grad_here, "mp", 1)
    q_relay = pair_swap(q_handed, "ctx", 1)
    (partial,) = kernel_call(
        upstream_chip_body, (tile32,), (grad_here, gi_core, out_weight), 0.5, "upstream_chip"
    )
    (turned,) = kernel_call(hold_body, (tile,), (gi_across, partial), 0.1, "turn", 1)
    gi_cross = pair_swap(turned, "mp", 1)
    (partial,) = kernel_call(
        upstream_across_body, (tile32,), (turned, out_weight, partial), 0.4, "upstream_across"
    )
    message, delta = kernel_call(
        upstream_body,
        (noted, tile32),
        (gi_cross, out_weight, att, lse, partial, q_relay),
        0.5, "upstream", 1,
    )

    m_near, m_first, m_second, m_relay = window_of(message)
    output, grad_input, grad_query = kernel_call(
        functools.partial(query_grad_body, scale),
        (tile, tile, tile),
        (q_own, message, lse, delta, output_here, grad_here, *keys, *values),
        1.8, "query_grad", 0,
        [pltpu.VMEM((frames, width), BF16), pltpu.SemaphoreType.DMA((3,))], HBM,
    )
    key_part, value_part, late = kernel_call(
        functools.partial(key_part_body, scale),
        (tile32, tile32, tile32),
        (key, value, q_own, q_near, q_first, q_second, q_relay, message, m_near, m_first, m_second),
        1.5, "key_part",
    )
    grad_key, grad_value = kernel_call(
        functools.partial(key_grad_body, scale),
        (tile, tile),
        (value, q_relay, m_relay, late, key_part, value_part),
        1.0, "key_grad", 0,
        [pltpu.VMEM((frames, width), BF16)] * 2 + [pltpu.SemaphoreType.DMA((2,))], HBM,
    )
    return (output, grad_input, grad_query, grad_key, grad_value)


def solution(mesh):
    rows = P("ctx", "mp")
    return jax.shard_map(
        per_device,
        mesh=mesh,
        in_specs=(rows, rows, rows, rows, P("mp", None), P(None, "mp"), rows),
        out_specs=(rows,) * 5,
        check_vma=False,
    )
```

```python
import functools
import math

import jax
import jax.numpy as jnp
from jax import lax
from jax.experimental import pallas as pl
from jax.experimental.pallas import tpu as pltpu
from jax.sharding import PartitionSpec as P

HDIM = 128
F32 = jnp.float32
BF16 = jnp.bfloat16
HALO = 16
NT = (((1,), (1,)), ((), ()))
NN = (((1,), (0,)), ((), ()))


def dot_nt(a, b):
    return lax.dot_general(a, b, NT, preferred_element_type=F32)


def dot_nn(a, b):
    return lax.dot_general(a, b, NN, preferred_element_type=F32)


def pair_swap(block, axis, bit):
    return lax.ppermute(block, axis, [(i, i ^ bit) for i in range(lax.axis_size(axis))])


def ring_routes(count):
    rise = [(i, i + 2) for i in range(0, count - 2, 2)] + [(count - 2, count - 1)]
    fall = [(i, i - 2) for i in range(count - 1, 2, -2)] + [(1, 0)]
    route = rise + fall
    return route, [(b, a) for a, b in route]


def ring(block, way):
    return lax.ppermute(block, "ctx", ring_routes(lax.axis_size("ctx"))[way])


def total_swap(block, partner_of):
    count, places = lax.axis_size("ctx"), lax.axis_size("mp")
    route = []
    for i in range(count):
        other = partner_of(i, count)
        for m in range(places):
            target = i * places + (m ^ 1) if other is None else other * places + m
            route.append((i * places + m, target))
    return lax.ppermute(block, ("ctx", "mp"), route)


def inner_swap(block):
    return total_swap(block, lambda i, count: i ^ 1 if 2 <= i < count - 2 else None)


def outer_swap(block):
    return total_swap(block, lambda i, count: ((i + 1) ^ 1) - 1 if 0 < i < count - 1 else None)


def window_of(block):
    second = ring(block, 1)
    first = ring(block, 0)
    near = inner_swap(block)
    return near, first, second, pair_swap(second, "ctx", 1)


VMEM = pl.BlockSpec(memory_space=pltpu.VMEM)
ANY = pl.BlockSpec(memory_space=pl.ANY)
HBM = pl.BlockSpec(memory_space=pltpu.HBM)


def kernel_call(body, outs, args, micros, name, unread=0, scratch=(), out_space=VMEM):
    return pl.pallas_call(
        body,
        out_shape=outs,
        in_specs=[VMEM] * (len(args) - unread) + [ANY] * unread,
        out_specs=tuple(out_space for _ in outs),
        scratch_shapes=scratch,
        compiler_params=pltpu.CompilerParams(vmem_limit_bytes=24 * 1024 * 1024),
        cost_estimate=pl.CostEstimate(
            flops=0, bytes_accessed=int(micros * 3.69e6), transcendentals=0
        ),
        name=name,
    )(*args)


def shaped(shape, dtype):
    return jax.ShapeDtypeStruct(shape, dtype)


def is_even():
    return lax.axis_index("ctx") % 2 == 0


def near_swapped():
    block = lax.axis_index("ctx")
    return (block >= 2) & (block < lax.axis_size("ctx") - 2)


def far_there():
    block = lax.axis_index("ctx")
    return jnp.where(is_even(), block >= 2, block < lax.axis_size("ctx") - 2)


def bias_of(there):
    return jnp.where(there, jnp.float32(0.0), jnp.float32(-jnp.inf))


def columns(width):
    return [slice(c, c + HDIM) for c in range(0, width, HDIM)]


def stacked(blocks, rows, cols):
    return jnp.concatenate([block[rows, cols] for block in blocks], axis=0)


def with_ones(values):
    return jnp.concatenate([values, jnp.ones_like(values)], axis=1)


def by_block(scores, biases, stats=None):
    parts = []
    for b, bias in enumerate(biases):
        part = scores[:, b * HDIM : (b + 1) * HDIM]
        if stats is not None:
            part = part - stats[b]
        parts.append(part if bias is None else part + bias)
    return jnp.concatenate(parts, axis=1)


def tile_of(wide):
    lane = lax.broadcasted_iota(jnp.int32, (wide[0].shape[0], HDIM), 1)
    tile = jnp.zeros((wide[0].shape[0], HDIM), F32)
    for h, part in enumerate(wide):
        tile = jnp.where(lane == h, part, tile)
    return tile


def term_rows(rows):
    at = lax.broadcasted_iota(jnp.int32, (16, rows[0].shape[1]), 0)
    block = jnp.zeros((16, rows[0].shape[1]), F32)
    for r, rest in enumerate(rows):
        for k in range(3):
            term = rest.astype(BF16).astype(F32)
            rest = rest - term
            block = jnp.where(at == 3 * r + k, term, block)
    return block.astype(BF16)


def stat_rows(message, frames, which, cols):
    terms = message[frames : frames + 16, cols].astype(F32)
    at = 3 * which
    return terms[at : at + 1] + terms[at + 1 : at + 2] + terms[at + 2 : at + 3]


def weight_columns(weight, flip):
    width = weight.shape[0]
    at = (lax.axis_index("mp") ^ flip) * width
    return weight[:, pl.ds(pl.multiple_of(at, 128), width)]


def split_body(joined, taps, seen, query, given):
    frames = query.shape[0]
    query[...] = joined[0:frames, :]
    given[0 : 2 * frames, :] = joined[frames : 3 * frames, :]
    rows, at = pad_rows(taps), 2 * frames
    for k in range(3):
        term = rows.astype(BF16)
        rows = rows - term.astype(F32)
        given[at + k * 2 * HALO : at + (k + 1) * 2 * HALO, :] = term


def pad_rows(taps):
    return jnp.concatenate([taps[...], jnp.zeros((2 * HALO - taps.shape[0], taps.shape[1]), F32)], axis=0)


def taps_of(other, frames):
    rows = other[2 * frames :, :].astype(F32)
    return rows[0 : 2 * HALO] + rows[2 * HALO : 4 * HALO] + rows[4 * HALO :]


def forward_body(scale, q, own, near, first, second, sums, tops, totals):
    frames, width = q.shape
    heads = columns(width)
    blocks = (near, own, first, second)
    biases = (bias_of(near_swapped()), None, None, None)
    keys, values = slice(0, frames), slice(frames, 2 * frames)
    scores = [dot_nt(q[:, c], stacked(blocks, keys, c)) * scale for c in heads]
    scores = [by_block(s, biases) for s in scores]
    top = [jnp.max(s, axis=1, keepdims=True) for s in scores]
    probs = [jnp.exp(s - t).astype(BF16) for s, t in zip(scores, top)]
    summed = [dot_nn(p, with_ones(stacked(blocks, values, c))) for p, c in zip(probs, heads)]
    for c, t, s in zip(heads, top, summed):
        tops[:, c] = jnp.broadcast_to(t, (frames, HDIM))
        sums[:, c] = s[:, 0:HDIM]
        totals[:, c] = s[:, HDIM:]


def project_body(scale, q, relay, sums, tops, totals, weight, att, lse, send, keep):
    frames, width = q.shape
    heads = columns(width)
    bias = bias_of(far_there())
    scores = [dot_nt(q[:, c], relay[0:frames, c]) * scale + bias for c in heads]
    before = [tops[:, c] for c in heads]
    top = [jnp.maximum(b, jnp.max(s, axis=1, keepdims=True)) for b, s in zip(before, scores)]
    shrink = [jnp.exp(b - t) for b, t in zip(before, top)]
    probs = [jnp.exp(s - t).astype(BF16) for s, t in zip(scores, top)]
    late = [dot_nn(p, with_ones(relay[frames : 2 * frames, c])) for p, c in zip(probs, heads)]
    total = [totals[:, c] * k + s[:, HDIM:] for c, k, s in zip(heads, shrink, late)]
    summed = [sums[:, c] * k + s[:, 0:HDIM] for c, k, s in zip(heads, shrink, late)]
    attended = jnp.concatenate([(s * (1.0 / t)).astype(BF16) for s, t in zip(summed, total)], axis=1)
    sent = [dot_nn(attended, weight_columns(weight, flip)).astype(BF16) for flip in (1, 3)]
    kept = [dot_nn(attended, weight_columns(weight, flip)).astype(BF16) for flip in (0, 2)]
    logs = [t + jnp.log(n) for t, n in zip(top, total)]
    att[...] = attended
    send[...] = jnp.concatenate(sent, axis=1)
    keep[...] = jnp.concatenate(kept, axis=1)
    for c, part in zip(heads, logs):
        lse[:, c] = part


def pass_body(send, q, q_second, seen, send_copy, q_copy, second_copy):
    send_copy[...] = send[...]
    q_copy[...] = q[...]
    second_copy[...] = q_second[...]


def join_body(keep, core, q, q_second, seen, chip, q_copy, second_copy):
    chip[...] = (keep[...].astype(F32) + core[...].astype(F32)).astype(BF16)
    q_copy[...] = q[...]
    second_copy[...] = q_second[...]


def hidden_body(chip, across, inputs, cot, other, hidden, rim_near, rim_far):
    frames, width = inputs.shape
    wide = 2 * HALO
    even = is_even()
    mine, its = slice(0, width), slice(width, 2 * width)
    every = slice(0, frames)
    for cols, back, rows, cots in (
        (mine, its, inputs[...], cot[...]),
        (its, mine, other[every, :], other[frames : 2 * frames, :]),
    ):
        mixed = chip[:, cols].astype(F32) + across[:, back].astype(F32)
        total = (rows.astype(F32) + mixed).astype(BF16)
        for at, first, last in (
            (slice(0, wide), total[0:wide], total[frames - wide :]),
            (slice(wide, wide + HALO), cots[0:HALO], cots[frames - HALO :]),
        ):
            first, last = first.astype(F32), last.astype(F32)
            rim_near[at, cols] = jnp.where(even, last, first).astype(BF16)
            rim_far[at, cols] = jnp.where(even, first, last).astype(BF16)
        hidden[:, cols] = total


def shifted_sum(rows, taps_of, count):
    total = None
    for b in range(8):
        part = None
        reach = count if b == 0 else count + 8
        for a in range(4):
            tap = taps_of(8 * a + b)
            if tap is None:
                continue
            term = tap * rows[8 * a : 8 * a + reach]
            part = term if part is None else part + term
        if b:
            part = pltpu.roll(part, reach - b, 0)[0:count]
        total = part if total is None else total + part
    return total


def silu_parts(conv, cots):
    gate = 1.0 / (1.0 + jnp.exp(-conv))
    grad = cots * (gate + conv * gate * (1.0 - gate))
    return conv * gate, grad.astype(BF16).astype(F32)


def taps_forward(taps, count, cols):
    return lambda s: taps[s - 1 : s, cols] if 1 <= s <= count else None


def taps_backward(taps, count, cols):
    return lambda s: taps[count - s : count - s + 1, cols] if 1 <= s <= count else None


def conv_chunks(frames, width, cot, other, taps):
    taps_other = taps_of(other, frames)
    for k, cols in enumerate(columns(2 * width)):
        own = k * HDIM < width
        local = cols if own else slice(cols.start - width, cols.stop - width)
        yield own, cols, local, 0 if own else frames, cot if own else other, taps if own else taps_other


def conv_inner_body(hidden, cot, other, taps, seen_a, seen_b, rows_out, edge_conv, part_grad):
    frames, width = cot.shape
    wide, count = 2 * HALO, taps.shape[0]
    inner = slice(HALO, frames - HALO)
    none = jnp.zeros((wide, HDIM), F32)
    for own, cols, local, at, cots_of, tap in conv_chunks(frames, width, cot, other, taps):
        rows = hidden[:, cols].astype(F32)
        cots = cots_of[at : at + frames, local].astype(F32)
        conv = shifted_sum(
            jnp.concatenate([none, rows, none], axis=0), taps_forward(tap, count, local), frames + wide
        )
        silu, grad = silu_parts(conv[wide:frames], cots[inner])
        back = shifted_sum(
            jnp.concatenate([none, grad, none], axis=0), taps_backward(tap, count, local), frames
        )
        edge_conv[0:wide, cols] = conv[0:wide]
        edge_conv[wide : 2 * wide, cols] = conv[frames : frames + wide]
        if own:
            rows_out[inner, cols] = (rows[inner] + silu).astype(BF16)
        part_grad[:, cols] = cots + back


def conv_edge_body(
    hidden, rim_near, rim_far, cot, other, taps, rows_in, edge_conv, part_grad, output, grad_input,
):
    frames, width = cot.shape
    wide, count = 2 * HALO, taps.shape[0]
    even, far = is_even(), far_there()
    rims, cots_of = slice(0, wide), slice(wide, wide + HALO)
    low, high = slice(0, HALO), slice(frames - HALO, frames)
    inner = slice(HALO, frames - HALO)
    none = jnp.zeros((wide, HDIM), F32)

    def sides(rows, cols):
        near = rim_near[rows, cols].astype(F32)
        beyond = jnp.where(far, rim_far[rows, cols].astype(F32), 0.0)
        return jnp.where(even, beyond, near), jnp.where(even, near, beyond)

    for own, cols, local, at, block, tap in conv_chunks(frames, width, cot, other, taps):
        row_low, row_high = sides(rims, cols)
        cot_low, cot_high = sides(cots_of, cols)
        conv = edge_conv[:, cols] + shifted_sum(
            jnp.concatenate([row_low, none, row_high], axis=0), taps_forward(tap, count, local), 2 * wide
        )
        first = block[at : at + HALO, local].astype(F32)
        last = block[at + frames - HALO : at + frames, local].astype(F32)
        cots = jnp.concatenate([cot_low, first, last, cot_high], axis=0)
        silu, grad = silu_parts(conv, cots)
        back = shifted_sum(
            jnp.concatenate([grad[0:wide], none, grad[wide:]], axis=0), taps_backward(tap, count, local), 2 * wide
        )
        part = part_grad[:, cols]
        grad_input[:, cols] = jnp.concatenate(
            [part[0:wide] + back[0:wide], part[wide : frames - wide], part[frames - wide :] + back[wide:]],
            axis=0,
        ).astype(BF16)
        if own:
            output[low, cols] = (hidden[low, cols].astype(F32) + silu[HALO:wide]).astype(BF16)
            output[inner, cols] = rows_in[inner, cols]
            output[high, cols] = (hidden[high, cols].astype(F32) + silu[wide : wide + HALO]).astype(BF16)


def upstream_part(grads, weight, flips):
    width = weight.shape[0]
    return sum(
        dot_nt(grads[:, k * width : (k + 1) * width], weight_columns(weight, flip))
        for k, flip in enumerate(flips)
    )


def upstream_own_body(own, weight, partial):
    partial[...] = upstream_part(own, weight, (0, 2))


def upstream_body(core, weight, att, lse, partial, message, delta):
    frames, width = att.shape
    heads = columns(width)
    up = (partial[...] + upstream_part(core, weight, (1, 3))).astype(BF16)
    products = [up[:, c].astype(F32) * att[:, c].astype(F32) for c in heads]
    deltas = [jnp.broadcast_to(jnp.sum(p, axis=1, keepdims=True), (frames, HDIM)) for p in products]
    lse_rows = tile_of([lse[:, c] for c in heads]).T
    delta_rows = tile_of(deltas).T
    terms = [term_rows([lse_rows[h : h + 1], delta_rows[h : h + 1]]) for h in range(len(heads))]
    message[0:frames, :] = up
    message[frames : frames + 16, :] = jnp.concatenate(terms, axis=1)
    for c, part in zip(heads, deltas):
        delta[:, c] = part


def query_grad_body(
    scale, q, own, near, first, second, relay, message, lse, delta, output_here, grad_here,
    output, grad_input, grad_query, held, sems,
):
    writes = [
        pltpu.make_async_copy(output_here, output, sems.at[0]),
        pltpu.make_async_copy(grad_here.at[:, pl.ds(0, q.shape[1])], grad_input, sems.at[1]),
    ]
    for write in writes:
        write.start()
    frames, width = q.shape
    heads = columns(width)
    blocks = (near, own, first, second, relay)
    biases = (bias_of(near_swapped()), None, None, None, bias_of(far_there()))
    above, below = slice(0, frames), slice(frames, 2 * frames)
    keys = [stacked(blocks, above, c) for c in heads]
    scores = [dot_nt(q[:, c], k) * scale for c, k in zip(heads, keys)]
    dots = [dot_nt(message[0:frames, c], stacked(blocks, below, c)) for c in heads]
    probs = [jnp.exp(by_block(s, biases, [lse[:, c]] * 5)) for c, s in zip(heads, scores)]
    drops = [by_block(d, (None,) * 5, [delta[:, c]] * 5) for c, d in zip(heads, dots)]
    grads = [(p * d * scale).astype(BF16) for p, d in zip(probs, drops)]
    held[...] = jnp.concatenate([dot_nn(g, k).astype(BF16) for g, k in zip(grads, keys)], axis=1)
    writes.append(pltpu.make_async_copy(held, grad_query, sems.at[2]))
    writes[2].start()
    for write in writes:
        write.wait()


def key_part_body(scale, own, *refs):
    queries, late_query, messages, (key_part, value_part, late) = refs[0:4], refs[4], refs[5:9], refs[9:12]
    frames = own.shape[0] // 2
    heads = columns(own.shape[1])
    above, below = slice(0, frames), slice(frames, 2 * frames)
    biases = (None, bias_of(near_swapped()), None, None)
    asks = [stacked(queries, above, c) for c in heads]
    ups = [stacked(messages, above, c) for c in heads]
    scores = [dot_nt(own[above, c], a) * scale for c, a in zip(heads, asks)]
    dots = [dot_nt(own[below, c], u) for c, u in zip(heads, ups)]
    last = [dot_nt(own[above, c], late_query[:, c]) * scale + bias_of(far_there()) for c in heads]
    logs = [[stat_rows(m, frames, 0, c) for m in messages] for c in heads]
    deltas = [[stat_rows(m, frames, 1, c) for m in messages] for c in heads]
    probs = [jnp.exp(by_block(s, biases, n)) for s, n in zip(scores, logs)]
    drops = [by_block(d, (None,) * 4, n) for d, n in zip(dots, deltas)]
    grads = [(p * d * scale).astype(BF16) for p, d in zip(probs, drops)]
    value_sums = [dot_nn(p.astype(BF16), u) for p, u in zip(probs, ups)]
    key_sums = [dot_nn(g, a) for g, a in zip(grads, asks)]
    for c, k, v, s in zip(heads, key_sums, value_sums, last):
        key_part[:, c] = k
        value_part[:, c] = v
        late[:, c] = s


def key_grad_body(
    scale, own, query, message, late, key_part, value_part, grad_key, grad_value, held_key, held_value, sems
):
    frames = own.shape[0] // 2
    heads = columns(own.shape[1])
    above, below = slice(0, frames), slice(frames, 2 * frames)
    ups = [message[above, c] for c in heads]
    probs = [jnp.exp(late[:, c] - stat_rows(message, frames, 0, c)) for c in heads]
    dots = [dot_nt(own[below, c], u) for c, u in zip(heads, ups)]
    values = [value_part[:, c] + dot_nn(p.astype(BF16), u) for c, p, u in zip(heads, probs, ups)]
    held_value[...] = jnp.concatenate([v.astype(BF16) for v in values], axis=1)
    value_write = pltpu.make_async_copy(held_value, grad_value, sems.at[0])
    value_write.start()
    drops = [d - stat_rows(message, frames, 1, c) for c, d in zip(heads, dots)]
    grads = [(p * d * scale).astype(BF16) for p, d in zip(probs, drops)]
    keys = [key_part[:, c] + dot_nn(g, query[:, c]) for c, g in zip(heads, grads)]
    held_key[...] = jnp.concatenate([k.astype(BF16) for k in keys], axis=1)
    key_write = pltpu.make_async_copy(held_key, grad_key, sems.at[1])
    key_write.start()
    value_write.wait()
    key_write.wait()


def per_device(query_rows, key_rows, value_rows, inputs, out_weight, kernel, cotangent):
    frames, width = query_rows.shape
    wide = 2 * HALO
    scale = 1.0 / math.sqrt(HDIM)
    tile = shaped((frames, width), BF16)
    tile32 = shaped((frames, width), F32)
    rim = shaped((wide + HALO, 2 * width), BF16)
    both = shaped((frames, 2 * width), BF16)
    noted = shaped((frames + 16, width), BF16)

    zero = jnp.zeros((), BF16)
    kv = lax.pad(key_rows, zero, ((0, frames, 0), (0, 0, 0))) + lax.pad(
        value_rows, zero, ((frames, 0, 0), (0, 0, 0))
    )
    near, first, second, relay = window_of(kv)
    joined = sum(
        lax.pad(rows, zero, ((k * frames, (2 - k) * frames, 0), (0, 0, 0)))
        for k, rows in enumerate((query_rows, inputs, cotangent))
    )
    q_early, given = kernel_call(
        split_body, (tile, shaped((2 * frames + 3 * wide, width), BF16)), (joined, kernel, second),
        0.02, "split", 1,
    )
    other = pair_swap(given, "mp", 2)
    q_second = ring(q_early, 1)
    q_first = ring(q_early, 0)
    sums, tops, totals = kernel_call(
        functools.partial(forward_body, scale),
        (tile32, tile32, tile32),
        (q_early, kv, near, first, second),
        1.0, "forward",
    )
    att, lse, send, keep = kernel_call(
        functools.partial(project_body, scale),
        (tile, tile32, both, both),
        (q_early, relay, sums, tops, totals, out_weight),
        1.0, "project",
    )

    send, q_own, q_handed = kernel_call(
        pass_body, (both, tile, tile), (send, q_early, q_second, q_first), 0.1, "pass", 1
    )
    core = pair_swap(send, "mp", 1)
    chip, q_own, q_handed = kernel_call(
        join_body, (both, tile, tile), (keep, core, q_own, q_handed, other), 0.02, "join", 1
    )
    across = pair_swap(chip, "mp", 2)
    q_near = inner_swap(q_own)
    q_relay = pair_swap(q_handed, "ctx", 1)
    hidden, rim_up, rim_down = kernel_call(
        hidden_body,
        (both, rim, rim),
        (chip, across, inputs, cotangent, other),
        0.2, "hidden",
    )

    rim_far = outer_swap(rim_down)
    rim_near = pair_swap(rim_up, "ctx", 1)
    rows_out, edge_conv, part_grad = kernel_call(
        conv_inner_body,
        (tile, shaped((2 * wide, 2 * width), F32), shaped((frames, 2 * width), F32)),
        (hidden, cotangent, other, kernel, q_near, q_relay),
        3.1, "conv_inner", 2,
    )
    output_here, grad_here = kernel_call(
        conv_edge_body,
        (tile, both),
        (hidden, rim_near, rim_far, cotangent, other, kernel, rows_out, edge_conv, part_grad),
        1.4, "conv_edge",
    )

    gi_core = pair_swap(grad_here, "mp", 1)
    (partial,) = kernel_call(upstream_own_body, (tile32,), (grad_here, out_weight), 0.5, "upstream_own")
    message, delta = kernel_call(
        upstream_body, (noted, tile32), (gi_core, out_weight, att, lse, partial), 0.6, "upstream"
    )

    m_near, m_first, m_second, m_relay = window_of(message)
    output, grad_input, grad_query = kernel_call(
        functools.partial(query_grad_body, scale),
        (tile, tile, tile),
        (q_own, kv, near, first, second, relay, message, lse, delta, output_here, grad_here),
        1.8, "query_grad", 0,
        [pltpu.VMEM((frames, width), BF16), pltpu.SemaphoreType.DMA((3,))], HBM,
    )
    key_part, value_part, late = kernel_call(
        functools.partial(key_part_body, scale),
        (tile32, tile32, tile32),
        (kv, q_own, q_near, q_first, q_second, q_relay, message, m_near, m_first, m_second),
        1.5, "key_part",
    )
    grad_key, grad_value = kernel_call(
        functools.partial(key_grad_body, scale),
        (tile, tile),
        (kv, q_relay, m_relay, late, key_part, value_part),
        1.0, "key_grad", 0,
        [pltpu.VMEM((frames, width), BF16)] * 2 + [pltpu.SemaphoreType.DMA((2,))], HBM,
    )
    return (output, grad_input, grad_query, grad_key, grad_value)


def solution(mesh):
    rows = P("ctx", "mp")
    return jax.shard_map(
        per_device,
        mesh=mesh,
        in_specs=(rows, rows, rows, rows, P("mp", None), P(None, "mp"), rows),
        out_specs=(rows,) * 5,
        check_vma=False,
    )
```

```python
import functools
import math

import jax
import jax.numpy as jnp
from jax import lax
from jax.experimental import pallas as pl
from jax.experimental.pallas import tpu as pltpu
from jax.sharding import PartitionSpec as P

HDIM = 128
F32 = jnp.float32
BF16 = jnp.bfloat16
HALO = 16
NT = (((1,), (1,)), ((), ()))
NN = (((1,), (0,)), ((), ()))


def dot_nt(a, b):
    return lax.dot_general(a, b, NT, preferred_element_type=F32)


def dot_nn(a, b):
    return lax.dot_general(a, b, NN, preferred_element_type=F32)


def pair_swap(block, axis, bit):
    return lax.ppermute(block, axis, [(i, i ^ bit) for i in range(lax.axis_size(axis))])


def ring_routes(count):
    rise = [(i, i + 2) for i in range(0, count - 2, 2)] + [(count - 2, count - 1)]
    fall = [(i, i - 2) for i in range(count - 1, 2, -2)] + [(1, 0)]
    route = rise + fall
    return route, [(b, a) for a, b in route]


def ring(block, way):
    return lax.ppermute(block, "ctx", ring_routes(lax.axis_size("ctx"))[way])


def total_swap(block, partner_of):
    count, places = lax.axis_size("ctx"), lax.axis_size("mp")
    route = []
    for i in range(count):
        other = partner_of(i, count)
        for m in range(places):
            target = i * places + (m ^ 1) if other is None else other * places + m
            route.append((i * places + m, target))
    return lax.ppermute(block, ("ctx", "mp"), route)


def inner_swap(block):
    return total_swap(block, lambda i, count: i ^ 1 if 2 <= i < count - 2 else None)


def outer_swap(block):
    return total_swap(block, lambda i, count: ((i + 1) ^ 1) - 1 if 0 < i < count - 1 else None)


def window_of(block, before_relay=lambda second: second):
    second = ring(block, 1)
    first = ring(block, 0)
    near = inner_swap(block)
    second = before_relay(second)
    return near, first, second, pair_swap(second, "ctx", 1)


VMEM = pl.BlockSpec(memory_space=pltpu.VMEM)
ANY = pl.BlockSpec(memory_space=pl.ANY)
HBM = pl.BlockSpec(memory_space=pltpu.HBM)


def kernel_call(body, outs, args, micros, name, unread=0, scratch=(), out_space=VMEM):
    return pl.pallas_call(
        body,
        out_shape=outs,
        in_specs=[VMEM] * (len(args) - unread) + [ANY] * unread,
        out_specs=tuple(out_space for _ in outs),
        scratch_shapes=scratch,
        compiler_params=pltpu.CompilerParams(vmem_limit_bytes=24 * 1024 * 1024),
        cost_estimate=pl.CostEstimate(
            flops=0, bytes_accessed=int(micros * 3.69e6), transcendentals=0
        ),
        name=name,
    )(*args)


def shaped(shape, dtype):
    return jax.ShapeDtypeStruct(shape, dtype)


def is_even():
    return lax.axis_index("ctx") % 2 == 0


def near_swapped():
    block = lax.axis_index("ctx")
    return (block >= 2) & (block < lax.axis_size("ctx") - 2)


def far_there():
    block = lax.axis_index("ctx")
    return jnp.where(is_even(), block >= 2, block < lax.axis_size("ctx") - 2)


def bias_of(there):
    return jnp.where(there, jnp.float32(0.0), jnp.float32(-jnp.inf))


def columns(width):
    return [slice(c, c + HDIM) for c in range(0, width, HDIM)]


def stacked(blocks, rows, cols):
    return jnp.concatenate([block[rows, cols] for block in blocks], axis=0)


def with_ones(values):
    return jnp.concatenate([values, jnp.ones_like(values)], axis=1)


def by_block(scores, biases, stats=None):
    parts = []
    for b, bias in enumerate(biases):
        part = scores[:, b * HDIM : (b + 1) * HDIM]
        if stats is not None:
            part = part - stats[b]
        parts.append(part if bias is None else part + bias)
    return jnp.concatenate(parts, axis=1)


def tile_of(wide):
    lane = lax.broadcasted_iota(jnp.int32, (wide[0].shape[0], HDIM), 1)
    tile = jnp.zeros((wide[0].shape[0], HDIM), F32)
    for h, part in enumerate(wide):
        tile = jnp.where(lane == h, part, tile)
    return tile


def term_rows(rows):
    at = lax.broadcasted_iota(jnp.int32, (16, rows[0].shape[1]), 0)
    block = jnp.zeros((16, rows[0].shape[1]), F32)
    for r, rest in enumerate(rows):
        for k in range(3):
            term = rest.astype(BF16).astype(F32)
            rest = rest - term
            block = jnp.where(at == 3 * r + k, term, block)
    return block.astype(BF16)


def stat_rows(message, frames, which, cols):
    terms = message[frames : frames + 16, cols].astype(F32)
    at = 3 * which
    return terms[at : at + 1] + terms[at + 1 : at + 2] + terms[at + 2 : at + 3]


def weight_columns(weight, flip):
    width = weight.shape[0]
    at = (lax.axis_index("mp") ^ flip) * width
    return weight[:, pl.ds(pl.multiple_of(at, 128), width)]


def hold_body(block, seen, held):
    held[...] = block[...]


def split_body(joined, seen, *parts):
    frames = parts[0].shape[0]
    for k, part in enumerate(parts):
        part[...] = joined[k * frames : (k + 1) * frames, :]


def forward_body(scale, q, own, near, first, second, *refs):
    sums, tops, totals = refs[-3:]
    frames, width = q.shape
    heads = columns(width)
    blocks = (near, own, first, second)
    biases = (bias_of(near_swapped()), None, None, None)
    keys, values = slice(0, frames), slice(frames, 2 * frames)
    scores = [dot_nt(q[:, c], stacked(blocks, keys, c)) * scale for c in heads]
    scores = [by_block(s, biases) for s in scores]
    top = [jnp.max(s, axis=1, keepdims=True) for s in scores]
    probs = [jnp.exp(s - t).astype(BF16) for s, t in zip(scores, top)]
    summed = [dot_nn(p, with_ones(stacked(blocks, values, c))) for p, c in zip(probs, heads)]
    for c, t, s in zip(heads, top, summed):
        tops[:, c] = jnp.broadcast_to(t, (frames, HDIM))
        sums[:, c] = s[:, 0:HDIM]
        totals[:, c] = s[:, HDIM:]


def project_body(scale, q, relay, sums, tops, totals, weight, att, lse, send, keep):
    frames, width = q.shape
    heads = columns(width)
    bias = bias_of(far_there())
    scores = [dot_nt(q[:, c], relay[0:frames, c]) * scale + bias for c in heads]
    before = [tops[:, c] for c in heads]
    top = [jnp.maximum(b, jnp.max(s, axis=1, keepdims=True)) for b, s in zip(before, scores)]
    shrink = [jnp.exp(b - t) for b, t in zip(before, top)]
    probs = [jnp.exp(s - t).astype(BF16) for s, t in zip(scores, top)]
    late = [dot_nn(p, with_ones(relay[frames : 2 * frames, c])) for p, c in zip(probs, heads)]
    total = [totals[:, c] * k + s[:, HDIM:] for c, k, s in zip(heads, shrink, late)]
    summed = [sums[:, c] * k + s[:, 0:HDIM] for c, k, s in zip(heads, shrink, late)]
    attended = jnp.concatenate([(s * (1.0 / t)).astype(BF16) for s, t in zip(summed, total)], axis=1)
    sent = [dot_nn(attended, weight_columns(weight, flip)).astype(BF16) for flip in (1, 3)]
    kept = [dot_nn(attended, weight_columns(weight, flip)).astype(BF16) for flip in (0, 2)]
    logs = [t + jnp.log(n) for t, n in zip(top, total)]
    att[...] = attended
    send[...] = jnp.concatenate(sent, axis=1)
    keep[...] = jnp.concatenate(kept, axis=1)
    for c, part in zip(heads, logs):
        lse[:, c] = part


def join_body(keep, core, q, chip, q_copy):
    chip[...] = (keep[...].astype(F32) + core[...].astype(F32)).astype(BF16)
    q_copy[...] = q[...]


def hidden_body(chip, across, inputs, cot, inputs_other, cot_other, hidden, rim_near, rim_far):
    frames, width = inputs.shape
    wide = 2 * HALO
    even = is_even()
    mine, its = slice(0, width), slice(width, 2 * width)
    for cols, back, rows, cots in (
        (mine, its, inputs[...], cot[...]),
        (its, mine, inputs_other[...], cot_other[...]),
    ):
        mixed = chip[:, cols].astype(F32) + across[:, back].astype(F32)
        total = (rows.astype(F32) + mixed).astype(BF16)
        for at, first, last in (
            (slice(0, wide), total[0:wide], total[frames - wide :]),
            (slice(wide, wide + HALO), cots[0:HALO], cots[frames - HALO :]),
        ):
            first, last = first.astype(F32), last.astype(F32)
            rim_near[at, cols] = jnp.where(even, last, first).astype(BF16)
            rim_far[at, cols] = jnp.where(even, first, last).astype(BF16)
        hidden[:, cols] = total


def shifted_sum(rows, taps_of, count):
    total = None
    for b in range(8):
        part = None
        reach = count if b == 0 else count + 8
        for a in range(4):
            tap = taps_of(8 * a + b)
            if tap is None:
                continue
            term = tap * rows[8 * a : 8 * a + reach]
            part = term if part is None else part + term
        if b:
            part = pltpu.roll(part, reach - b, 0)[0:count]
        total = part if total is None else total + part
    return total


def silu_parts(conv, cots):
    gate = 1.0 / (1.0 + jnp.exp(-conv))
    grad = cots * (gate + conv * gate * (1.0 - gate))
    return conv * gate, grad.astype(BF16).astype(F32)


def taps_forward(taps, count, cols):
    return lambda s: taps[s - 1 : s, cols] if 1 <= s <= count else None


def taps_backward(taps, count, cols):
    return lambda s: taps[count - s : count - s + 1, cols] if 1 <= s <= count else None


def conv_chunks(width, cot, cot_other, taps, taps_other):
    for k, cols in enumerate(columns(2 * width)):
        own = k * HDIM < width
        local = cols if own else slice(cols.start - width, cols.stop - width)
        yield own, cols, local, cot if own else cot_other, taps if own else taps_other


def conv_inner_body(hidden, cot, cot_other, taps, taps_other, seen_a, seen_b, rows_out, edge_conv, part_grad):
    frames, width = cot.shape
    wide, count = 2 * HALO, taps.shape[0]
    inner = slice(HALO, frames - HALO)
    none = jnp.zeros((wide, HDIM), F32)
    for own, cols, local, cots_of, tap in conv_chunks(width, cot, cot_other, taps, taps_other):
        rows = hidden[:, cols].astype(F32)
        cots = cots_of[:, local].astype(F32)
        conv = shifted_sum(
            jnp.concatenate([none, rows, none], axis=0), taps_forward(tap, count, local), frames + wide
        )
        silu, grad = silu_parts(conv[wide:frames], cots[inner])
        back = shifted_sum(
            jnp.concatenate([none, grad, none], axis=0), taps_backward(tap, count, local), frames
        )
        edge_conv[0:wide, cols] = conv[0:wide]
        edge_conv[wide : 2 * wide, cols] = conv[frames : frames + wide]
        if own:
            rows_out[inner, cols] = (rows[inner] + silu).astype(BF16)
        part_grad[:, cols] = cots + back


def conv_edge_body(
    hidden, rim_near, rim_far, cot, cot_other, taps, taps_other, rows_in, edge_conv, part_grad,
    q_second, output, grad_input, second_copy,
):
    frames, width = cot.shape
    wide, count = 2 * HALO, taps.shape[0]
    even, far = is_even(), far_there()
    rims, cots_of = slice(0, wide), slice(wide, wide + HALO)
    low, high = slice(0, HALO), slice(frames - HALO, frames)
    inner = slice(HALO, frames - HALO)
    none = jnp.zeros((wide, HDIM), F32)

    def sides(rows, cols):
        near = rim_near[rows, cols].astype(F32)
        beyond = jnp.where(far, rim_far[rows, cols].astype(F32), 0.0)
        return jnp.where(even, beyond, near), jnp.where(even, near, beyond)

    for own, cols, local, block, tap in conv_chunks(width, cot, cot_other, taps, taps_other):
        row_low, row_high = sides(rims, cols)
        cot_low, cot_high = sides(cots_of, cols)
        conv = edge_conv[:, cols] + shifted_sum(
            jnp.concatenate([row_low, none, row_high], axis=0), taps_forward(tap, count, local), 2 * wide
        )
        first = block[low, local].astype(F32)
        last = block[high, local].astype(F32)
        cots = jnp.concatenate([cot_low, first, last, cot_high], axis=0)
        silu, grad = silu_parts(conv, cots)
        back = shifted_sum(
            jnp.concatenate([grad[0:wide], none, grad[wide:]], axis=0), taps_backward(tap, count, local), 2 * wide
        )
        part = part_grad[:, cols]
        grad_input[:, cols] = jnp.concatenate(
            [part[0:wide] + back[0:wide], part[wide : frames - wide], part[frames - wide :] + back[wide:]],
            axis=0,
        ).astype(BF16)
        if own:
            output[low, cols] = (hidden[low, cols].astype(F32) + silu[HALO:wide]).astype(BF16)
            output[inner, cols] = rows_in[inner, cols]
            output[high, cols] = (hidden[high, cols].astype(F32) + silu[wide : wide + HALO]).astype(BF16)
    second_copy[...] = q_second[...]


def upstream_part(grads, weight, flips):
    width = weight.shape[0]
    return sum(
        dot_nt(grads[:, k * width : (k + 1) * width], weight_columns(weight, flip))
        for k, flip in enumerate(flips)
    )


def upstream_own_body(own, weight, partial):
    partial[...] = upstream_part(own, weight, (0, 2))


def upstream_body(core, weight, att, lse, partial, seen, message, delta):
    frames, width = att.shape
    heads = columns(width)
    up = (partial[...] + upstream_part(core, weight, (1, 3))).astype(BF16)
    products = [up[:, c].astype(F32) * att[:, c].astype(F32) for c in heads]
    deltas = [jnp.broadcast_to(jnp.sum(p, axis=1, keepdims=True), (frames, HDIM)) for p in products]
    lse_rows = tile_of([lse[:, c] for c in heads]).T
    delta_rows = tile_of(deltas).T
    terms = [term_rows([lse_rows[h : h + 1], delta_rows[h : h + 1]]) for h in range(len(heads))]
    message[0:frames, :] = up
    message[frames : frames + 16, :] = jnp.concatenate(terms, axis=1)
    for c, part in zip(heads, deltas):
        delta[:, c] = part


def query_grad_body(
    scale, q, own, near, first, second, relay, message, lse, delta, output_here, grad_here,
    output, grad_input, grad_query, held, sems,
):
    writes = [
        pltpu.make_async_copy(output_here, output, sems.at[0]),
        pltpu.make_async_copy(grad_here.at[:, pl.ds(0, q.shape[1])], grad_input, sems.at[1]),
    ]
    for write in writes:
        write.start()
    frames, width = q.shape
    heads = columns(width)
    blocks = (near, own, first, second, relay)
    biases = (bias_of(near_swapped()), None, None, None, bias_of(far_there()))
    above, below = slice(0, frames), slice(frames, 2 * frames)
    keys = [stacked(blocks, above, c) for c in heads]
    scores = [dot_nt(q[:, c], k) * scale for c, k in zip(heads, keys)]
    dots = [dot_nt(message[0:frames, c], stacked(blocks, below, c)) for c in heads]
    probs = [jnp.exp(by_block(s, biases, [lse[:, c]] * 5)) for c, s in zip(heads, scores)]
    drops = [by_block(d, (None,) * 5, [delta[:, c]] * 5) for c, d in zip(heads, dots)]
    grads = [(p * d * scale).astype(BF16) for p, d in zip(probs, drops)]
    held[...] = jnp.concatenate([dot_nn(g, k).astype(BF16) for g, k in zip(grads, keys)], axis=1)
    writes.append(pltpu.make_async_copy(held, grad_query, sems.at[2]))
    writes[2].start()
    for write in writes:
        write.wait()


def key_part_body(scale, own, *refs):
    queries, late_query, messages, (key_part, value_part, late) = refs[0:4], refs[4], refs[5:9], refs[9:12]
    frames = own.shape[0] // 2
    heads = columns(own.shape[1])
    above, below = slice(0, frames), slice(frames, 2 * frames)
    biases = (None, bias_of(near_swapped()), None, None)
    asks = [stacked(queries, above, c) for c in heads]
    ups = [stacked(messages, above, c) for c in heads]
    scores = [dot_nt(own[above, c], a) * scale for c, a in zip(heads, asks)]
    dots = [dot_nt(own[below, c], u) for c, u in zip(heads, ups)]
    last = [dot_nt(own[above, c], late_query[:, c]) * scale + bias_of(far_there()) for c in heads]
    logs = [[stat_rows(m, frames, 0, c) for m in messages] for c in heads]
    deltas = [[stat_rows(m, frames, 1, c) for m in messages] for c in heads]
    probs = [jnp.exp(by_block(s, biases, n)) for s, n in zip(scores, logs)]
    drops = [by_block(d, (None,) * 4, n) for d, n in zip(dots, deltas)]
    grads = [(p * d * scale).astype(BF16) for p, d in zip(probs, drops)]
    value_sums = [dot_nn(p.astype(BF16), u) for p, u in zip(probs, ups)]
    key_sums = [dot_nn(g, a) for g, a in zip(grads, asks)]
    for c, k, v, s in zip(heads, key_sums, value_sums, last):
        key_part[:, c] = k
        value_part[:, c] = v
        late[:, c] = s


def key_grad_body(
    scale, own, query, message, late, key_part, value_part, grad_key, grad_value, held_key, held_value, sems
):
    frames = own.shape[0] // 2
    heads = columns(own.shape[1])
    above, below = slice(0, frames), slice(frames, 2 * frames)
    ups = [message[above, c] for c in heads]
    probs = [jnp.exp(late[:, c] - stat_rows(message, frames, 0, c)) for c in heads]
    dots = [dot_nt(own[below, c], u) for c, u in zip(heads, ups)]
    values = [value_part[:, c] + dot_nn(p.astype(BF16), u) for c, p, u in zip(heads, probs, ups)]
    held_value[...] = jnp.concatenate([v.astype(BF16) for v in values], axis=1)
    value_write = pltpu.make_async_copy(held_value, grad_value, sems.at[0])
    value_write.start()
    drops = [d - stat_rows(message, frames, 1, c) for c, d in zip(heads, dots)]
    grads = [(p * d * scale).astype(BF16) for p, d in zip(probs, drops)]
    keys = [key_part[:, c] + dot_nn(g, query[:, c]) for c, g in zip(heads, grads)]
    held_key[...] = jnp.concatenate([k.astype(BF16) for k in keys], axis=1)
    key_write = pltpu.make_async_copy(held_key, grad_key, sems.at[1])
    key_write.start()
    value_write.wait()
    key_write.wait()


def per_device(query_rows, key_rows, value_rows, inputs, out_weight, kernel, cotangent):
    frames, width = query_rows.shape
    wide = 2 * HALO
    scale = 1.0 / math.sqrt(HDIM)
    tile = shaped((frames, width), BF16)
    tile32 = shaped((frames, width), F32)
    rim = shaped((wide + HALO, 2 * width), BF16)
    both = shaped((frames, 2 * width), BF16)
    noted = shaped((frames + 16, width), BF16)

    zero = jnp.zeros((), BF16)
    kv = lax.pad(key_rows, zero, ((0, frames, 0), (0, 0, 0))) + lax.pad(
        value_rows, zero, ((frames, 0, 0), (0, 0, 0))
    )
    other = [pair_swap(block, "mp", 2) for block in (inputs, cotangent, kernel)]
    near, first, second, relay = window_of(
        kv,
        lambda second: kernel_call(
            hold_body, (shaped(kv.shape, BF16),), (second, other[0]), 0.1, "turn", 1
        )[0],
    )
    joined = sum(
        lax.pad(rows, zero, ((k * frames, (2 - k) * frames, 0), (0, 0, 0)))
        for k, rows in enumerate((query_rows, inputs, cotangent))
    )
    query, inputs, cotangent = kernel_call(
        split_body, (tile, tile, tile), (joined, second), 0.1, "split", 1
    )
    sums, tops, totals = kernel_call(
        functools.partial(forward_body, scale),
        (tile32, tile32, tile32),
        (query, kv, near, first, second, *other[1:]),
        1.0, "forward", 2,
    )
    att, lse, send, keep = kernel_call(
        functools.partial(project_body, scale),
        (tile, tile32, both, both),
        (query, relay, sums, tops, totals, out_weight),
        1.0, "project",
    )

    core = pair_swap(send, "mp", 1)
    chip, q_own = kernel_call(join_body, (both, tile), (keep, core, query), 0.1, "join")
    across = pair_swap(chip, "mp", 2)
    q_second = ring(q_own, 1)
    q_first = ring(q_own, 0)
    q_near = inner_swap(q_own)
    hidden, rim_up, rim_down = kernel_call(
        hidden_body,
        (both, rim, rim),
        (chip, across, inputs, cotangent, *other[0:2]),
        0.2, "hidden",
    )

    rim_far = outer_swap(rim_down)
    rim_near = pair_swap(rim_up, "ctx", 1)
    rows_out, edge_conv, part_grad = kernel_call(
        conv_inner_body,
        (tile, shaped((2 * wide, 2 * width), F32), shaped((frames, 2 * width), F32)),
        (hidden, cotangent, other[1], kernel, other[2], q_near, q_first),
        3.1, "conv_inner", 2,
    )
    output_here, grad_here, q_handed = kernel_call(
        conv_edge_body,
        (tile, both, tile),
        (hidden, rim_near, rim_far, cotangent, other[1], kernel, other[2], rows_out, edge_conv, part_grad)
        + (q_second,),
        1.4, "conv_edge",
    )

    gi_core = pair_swap(grad_here, "mp", 1)
    q_relay = pair_swap(q_handed, "ctx", 1)
    (partial,) = kernel_call(upstream_own_body, (tile32,), (grad_here, out_weight), 0.5, "upstream_own")
    message, delta = kernel_call(
        upstream_body, (noted, tile32), (gi_core, out_weight, att, lse, partial, q_relay), 0.6,
        "upstream", 1,
    )

    m_near, m_first, m_second, m_relay = window_of(message)
    output, grad_input, grad_query = kernel_call(
        functools.partial(query_grad_body, scale),
        (tile, tile, tile),
        (q_own, kv, near, first, second, relay, message, lse, delta, output_here, grad_here),
        1.8, "query_grad", 0,
        [pltpu.VMEM((frames, width), BF16), pltpu.SemaphoreType.DMA((3,))], HBM,
    )
    key_part, value_part, late = kernel_call(
        functools.partial(key_part_body, scale),
        (tile32, tile32, tile32),
        (kv, q_own, q_near, q_first, q_second, q_relay, message, m_near, m_first, m_second),
        1.5, "key_part",
    )
    grad_key, grad_value = kernel_call(
        functools.partial(key_grad_body, scale),
        (tile, tile),
        (kv, q_relay, m_relay, late, key_part, value_part),
        1.0, "key_grad", 0,
        [pltpu.VMEM((frames, width), BF16)] * 2 + [pltpu.SemaphoreType.DMA((2,))], HBM,
    )
    return (output, grad_input, grad_query, grad_key, grad_value)


def solution(mesh):
    rows = P("ctx", "mp")
    return jax.shard_map(
        per_device,
        mesh=mesh,
        in_specs=(rows, rows, rows, rows, P("mp", None), P(None, "mp"), rows),
        out_specs=(rows,) * 5,
        check_vma=False,
    )
```

```python
import functools
import math

import jax
import jax.numpy as jnp
from jax import lax
from jax.experimental import pallas as pl
from jax.experimental.pallas import tpu as pltpu
from jax.sharding import PartitionSpec as P

HDIM = 128
F32 = jnp.float32
BF16 = jnp.bfloat16
HALO = 16
NT = (((1,), (1,)), ((), ()))
NN = (((1,), (0,)), ((), ()))


def dot_nt(a, b):
    return lax.dot_general(a, b, NT, preferred_element_type=F32)


def dot_nn(a, b):
    return lax.dot_general(a, b, NN, preferred_element_type=F32)


def pair_swap(block, axis, bit):
    return lax.ppermute(block, axis, [(i, i ^ bit) for i in range(lax.axis_size(axis))])


def ring_routes(count):
    rise = [(i, i + 2) for i in range(0, count - 2, 2)] + [(count - 2, count - 1)]
    fall = [(i, i - 2) for i in range(count - 1, 2, -2)] + [(1, 0)]
    route = rise + fall
    return route, [(b, a) for a, b in route]


def ring(block, way):
    return lax.ppermute(block, "ctx", ring_routes(lax.axis_size("ctx"))[way])


def total_swap(block, partner_of):
    count, places = lax.axis_size("ctx"), lax.axis_size("mp")
    route = []
    for i in range(count):
        other = partner_of(i, count)
        for m in range(places):
            target = i * places + (m ^ 1) if other is None else other * places + m
            route.append((i * places + m, target))
    return lax.ppermute(block, ("ctx", "mp"), route)


def inner_swap(block):
    return total_swap(block, lambda i, count: i ^ 1 if 2 <= i < count - 2 else None)


def outer_swap(block):
    return total_swap(block, lambda i, count: ((i + 1) ^ 1) - 1 if 0 < i < count - 1 else None)


def window_of(block, before_relay=lambda second: second):
    second = ring(block, 1)
    first = ring(block, 0)
    near = inner_swap(block)
    second = before_relay(second)
    return near, first, second, pair_swap(second, "ctx", 1)


VMEM = pl.BlockSpec(memory_space=pltpu.VMEM)
ANY = pl.BlockSpec(memory_space=pl.ANY)
HBM = pl.BlockSpec(memory_space=pltpu.HBM)


def kernel_call(body, outs, args, micros, name, unread=0, scratch=(), out_space=VMEM):
    return pl.pallas_call(
        body,
        out_shape=outs,
        in_specs=[VMEM] * (len(args) - unread) + [ANY] * unread,
        out_specs=tuple(out_space for _ in outs),
        scratch_shapes=scratch,
        compiler_params=pltpu.CompilerParams(vmem_limit_bytes=24 * 1024 * 1024),
        cost_estimate=pl.CostEstimate(
            flops=0, bytes_accessed=int(micros * 3.69e6), transcendentals=0
        ),
        name=name,
    )(*args)


def shaped(shape, dtype):
    return jax.ShapeDtypeStruct(shape, dtype)


def is_even():
    return lax.axis_index("ctx") % 2 == 0


def near_swapped():
    block = lax.axis_index("ctx")
    return (block >= 2) & (block < lax.axis_size("ctx") - 2)


def far_there():
    block = lax.axis_index("ctx")
    return jnp.where(is_even(), block >= 2, block < lax.axis_size("ctx") - 2)


def bias_of(there):
    return jnp.where(there, jnp.float32(0.0), jnp.float32(-jnp.inf))


def columns(width):
    return [slice(c, c + HDIM) for c in range(0, width, HDIM)]


def stacked(blocks, rows, cols):
    return jnp.concatenate([block[rows, cols] for block in blocks], axis=0)


def with_ones(values):
    return jnp.concatenate([values, jnp.ones_like(values)], axis=1)


def by_block(scores, biases, stats=None):
    parts = []
    for b, bias in enumerate(biases):
        part = scores[:, b * HDIM : (b + 1) * HDIM]
        if stats is not None:
            part = part - stats[b]
        parts.append(part if bias is None else part + bias)
    return jnp.concatenate(parts, axis=1)


def tile_of(wide):
    lane = lax.broadcasted_iota(jnp.int32, (wide[0].shape[0], HDIM), 1)
    tile = jnp.zeros((wide[0].shape[0], HDIM), F32)
    for h, part in enumerate(wide):
        tile = jnp.where(lane == h, part, tile)
    return tile


def term_rows(rows):
    at = lax.broadcasted_iota(jnp.int32, (16, rows[0].shape[1]), 0)
    block = jnp.zeros((16, rows[0].shape[1]), F32)
    for r, rest in enumerate(rows):
        for k in range(3):
            term = rest.astype(BF16).astype(F32)
            rest = rest - term
            block = jnp.where(at == 3 * r + k, term, block)
    return block.astype(BF16)


def stat_rows(message, frames, which, cols):
    terms = message[frames : frames + 16, cols].astype(F32)
    at = 3 * which
    return terms[at : at + 1] + terms[at + 1 : at + 2] + terms[at + 2 : at + 3]


def weight_columns(weight, flip):
    width = weight.shape[0]
    at = (lax.axis_index("mp") ^ flip) * width
    return weight[:, pl.ds(pl.multiple_of(at, 128), width)]


def hold_body(block, seen_a, seen_b, held):
    held[...] = block[...]


def split_body(joined, seen, *parts):
    frames = parts[0].shape[0]
    for k, part in enumerate(parts):
        part[...] = joined[k * frames : (k + 1) * frames, :]


def forward_body(scale, q, own, near, first, second, *refs):
    sums, tops, totals = refs[-3:]
    frames, width = q.shape
    heads = columns(width)
    blocks = (near, own, first, second)
    biases = (bias_of(near_swapped()), None, None, None)
    keys, values = slice(0, frames), slice(frames, 2 * frames)
    scores = [dot_nt(q[:, c], stacked(blocks, keys, c)) * scale for c in heads]
    scores = [by_block(s, biases) for s in scores]
    top = [jnp.max(s, axis=1, keepdims=True) for s in scores]
    probs = [jnp.exp(s - t).astype(BF16) for s, t in zip(scores, top)]
    summed = [dot_nn(p, with_ones(stacked(blocks, values, c))) for p, c in zip(probs, heads)]
    for c, t, s in zip(heads, top, summed):
        tops[:, c] = jnp.broadcast_to(t, (frames, HDIM))
        sums[:, c] = s[:, 0:HDIM]
        totals[:, c] = s[:, HDIM:]


def project_body(scale, q, relay, sums, tops, totals, weight, att, lse, send, keep):
    frames, width = q.shape
    heads = columns(width)
    bias = bias_of(far_there())
    scores = [dot_nt(q[:, c], relay[0:frames, c]) * scale + bias for c in heads]
    before = [tops[:, c] for c in heads]
    top = [jnp.maximum(b, jnp.max(s, axis=1, keepdims=True)) for b, s in zip(before, scores)]
    shrink = [jnp.exp(b - t) for b, t in zip(before, top)]
    probs = [jnp.exp(s - t).astype(BF16) for s, t in zip(scores, top)]
    late = [dot_nn(p, with_ones(relay[frames : 2 * frames, c])) for p, c in zip(probs, heads)]
    total = [totals[:, c] * k + s[:, HDIM:] for c, k, s in zip(heads, shrink, late)]
    summed = [sums[:, c] * k + s[:, 0:HDIM] for c, k, s in zip(heads, shrink, late)]
    attended = jnp.concatenate([(s * (1.0 / t)).astype(BF16) for s, t in zip(summed, total)], axis=1)
    sent = [dot_nn(attended, weight_columns(weight, flip)).astype(BF16) for flip in (1, 3)]
    kept = [dot_nn(attended, weight_columns(weight, flip)).astype(BF16) for flip in (0, 2)]
    logs = [t + jnp.log(n) for t, n in zip(top, total)]
    att[...] = attended
    send[...] = jnp.concatenate(sent, axis=1)
    keep[...] = jnp.concatenate(kept, axis=1)
    for c, part in zip(heads, logs):
        lse[:, c] = part


def join_body(keep, core, q, chip, q_copy):
    chip[...] = (keep[...].astype(F32) + core[...].astype(F32)).astype(BF16)
    q_copy[...] = q[...]


def hidden_body(chip, across, inputs, cot, inputs_other, cot_other, hidden, rim_near, rim_far):
    frames, width = inputs.shape
    wide = 2 * HALO
    even = is_even()
    mine, its = slice(0, width), slice(width, 2 * width)
    for cols, back, rows, cots in (
        (mine, its, inputs[...], cot[...]),
        (its, mine, inputs_other[...], cot_other[...]),
    ):
        mixed = chip[:, cols].astype(F32) + across[:, back].astype(F32)
        total = (rows.astype(F32) + mixed).astype(BF16)
        for at, first, last in (
            (slice(0, wide), total[0:wide], total[frames - wide :]),
            (slice(wide, wide + HALO), cots[0:HALO], cots[frames - HALO :]),
        ):
            first, last = first.astype(F32), last.astype(F32)
            rim_near[at, cols] = jnp.where(even, last, first).astype(BF16)
            rim_far[at, cols] = jnp.where(even, first, last).astype(BF16)
        hidden[:, cols] = total


def shifted_sum(rows, taps_of, count):
    total = None
    for b in range(8):
        part = None
        reach = count if b == 0 else count + 8
        for a in range(4):
            tap = taps_of(8 * a + b)
            if tap is None:
                continue
            term = tap * rows[8 * a : 8 * a + reach]
            part = term if part is None else part + term
        if b:
            part = pltpu.roll(part, reach - b, 0)[0:count]
        total = part if total is None else total + part
    return total


def silu_parts(conv, cots):
    gate = 1.0 / (1.0 + jnp.exp(-conv))
    grad = cots * (gate + conv * gate * (1.0 - gate))
    return conv * gate, grad.astype(BF16).astype(F32)


def taps_forward(taps, count, cols):
    return lambda s: taps[s - 1 : s, cols] if 1 <= s <= count else None


def taps_backward(taps, count, cols):
    return lambda s: taps[count - s : count - s + 1, cols] if 1 <= s <= count else None


def conv_chunks(width, cot, cot_other, taps, taps_other):
    for k, cols in enumerate(columns(2 * width)):
        own = k * HDIM < width
        local = cols if own else slice(cols.start - width, cols.stop - width)
        yield own, cols, local, cot if own else cot_other, taps if own else taps_other


def conv_inner_body(hidden, cot, cot_other, taps, taps_other, seen_a, seen_b, rows_out, edge_conv, part_grad):
    frames, width = cot.shape
    wide, count = 2 * HALO, taps.shape[0]
    inner = slice(HALO, frames - HALO)
    none = jnp.zeros((wide, HDIM), F32)
    for own, cols, local, cots_of, tap in conv_chunks(width, cot, cot_other, taps, taps_other):
        rows = hidden[:, cols].astype(F32)
        cots = cots_of[:, local].astype(F32)
        conv = shifted_sum(
            jnp.concatenate([none, rows, none], axis=0), taps_forward(tap, count, local), frames + wide
        )
        silu, grad = silu_parts(conv[wide:frames], cots[inner])
        back = shifted_sum(
            jnp.concatenate([none, grad, none], axis=0), taps_backward(tap, count, local), frames
        )
        edge_conv[0:wide, cols] = conv[0:wide]
        edge_conv[wide : 2 * wide, cols] = conv[frames : frames + wide]
        if own:
            rows_out[inner, cols] = (rows[inner] + silu).astype(BF16)
        part_grad[:, cols] = cots + back


def conv_edge_body(
    hidden, rim_near, rim_far, cot, cot_other, taps, taps_other, rows_in, edge_conv, part_grad,
    seen, output, grad_input,
):
    frames, width = cot.shape
    wide, count = 2 * HALO, taps.shape[0]
    even, far = is_even(), far_there()
    rims, cots_of = slice(0, wide), slice(wide, wide + HALO)
    low, high = slice(0, HALO), slice(frames - HALO, frames)
    inner = slice(HALO, frames - HALO)
    none = jnp.zeros((wide, HDIM), F32)

    def sides(rows, cols):
        near = rim_near[rows, cols].astype(F32)
        beyond = jnp.where(far, rim_far[rows, cols].astype(F32), 0.0)
        return jnp.where(even, beyond, near), jnp.where(even, near, beyond)

    for own, cols, local, block, tap in conv_chunks(width, cot, cot_other, taps, taps_other):
        row_low, row_high = sides(rims, cols)
        cot_low, cot_high = sides(cots_of, cols)
        conv = edge_conv[:, cols] + shifted_sum(
            jnp.concatenate([row_low, none, row_high], axis=0), taps_forward(tap, count, local), 2 * wide
        )
        first = block[low, local].astype(F32)
        last = block[high, local].astype(F32)
        cots = jnp.concatenate([cot_low, first, last, cot_high], axis=0)
        silu, grad = silu_parts(conv, cots)
        back = shifted_sum(
            jnp.concatenate([grad[0:wide], none, grad[wide:]], axis=0), taps_backward(tap, count, local), 2 * wide
        )
        part = part_grad[:, cols]
        grad_input[:, cols] = jnp.concatenate(
            [part[0:wide] + back[0:wide], part[wide : frames - wide], part[frames - wide :] + back[wide:]],
            axis=0,
        ).astype(BF16)
        if own:
            output[low, cols] = (hidden[low, cols].astype(F32) + silu[HALO:wide]).astype(BF16)
            output[inner, cols] = rows_in[inner, cols]
            output[high, cols] = (hidden[high, cols].astype(F32) + silu[wide : wide + HALO]).astype(BF16)


def upstream_part(grads, weight, flips):
    width = weight.shape[0]
    return sum(
        dot_nt(grads[:, k * width : (k + 1) * width], weight_columns(weight, flip))
        for k, flip in enumerate(flips)
    )


def upstream_own_body(own, weight, partial):
    partial[...] = upstream_part(own, weight, (0, 2))


def upstream_body(core, weight, att, lse, partial, message, delta):
    frames, width = att.shape
    heads = columns(width)
    up = (partial[...] + upstream_part(core, weight, (1, 3))).astype(BF16)
    products = [up[:, c].astype(F32) * att[:, c].astype(F32) for c in heads]
    deltas = [jnp.broadcast_to(jnp.sum(p, axis=1, keepdims=True), (frames, HDIM)) for p in products]
    lse_rows = tile_of([lse[:, c] for c in heads]).T
    delta_rows = tile_of(deltas).T
    terms = [term_rows([lse_rows[h : h + 1], delta_rows[h : h + 1]]) for h in range(len(heads))]
    message[0:frames, :] = up
    message[frames : frames + 16, :] = jnp.concatenate(terms, axis=1)
    for c, part in zip(heads, deltas):
        delta[:, c] = part


def query_grad_body(
    scale, q, own, near, first, second, relay, message, lse, delta, output_here, grad_here,
    output, grad_input, grad_query, held, sems,
):
    writes = [
        pltpu.make_async_copy(output_here, output, sems.at[0]),
        pltpu.make_async_copy(grad_here.at[:, pl.ds(0, q.shape[1])], grad_input, sems.at[1]),
    ]
    for write in writes:
        write.start()
    frames, width = q.shape
    heads = columns(width)
    blocks = (near, own, first, second, relay)
    biases = (bias_of(near_swapped()), None, None, None, bias_of(far_there()))
    above, below = slice(0, frames), slice(frames, 2 * frames)
    keys = [stacked(blocks, above, c) for c in heads]
    scores = [dot_nt(q[:, c], k) * scale for c, k in zip(heads, keys)]
    dots = [dot_nt(message[0:frames, c], stacked(blocks, below, c)) for c in heads]
    probs = [jnp.exp(by_block(s, biases, [lse[:, c]] * 5)) for c, s in zip(heads, scores)]
    drops = [by_block(d, (None,) * 5, [delta[:, c]] * 5) for c, d in zip(heads, dots)]
    grads = [(p * d * scale).astype(BF16) for p, d in zip(probs, drops)]
    held[...] = jnp.concatenate([dot_nn(g, k).astype(BF16) for g, k in zip(grads, keys)], axis=1)
    writes.append(pltpu.make_async_copy(held, grad_query, sems.at[2]))
    writes[2].start()
    for write in writes:
        write.wait()


def key_part_body(scale, own, *refs):
    queries, late_query, messages, (key_part, value_part, late) = refs[0:4], refs[4], refs[5:9], refs[9:12]
    frames = own.shape[0] // 2
    heads = columns(own.shape[1])
    above, below = slice(0, frames), slice(frames, 2 * frames)
    biases = (None, bias_of(near_swapped()), None, None)
    asks = [stacked(queries, above, c) for c in heads]
    ups = [stacked(messages, above, c) for c in heads]
    scores = [dot_nt(own[above, c], a) * scale for c, a in zip(heads, asks)]
    dots = [dot_nt(own[below, c], u) for c, u in zip(heads, ups)]
    last = [dot_nt(own[above, c], late_query[:, c]) * scale + bias_of(far_there()) for c in heads]
    logs = [[stat_rows(m, frames, 0, c) for m in messages] for c in heads]
    deltas = [[stat_rows(m, frames, 1, c) for m in messages] for c in heads]
    probs = [jnp.exp(by_block(s, biases, n)) for s, n in zip(scores, logs)]
    drops = [by_block(d, (None,) * 4, n) for d, n in zip(dots, deltas)]
    grads = [(p * d * scale).astype(BF16) for p, d in zip(probs, drops)]
    value_sums = [dot_nn(p.astype(BF16), u) for p, u in zip(probs, ups)]
    key_sums = [dot_nn(g, a) for g, a in zip(grads, asks)]
    for c, k, v, s in zip(heads, key_sums, value_sums, last):
        key_part[:, c] = k
        value_part[:, c] = v
        late[:, c] = s


def key_grad_body(
    scale, own, query, message, late, key_part, value_part, grad_key, grad_value, held_key, held_value, sems
):
    frames = own.shape[0] // 2
    heads = columns(own.shape[1])
    above, below = slice(0, frames), slice(frames, 2 * frames)
    ups = [message[above, c] for c in heads]
    probs = [jnp.exp(late[:, c] - stat_rows(message, frames, 0, c)) for c in heads]
    dots = [dot_nt(own[below, c], u) for c, u in zip(heads, ups)]
    values = [value_part[:, c] + dot_nn(p.astype(BF16), u) for c, p, u in zip(heads, probs, ups)]
    held_value[...] = jnp.concatenate([v.astype(BF16) for v in values], axis=1)
    value_write = pltpu.make_async_copy(held_value, grad_value, sems.at[0])
    value_write.start()
    drops = [d - stat_rows(message, frames, 1, c) for c, d in zip(heads, dots)]
    grads = [(p * d * scale).astype(BF16) for p, d in zip(probs, drops)]
    keys = [key_part[:, c] + dot_nn(g, query[:, c]) for c, g in zip(heads, grads)]
    held_key[...] = jnp.concatenate([k.astype(BF16) for k in keys], axis=1)
    key_write = pltpu.make_async_copy(held_key, grad_key, sems.at[1])
    key_write.start()
    value_write.wait()
    key_write.wait()


def per_device(query_rows, key_rows, value_rows, inputs, out_weight, kernel, cotangent):
    frames, width = query_rows.shape
    wide = 2 * HALO
    scale = 1.0 / math.sqrt(HDIM)
    tile = shaped((frames, width), BF16)
    tile32 = shaped((frames, width), F32)
    rim = shaped((wide + HALO, 2 * width), BF16)
    both = shaped((frames, 2 * width), BF16)
    noted = shaped((frames + 16, width), BF16)

    zero = jnp.zeros((), BF16)
    kv = lax.pad(key_rows, zero, ((0, frames, 0), (0, 0, 0))) + lax.pad(
        value_rows, zero, ((frames, 0, 0), (0, 0, 0))
    )
    other = [pair_swap(block, "mp", 2) for block in (inputs, cotangent, kernel)]
    near, first, second, relay = window_of(
        kv,
        lambda second: kernel_call(
            hold_body, (shaped(kv.shape, BF16),), (second, other[0], other[2]), 0.1, "turn", 2
        )[0],
    )
    joined = sum(
        lax.pad(rows, zero, ((k * frames, (2 - k) * frames, 0), (0, 0, 0)))
        for k, rows in enumerate((query_rows, inputs, cotangent))
    )
    query, inputs, cotangent = kernel_call(
        split_body, (tile, tile, tile), (joined, second), 0.1, "split", 1
    )
    sums, tops, totals = kernel_call(
        functools.partial(forward_body, scale),
        (tile32, tile32, tile32),
        (query, kv, near, first, second, other[1]),
        1.0, "forward", 1,
    )
    att, lse, send, keep = kernel_call(
        functools.partial(project_body, scale),
        (tile, tile32, both, both),
        (query, relay, sums, tops, totals, out_weight),
        1.0, "project",
    )

    core = pair_swap(send, "mp", 1)
    chip, q_own = kernel_call(join_body, (both, tile), (keep, core, query), 0.1, "join")
    across = pair_swap(chip, "mp", 2)
    q_second = ring(q_own, 1)
    q_first = ring(q_own, 0)
    q_near = inner_swap(q_own)
    q_relay = pair_swap(q_second, "ctx", 1)
    hidden, rim_up, rim_down = kernel_call(
        hidden_body,
        (both, rim, rim),
        (chip, across, inputs, cotangent, *other[0:2]),
        0.2, "hidden",
    )

    rim_far = outer_swap(rim_down)
    rim_near = pair_swap(rim_up, "ctx", 1)
    rows_out, edge_conv, part_grad = kernel_call(
        conv_inner_body,
        (tile, shaped((2 * wide, 2 * width), F32), shaped((frames, 2 * width), F32)),
        (hidden, cotangent, other[1], kernel, other[2], q_near, q_first),
        3.1, "conv_inner", 2,
    )
    output_here, grad_here = kernel_call(
        conv_edge_body,
        (tile, both),
        (hidden, rim_near, rim_far, cotangent, other[1], kernel, other[2], rows_out, edge_conv, part_grad)
        + (q_relay,),
        1.4, "conv_edge", 1,
    )

    gi_core = pair_swap(grad_here, "mp", 1)
    (partial,) = kernel_call(upstream_own_body, (tile32,), (grad_here, out_weight), 0.5, "upstream_own")
    message, delta = kernel_call(
        upstream_body, (noted, tile32), (gi_core, out_weight, att, lse, partial), 0.6, "upstream"
    )

    m_near, m_first, m_second, m_relay = window_of(message)
    output, grad_input, grad_query = kernel_call(
        functools.partial(query_grad_body, scale),
        (tile, tile, tile),
        (q_own, kv, near, first, second, relay, message, lse, delta, output_here, grad_here),
        1.8, "query_grad", 0,
        [pltpu.VMEM((frames, width), BF16), pltpu.SemaphoreType.DMA((3,))], HBM,
    )
    key_part, value_part, late = kernel_call(
        functools.partial(key_part_body, scale),
        (tile32, tile32, tile32),
        (kv, q_own, q_near, q_first, q_second, q_relay, message, m_near, m_first, m_second),
        1.5, "key_part",
    )
    grad_key, grad_value = kernel_call(
        functools.partial(key_grad_body, scale),
        (tile, tile),
        (kv, q_relay, m_relay, late, key_part, value_part),
        1.0, "key_grad", 0,
        [pltpu.VMEM((frames, width), BF16)] * 2 + [pltpu.SemaphoreType.DMA((2,))], HBM,
    )
    return (output, grad_input, grad_query, grad_key, grad_value)


def solution(mesh):
    rows = P("ctx", "mp")
    return jax.shard_map(
        per_device,
        mesh=mesh,
        in_specs=(rows, rows, rows, rows, P("mp", None), P(None, "mp"), rows),
        out_specs=(rows,) * 5,
        check_vma=False,
    )
```

```python
import functools
import math

import jax
import jax.numpy as jnp
from jax import lax
from jax.experimental import pallas as pl
from jax.experimental.pallas import tpu as pltpu
from jax.sharding import PartitionSpec as P

HDIM = 128
F32 = jnp.float32
BF16 = jnp.bfloat16
HALO = 16
NT = (((1,), (1,)), ((), ()))
NN = (((1,), (0,)), ((), ()))


def dot_nt(a, b):
    return lax.dot_general(a, b, NT, preferred_element_type=F32)


def dot_nn(a, b):
    return lax.dot_general(a, b, NN, preferred_element_type=F32)


def pair_swap(block, axis, bit):
    return lax.ppermute(block, axis, [(i, i ^ bit) for i in range(lax.axis_size(axis))])


def ring_routes(count):
    rise = [(i, i + 2) for i in range(0, count - 2, 2)] + [(count - 2, count - 1)]
    fall = [(i, i - 2) for i in range(count - 1, 2, -2)] + [(1, 0)]
    route = rise + fall
    return route, [(b, a) for a, b in route]


def ring(block, way):
    return lax.ppermute(block, "ctx", ring_routes(lax.axis_size("ctx"))[way])


def total_swap(block, partner_of):
    count, places = lax.axis_size("ctx"), lax.axis_size("mp")
    route = []
    for i in range(count):
        other = partner_of(i, count)
        for m in range(places):
            target = i * places + (m ^ 1) if other is None else other * places + m
            route.append((i * places + m, target))
    return lax.ppermute(block, ("ctx", "mp"), route)


def inner_swap(block):
    return total_swap(block, lambda i, count: i ^ 1 if 2 <= i < count - 2 else None)


def outer_swap(block):
    return total_swap(block, lambda i, count: ((i + 1) ^ 1) - 1 if 0 < i < count - 1 else None)


def window_of(block):
    second = ring(block, 1)
    first = ring(block, 0)
    near = inner_swap(block)
    return near, first, second, pair_swap(second, "ctx", 1)


VMEM = pl.BlockSpec(memory_space=pltpu.VMEM)
ANY = pl.BlockSpec(memory_space=pl.ANY)
HBM = pl.BlockSpec(memory_space=pltpu.HBM)


def kernel_call(body, outs, args, micros, name, unread=0, scratch=(), out_space=VMEM):
    return pl.pallas_call(
        body,
        out_shape=outs,
        in_specs=[VMEM] * (len(args) - unread) + [ANY] * unread,
        out_specs=tuple(out_space for _ in outs),
        scratch_shapes=scratch,
        compiler_params=pltpu.CompilerParams(vmem_limit_bytes=24 * 1024 * 1024),
        cost_estimate=pl.CostEstimate(
            flops=0, bytes_accessed=int(micros * 3.69e6), transcendentals=0
        ),
        name=name,
    )(*args)


def shaped(shape, dtype):
    return jax.ShapeDtypeStruct(shape, dtype)


def is_even():
    return lax.axis_index("ctx") % 2 == 0


def near_swapped():
    block = lax.axis_index("ctx")
    return (block >= 2) & (block < lax.axis_size("ctx") - 2)


def far_there():
    block = lax.axis_index("ctx")
    return jnp.where(is_even(), block >= 2, block < lax.axis_size("ctx") - 2)


def bias_of(there):
    return jnp.where(there, jnp.float32(0.0), jnp.float32(-jnp.inf))


def columns(width):
    return [slice(c, c + HDIM) for c in range(0, width, HDIM)]


def stacked(blocks, rows, cols):
    return jnp.concatenate([block[rows, cols] for block in blocks], axis=0)


def with_ones(values):
    return jnp.concatenate([values, jnp.ones_like(values)], axis=1)


def by_block(scores, biases, stats=None):
    parts = []
    for b, bias in enumerate(biases):
        part = scores[:, b * HDIM : (b + 1) * HDIM]
        if stats is not None:
            part = part - stats[b]
        parts.append(part if bias is None else part + bias)
    return jnp.concatenate(parts, axis=1)


def tile_of(wide):
    lane = lax.broadcasted_iota(jnp.int32, (wide[0].shape[0], HDIM), 1)
    tile = jnp.zeros((wide[0].shape[0], HDIM), F32)
    for h, part in enumerate(wide):
        tile = jnp.where(lane == h, part, tile)
    return tile


def term_rows(rows):
    at = lax.broadcasted_iota(jnp.int32, (16, rows[0].shape[1]), 0)
    block = jnp.zeros((16, rows[0].shape[1]), F32)
    for r, rest in enumerate(rows):
        for k in range(3):
            term = rest.astype(BF16).astype(F32)
            rest = rest - term
            block = jnp.where(at == 3 * r + k, term, block)
    return block.astype(BF16)


def stat_rows(message, frames, which, cols):
    terms = message[frames : frames + 16, cols].astype(F32)
    at = 3 * which
    return terms[at : at + 1] + terms[at + 1 : at + 2] + terms[at + 2 : at + 3]


def weight_columns(weight, flip):
    width = weight.shape[0]
    at = (lax.axis_index("mp") ^ flip) * width
    return weight[:, pl.ds(pl.multiple_of(at, 128), width)]


def split_body(joined, seen, *parts):
    frames = parts[0].shape[0]
    for k, part in enumerate(parts):
        part[...] = joined[k * frames : (k + 1) * frames, :]


def forward_body(scale, q, own, near, first, second, *refs):
    sums, tops, totals = refs[-3:]
    frames, width = q.shape
    heads = columns(width)
    blocks = (near, own, first, second)
    biases = (bias_of(near_swapped()), None, None, None)
    keys, values = slice(0, frames), slice(frames, 2 * frames)
    scores = [dot_nt(q[:, c], stacked(blocks, keys, c)) * scale for c in heads]
    scores = [by_block(s, biases) for s in scores]
    top = [jnp.max(s, axis=1, keepdims=True) for s in scores]
    probs = [jnp.exp(s - t).astype(BF16) for s, t in zip(scores, top)]
    summed = [dot_nn(p, with_ones(stacked(blocks, values, c))) for p, c in zip(probs, heads)]
    for c, t, s in zip(heads, top, summed):
        tops[:, c] = jnp.broadcast_to(t, (frames, HDIM))
        sums[:, c] = s[:, 0:HDIM]
        totals[:, c] = s[:, HDIM:]


def project_body(scale, q, relay, sums, tops, totals, weight, seen_a, seen_b, att, lse, send, keep):
    frames, width = q.shape
    heads = columns(width)
    bias = bias_of(far_there())
    scores = [dot_nt(q[:, c], relay[0:frames, c]) * scale + bias for c in heads]
    before = [tops[:, c] for c in heads]
    top = [jnp.maximum(b, jnp.max(s, axis=1, keepdims=True)) for b, s in zip(before, scores)]
    shrink = [jnp.exp(b - t) for b, t in zip(before, top)]
    probs = [jnp.exp(s - t).astype(BF16) for s, t in zip(scores, top)]
    late = [dot_nn(p, with_ones(relay[frames : 2 * frames, c])) for p, c in zip(probs, heads)]
    total = [totals[:, c] * k + s[:, HDIM:] for c, k, s in zip(heads, shrink, late)]
    summed = [sums[:, c] * k + s[:, 0:HDIM] for c, k, s in zip(heads, shrink, late)]
    attended = jnp.concatenate([(s * (1.0 / t)).astype(BF16) for s, t in zip(summed, total)], axis=1)
    sent = [dot_nn(attended, weight_columns(weight, flip)).astype(BF16) for flip in (1, 3)]
    kept = [dot_nn(attended, weight_columns(weight, flip)).astype(BF16) for flip in (0, 2)]
    logs = [t + jnp.log(n) for t, n in zip(top, total)]
    att[...] = attended
    send[...] = jnp.concatenate(sent, axis=1)
    keep[...] = jnp.concatenate(kept, axis=1)
    for c, part in zip(heads, logs):
        lse[:, c] = part


def pass_body(send, q_second, send_copy, second_copy):
    send_copy[...] = send[...]
    second_copy[...] = q_second[...]


def join_body(keep, core, inputs, cot, cot_other, q, q_second, chip, rim_near, rim_far, q_copy, second_copy):
    frames, width = inputs.shape
    wide = 2 * HALO
    even = is_even()
    for cols, rows, cots in (
        (slice(0, width), inputs[...].astype(F32), cot),
        (slice(width, 2 * width), 0.0, cot_other),
    ):
        total = (rows + (keep[:, cols].astype(F32) + core[:, cols].astype(F32))).astype(BF16)
        for at, first, last in (
            (slice(0, wide), total[0:wide], total[frames - wide :]),
            (slice(wide, wide + HALO), cots[0:HALO, :], cots[frames - HALO : frames, :]),
        ):
            first, last = first.astype(F32), last.astype(F32)
            rim_near[at, cols] = jnp.where(even, last, first).astype(BF16)
            rim_far[at, cols] = jnp.where(even, first, last).astype(BF16)
        chip[:, cols] = total
    q_copy[...] = q[...]
    second_copy[...] = q_second[...]


def stack_body(rim_near, rim_far, q, q_second, ends, q_copy, second_copy):
    wide = 2 * HALO
    ends[0:wide, :] = rim_near[0:wide, :]
    ends[wide : 2 * wide, :] = rim_far[0:wide, :]
    q_copy[...] = q[...]
    second_copy[...] = q_second[...]


def summed(share, across, rows, cols, width):
    back = slice((cols.start + width) % (2 * width), (cols.stop - 1 + width) % (2 * width) + 1)
    total = share[rows, cols].astype(F32) + across[rows, back].astype(F32)
    return total.astype(BF16).astype(F32)


def shifted_sum(rows, taps_of, count):
    total = None
    for b in range(8):
        part = None
        reach = count if b == 0 else count + 8
        for a in range(4):
            tap = taps_of(8 * a + b)
            if tap is None:
                continue
            term = tap * rows[8 * a : 8 * a + reach]
            part = term if part is None else part + term
        if b:
            part = pltpu.roll(part, reach - b, 0)[0:count]
        total = part if total is None else total + part
    return total


def silu_parts(conv, cots):
    gate = 1.0 / (1.0 + jnp.exp(-conv))
    grad = cots * (gate + conv * gate * (1.0 - gate))
    return conv * gate, grad.astype(BF16).astype(F32)


def taps_forward(taps, count, cols):
    return lambda s: taps[s - 1 : s, cols] if 1 <= s <= count else None


def taps_backward(taps, count, cols):
    return lambda s: taps[count - s : count - s + 1, cols] if 1 <= s <= count else None


def conv_chunks(width, cot, cot_other, taps, taps_other):
    for k, cols in enumerate(columns(2 * width)):
        own = k * HDIM < width
        local = cols if own else slice(cols.start - width, cols.stop - width)
        yield own, cols, local, cot if own else cot_other, taps if own else taps_other


def conv_inner_body(
    chip, across, cot, cot_other, taps, taps_other, rows_out, edge_rows, edge_conv, part_grad
):
    frames, width = cot.shape
    wide, count = 2 * HALO, taps.shape[0]
    inner = slice(HALO, frames - HALO)
    none = jnp.zeros((wide, HDIM), F32)
    for own, cols, local, cots_of, tap in conv_chunks(width, cot, cot_other, taps, taps_other):
        rows = summed(chip, across, slice(0, frames), cols, width)
        cots = cots_of[:, local].astype(F32)
        conv = shifted_sum(
            jnp.concatenate([none, rows, none], axis=0), taps_forward(tap, count, local), frames + wide
        )
        silu, grad = silu_parts(conv[wide:frames], cots[inner])
        back = shifted_sum(
            jnp.concatenate([none, grad, none], axis=0), taps_backward(tap, count, local), frames
        )
        edge_conv[0:wide, cols] = conv[0:wide]
        edge_conv[wide : 2 * wide, cols] = conv[frames : frames + wide]
        if own:
            rows_out[inner, cols] = (rows[inner] + silu).astype(BF16)
            edge_rows[0:HALO, cols] = rows[0:HALO]
            edge_rows[HALO:wide, cols] = rows[frames - HALO :]
        part_grad[:, cols] = cots + back


def conv_edge_body(
    ends, ends_across, rim_near, rim_far, cot, cot_other, taps, taps_other,
    rows_in, edge_rows, edge_conv, part_grad, seen_a, seen_b, seen_c, output, grad_input,
):
    frames, width = cot.shape
    wide, count = 2 * HALO, taps.shape[0]
    even, far = is_even(), far_there()
    low, high = slice(0, HALO), slice(frames - HALO, frames)
    inner = slice(HALO, frames - HALO)
    none = jnp.zeros((wide, HDIM), F32)
    cots_of = slice(wide, wide + HALO)

    def sides(near, beyond):
        beyond = jnp.where(far, beyond, 0.0)
        return jnp.where(even, beyond, near), jnp.where(even, near, beyond)

    for own, cols, local, block, tap in conv_chunks(width, cot, cot_other, taps, taps_other):
        rows = summed(ends, ends_across, slice(0, 2 * wide), cols, width)
        row_low, row_high = sides(rows[0:wide], rows[wide:])
        cot_low, cot_high = sides(rim_near[cots_of, cols].astype(F32), rim_far[cots_of, cols].astype(F32))
        conv = edge_conv[:, cols] + shifted_sum(
            jnp.concatenate([row_low, none, row_high], axis=0), taps_forward(tap, count, local), 2 * wide
        )
        first = block[low, local].astype(F32)
        last = block[high, local].astype(F32)
        cots = jnp.concatenate([cot_low, first, last, cot_high], axis=0)
        silu, grad = silu_parts(conv, cots)
        back = shifted_sum(
            jnp.concatenate([grad[0:wide], none, grad[wide:]], axis=0), taps_backward(tap, count, local), 2 * wide
        )
        part = part_grad[:, cols]
        grad_input[:, cols] = jnp.concatenate(
            [part[0:wide] + back[0:wide], part[wide : frames - wide], part[frames - wide :] + back[wide:]],
            axis=0,
        ).astype(BF16)
        if own:
            output[low, cols] = (edge_rows[0:HALO, cols] + silu[HALO:wide]).astype(BF16)
            output[inner, cols] = rows_in[inner, cols]
            output[high, cols] = (edge_rows[HALO:wide, cols] + silu[wide : wide + HALO]).astype(BF16)


def upstream_part(grads, weight, flips):
    width = weight.shape[0]
    return sum(
        dot_nt(grads[:, k * width : (k + 1) * width], weight_columns(weight, flip))
        for k, flip in enumerate(flips)
    )


def upstream_own_body(own, weight, partial):
    partial[...] = upstream_part(own, weight, (0, 2))


def upstream_body(core, weight, att, lse, partial, message, delta):
    frames, width = att.shape
    heads = columns(width)
    up = (partial[...] + upstream_part(core, weight, (1, 3))).astype(BF16)
    products = [up[:, c].astype(F32) * att[:, c].astype(F32) for c in heads]
    deltas = [jnp.broadcast_to(jnp.sum(p, axis=1, keepdims=True), (frames, HDIM)) for p in products]
    lse_rows = tile_of([lse[:, c] for c in heads]).T
    delta_rows = tile_of(deltas).T
    terms = [term_rows([lse_rows[h : h + 1], delta_rows[h : h + 1]]) for h in range(len(heads))]
    message[0:frames, :] = up
    message[frames : frames + 16, :] = jnp.concatenate(terms, axis=1)
    for c, part in zip(heads, deltas):
        delta[:, c] = part


def query_grad_body(
    scale, q, own, near, first, second, relay, message, lse, delta, output_here, grad_here,
    output, grad_input, grad_query, held, sems,
):
    writes = [
        pltpu.make_async_copy(output_here, output, sems.at[0]),
        pltpu.make_async_copy(grad_here.at[:, pl.ds(0, q.shape[1])], grad_input, sems.at[1]),
    ]
    for write in writes:
        write.start()
    frames, width = q.shape
    heads = columns(width)
    blocks = (near, own, first, second, relay)
    biases = (bias_of(near_swapped()), None, None, None, bias_of(far_there()))
    above, below = slice(0, frames), slice(frames, 2 * frames)
    keys = [stacked(blocks, above, c) for c in heads]
    scores = [dot_nt(q[:, c], k) * scale for c, k in zip(heads, keys)]
    dots = [dot_nt(message[0:frames, c], stacked(blocks, below, c)) for c in heads]
    probs = [jnp.exp(by_block(s, biases, [lse[:, c]] * 5)) for c, s in zip(heads, scores)]
    drops = [by_block(d, (None,) * 5, [delta[:, c]] * 5) for c, d in zip(heads, dots)]
    grads = [(p * d * scale).astype(BF16) for p, d in zip(probs, drops)]
    held[...] = jnp.concatenate([dot_nn(g, k).astype(BF16) for g, k in zip(grads, keys)], axis=1)
    writes.append(pltpu.make_async_copy(held, grad_query, sems.at[2]))
    writes[2].start()
    for write in writes:
        write.wait()


def key_part_body(scale, own, *refs):
    queries, late_query, messages, (key_part, value_part, late) = refs[0:4], refs[4], refs[5:9], refs[9:12]
    frames = own.shape[0] // 2
    heads = columns(own.shape[1])
    above, below = slice(0, frames), slice(frames, 2 * frames)
    biases = (None, bias_of(near_swapped()), None, None)
    asks = [stacked(queries, above, c) for c in heads]
    ups = [stacked(messages, above, c) for c in heads]
    scores = [dot_nt(own[above, c], a) * scale for c, a in zip(heads, asks)]
    dots = [dot_nt(own[below, c], u) for c, u in zip(heads, ups)]
    last = [dot_nt(own[above, c], late_query[:, c]) * scale + bias_of(far_there()) for c in heads]
    logs = [[stat_rows(m, frames, 0, c) for m in messages] for c in heads]
    deltas = [[stat_rows(m, frames, 1, c) for m in messages] for c in heads]
    probs = [jnp.exp(by_block(s, biases, n)) for s, n in zip(scores, logs)]
    drops = [by_block(d, (None,) * 4, n) for d, n in zip(dots, deltas)]
    grads = [(p * d * scale).astype(BF16) for p, d in zip(probs, drops)]
    value_sums = [dot_nn(p.astype(BF16), u) for p, u in zip(probs, ups)]
    key_sums = [dot_nn(g, a) for g, a in zip(grads, asks)]
    for c, k, v, s in zip(heads, key_sums, value_sums, last):
        key_part[:, c] = k
        value_part[:, c] = v
        late[:, c] = s


def key_grad_body(
    scale, own, query, message, late, key_part, value_part, grad_key, grad_value, held_key, held_value, sems
):
    frames = own.shape[0] // 2
    heads = columns(own.shape[1])
    above, below = slice(0, frames), slice(frames, 2 * frames)
    ups = [message[above, c] for c in heads]
    probs = [jnp.exp(late[:, c] - stat_rows(message, frames, 0, c)) for c in heads]
    dots = [dot_nt(own[below, c], u) for c, u in zip(heads, ups)]
    values = [value_part[:, c] + dot_nn(p.astype(BF16), u) for c, p, u in zip(heads, probs, ups)]
    held_value[...] = jnp.concatenate([v.astype(BF16) for v in values], axis=1)
    value_write = pltpu.make_async_copy(held_value, grad_value, sems.at[0])
    value_write.start()
    drops = [d - stat_rows(message, frames, 1, c) for c, d in zip(heads, dots)]
    grads = [(p * d * scale).astype(BF16) for p, d in zip(probs, drops)]
    keys = [key_part[:, c] + dot_nn(g, query[:, c]) for c, g in zip(heads, grads)]
    held_key[...] = jnp.concatenate([k.astype(BF16) for k in keys], axis=1)
    key_write = pltpu.make_async_copy(held_key, grad_key, sems.at[1])
    key_write.start()
    value_write.wait()
    key_write.wait()


def per_device(query_rows, key_rows, value_rows, inputs, out_weight, kernel, cotangent):
    frames, width = query_rows.shape
    wide = 2 * HALO
    scale = 1.0 / math.sqrt(HDIM)
    tile = shaped((frames, width), BF16)
    tile32 = shaped((frames, width), F32)
    rim = shaped((wide + HALO, 2 * width), BF16)
    both = shaped((frames, 2 * width), BF16)
    noted = shaped((frames + 16, width), BF16)

    zero = jnp.zeros((), BF16)
    kv = lax.pad(key_rows, zero, ((0, frames, 0), (0, 0, 0))) + lax.pad(
        value_rows, zero, ((frames, 0, 0), (0, 0, 0))
    )
    near, first, second, relay = window_of(kv)
    cot_other = pair_swap(cotangent, "mp", 2)
    taps_other = pair_swap(kernel, "mp", 2)
    joined = sum(
        lax.pad(rows, zero, ((k * frames, (2 - k) * frames, 0), (0, 0, 0)))
        for k, rows in enumerate((query_rows, inputs, cotangent))
    )
    query, inputs, cotangent = kernel_call(
        split_body, (tile, tile, tile), (joined, second), 0.1, "split", 1
    )
    q_second = ring(query, 1)
    sums, tops, totals = kernel_call(
        functools.partial(forward_body, scale),
        (tile32, tile32, tile32),
        (query, kv, near, first, second),
        1.0, "forward",
    )
    att, lse, send, keep = kernel_call(
        functools.partial(project_body, scale),
        (tile, tile32, both, both),
        (query, relay, sums, tops, totals, out_weight, cot_other, taps_other),
        1.0, "project", 2,
    )

    send, q_second = kernel_call(pass_body, (both, tile), (send, q_second), 0.1, "pass")
    core = pair_swap(send, "mp", 1)
    chip, rim_up, rim_down, q_own, q_handed = kernel_call(
        join_body,
        (both, rim, rim, tile, tile),
        (keep, core, inputs, cotangent, cot_other, query, q_second),
        0.2, "join",
    )
    across = pair_swap(chip, "mp", 2)
    rim_far = outer_swap(rim_down)
    rim_near = pair_swap(rim_up, "ctx", 1)
    ends, q_own, q_handed = kernel_call(
        stack_body,
        (shaped((2 * wide, 2 * width), BF16), tile, tile),
        (rim_near, rim_far, q_own, q_handed),
        0.1, "stack",
    )
    ends_across = pair_swap(ends, "mp", 2)
    q_first = ring(q_own, 0)
    q_near = inner_swap(q_own)
    q_relay = pair_swap(q_handed, "ctx", 1)
    rows_out, edge_rows, edge_conv, part_grad = kernel_call(
        conv_inner_body,
        (
            tile,
            shaped((wide, width), F32),
            shaped((2 * wide, 2 * width), F32),
            shaped((frames, 2 * width), F32),
        ),
        (chip, across, cotangent, cot_other, kernel, taps_other),
        3.1, "conv_inner",
    )
    output_here, grad_here = kernel_call(
        conv_edge_body,
        (tile, both),
        (ends, ends_across, rim_near, rim_far, cotangent, cot_other, kernel, taps_other)
        + (rows_out, edge_rows, edge_conv, part_grad, q_first, q_near, q_relay),
        1.4, "conv_edge", 3,
    )

    gi_core = pair_swap(grad_here, "mp", 1)
    (partial,) = kernel_call(upstream_own_body, (tile32,), (grad_here, out_weight), 0.5, "upstream_own")
    message, delta = kernel_call(
        upstream_body, (noted, tile32), (gi_core, out_weight, att, lse, partial), 0.6, "upstream"
    )

    m_near, m_first, m_second, m_relay = window_of(message)
    output, grad_input, grad_query = kernel_call(
        functools.partial(query_grad_body, scale),
        (tile, tile, tile),
        (q_own, kv, near, first, second, relay, message, lse, delta, output_here, grad_here),
        1.8, "query_grad", 0,
        [pltpu.VMEM((frames, width), BF16), pltpu.SemaphoreType.DMA((3,))], HBM,
    )
    key_part, value_part, late = kernel_call(
        functools.partial(key_part_body, scale),
        (tile32, tile32, tile32),
        (kv, q_own, q_near, q_first, q_second, q_relay, message, m_near, m_first, m_second),
        1.5, "key_part",
    )
    grad_key, grad_value = kernel_call(
        functools.partial(key_grad_body, scale),
        (tile, tile),
        (kv, q_relay, m_relay, late, key_part, value_part),
        1.0, "key_grad", 0,
        [pltpu.VMEM((frames, width), BF16)] * 2 + [pltpu.SemaphoreType.DMA((2,))], HBM,
    )
    return (output, grad_input, grad_query, grad_key, grad_value)


def solution(mesh):
    rows = P("ctx", "mp")
    return jax.shard_map(
        per_device,
        mesh=mesh,
        in_specs=(rows, rows, rows, rows, P("mp", None), P(None, "mp"), rows),
        out_specs=(rows,) * 5,
        check_vma=False,
    )
```

```python
import functools
import math

import jax
import jax.numpy as jnp
from jax import lax
from jax.experimental import pallas as pl
from jax.experimental.pallas import tpu as pltpu
from jax.sharding import PartitionSpec as P

HDIM = 128
F32 = jnp.float32
BF16 = jnp.bfloat16
HALO = 16
NT = (((1,), (1,)), ((), ()))
NN = (((1,), (0,)), ((), ()))


def dot_nt(a, b):
    return lax.dot_general(a, b, NT, preferred_element_type=F32)


def dot_nn(a, b):
    return lax.dot_general(a, b, NN, preferred_element_type=F32)


def pair_swap(block, axis, bit):
    return lax.ppermute(block, axis, [(i, i ^ bit) for i in range(lax.axis_size(axis))])


def ring_routes(count):
    rise = [(i, i + 2) for i in range(0, count - 2, 2)] + [(count - 2, count - 1)]
    fall = [(i, i - 2) for i in range(count - 1, 2, -2)] + [(1, 0)]
    route = rise + fall
    return route, [(b, a) for a, b in route]


def ring(block, way):
    return lax.ppermute(block, "ctx", ring_routes(lax.axis_size("ctx"))[way])


def total_swap(block, partner_of):
    count, places = lax.axis_size("ctx"), lax.axis_size("mp")
    route = []
    for i in range(count):
        other = partner_of(i, count)
        for m in range(places):
            target = i * places + (m ^ 1) if other is None else other * places + m
            route.append((i * places + m, target))
    return lax.ppermute(block, ("ctx", "mp"), route)


def inner_swap(block):
    return total_swap(block, lambda i, count: i ^ 1 if 2 <= i < count - 2 else None)


def outer_swap(block):
    return total_swap(block, lambda i, count: ((i + 1) ^ 1) - 1 if 0 < i < count - 1 else None)


def window_of(block):
    second = ring(block, 1)
    first = ring(block, 0)
    near = inner_swap(block)
    return near, first, second, pair_swap(second, "ctx", 1)


VMEM = pl.BlockSpec(memory_space=pltpu.VMEM)
ANY = pl.BlockSpec(memory_space=pl.ANY)
HBM = pl.BlockSpec(memory_space=pltpu.HBM)


def kernel_call(body, outs, args, micros, name, unread=0, scratch=(), out_space=VMEM):
    return pl.pallas_call(
        body,
        out_shape=outs,
        in_specs=[VMEM] * (len(args) - unread) + [ANY] * unread,
        out_specs=tuple(out_space for _ in outs),
        scratch_shapes=scratch,
        compiler_params=pltpu.CompilerParams(vmem_limit_bytes=24 * 1024 * 1024),
        cost_estimate=pl.CostEstimate(
            flops=0, bytes_accessed=int(micros * 3.69e6), transcendentals=0
        ),
        name=name,
    )(*args)


def shaped(shape, dtype):
    return jax.ShapeDtypeStruct(shape, dtype)


def is_even():
    return lax.axis_index("ctx") % 2 == 0


def near_swapped():
    block = lax.axis_index("ctx")
    return (block >= 2) & (block < lax.axis_size("ctx") - 2)


def far_there():
    block = lax.axis_index("ctx")
    return jnp.where(is_even(), block >= 2, block < lax.axis_size("ctx") - 2)


def bias_of(there):
    return jnp.where(there, jnp.float32(0.0), jnp.float32(-jnp.inf))


def columns(width):
    return [slice(c, c + HDIM) for c in range(0, width, HDIM)]


def stacked(blocks, rows, cols):
    return jnp.concatenate([block[rows, cols] for block in blocks], axis=0)


def with_ones(values):
    return jnp.concatenate([values, jnp.ones_like(values)], axis=1)


def by_block(scores, biases, stats=None):
    parts = []
    for b, bias in enumerate(biases):
        part = scores[:, b * HDIM : (b + 1) * HDIM]
        if stats is not None:
            part = part - stats[b]
        parts.append(part if bias is None else part + bias)
    return jnp.concatenate(parts, axis=1)


def tile_of(wide):
    lane = lax.broadcasted_iota(jnp.int32, (wide[0].shape[0], HDIM), 1)
    tile = jnp.zeros((wide[0].shape[0], HDIM), F32)
    for h, part in enumerate(wide):
        tile = jnp.where(lane == h, part, tile)
    return tile


def term_rows(rows):
    at = lax.broadcasted_iota(jnp.int32, (16, rows[0].shape[1]), 0)
    block = jnp.zeros((16, rows[0].shape[1]), F32)
    for r, rest in enumerate(rows):
        for k in range(3):
            term = rest.astype(BF16).astype(F32)
            rest = rest - term
            block = jnp.where(at == 3 * r + k, term, block)
    return block.astype(BF16)


def stat_rows(message, frames, which, cols):
    terms = message[frames : frames + 16, cols].astype(F32)
    at = 3 * which
    return terms[at : at + 1] + terms[at + 1 : at + 2] + terms[at + 2 : at + 3]


def weight_columns(weight, flip):
    width = weight.shape[0]
    at = (lax.axis_index("mp") ^ flip) * width
    return weight[:, pl.ds(pl.multiple_of(at, 128), width)]


def split_body(joined, seen, *parts):
    frames = parts[0].shape[0]
    for k, part in enumerate(parts):
        part[...] = joined[k * frames : (k + 1) * frames, :]


def forward_body(scale, q, own, near, first, second, *refs):
    sums, tops, totals = refs[-3:]
    frames, width = q.shape
    heads = columns(width)
    blocks = (near, own, first, second)
    biases = (bias_of(near_swapped()), None, None, None)
    keys, values = slice(0, frames), slice(frames, 2 * frames)
    scores = [dot_nt(q[:, c], stacked(blocks, keys, c)) * scale for c in heads]
    scores = [by_block(s, biases) for s in scores]
    top = [jnp.max(s, axis=1, keepdims=True) for s in scores]
    probs = [jnp.exp(s - t).astype(BF16) for s, t in zip(scores, top)]
    summed = [dot_nn(p, with_ones(stacked(blocks, values, c))) for p, c in zip(probs, heads)]
    for c, t, s in zip(heads, top, summed):
        tops[:, c] = jnp.broadcast_to(t, (frames, HDIM))
        sums[:, c] = s[:, 0:HDIM]
        totals[:, c] = s[:, HDIM:]


def project_body(scale, q, relay, sums, tops, totals, weight, att, lse, send, keep):
    frames, width = q.shape
    heads = columns(width)
    bias = bias_of(far_there())
    scores = [dot_nt(q[:, c], relay[0:frames, c]) * scale + bias for c in heads]
    before = [tops[:, c] for c in heads]
    top = [jnp.maximum(b, jnp.max(s, axis=1, keepdims=True)) for b, s in zip(before, scores)]
    shrink = [jnp.exp(b - t) for b, t in zip(before, top)]
    probs = [jnp.exp(s - t).astype(BF16) for s, t in zip(scores, top)]
    late = [dot_nn(p, with_ones(relay[frames : 2 * frames, c])) for p, c in zip(probs, heads)]
    total = [totals[:, c] * k + s[:, HDIM:] for c, k, s in zip(heads, shrink, late)]
    summed = [sums[:, c] * k + s[:, 0:HDIM] for c, k, s in zip(heads, shrink, late)]
    attended = jnp.concatenate([(s * (1.0 / t)).astype(BF16) for s, t in zip(summed, total)], axis=1)
    sent = [dot_nn(attended, weight_columns(weight, flip)).astype(BF16) for flip in (1, 3)]
    kept = [dot_nn(attended, weight_columns(weight, flip)).astype(BF16) for flip in (0, 2)]
    logs = [t + jnp.log(n) for t, n in zip(top, total)]
    att[...] = attended
    send[...] = jnp.concatenate(sent, axis=1)
    keep[...] = jnp.concatenate(kept, axis=1)
    for c, part in zip(heads, logs):
        lse[:, c] = part


def pass_body(send, q_second, seen_a, seen_b, send_copy, second_copy):
    send_copy[...] = send[...]
    second_copy[...] = q_second[...]


def join_body(keep, core, inputs, cot, cot_other, q, q_second, chip, rim_near, rim_far, q_copy, second_copy):
    frames, width = inputs.shape
    wide = 2 * HALO
    even = is_even()
    for cols, rows, cots in (
        (slice(0, width), inputs[...].astype(F32), cot),
        (slice(width, 2 * width), 0.0, cot_other),
    ):
        total = (rows + (keep[:, cols].astype(F32) + core[:, cols].astype(F32))).astype(BF16)
        for at, first, last in (
            (slice(0, wide), total[0:wide], total[frames - wide :]),
            (slice(wide, wide + HALO), cots[0:HALO, :], cots[frames - HALO : frames, :]),
        ):
            first, last = first.astype(F32), last.astype(F32)
            rim_near[at, cols] = jnp.where(even, last, first).astype(BF16)
            rim_far[at, cols] = jnp.where(even, first, last).astype(BF16)
        chip[:, cols] = total
    q_copy[...] = q[...]
    second_copy[...] = q_second[...]


def stack_body(rim_near, rim_far, ends):
    wide = 2 * HALO
    ends[0:wide, :] = rim_near[0:wide, :]
    ends[wide : 2 * wide, :] = rim_far[0:wide, :]


def summed(share, across, rows, cols, width):
    back = slice((cols.start + width) % (2 * width), (cols.stop - 1 + width) % (2 * width) + 1)
    total = share[rows, cols].astype(F32) + across[rows, back].astype(F32)
    return total.astype(BF16).astype(F32)


def shifted_sum(rows, taps_of, count):
    total = None
    for b in range(8):
        part = None
        reach = count if b == 0 else count + 8
        for a in range(4):
            tap = taps_of(8 * a + b)
            if tap is None:
                continue
            term = tap * rows[8 * a : 8 * a + reach]
            part = term if part is None else part + term
        if b:
            part = pltpu.roll(part, reach - b, 0)[0:count]
        total = part if total is None else total + part
    return total


def silu_parts(conv, cots):
    gate = 1.0 / (1.0 + jnp.exp(-conv))
    grad = cots * (gate + conv * gate * (1.0 - gate))
    return conv * gate, grad.astype(BF16).astype(F32)


def taps_forward(taps, count, cols):
    return lambda s: taps[s - 1 : s, cols] if 1 <= s <= count else None


def taps_backward(taps, count, cols):
    return lambda s: taps[count - s : count - s + 1, cols] if 1 <= s <= count else None


def conv_chunks(width, cot, cot_other, taps, taps_other):
    for k, cols in enumerate(columns(2 * width)):
        own = k * HDIM < width
        local = cols if own else slice(cols.start - width, cols.stop - width)
        yield own, cols, local, cot if own else cot_other, taps if own else taps_other


def conv_inner_body(
    chip, across, cot, cot_other, taps, taps_other, seen_a, seen_b, rows_out, edge_rows, edge_conv, part_grad
):
    frames, width = cot.shape
    wide, count = 2 * HALO, taps.shape[0]
    inner = slice(HALO, frames - HALO)
    none = jnp.zeros((wide, HDIM), F32)
    for own, cols, local, cots_of, tap in conv_chunks(width, cot, cot_other, taps, taps_other):
        rows = summed(chip, across, slice(0, frames), cols, width)
        cots = cots_of[:, local].astype(F32)
        conv = shifted_sum(
            jnp.concatenate([none, rows, none], axis=0), taps_forward(tap, count, local), frames + wide
        )
        silu, grad = silu_parts(conv[wide:frames], cots[inner])
        back = shifted_sum(
            jnp.concatenate([none, grad, none], axis=0), taps_backward(tap, count, local), frames
        )
        edge_conv[0:wide, cols] = conv[0:wide]
        edge_conv[wide : 2 * wide, cols] = conv[frames : frames + wide]
        if own:
            rows_out[inner, cols] = (rows[inner] + silu).astype(BF16)
            edge_rows[0:HALO, cols] = rows[0:HALO]
            edge_rows[HALO:wide, cols] = rows[frames - HALO :]
        part_grad[:, cols] = cots + back


def conv_edge_body(
    ends, ends_across, rim_near, rim_far, cot, cot_other, taps, taps_other,
    rows_in, edge_rows, edge_conv, part_grad, seen, output, grad_input,
):
    frames, width = cot.shape
    wide, count = 2 * HALO, taps.shape[0]
    even, far = is_even(), far_there()
    low, high = slice(0, HALO), slice(frames - HALO, frames)
    inner = slice(HALO, frames - HALO)
    none = jnp.zeros((wide, HDIM), F32)
    cots_of = slice(wide, wide + HALO)

    def sides(near, beyond):
        beyond = jnp.where(far, beyond, 0.0)
        return jnp.where(even, beyond, near), jnp.where(even, near, beyond)

    for own, cols, local, block, tap in conv_chunks(width, cot, cot_other, taps, taps_other):
        rows = summed(ends, ends_across, slice(0, 2 * wide), cols, width)
        row_low, row_high = sides(rows[0:wide], rows[wide:])
        cot_low, cot_high = sides(rim_near[cots_of, cols].astype(F32), rim_far[cots_of, cols].astype(F32))
        conv = edge_conv[:, cols] + shifted_sum(
            jnp.concatenate([row_low, none, row_high], axis=0), taps_forward(tap, count, local), 2 * wide
        )
        first = block[low, local].astype(F32)
        last = block[high, local].astype(F32)
        cots = jnp.concatenate([cot_low, first, last, cot_high], axis=0)
        silu, grad = silu_parts(conv, cots)
        back = shifted_sum(
            jnp.concatenate([grad[0:wide], none, grad[wide:]], axis=0), taps_backward(tap, count, local), 2 * wide
        )
        part = part_grad[:, cols]
        grad_input[:, cols] = jnp.concatenate(
            [part[0:wide] + back[0:wide], part[wide : frames - wide], part[frames - wide :] + back[wide:]],
            axis=0,
        ).astype(BF16)
        if own:
            output[low, cols] = (edge_rows[0:HALO, cols] + silu[HALO:wide]).astype(BF16)
            output[inner, cols] = rows_in[inner, cols]
            output[high, cols] = (edge_rows[HALO:wide, cols] + silu[wide : wide + HALO]).astype(BF16)


def upstream_part(grads, weight, flips):
    width = weight.shape[0]
    return sum(
        dot_nt(grads[:, k * width : (k + 1) * width], weight_columns(weight, flip))
        for k, flip in enumerate(flips)
    )


def upstream_own_body(own, weight, partial):
    partial[...] = upstream_part(own, weight, (0, 2))


def upstream_body(core, weight, att, lse, partial, message, delta):
    frames, width = att.shape
    heads = columns(width)
    up = (partial[...] + upstream_part(core, weight, (1, 3))).astype(BF16)
    products = [up[:, c].astype(F32) * att[:, c].astype(F32) for c in heads]
    deltas = [jnp.broadcast_to(jnp.sum(p, axis=1, keepdims=True), (frames, HDIM)) for p in products]
    lse_rows = tile_of([lse[:, c] for c in heads]).T
    delta_rows = tile_of(deltas).T
    terms = [term_rows([lse_rows[h : h + 1], delta_rows[h : h + 1]]) for h in range(len(heads))]
    message[0:frames, :] = up
    message[frames : frames + 16, :] = jnp.concatenate(terms, axis=1)
    for c, part in zip(heads, deltas):
        delta[:, c] = part


def query_grad_body(
    scale, q, own, near, first, second, relay, message, lse, delta, output_here, grad_here,
    output, grad_input, grad_query, held, sems,
):
    writes = [
        pltpu.make_async_copy(output_here, output, sems.at[0]),
        pltpu.make_async_copy(grad_here.at[:, pl.ds(0, q.shape[1])], grad_input, sems.at[1]),
    ]
    for write in writes:
        write.start()
    frames, width = q.shape
    heads = columns(width)
    blocks = (near, own, first, second, relay)
    biases = (bias_of(near_swapped()), None, None, None, bias_of(far_there()))
    above, below = slice(0, frames), slice(frames, 2 * frames)
    keys = [stacked(blocks, above, c) for c in heads]
    scores = [dot_nt(q[:, c], k) * scale for c, k in zip(heads, keys)]
    dots = [dot_nt(message[0:frames, c], stacked(blocks, below, c)) for c in heads]
    probs = [jnp.exp(by_block(s, biases, [lse[:, c]] * 5)) for c, s in zip(heads, scores)]
    drops = [by_block(d, (None,) * 5, [delta[:, c]] * 5) for c, d in zip(heads, dots)]
    grads = [(p * d * scale).astype(BF16) for p, d in zip(probs, drops)]
    held[...] = jnp.concatenate([dot_nn(g, k).astype(BF16) for g, k in zip(grads, keys)], axis=1)
    writes.append(pltpu.make_async_copy(held, grad_query, sems.at[2]))
    writes[2].start()
    for write in writes:
        write.wait()


def key_part_body(scale, own, *refs):
    queries, late_query, messages, (key_part, value_part, late) = refs[0:4], refs[4], refs[5:9], refs[9:12]
    frames = own.shape[0] // 2
    heads = columns(own.shape[1])
    above, below = slice(0, frames), slice(frames, 2 * frames)
    biases = (None, bias_of(near_swapped()), None, None)
    asks = [stacked(queries, above, c) for c in heads]
    ups = [stacked(messages, above, c) for c in heads]
    scores = [dot_nt(own[above, c], a) * scale for c, a in zip(heads, asks)]
    dots = [dot_nt(own[below, c], u) for c, u in zip(heads, ups)]
    last = [dot_nt(own[above, c], late_query[:, c]) * scale + bias_of(far_there()) for c in heads]
    logs = [[stat_rows(m, frames, 0, c) for m in messages] for c in heads]
    deltas = [[stat_rows(m, frames, 1, c) for m in messages] for c in heads]
    probs = [jnp.exp(by_block(s, biases, n)) for s, n in zip(scores, logs)]
    drops = [by_block(d, (None,) * 4, n) for d, n in zip(dots, deltas)]
    grads = [(p * d * scale).astype(BF16) for p, d in zip(probs, drops)]
    value_sums = [dot_nn(p.astype(BF16), u) for p, u in zip(probs, ups)]
    key_sums = [dot_nn(g, a) for g, a in zip(grads, asks)]
    for c, k, v, s in zip(heads, key_sums, value_sums, last):
        key_part[:, c] = k
        value_part[:, c] = v
        late[:, c] = s


def key_grad_body(
    scale, own, query, message, late, key_part, value_part, grad_key, grad_value, held_key, held_value, sems
):
    frames = own.shape[0] // 2
    heads = columns(own.shape[1])
    above, below = slice(0, frames), slice(frames, 2 * frames)
    ups = [message[above, c] for c in heads]
    probs = [jnp.exp(late[:, c] - stat_rows(message, frames, 0, c)) for c in heads]
    dots = [dot_nt(own[below, c], u) for c, u in zip(heads, ups)]
    values = [value_part[:, c] + dot_nn(p.astype(BF16), u) for c, p, u in zip(heads, probs, ups)]
    held_value[...] = jnp.concatenate([v.astype(BF16) for v in values], axis=1)
    value_write = pltpu.make_async_copy(held_value, grad_value, sems.at[0])
    value_write.start()
    drops = [d - stat_rows(message, frames, 1, c) for c, d in zip(heads, dots)]
    grads = [(p * d * scale).astype(BF16) for p, d in zip(probs, drops)]
    keys = [key_part[:, c] + dot_nn(g, query[:, c]) for c, g in zip(heads, grads)]
    held_key[...] = jnp.concatenate([k.astype(BF16) for k in keys], axis=1)
    key_write = pltpu.make_async_copy(held_key, grad_key, sems.at[1])
    key_write.start()
    value_write.wait()
    key_write.wait()


def per_device(query_rows, key_rows, value_rows, inputs, out_weight, kernel, cotangent):
    frames, width = query_rows.shape
    wide = 2 * HALO
    scale = 1.0 / math.sqrt(HDIM)
    tile = shaped((frames, width), BF16)
    tile32 = shaped((frames, width), F32)
    rim = shaped((wide + HALO, 2 * width), BF16)
    both = shaped((frames, 2 * width), BF16)
    noted = shaped((frames + 16, width), BF16)

    zero = jnp.zeros((), BF16)
    kv = lax.pad(key_rows, zero, ((0, frames, 0), (0, 0, 0))) + lax.pad(
        value_rows, zero, ((frames, 0, 0), (0, 0, 0))
    )
    near, first, second, relay = window_of(kv)
    cot_other = pair_swap(cotangent, "mp", 2)
    taps_other = pair_swap(kernel, "mp", 2)
    joined = sum(
        lax.pad(rows, zero, ((k * frames, (2 - k) * frames, 0), (0, 0, 0)))
        for k, rows in enumerate((query_rows, inputs, cotangent))
    )
    query, inputs, cotangent = kernel_call(
        split_body, (tile, tile, tile), (joined, second), 0.1, "split", 1
    )
    q_second = ring(query, 1)
    sums, tops, totals = kernel_call(
        functools.partial(forward_body, scale),
        (tile32, tile32, tile32),
        (query, kv, near, first, second),
        1.0, "forward",
    )
    att, lse, send, keep = kernel_call(
        functools.partial(project_body, scale),
        (tile, tile32, both, both),
        (query, relay, sums, tops, totals, out_weight),
        1.0, "project",
    )

    send, q_second = kernel_call(pass_body, (both, tile), (send, q_second, cot_other, taps_other), 0.1, "pass", 2)
    core = pair_swap(send, "mp", 1)
    chip, rim_up, rim_down, q_own, q_handed = kernel_call(
        join_body,
        (both, rim, rim, tile, tile),
        (keep, core, inputs, cotangent, cot_other, query, q_second),
        0.2, "join",
    )
    across = pair_swap(chip, "mp", 2)
    rim_far = outer_swap(rim_down)
    rim_near = pair_swap(rim_up, "ctx", 1)
    (ends,) = kernel_call(
        stack_body, (shaped((2 * wide, 2 * width), BF16),), (rim_near, rim_far), 0.1, "stack"
    )
    ends_across = pair_swap(ends, "mp", 2)
    q_first = ring(q_own, 0)
    q_near = inner_swap(q_own)
    q_relay = pair_swap(q_handed, "ctx", 1)
    rows_out, edge_rows, edge_conv, part_grad = kernel_call(
        conv_inner_body,
        (
            tile,
            shaped((wide, width), F32),
            shaped((2 * wide, 2 * width), F32),
            shaped((frames, 2 * width), F32),
        ),
        (chip, across, cotangent, cot_other, kernel, taps_other, q_first, q_near),
        3.1, "conv_inner", 2,
    )
    output_here, grad_here = kernel_call(
        conv_edge_body,
        (tile, both),
        (ends, ends_across, rim_near, rim_far, cotangent, cot_other, kernel, taps_other)
        + (rows_out, edge_rows, edge_conv, part_grad, q_relay),
        1.4, "conv_edge", 1,
    )

    gi_core = pair_swap(grad_here, "mp", 1)
    (partial,) = kernel_call(upstream_own_body, (tile32,), (grad_here, out_weight), 0.5, "upstream_own")
    message, delta = kernel_call(
        upstream_body, (noted, tile32), (gi_core, out_weight, att, lse, partial), 0.6, "upstream"
    )

    m_near, m_first, m_second, m_relay = window_of(message)
    output, grad_input, grad_query = kernel_call(
        functools.partial(query_grad_body, scale),
        (tile, tile, tile),
        (q_own, kv, near, first, second, relay, message, lse, delta, output_here, grad_here),
        1.8, "query_grad", 0,
        [pltpu.VMEM((frames, width), BF16), pltpu.SemaphoreType.DMA((3,))], HBM,
    )
    key_part, value_part, late = kernel_call(
        functools.partial(key_part_body, scale),
        (tile32, tile32, tile32),
        (kv, q_own, q_near, q_first, q_second, q_relay, message, m_near, m_first, m_second),
        1.5, "key_part",
    )
    grad_key, grad_value = kernel_call(
        functools.partial(key_grad_body, scale),
        (tile, tile),
        (kv, q_relay, m_relay, late, key_part, value_part),
        1.0, "key_grad", 0,
        [pltpu.VMEM((frames, width), BF16)] * 2 + [pltpu.SemaphoreType.DMA((2,))], HBM,
    )
    return (output, grad_input, grad_query, grad_key, grad_value)


def solution(mesh):
    rows = P("ctx", "mp")
    return jax.shard_map(
        per_device,
        mesh=mesh,
        in_specs=(rows, rows, rows, rows, P("mp", None), P(None, "mp"), rows),
        out_specs=(rows,) * 5,
        check_vma=False,
    )
```

```python
import functools
import math

import jax
import jax.numpy as jnp
from jax import lax
from jax.experimental import pallas as pl
from jax.experimental.pallas import tpu as pltpu
from jax.sharding import PartitionSpec as P

HDIM = 128
F32 = jnp.float32
BF16 = jnp.bfloat16
CHUNK = 256
HALO = 16
NT = (((1,), (1,)), ((), ()))
NN = (((1,), (0,)), ((), ()))


def dot_nt(a, b):
    return lax.dot_general(a, b, NT, preferred_element_type=F32)


def dot_nn(a, b):
    return lax.dot_general(a, b, NN, preferred_element_type=F32)


def pair_swap(block, axis, bit):
    return lax.ppermute(block, axis, [(i, i ^ bit) for i in range(lax.axis_size(axis))])


def ring_routes(count):
    rise = [(i, i + 2) for i in range(0, count - 2, 2)] + [(count - 2, count - 1)]
    fall = [(i, i - 2) for i in range(count - 1, 2, -2)] + [(1, 0)]
    route = rise + fall
    return route, [(b, a) for a, b in route]


def ring(block, way):
    return lax.ppermute(block, "ctx", ring_routes(lax.axis_size("ctx"))[way])


def total_swap(block, partner_of):
    count, places = lax.axis_size("ctx"), lax.axis_size("mp")
    route = []
    for i in range(count):
        other = partner_of(i, count)
        for m in range(places):
            target = i * places + (m ^ 1) if other is None else other * places + m
            route.append((i * places + m, target))
    return lax.ppermute(block, ("ctx", "mp"), route)


def inner_swap(block):
    return total_swap(block, lambda i, count: i ^ 1 if 2 <= i < count - 2 else None)


def outer_swap(block):
    return total_swap(block, lambda i, count: ((i + 1) ^ 1) - 1 if 0 < i < count - 1 else None)


def window_of(block, before_relay=lambda second: second):
    second = ring(block, 1)
    first = ring(block, 0)
    near = inner_swap(block)
    second = before_relay(second)
    return near, first, second, pair_swap(second, "ctx", 1)


VMEM = pl.BlockSpec(memory_space=pltpu.VMEM)
ANY = pl.BlockSpec(memory_space=pl.ANY)
HBM = pl.BlockSpec(memory_space=pltpu.HBM)


def kernel_call(body, outs, args, micros, name, unread=0, scratch=(), out_space=VMEM):
    return pl.pallas_call(
        body,
        out_shape=outs,
        in_specs=[VMEM] * (len(args) - unread) + [ANY] * unread,
        out_specs=tuple(out_space for _ in outs),
        scratch_shapes=scratch,
        compiler_params=pltpu.CompilerParams(vmem_limit_bytes=24 * 1024 * 1024),
        cost_estimate=pl.CostEstimate(
            flops=0, bytes_accessed=int(micros * 3.69e6), transcendentals=0
        ),
        name=name,
    )(*args)


def shaped(shape, dtype):
    return jax.ShapeDtypeStruct(shape, dtype)


def is_even():
    return lax.axis_index("ctx") % 2 == 0


def near_swapped():
    block = lax.axis_index("ctx")
    return (block >= 2) & (block < lax.axis_size("ctx") - 2)


def far_there():
    block = lax.axis_index("ctx")
    return jnp.where(is_even(), block >= 2, block < lax.axis_size("ctx") - 2)


def bias_of(there):
    return jnp.where(there, jnp.float32(0.0), jnp.float32(-jnp.inf))


def columns(width):
    return [slice(c, c + HDIM) for c in range(0, width, HDIM)]


def stacked(blocks, rows, cols):
    return jnp.concatenate([block[rows, cols] for block in blocks], axis=0)


def with_ones(values):
    return jnp.concatenate([values, jnp.ones_like(values)], axis=1)


def by_block(scores, biases, stats=None):
    parts = []
    for b, bias in enumerate(biases):
        part = scores[:, b * HDIM : (b + 1) * HDIM]
        if stats is not None:
            part = part - stats[b]
        parts.append(part if bias is None else part + bias)
    return jnp.concatenate(parts, axis=1)


def tile_of(wide):
    lane = lax.broadcasted_iota(jnp.int32, (wide[0].shape[0], HDIM), 1)
    tile = jnp.zeros((wide[0].shape[0], HDIM), F32)
    for h, part in enumerate(wide):
        tile = jnp.where(lane == h, part, tile)
    return tile


def term_rows(rows):
    at = lax.broadcasted_iota(jnp.int32, (16, rows[0].shape[1]), 0)
    block = jnp.zeros((16, rows[0].shape[1]), F32)
    for r, rest in enumerate(rows):
        for k in range(3):
            term = rest.astype(BF16).astype(F32)
            rest = rest - term
            block = jnp.where(at == 3 * r + k, term, block)
    return block.astype(BF16)


def stat_rows(message, frames, which, cols):
    terms = message[frames : frames + 16, cols].astype(F32)
    at = 3 * which
    return terms[at : at + 1] + terms[at + 1 : at + 2] + terms[at + 2 : at + 3]


def weight_columns(weight, flip):
    width = weight.shape[0]
    at = (lax.axis_index("mp") ^ flip) * width
    return weight[:, pl.ds(pl.multiple_of(at, 128), width)]


def turn_body(block, seen, copy):
    copy[...] = block[...]


def split_body(joined, seen, *parts):
    frames = parts[0].shape[0]
    for k, part in enumerate(parts):
        part[...] = joined[k * frames : (k + 1) * frames, :]


def forward_body(scale, q, own, near, first, second, *refs):
    sums, tops, totals = refs[-3:]
    frames, width = q.shape
    heads = columns(width)
    blocks = (near, own, first, second)
    biases = (bias_of(near_swapped()), None, None, None)
    keys, values = slice(0, frames), slice(frames, 2 * frames)
    scores = [dot_nt(q[:, c], stacked(blocks, keys, c)) * scale for c in heads]
    scores = [by_block(s, biases) for s in scores]
    top = [jnp.max(s, axis=1, keepdims=True) for s in scores]
    probs = [jnp.exp(s - t).astype(BF16) for s, t in zip(scores, top)]
    summed = [dot_nn(p, with_ones(stacked(blocks, values, c))) for p, c in zip(probs, heads)]
    for c, t, s in zip(heads, top, summed):
        tops[:, c] = jnp.broadcast_to(t, (frames, HDIM))
        sums[:, c] = s[:, 0:HDIM]
        totals[:, c] = s[:, HDIM:]


def project_body(scale, q, relay, sums, tops, totals, weight, att, lse, send, keep):
    frames, width = q.shape
    heads = columns(width)
    bias = bias_of(far_there())
    scores = [dot_nt(q[:, c], relay[0:frames, c]) * scale + bias for c in heads]
    before = [tops[:, c] for c in heads]
    top = [jnp.maximum(b, jnp.max(s, axis=1, keepdims=True)) for b, s in zip(before, scores)]
    shrink = [jnp.exp(b - t) for b, t in zip(before, top)]
    probs = [jnp.exp(s - t).astype(BF16) for s, t in zip(scores, top)]
    late = [dot_nn(p, with_ones(relay[frames : 2 * frames, c])) for p, c in zip(probs, heads)]
    total = [totals[:, c] * k + s[:, HDIM:] for c, k, s in zip(heads, shrink, late)]
    summed = [sums[:, c] * k + s[:, 0:HDIM] for c, k, s in zip(heads, shrink, late)]
    attended = jnp.concatenate([(s * (1.0 / t)).astype(BF16) for s, t in zip(summed, total)], axis=1)
    sent = [dot_nn(attended, weight_columns(weight, flip)).astype(BF16) for flip in (1, 3)]
    kept = [dot_nn(attended, weight_columns(weight, flip)).astype(BF16) for flip in (0, 2)]
    logs = [t + jnp.log(n) for t, n in zip(top, total)]
    att[...] = attended
    send[...] = jnp.concatenate(sent, axis=1)
    keep[...] = jnp.concatenate(kept, axis=1)
    for c, part in zip(heads, logs):
        lse[:, c] = part


def pass_body(send, q_second, seen_a, seen_b, send_copy, second_copy):
    send_copy[...] = send[...]
    second_copy[...] = q_second[...]


def join_body(keep, core, inputs, cot, cot_other, q, chip, rim_near, rim_far, q_copy):
    frames, width = inputs.shape
    wide = 2 * HALO
    even = is_even()
    for cols, rows, cots in (
        (slice(0, width), inputs[...].astype(F32), cot),
        (slice(width, 2 * width), 0.0, cot_other),
    ):
        total = (rows + (keep[:, cols].astype(F32) + core[:, cols].astype(F32))).astype(BF16)
        for at, first, last in (
            (slice(0, wide), total[0:wide], total[frames - wide :]),
            (slice(wide, wide + HALO), cots[0:HALO, :], cots[frames - HALO : frames, :]),
        ):
            first, last = first.astype(F32), last.astype(F32)
            rim_near[at, cols] = jnp.where(even, last, first).astype(BF16)
            rim_far[at, cols] = jnp.where(even, first, last).astype(BF16)
        chip[:, cols] = total
    q_copy[...] = q[...]


def stack_body(rim_near, rim_far, q_second, ends, second_copy):
    wide = 2 * HALO
    ends[0:wide, :] = rim_near[0:wide, :]
    ends[wide : 2 * wide, :] = rim_far[0:wide, :]
    second_copy[...] = q_second[...]


def summed(share, across, rows, cols, width):
    back = slice((cols.start + width) % (2 * width), (cols.stop - 1 + width) % (2 * width) + 1)
    total = share[rows, cols].astype(F32) + across[rows, back].astype(F32)
    return total.astype(BF16).astype(F32)


def tiles_of(rows):
    return [rows[at : at + 8] for at in range(0, rows.shape[0], 8)]


def shifted_sum(tiles, taps_of, count):
    at = lax.broadcasted_iota(jnp.int32, (8, CHUNK), 0)
    sums = [None] * (count // 8)

    def add(k, term):
        sums[k] = term if sums[k] is None else sums[k] + term

    for b in range(8):
        parts = []
        for k in range(count // 8 + (b > 0)):
            part = None
            for a in range(4):
                tap = taps_of(8 * a + b)
                if tap is None or tiles[k + a] is None:
                    continue
                term = tap * tiles[k + a]
                part = term if part is None else part + term
            parts.append(part if part is None or b == 0 else pltpu.roll(part, 8 - b, 0))
        for k in range(count // 8):
            if b == 0:
                if parts[k] is not None:
                    add(k, parts[k])
            elif parts[k] is not None and parts[k + 1] is not None:
                add(k, jnp.where(at < 8 - b, parts[k], parts[k + 1]))
            elif parts[k] is not None:
                add(k, jnp.where(at < 8 - b, parts[k], 0.0))
            elif parts[k + 1] is not None:
                add(k, jnp.where(at < 8 - b, 0.0, parts[k + 1]))
    zero = jnp.zeros((8, CHUNK), F32)
    return jnp.concatenate([zero if part is None else part for part in sums], axis=0)


def silu_parts(conv, cots):
    gate = 1.0 / (1.0 + jnp.exp(-conv))
    grad = cots * (gate + conv * gate * (1.0 - gate))
    return conv * gate, grad.astype(BF16).astype(F32)


def taps_forward(taps, count, cols):
    return lambda s: taps[s - 1 : s, cols] if 1 <= s <= count else None


def taps_backward(taps, count, cols):
    return lambda s: taps[count - s : count - s + 1, cols] if 1 <= s <= count else None


def conv_chunks(width, cot, cot_other, taps, taps_other):
    for c in range(0, 2 * width, CHUNK):
        own, cols = c < width, slice(c, c + CHUNK)
        local = cols if own else slice(cols.start - width, cols.stop - width)
        yield own, cols, local, cot if own else cot_other, taps if own else taps_other


def conv_inner_body(
    chip, across, cot, cot_other, taps, taps_other, seen, rows_out, edge_rows, edge_conv, part_grad
):
    frames, width = cot.shape
    wide, count = 2 * HALO, taps.shape[0]
    inner = slice(HALO, frames - HALO)
    none = [None] * (wide // 8)
    for own, cols, local, cots_of, tap in conv_chunks(width, cot, cot_other, taps, taps_other):
        rows = summed(chip, across, slice(0, frames), cols, width)
        cots = cots_of[:, local].astype(F32)
        conv = shifted_sum(
            none + tiles_of(rows) + none, taps_forward(tap, count, local), frames + wide
        )
        silu, grad = silu_parts(conv[wide:frames], cots[inner])
        back = shifted_sum(
            none + tiles_of(grad) + none, taps_backward(tap, count, local), frames
        )
        edge_conv[0:wide, cols] = conv[0:wide]
        edge_conv[wide : 2 * wide, cols] = conv[frames : frames + wide]
        if own:
            rows_out[inner, cols] = (rows[inner] + silu).astype(BF16)
            edge_rows[0:HALO, cols] = rows[0:HALO]
            edge_rows[HALO:wide, cols] = rows[frames - HALO :]
        part_grad[:, cols] = cots + back


def conv_edge_body(
    ends, ends_across, rim_near, rim_far, cot, cot_other, taps, taps_other,
    rows_in, edge_rows, edge_conv, part_grad, seen_a, seen_b, output, grad_input,
):
    frames, width = cot.shape
    wide, count = 2 * HALO, taps.shape[0]
    even, far = is_even(), far_there()
    low, high = slice(0, HALO), slice(frames - HALO, frames)
    inner = slice(HALO, frames - HALO)
    none = [None] * (wide // 8)
    cots_of = slice(wide, wide + HALO)

    def sides(near, beyond):
        beyond = jnp.where(far, beyond, 0.0)
        return jnp.where(even, beyond, near), jnp.where(even, near, beyond)

    for own, cols, local, block, tap in conv_chunks(width, cot, cot_other, taps, taps_other):
        rows = summed(ends, ends_across, slice(0, 2 * wide), cols, width)
        row_low, row_high = sides(rows[0:wide], rows[wide:])
        cot_low, cot_high = sides(rim_near[cots_of, cols].astype(F32), rim_far[cots_of, cols].astype(F32))
        conv = edge_conv[:, cols] + shifted_sum(
            tiles_of(row_low) + none + tiles_of(row_high), taps_forward(tap, count, local), 2 * wide
        )
        first = block[low, local].astype(F32)
        last = block[high, local].astype(F32)
        cots = jnp.concatenate([cot_low, first, last, cot_high], axis=0)
        silu, grad = silu_parts(conv, cots)
        back = shifted_sum(
            tiles_of(grad[0:wide]) + none + tiles_of(grad[wide:]), taps_backward(tap, count, local), 2 * wide
        )
        part = part_grad[:, cols]
        grad_input[:, cols] = jnp.concatenate(
            [part[0:wide] + back[0:wide], part[wide : frames - wide], part[frames - wide :] + back[wide:]],
            axis=0,
        ).astype(BF16)
        if own:
            output[low, cols] = (edge_rows[0:HALO, cols] + silu[HALO:wide]).astype(BF16)
            output[inner, cols] = rows_in[inner, cols]
            output[high, cols] = (edge_rows[HALO:wide, cols] + silu[wide : wide + HALO]).astype(BF16)


def upstream_part(grads, weight, flips):
    width = weight.shape[0]
    return sum(
        dot_nt(grads[:, k * width : (k + 1) * width], weight_columns(weight, flip))
        for k, flip in enumerate(flips)
    )


def upstream_own_body(own, weight, partial):
    partial[...] = upstream_part(own, weight, (0, 2))


def upstream_body(core, weight, att, lse, partial, message, delta):
    frames, width = att.shape
    heads = columns(width)
    up = (partial[...] + upstream_part(core, weight, (1, 3))).astype(BF16)
    products = [up[:, c].astype(F32) * att[:, c].astype(F32) for c in heads]
    deltas = [jnp.broadcast_to(jnp.sum(p, axis=1, keepdims=True), (frames, HDIM)) for p in products]
    lse_rows = tile_of([lse[:, c] for c in heads]).T
    delta_rows = tile_of(deltas).T
    terms = [term_rows([lse_rows[h : h + 1], delta_rows[h : h + 1]]) for h in range(len(heads))]
    message[0:frames, :] = up
    message[frames : frames + 16, :] = jnp.concatenate(terms, axis=1)
    for c, part in zip(heads, deltas):
        delta[:, c] = part


def query_grad_body(
    scale, q, own, near, first, second, relay, message, lse, delta, output_here, grad_here,
    output, grad_input, grad_query, held, sems,
):
    writes = [
        pltpu.make_async_copy(output_here, output, sems.at[0]),
        pltpu.make_async_copy(grad_here.at[:, pl.ds(0, q.shape[1])], grad_input, sems.at[1]),
    ]
    for write in writes:
        write.start()
    frames, width = q.shape
    heads = columns(width)
    blocks = (near, own, first, second, relay)
    biases = (bias_of(near_swapped()), None, None, None, bias_of(far_there()))
    above, below = slice(0, frames), slice(frames, 2 * frames)
    keys = [stacked(blocks, above, c) for c in heads]
    scores = [dot_nt(q[:, c], k) * scale for c, k in zip(heads, keys)]
    dots = [dot_nt(message[0:frames, c], stacked(blocks, below, c)) for c in heads]
    probs = [jnp.exp(by_block(s, biases, [lse[:, c]] * 5)) for c, s in zip(heads, scores)]
    drops = [by_block(d, (None,) * 5, [delta[:, c]] * 5) for c, d in zip(heads, dots)]
    grads = [(p * d * scale).astype(BF16) for p, d in zip(probs, drops)]
    held[...] = jnp.concatenate([dot_nn(g, k).astype(BF16) for g, k in zip(grads, keys)], axis=1)
    writes.append(pltpu.make_async_copy(held, grad_query, sems.at[2]))
    writes[2].start()
    for write in writes:
        write.wait()


def key_part_body(scale, own, *refs):
    queries, late_query, messages, (key_part, value_part, late) = refs[0:4], refs[4], refs[5:9], refs[9:12]
    frames = own.shape[0] // 2
    heads = columns(own.shape[1])
    above, below = slice(0, frames), slice(frames, 2 * frames)
    biases = (None, bias_of(near_swapped()), None, None)
    asks = [stacked(queries, above, c) for c in heads]
    ups = [stacked(messages, above, c) for c in heads]
    scores = [dot_nt(own[above, c], a) * scale for c, a in zip(heads, asks)]
    dots = [dot_nt(own[below, c], u) for c, u in zip(heads, ups)]
    last = [dot_nt(own[above, c], late_query[:, c]) * scale + bias_of(far_there()) for c in heads]
    logs = [[stat_rows(m, frames, 0, c) for m in messages] for c in heads]
    deltas = [[stat_rows(m, frames, 1, c) for m in messages] for c in heads]
    probs = [jnp.exp(by_block(s, biases, n)) for s, n in zip(scores, logs)]
    drops = [by_block(d, (None,) * 4, n) for d, n in zip(dots, deltas)]
    grads = [(p * d * scale).astype(BF16) for p, d in zip(probs, drops)]
    value_sums = [dot_nn(p.astype(BF16), u) for p, u in zip(probs, ups)]
    key_sums = [dot_nn(g, a) for g, a in zip(grads, asks)]
    for c, k, v, s in zip(heads, key_sums, value_sums, last):
        key_part[:, c] = k
        value_part[:, c] = v
        late[:, c] = s


def key_grad_body(
    scale, own, query, message, late, key_part, value_part, grad_key, grad_value, held_key, held_value, sems
):
    frames = own.shape[0] // 2
    heads = columns(own.shape[1])
    above, below = slice(0, frames), slice(frames, 2 * frames)
    ups = [message[above, c] for c in heads]
    probs = [jnp.exp(late[:, c] - stat_rows(message, frames, 0, c)) for c in heads]
    dots = [dot_nt(own[below, c], u) for c, u in zip(heads, ups)]
    values = [value_part[:, c] + dot_nn(p.astype(BF16), u) for c, p, u in zip(heads, probs, ups)]
    held_value[...] = jnp.concatenate([v.astype(BF16) for v in values], axis=1)
    value_write = pltpu.make_async_copy(held_value, grad_value, sems.at[0])
    value_write.start()
    drops = [d - stat_rows(message, frames, 1, c) for c, d in zip(heads, dots)]
    grads = [(p * d * scale).astype(BF16) for p, d in zip(probs, drops)]
    keys = [key_part[:, c] + dot_nn(g, query[:, c]) for c, g in zip(heads, grads)]
    held_key[...] = jnp.concatenate([k.astype(BF16) for k in keys], axis=1)
    key_write = pltpu.make_async_copy(held_key, grad_key, sems.at[1])
    key_write.start()
    value_write.wait()
    key_write.wait()


def per_device(query_rows, key_rows, value_rows, inputs, out_weight, kernel, cotangent):
    frames, width = query_rows.shape
    wide = 2 * HALO
    scale = 1.0 / math.sqrt(HDIM)
    tile = shaped((frames, width), BF16)
    tile32 = shaped((frames, width), F32)
    rim = shaped((wide + HALO, 2 * width), BF16)
    both = shaped((frames, 2 * width), BF16)
    noted = shaped((frames + 16, width), BF16)

    zero = jnp.zeros((), BF16)
    kv = lax.pad(key_rows, zero, ((0, frames, 0), (0, 0, 0))) + lax.pad(
        value_rows, zero, ((frames, 0, 0), (0, 0, 0))
    )
    joined = sum(
        lax.pad(rows, zero, ((k * frames, (2 - k) * frames, 0), (0, 0, 0)))
        for k, rows in enumerate((query_rows, inputs, cotangent))
    )
    near, first, second, relay = window_of(
        kv,
        lambda second: kernel_call(
            turn_body, (shaped(kv.shape, BF16),), (second, joined), 0.1, "turn", 1
        )[0],
    )
    cot_other = pair_swap(cotangent, "mp", 2)
    taps_other = pair_swap(kernel, "mp", 2)
    query, inputs, cotangent = kernel_call(
        split_body, (tile, tile, tile), (joined, second), 0.1, "split", 1
    )
    q_second = ring(query, 1)
    sums, tops, totals = kernel_call(
        functools.partial(forward_body, scale),
        (tile32, tile32, tile32),
        (query, kv, near, first, second),
        1.0, "forward",
    )
    att, lse, send, keep = kernel_call(
        functools.partial(project_body, scale),
        (tile, tile32, both, both),
        (query, relay, sums, tops, totals, out_weight),
        1.0, "project",
    )

    send, q_second = kernel_call(pass_body, (both, tile), (send, q_second, cot_other, taps_other), 0.1, "pass", 2)
    core = pair_swap(send, "mp", 1)
    chip, rim_up, rim_down, q_own = kernel_call(
        join_body,
        (both, rim, rim, tile),
        (keep, core, inputs, cotangent, cot_other, query),
        0.2, "join",
    )
    across = pair_swap(chip, "mp", 2)
    rim_far = outer_swap(rim_down)
    rim_near = pair_swap(rim_up, "ctx", 1)
    ends, q_handed = kernel_call(
        stack_body,
        (shaped((2 * wide, 2 * width), BF16), tile),
        (rim_near, rim_far, q_second),
        0.1, "stack",
    )
    ends_across = pair_swap(ends, "mp", 2)
    q_first = ring(q_own, 0)
    q_near = inner_swap(q_own)
    q_relay = pair_swap(q_handed, "ctx", 1)
    rows_out, edge_rows, edge_conv, part_grad = kernel_call(
        conv_inner_body,
        (
            tile,
            shaped((wide, width), F32),
            shaped((2 * wide, 2 * width), F32),
            shaped((frames, 2 * width), F32),
        ),
        (chip, across, cotangent, cot_other, kernel, taps_other, q_first),
        3.1, "conv_inner", 1,
    )
    output_here, grad_here = kernel_call(
        conv_edge_body,
        (tile, both),
        (ends, ends_across, rim_near, rim_far, cotangent, cot_other, kernel, taps_other)
        + (rows_out, edge_rows, edge_conv, part_grad, q_near, q_relay),
        1.4, "conv_edge", 2,
    )

    gi_core = pair_swap(grad_here, "mp", 1)
    (partial,) = kernel_call(upstream_own_body, (tile32,), (grad_here, out_weight), 0.5, "upstream_own")
    message, delta = kernel_call(
        upstream_body, (noted, tile32), (gi_core, out_weight, att, lse, partial), 0.6, "upstream"
    )

    m_near, m_first, m_second, m_relay = window_of(message)
    output, grad_input, grad_query = kernel_call(
        functools.partial(query_grad_body, scale),
        (tile, tile, tile),
        (q_own, kv, near, first, second, relay, message, lse, delta, output_here, grad_here),
        1.8, "query_grad", 0,
        [pltpu.VMEM((frames, width), BF16), pltpu.SemaphoreType.DMA((3,))], HBM,
    )
    key_part, value_part, late = kernel_call(
        functools.partial(key_part_body, scale),
        (tile32, tile32, tile32),
        (kv, q_own, q_near, q_first, q_second, q_relay, message, m_near, m_first, m_second),
        1.5, "key_part",
    )
    grad_key, grad_value = kernel_call(
        functools.partial(key_grad_body, scale),
        (tile, tile),
        (kv, q_relay, m_relay, late, key_part, value_part),
        1.0, "key_grad", 0,
        [pltpu.VMEM((frames, width), BF16)] * 2 + [pltpu.SemaphoreType.DMA((2,))], HBM,
    )
    return (output, grad_input, grad_query, grad_key, grad_value)


def solution(mesh):
    rows = P("ctx", "mp")
    return jax.shard_map(
        per_device,
        mesh=mesh,
        in_specs=(rows, rows, rows, rows, P("mp", None), P(None, "mp"), rows),
        out_specs=(rows,) * 5,
        check_vma=False,
    )
```

```python
import functools
import math

import jax
import jax.numpy as jnp
from jax import lax
from jax.experimental import pallas as pl
from jax.experimental.pallas import tpu as pltpu
from jax.sharding import PartitionSpec as P

HDIM = 128
F32 = jnp.float32
BF16 = jnp.bfloat16
CHUNK = 256
HALO = 16
NT = (((1,), (1,)), ((), ()))
NN = (((1,), (0,)), ((), ()))


def dot_nt(a, b):
    return lax.dot_general(a, b, NT, preferred_element_type=F32)


def dot_nn(a, b):
    return lax.dot_general(a, b, NN, preferred_element_type=F32)


def pair_swap(block, axis, bit):
    return lax.ppermute(block, axis, [(i, i ^ bit) for i in range(lax.axis_size(axis))])


def ring_routes(count):
    rise = [(i, i + 2) for i in range(0, count - 2, 2)] + [(count - 2, count - 1)]
    fall = [(i, i - 2) for i in range(count - 1, 2, -2)] + [(1, 0)]
    route = rise + fall
    return route, [(b, a) for a, b in route]


def ring(block, way):
    return lax.ppermute(block, "ctx", ring_routes(lax.axis_size("ctx"))[way])


def total_swap(block, partner_of):
    count, places = lax.axis_size("ctx"), lax.axis_size("mp")
    route = []
    for i in range(count):
        other = partner_of(i, count)
        for m in range(places):
            target = i * places + (m ^ 1) if other is None else other * places + m
            route.append((i * places + m, target))
    return lax.ppermute(block, ("ctx", "mp"), route)


def inner_swap(block):
    return total_swap(block, lambda i, count: i ^ 1 if 2 <= i < count - 2 else None)


def outer_swap(block):
    return total_swap(block, lambda i, count: ((i + 1) ^ 1) - 1 if 0 < i < count - 1 else None)


def window_of(block):
    second = ring(block, 1)
    first = ring(block, 0)
    near = inner_swap(block)
    return near, first, second, pair_swap(second, "ctx", 1)


VMEM = pl.BlockSpec(memory_space=pltpu.VMEM)
ANY = pl.BlockSpec(memory_space=pl.ANY)
HBM = pl.BlockSpec(memory_space=pltpu.HBM)


def kernel_call(body, outs, args, micros, name, unread=0, scratch=(), out_space=VMEM):
    return pl.pallas_call(
        body,
        out_shape=outs,
        in_specs=[VMEM] * (len(args) - unread) + [ANY] * unread,
        out_specs=tuple(out_space for _ in outs),
        scratch_shapes=scratch,
        compiler_params=pltpu.CompilerParams(vmem_limit_bytes=24 * 1024 * 1024),
        cost_estimate=pl.CostEstimate(
            flops=0, bytes_accessed=int(micros * 3.69e6), transcendentals=0
        ),
        name=name,
    )(*args)


def shaped(shape, dtype):
    return jax.ShapeDtypeStruct(shape, dtype)


def is_even():
    return lax.axis_index("ctx") % 2 == 0


def near_swapped():
    block = lax.axis_index("ctx")
    return (block >= 2) & (block < lax.axis_size("ctx") - 2)


def far_there():
    block = lax.axis_index("ctx")
    return jnp.where(is_even(), block >= 2, block < lax.axis_size("ctx") - 2)


def bias_of(there):
    return jnp.where(there, jnp.float32(0.0), jnp.float32(-jnp.inf))


def columns(width):
    return [slice(c, c + HDIM) for c in range(0, width, HDIM)]


def stacked(blocks, rows, cols):
    return jnp.concatenate([block[rows, cols] for block in blocks], axis=0)


def window_keys(joined, single, frames, cols):
    return jnp.concatenate([b[0:frames, cols] for b in joined] + [b[:, cols] for b in single], axis=0)


def window_values(joined, single, frames, cols):
    return jnp.concatenate(
        [b[frames : 2 * frames, cols] for b in joined] + [b[:, cols] for b in single], axis=0
    )


def with_ones(values):
    return jnp.concatenate([values, jnp.ones_like(values)], axis=1)


def by_block(scores, biases, stats=None):
    parts = []
    for b, bias in enumerate(biases):
        part = scores[:, b * HDIM : (b + 1) * HDIM]
        if stats is not None:
            part = part - stats[b]
        parts.append(part if bias is None else part + bias)
    return jnp.concatenate(parts, axis=1)


def tile_of(wide):
    lane = lax.broadcasted_iota(jnp.int32, (wide[0].shape[0], HDIM), 1)
    tile = jnp.zeros((wide[0].shape[0], HDIM), F32)
    for h, part in enumerate(wide):
        tile = jnp.where(lane == h, part, tile)
    return tile


def term_rows(rows):
    at = lax.broadcasted_iota(jnp.int32, (16, rows[0].shape[1]), 0)
    block = jnp.zeros((16, rows[0].shape[1]), F32)
    for r, rest in enumerate(rows):
        for k in range(3):
            term = rest.astype(BF16).astype(F32)
            rest = rest - term
            block = jnp.where(at == 3 * r + k, term, block)
    return block.astype(BF16)


def stat_rows(message, frames, which, cols):
    terms = message[frames : frames + 16, cols].astype(F32)
    at = 3 * which
    return terms[at : at + 1] + terms[at + 1 : at + 2] + terms[at + 2 : at + 3]


def weight_columns(weight, flip):
    width = weight.shape[0]
    at = (lax.axis_index("mp") ^ flip) * width
    return weight[:, pl.ds(pl.multiple_of(at, 128), width)]


def turn_body(block, seen, copy):
    copy[...] = block[...]


def split_body(joined, seen, *parts):
    frames = parts[0].shape[0]
    for k, part in enumerate(parts):
        part[...] = joined[k * frames : (k + 1) * frames, :]


def forward_body(scale, q, own, near, first, second_key, second_value, *refs):
    sums, tops, totals = refs[-3:]
    frames, width = q.shape
    heads = columns(width)
    blocks = (near, own, first)
    biases = (bias_of(near_swapped()), None, None, None)
    scores = [dot_nt(q[:, c], window_keys(blocks, (second_key,), frames, c)) * scale for c in heads]
    scores = [by_block(s, biases) for s in scores]
    top = [jnp.max(s, axis=1, keepdims=True) for s in scores]
    probs = [jnp.exp(s - t).astype(BF16) for s, t in zip(scores, top)]
    summed = [dot_nn(p, with_ones(window_values(blocks, (second_value,), frames, c))) for p, c in zip(probs, heads)]
    for c, t, s in zip(heads, top, summed):
        tops[:, c] = jnp.broadcast_to(t, (frames, HDIM))
        sums[:, c] = s[:, 0:HDIM]
        totals[:, c] = s[:, HDIM:]


def project_body(scale, q, relay_key, relay_value, sums, tops, totals, weight, att, lse, send):
    frames, width = q.shape
    heads = columns(width)
    bias = bias_of(far_there())
    scores = [dot_nt(q[:, c], relay_key[:, c]) * scale + bias for c in heads]
    before = [tops[:, c] for c in heads]
    top = [jnp.maximum(b, jnp.max(s, axis=1, keepdims=True)) for b, s in zip(before, scores)]
    shrink = [jnp.exp(b - t) for b, t in zip(before, top)]
    probs = [jnp.exp(s - t).astype(BF16) for s, t in zip(scores, top)]
    late = [dot_nn(p, with_ones(relay_value[:, c])) for p, c in zip(probs, heads)]
    total = [totals[:, c] * k + s[:, HDIM:] for c, k, s in zip(heads, shrink, late)]
    summed = [sums[:, c] * k + s[:, 0:HDIM] for c, k, s in zip(heads, shrink, late)]
    attended = jnp.concatenate([(s * (1.0 / t)).astype(BF16) for s, t in zip(summed, total)], axis=1)
    sent = [dot_nn(attended, weight_columns(weight, flip)).astype(BF16) for flip in (1, 3)]
    logs = [t + jnp.log(n) for t, n in zip(top, total)]
    att[...] = attended
    send[...] = jnp.concatenate(sent, axis=1)
    for c, part in zip(heads, logs):
        lse[:, c] = part


def project_own_body(att, weight, keep):
    kept = [dot_nn(att[...], weight_columns(weight, flip)).astype(BF16) for flip in (0, 2)]
    keep[...] = jnp.concatenate(kept, axis=1)


def pass_body(send, q_second, seen_a, seen_b, send_copy, second_copy):
    send_copy[...] = send[...]
    second_copy[...] = q_second[...]


def join_body(keep, core, inputs, cot, cot_other, q, chip, rim_near, rim_far, q_copy):
    frames, width = inputs.shape
    wide = 2 * HALO
    even = is_even()
    for cols, rows, cots in (
        (slice(0, width), inputs[...].astype(F32), cot),
        (slice(width, 2 * width), 0.0, cot_other),
    ):
        total = (rows + (keep[:, cols].astype(F32) + core[:, cols].astype(F32))).astype(BF16)
        for at, first, last in (
            (slice(0, wide), total[0:wide], total[frames - wide :]),
            (slice(wide, wide + HALO), cots[0:HALO, :], cots[frames - HALO : frames, :]),
        ):
            first, last = first.astype(F32), last.astype(F32)
            rim_near[at, cols] = jnp.where(even, last, first).astype(BF16)
            rim_far[at, cols] = jnp.where(even, first, last).astype(BF16)
        chip[:, cols] = total
    q_copy[...] = q[...]


def stack_body(rim_near, rim_far, q_second, ends, second_copy):
    wide = 2 * HALO
    ends[0:wide, :] = rim_near[0:wide, :]
    ends[wide : 2 * wide, :] = rim_far[0:wide, :]
    second_copy[...] = q_second[...]


def summed(share, across, rows, cols, width):
    back = slice((cols.start + width) % (2 * width), (cols.stop - 1 + width) % (2 * width) + 1)
    total = share[rows, cols].astype(F32) + across[rows, back].astype(F32)
    return total.astype(BF16).astype(F32)


def tiles_of(rows):
    return [rows[at : at + 8] for at in range(0, rows.shape[0], 8)]


def shifted_sum(tiles, taps_of, count):
    at = lax.broadcasted_iota(jnp.int32, (8, CHUNK), 0)
    sums = [None] * (count // 8)

    def add(k, term):
        sums[k] = term if sums[k] is None else sums[k] + term

    for b in range(8):
        parts = []
        for k in range(count // 8 + (b > 0)):
            part = None
            for a in range(4):
                tap = taps_of(8 * a + b)
                if tap is None or tiles[k + a] is None:
                    continue
                term = tap * tiles[k + a]
                part = term if part is None else part + term
            parts.append(part if part is None or b == 0 else pltpu.roll(part, 8 - b, 0))
        for k in range(count // 8):
            if b == 0:
                if parts[k] is not None:
                    add(k, parts[k])
            elif parts[k] is not None and parts[k + 1] is not None:
                add(k, jnp.where(at < 8 - b, parts[k], parts[k + 1]))
            elif parts[k] is not None:
                add(k, jnp.where(at < 8 - b, parts[k], 0.0))
            elif parts[k + 1] is not None:
                add(k, jnp.where(at < 8 - b, 0.0, parts[k + 1]))
    zero = jnp.zeros((8, CHUNK), F32)
    return jnp.concatenate([zero if part is None else part for part in sums], axis=0)


def silu_parts(conv, cots):
    gate = 1.0 / (1.0 + jnp.exp(-conv))
    grad = cots * (gate + conv * gate * (1.0 - gate))
    return conv * gate, grad.astype(BF16).astype(F32)


def taps_forward(taps, count, cols):
    return lambda s: taps[s - 1 : s, cols] if 1 <= s <= count else None


def taps_backward(taps, count, cols):
    return lambda s: taps[count - s : count - s + 1, cols] if 1 <= s <= count else None


def conv_chunks(width, cot, cot_other, taps, taps_other):
    for c in range(0, 2 * width, CHUNK):
        own, cols = c < width, slice(c, c + CHUNK)
        local = cols if own else slice(cols.start - width, cols.stop - width)
        yield own, cols, local, cot if own else cot_other, taps if own else taps_other


def conv_inner_body(
    chip, across, cot, cot_other, taps, taps_other, seen, rows_out, edge_rows, edge_conv, part_grad
):
    frames, width = cot.shape
    wide, count = 2 * HALO, taps.shape[0]
    inner = slice(HALO, frames - HALO)
    none = [None] * (wide // 8)
    for own, cols, local, cots_of, tap in conv_chunks(width, cot, cot_other, taps, taps_other):
        rows = summed(chip, across, slice(0, frames), cols, width)
        cots = cots_of[:, local].astype(F32)
        conv = shifted_sum(
            none + tiles_of(rows) + none, taps_forward(tap, count, local), frames + wide
        )
        silu, grad = silu_parts(conv[wide:frames], cots[inner])
        back = shifted_sum(
            none + tiles_of(grad) + none, taps_backward(tap, count, local), frames
        )
        edge_conv[0:wide, cols] = conv[0:wide]
        edge_conv[wide : 2 * wide, cols] = conv[frames : frames + wide]
        if own:
            rows_out[inner, cols] = (rows[inner] + silu).astype(BF16)
            edge_rows[0:HALO, cols] = rows[0:HALO]
            edge_rows[HALO:wide, cols] = rows[frames - HALO :]
        part_grad[:, cols] = cots + back


def conv_edge_body(
    ends, ends_across, rim_near, rim_far, cot, cot_other, taps, taps_other,
    rows_in, edge_rows, edge_conv, part_grad, seen_a, seen_b, output, grad_input,
):
    frames, width = cot.shape
    wide, count = 2 * HALO, taps.shape[0]
    even, far = is_even(), far_there()
    low, high = slice(0, HALO), slice(frames - HALO, frames)
    inner = slice(HALO, frames - HALO)
    none = [None] * (wide // 8)
    cots_of = slice(wide, wide + HALO)

    def sides(near, beyond):
        beyond = jnp.where(far, beyond, 0.0)
        return jnp.where(even, beyond, near), jnp.where(even, near, beyond)

    for own, cols, local, block, tap in conv_chunks(width, cot, cot_other, taps, taps_other):
        rows = summed(ends, ends_across, slice(0, 2 * wide), cols, width)
        row_low, row_high = sides(rows[0:wide], rows[wide:])
        cot_low, cot_high = sides(rim_near[cots_of, cols].astype(F32), rim_far[cots_of, cols].astype(F32))
        conv = edge_conv[:, cols] + shifted_sum(
            tiles_of(row_low) + none + tiles_of(row_high), taps_forward(tap, count, local), 2 * wide
        )
        first = block[low, local].astype(F32)
        last = block[high, local].astype(F32)
        cots = jnp.concatenate([cot_low, first, last, cot_high], axis=0)
        silu, grad = silu_parts(conv, cots)
        back = shifted_sum(
            tiles_of(grad[0:wide]) + none + tiles_of(grad[wide:]), taps_backward(tap, count, local), 2 * wide
        )
        part = part_grad[:, cols]
        grad_input[:, cols] = jnp.concatenate(
            [part[0:wide] + back[0:wide], part[wide : frames - wide], part[frames - wide :] + back[wide:]],
            axis=0,
        ).astype(BF16)
        if own:
            output[low, cols] = (edge_rows[0:HALO, cols] + silu[HALO:wide]).astype(BF16)
            output[inner, cols] = rows_in[inner, cols]
            output[high, cols] = (edge_rows[HALO:wide, cols] + silu[wide : wide + HALO]).astype(BF16)


def upstream_part(grads, weight, flips):
    width = weight.shape[0]
    return sum(
        dot_nt(grads[:, k * width : (k + 1) * width], weight_columns(weight, flip))
        for k, flip in enumerate(flips)
    )


def upstream_own_body(own, weight, partial):
    partial[...] = upstream_part(own, weight, (0, 2))


def upstream_body(core, weight, att, lse, partial, message, delta):
    frames, width = att.shape
    heads = columns(width)
    up = (partial[...] + upstream_part(core, weight, (1, 3))).astype(BF16)
    products = [up[:, c].astype(F32) * att[:, c].astype(F32) for c in heads]
    deltas = [jnp.broadcast_to(jnp.sum(p, axis=1, keepdims=True), (frames, HDIM)) for p in products]
    lse_rows = tile_of([lse[:, c] for c in heads]).T
    delta_rows = tile_of(deltas).T
    terms = [term_rows([lse_rows[h : h + 1], delta_rows[h : h + 1]]) for h in range(len(heads))]
    message[0:frames, :] = up
    message[frames : frames + 16, :] = jnp.concatenate(terms, axis=1)
    for c, part in zip(heads, deltas):
        delta[:, c] = part


def query_grad_body(
    scale, q, own, near, first, second_key, second_value, relay_key, relay_value, message, lse, delta,
    output_here, grad_here,
    output, grad_input, grad_query, held, sems,
):
    writes = [
        pltpu.make_async_copy(output_here, output, sems.at[0]),
        pltpu.make_async_copy(grad_here.at[:, pl.ds(0, q.shape[1])], grad_input, sems.at[1]),
    ]
    for write in writes:
        write.start()
    frames, width = q.shape
    heads = columns(width)
    blocks = (near, own, first)
    biases = (bias_of(near_swapped()), None, None, None, bias_of(far_there()))
    keys = [window_keys(blocks, (second_key, relay_key), frames, c) for c in heads]
    values = [window_values(blocks, (second_value, relay_value), frames, c) for c in heads]
    scores = [dot_nt(q[:, c], k) * scale for c, k in zip(heads, keys)]
    dots = [dot_nt(message[0:frames, c], v) for c, v in zip(heads, values)]
    probs = [jnp.exp(by_block(s, biases, [lse[:, c]] * 5)) for c, s in zip(heads, scores)]
    drops = [by_block(d, (None,) * 5, [delta[:, c]] * 5) for c, d in zip(heads, dots)]
    grads = [(p * d * scale).astype(BF16) for p, d in zip(probs, drops)]
    held[...] = jnp.concatenate([dot_nn(g, k).astype(BF16) for g, k in zip(grads, keys)], axis=1)
    writes.append(pltpu.make_async_copy(held, grad_query, sems.at[2]))
    writes[2].start()
    for write in writes:
        write.wait()


def key_part_body(scale, own, *refs):
    queries, late_query, messages, (key_part, value_part, late) = refs[0:4], refs[4], refs[5:9], refs[9:12]
    frames = own.shape[0] // 2
    heads = columns(own.shape[1])
    above, below = slice(0, frames), slice(frames, 2 * frames)
    biases = (None, bias_of(near_swapped()), None, None)
    asks = [stacked(queries, above, c) for c in heads]
    ups = [stacked(messages, above, c) for c in heads]
    scores = [dot_nt(own[above, c], a) * scale for c, a in zip(heads, asks)]
    dots = [dot_nt(own[below, c], u) for c, u in zip(heads, ups)]
    last = [dot_nt(own[above, c], late_query[:, c]) * scale + bias_of(far_there()) for c in heads]
    logs = [[stat_rows(m, frames, 0, c) for m in messages] for c in heads]
    deltas = [[stat_rows(m, frames, 1, c) for m in messages] for c in heads]
    probs = [jnp.exp(by_block(s, biases, n)) for s, n in zip(scores, logs)]
    drops = [by_block(d, (None,) * 4, n) for d, n in zip(dots, deltas)]
    grads = [(p * d * scale).astype(BF16) for p, d in zip(probs, drops)]
    value_sums = [dot_nn(p.astype(BF16), u) for p, u in zip(probs, ups)]
    key_sums = [dot_nn(g, a) for g, a in zip(grads, asks)]
    for c, k, v, s in zip(heads, key_sums, value_sums, last):
        key_part[:, c] = k
        value_part[:, c] = v
        late[:, c] = s


def key_grad_body(
    scale, own, query, message, late, key_part, value_part, grad_key, grad_value, held_key, held_value, sems
):
    frames = own.shape[0] // 2
    heads = columns(own.shape[1])
    above, below = slice(0, frames), slice(frames, 2 * frames)
    ups = [message[above, c] for c in heads]
    probs = [jnp.exp(late[:, c] - stat_rows(message, frames, 0, c)) for c in heads]
    dots = [dot_nt(own[below, c], u) for c, u in zip(heads, ups)]
    values = [value_part[:, c] + dot_nn(p.astype(BF16), u) for c, p, u in zip(heads, probs, ups)]
    held_value[...] = jnp.concatenate([v.astype(BF16) for v in values], axis=1)
    value_write = pltpu.make_async_copy(held_value, grad_value, sems.at[0])
    value_write.start()
    drops = [d - stat_rows(message, frames, 1, c) for c, d in zip(heads, dots)]
    grads = [(p * d * scale).astype(BF16) for p, d in zip(probs, drops)]
    keys = [key_part[:, c] + dot_nn(g, query[:, c]) for c, g in zip(heads, grads)]
    held_key[...] = jnp.concatenate([k.astype(BF16) for k in keys], axis=1)
    key_write = pltpu.make_async_copy(held_key, grad_key, sems.at[1])
    key_write.start()
    value_write.wait()
    key_write.wait()


def per_device(query_rows, key_rows, value_rows, inputs, out_weight, kernel, cotangent):
    frames, width = query_rows.shape
    wide = 2 * HALO
    scale = 1.0 / math.sqrt(HDIM)
    tile = shaped((frames, width), BF16)
    tile32 = shaped((frames, width), F32)
    rim = shaped((wide + HALO, 2 * width), BF16)
    both = shaped((frames, 2 * width), BF16)
    noted = shaped((frames + 16, width), BF16)

    zero = jnp.zeros((), BF16)
    kv = lax.pad(key_rows, zero, ((0, frames, 0), (0, 0, 0))) + lax.pad(
        value_rows, zero, ((frames, 0, 0), (0, 0, 0))
    )
    joined = sum(
        lax.pad(rows, zero, ((k * frames, (2 - k) * frames, 0), (0, 0, 0)))
        for k, rows in enumerate((query_rows, inputs, cotangent))
    )
    second_key, second_value = ring(key_rows, 1), ring(value_rows, 1)
    near, first = inner_swap(kv), ring(kv, 0)
    (second_key,) = kernel_call(turn_body, (tile,), (second_key, joined), 0.1, "turn", 1)
    relay_key = pair_swap(second_key, "ctx", 1)
    relay_value = pair_swap(second_value, "ctx", 1)
    cot_other = pair_swap(cotangent, "mp", 2)
    taps_other = pair_swap(kernel, "mp", 2)
    query, inputs, cotangent = kernel_call(
        split_body, (tile, tile, tile), (joined, second_value), 0.1, "split", 1
    )
    q_second = ring(query, 1)
    sums, tops, totals = kernel_call(
        functools.partial(forward_body, scale),
        (tile32, tile32, tile32),
        (query, kv, near, first, second_key, second_value),
        1.0, "forward",
    )
    att, lse, send = kernel_call(
        functools.partial(project_body, scale),
        (tile, tile32, both),
        (query, relay_key, relay_value, sums, tops, totals, out_weight),
        1.0, "project",
    )

    send, q_second = kernel_call(pass_body, (both, tile), (send, q_second, cot_other, taps_other), 0.1, "pass", 2)
    core = pair_swap(send, "mp", 1)
    (keep,) = kernel_call(project_own_body, (both,), (att, out_weight), 0.4, "project_own")
    chip, rim_up, rim_down, q_own = kernel_call(
        join_body,
        (both, rim, rim, tile),
        (keep, core, inputs, cotangent, cot_other, query),
        0.2, "join",
    )
    across = pair_swap(chip, "mp", 2)
    rim_near = pair_swap(rim_up, "ctx", 1)
    rim_far = outer_swap(rim_down)
    ends, q_handed = kernel_call(
        stack_body,
        (shaped((2 * wide, 2 * width), BF16), tile),
        (rim_near, rim_far, q_second),
        0.1, "stack",
    )
    ends_across = pair_swap(ends, "mp", 2)
    q_first = ring(q_own, 0)
    q_near = inner_swap(q_own)
    q_relay = pair_swap(q_handed, "ctx", 1)
    rows_out, edge_rows, edge_conv, part_grad = kernel_call(
        conv_inner_body,
        (
            tile,
            shaped((wide, width), F32),
            shaped((2 * wide, 2 * width), F32),
            shaped((frames, 2 * width), F32),
        ),
        (chip, across, cotangent, cot_other, kernel, taps_other, q_first),
        3.1, "conv_inner", 1,
    )
    output_here, grad_here = kernel_call(
        conv_edge_body,
        (tile, both),
        (ends, ends_across, rim_near, rim_far, cotangent, cot_other, kernel, taps_other)
        + (rows_out, edge_rows, edge_conv, part_grad, q_near, q_relay),
        1.4, "conv_edge", 2,
    )

    gi_core = pair_swap(grad_here, "mp", 1)
    (partial,) = kernel_call(upstream_own_body, (tile32,), (grad_here, out_weight), 0.5, "upstream_own")
    message, delta = kernel_call(
        upstream_body, (noted, tile32), (gi_core, out_weight, att, lse, partial), 0.6, "upstream"
    )

    m_near, m_first, m_second, m_relay = window_of(message)
    output, grad_input, grad_query = kernel_call(
        functools.partial(query_grad_body, scale),
        (tile, tile, tile),
        (q_own, kv, near, first, second_key, second_value, relay_key, relay_value)
        + (message, lse, delta, output_here, grad_here),
        1.8, "query_grad", 0,
        [pltpu.VMEM((frames, width), BF16), pltpu.SemaphoreType.DMA((3,))], HBM,
    )
    key_part, value_part, late = kernel_call(
        functools.partial(key_part_body, scale),
        (tile32, tile32, tile32),
        (kv, q_own, q_near, q_first, q_second, q_relay, message, m_near, m_first, m_second),
        1.5, "key_part",
    )
    grad_key, grad_value = kernel_call(
        functools.partial(key_grad_body, scale),
        (tile, tile),
        (kv, q_relay, m_relay, late, key_part, value_part),
        1.0, "key_grad", 0,
        [pltpu.VMEM((frames, width), BF16)] * 2 + [pltpu.SemaphoreType.DMA((2,))], HBM,
    )
    return (output, grad_input, grad_query, grad_key, grad_value)


def solution(mesh):
    rows = P("ctx", "mp")
    return jax.shard_map(
        per_device,
        mesh=mesh,
        in_specs=(rows, rows, rows, rows, P("mp", None), P(None, "mp"), rows),
        out_specs=(rows,) * 5,
        check_vma=False,
    )
```

```python
import functools
import math

import jax
import jax.numpy as jnp
from jax import lax
from jax.experimental import pallas as pl
from jax.experimental.pallas import tpu as pltpu
from jax.sharding import PartitionSpec as P

HDIM = 128
F32 = jnp.float32
BF16 = jnp.bfloat16
CHUNK = 256
HALO = 16
NT = (((1,), (1,)), ((), ()))
NN = (((1,), (0,)), ((), ()))


def dot_nt(a, b):
    return lax.dot_general(a, b, NT, preferred_element_type=F32)


def dot_nn(a, b):
    return lax.dot_general(a, b, NN, preferred_element_type=F32)


def pair_swap(block, axis, bit):
    return lax.ppermute(block, axis, [(i, i ^ bit) for i in range(lax.axis_size(axis))])


def ring_routes(count):
    rise = [(i, i + 2) for i in range(0, count - 2, 2)] + [(count - 2, count - 1)]
    fall = [(i, i - 2) for i in range(count - 1, 2, -2)] + [(1, 0)]
    route = rise + fall
    return route, [(b, a) for a, b in route]


def ring(block, way):
    return lax.ppermute(block, "ctx", ring_routes(lax.axis_size("ctx"))[way])


def total_swap(block, partner_of):
    count, places = lax.axis_size("ctx"), lax.axis_size("mp")
    route = []
    for i in range(count):
        other = partner_of(i, count)
        for m in range(places):
            target = i * places + (m ^ 1) if other is None else other * places + m
            route.append((i * places + m, target))
    return lax.ppermute(block, ("ctx", "mp"), route)


def inner_swap(block):
    return total_swap(block, lambda i, count: i ^ 1 if 2 <= i < count - 2 else None)


def outer_swap(block):
    return total_swap(block, lambda i, count: ((i + 1) ^ 1) - 1 if 0 < i < count - 1 else None)


def window_of(block, before_relay=lambda second: second):
    second = ring(block, 1)
    first = ring(block, 0)
    near = inner_swap(block)
    second = before_relay(second)
    return near, first, second, pair_swap(second, "ctx", 1)


VMEM = pl.BlockSpec(memory_space=pltpu.VMEM)
ANY = pl.BlockSpec(memory_space=pl.ANY)
HBM = pl.BlockSpec(memory_space=pltpu.HBM)


def kernel_call(body, outs, args, micros, name, unread=0, scratch=(), out_space=VMEM):
    return pl.pallas_call(
        body,
        out_shape=outs,
        in_specs=[VMEM] * (len(args) - unread) + [ANY] * unread,
        out_specs=tuple(out_space for _ in outs),
        scratch_shapes=scratch,
        compiler_params=pltpu.CompilerParams(vmem_limit_bytes=24 * 1024 * 1024),
        cost_estimate=pl.CostEstimate(
            flops=0, bytes_accessed=int(micros * 3.69e6), transcendentals=0
        ),
        name=name,
    )(*args)


def shaped(shape, dtype):
    return jax.ShapeDtypeStruct(shape, dtype)


def is_even():
    return lax.axis_index("ctx") % 2 == 0


def near_swapped():
    block = lax.axis_index("ctx")
    return (block >= 2) & (block < lax.axis_size("ctx") - 2)


def far_there():
    block = lax.axis_index("ctx")
    return jnp.where(is_even(), block >= 2, block < lax.axis_size("ctx") - 2)


def bias_of(there):
    return jnp.where(there, jnp.float32(0.0), jnp.float32(-jnp.inf))


def columns(width):
    return [slice(c, c + HDIM) for c in range(0, width, HDIM)]


def stacked(blocks, rows, cols):
    return jnp.concatenate([block[rows, cols] for block in blocks], axis=0)


def with_ones(values):
    return jnp.concatenate([values, jnp.ones_like(values)], axis=1)


def by_block(scores, biases, stats=None):
    parts = []
    for b, bias in enumerate(biases):
        part = scores[:, b * HDIM : (b + 1) * HDIM]
        if stats is not None:
            part = part - stats[b]
        parts.append(part if bias is None else part + bias)
    return jnp.concatenate(parts, axis=1)


def tile_of(wide):
    lane = lax.broadcasted_iota(jnp.int32, (wide[0].shape[0], HDIM), 1)
    tile = jnp.zeros((wide[0].shape[0], HDIM), F32)
    for h, part in enumerate(wide):
        tile = jnp.where(lane == h, part, tile)
    return tile


def term_rows(row, first):
    at = lax.broadcasted_iota(jnp.int32, (16, row.shape[1]), 0)
    block = jnp.zeros((16, row.shape[1]), F32)
    for k in range(3):
        term = row.astype(BF16).astype(F32)
        row = row - term
        block = jnp.where(at == first + k, term, block)
    return block


def stat_terms(wide, first):
    rows = tile_of(wide).T
    return jnp.concatenate([term_rows(rows[h : h + 1], first) for h in range(len(wide))], axis=1)


def stat_rows(message, frames, which, cols):
    terms = message[frames : frames + 16, cols].astype(F32)
    at = 3 * which
    return terms[at : at + 1] + terms[at + 1 : at + 2] + terms[at + 2 : at + 3]


def weight_columns(weight, flip):
    width = weight.shape[0]
    at = (lax.axis_index("mp") ^ flip) * width
    return weight[:, pl.ds(pl.multiple_of(at, 128), width)]


def turn_body(block, seen, copy):
    copy[...] = block[...]


def split_body(joined, seen, *parts):
    frames = parts[0].shape[0]
    for k, part in enumerate(parts):
        part[...] = joined[k * frames : (k + 1) * frames, :]


def forward_body(scale, q, own, near, first, second, *refs):
    sums, tops, totals = refs[-3:]
    frames, width = q.shape
    heads = columns(width)
    blocks = (near, own, first, second)
    biases = (bias_of(near_swapped()), None, None, None)
    keys, values = slice(0, frames), slice(frames, 2 * frames)
    scores = [dot_nt(q[:, c], stacked(blocks, keys, c)) * scale for c in heads]
    scores = [by_block(s, biases) for s in scores]
    top = [jnp.max(s, axis=1, keepdims=True) for s in scores]
    probs = [jnp.exp(s - t).astype(BF16) for s, t in zip(scores, top)]
    summed = [dot_nn(p, with_ones(stacked(blocks, values, c))) for p, c in zip(probs, heads)]
    for c, t, s in zip(heads, top, summed):
        tops[:, c] = jnp.broadcast_to(t, (frames, HDIM))
        sums[:, c] = s[:, 0:HDIM]
        totals[:, c] = s[:, HDIM:]


def project_body(scale, q, relay, sums, tops, totals, weight, att, lse, send, keep):
    frames, width = q.shape
    heads = columns(width)
    bias = bias_of(far_there())
    scores = [dot_nt(q[:, c], relay[0:frames, c]) * scale + bias for c in heads]
    before = [tops[:, c] for c in heads]
    top = [jnp.maximum(b, jnp.max(s, axis=1, keepdims=True)) for b, s in zip(before, scores)]
    shrink = [jnp.exp(b - t) for b, t in zip(before, top)]
    probs = [jnp.exp(s - t).astype(BF16) for s, t in zip(scores, top)]
    late = [dot_nn(p, with_ones(relay[frames : 2 * frames, c])) for p, c in zip(probs, heads)]
    total = [totals[:, c] * k + s[:, HDIM:] for c, k, s in zip(heads, shrink, late)]
    summed = [sums[:, c] * k + s[:, 0:HDIM] for c, k, s in zip(heads, shrink, late)]
    attended = jnp.concatenate([(s * (1.0 / t)).astype(BF16) for s, t in zip(summed, total)], axis=1)
    sent = [dot_nn(attended, weight_columns(weight, flip)).astype(BF16) for flip in (1, 3)]
    kept = [dot_nn(attended, weight_columns(weight, flip)).astype(BF16) for flip in (0, 2)]
    logs = [t + jnp.log(n) for t, n in zip(top, total)]
    att[...] = attended
    send[...] = jnp.concatenate(sent, axis=1)
    keep[...] = jnp.concatenate(kept, axis=1)
    for c, part in zip(heads, logs):
        lse[:, c] = part


def pass_body(send, q_second, seen_a, seen_b, send_copy, second_copy):
    send_copy[...] = send[...]
    second_copy[...] = q_second[...]


def join_body(keep, core, inputs, cot, cot_other, q, chip, rim_near, rim_far, q_copy):
    frames, width = inputs.shape
    wide = 2 * HALO
    even = is_even()
    for cols, rows, cots in (
        (slice(0, width), inputs[...].astype(F32), cot),
        (slice(width, 2 * width), 0.0, cot_other),
    ):
        total = (rows + (keep[:, cols].astype(F32) + core[:, cols].astype(F32))).astype(BF16)
        for at, first, last in (
            (slice(0, wide), total[0:wide], total[frames - wide :]),
            (slice(wide, wide + HALO), cots[0:HALO, :], cots[frames - HALO : frames, :]),
        ):
            first, last = first.astype(F32), last.astype(F32)
            rim_near[at, cols] = jnp.where(even, last, first).astype(BF16)
            rim_far[at, cols] = jnp.where(even, first, last).astype(BF16)
        chip[:, cols] = total
    q_copy[...] = q[...]


def stack_body(rim_near, rim_far, q_second, ends, second_copy):
    wide = 2 * HALO
    ends[0:wide, :] = rim_near[0:wide, :]
    ends[wide : 2 * wide, :] = rim_far[0:wide, :]
    second_copy[...] = q_second[...]


def summed(share, across, rows, cols, width):
    back = slice((cols.start + width) % (2 * width), (cols.stop - 1 + width) % (2 * width) + 1)
    total = share[rows, cols].astype(F32) + across[rows, back].astype(F32)
    return total.astype(BF16).astype(F32)


def tiles_of(rows):
    return [rows[at : at + 8] for at in range(0, rows.shape[0], 8)]


def shifted_sum(tiles, taps_of, count):
    at = lax.broadcasted_iota(jnp.int32, (8, CHUNK), 0)
    sums = [None] * (count // 8)

    def add(k, term):
        sums[k] = term if sums[k] is None else sums[k] + term

    for b in range(8):
        parts = []
        for k in range(count // 8 + (b > 0)):
            part = None
            for a in range(4):
                tap = taps_of(8 * a + b)
                if tap is None or tiles[k + a] is None:
                    continue
                term = tap * tiles[k + a]
                part = term if part is None else part + term
            parts.append(part if part is None or b == 0 else pltpu.roll(part, 8 - b, 0))
        for k in range(count // 8):
            if b == 0:
                if parts[k] is not None:
                    add(k, parts[k])
            elif parts[k] is not None and parts[k + 1] is not None:
                add(k, jnp.where(at < 8 - b, parts[k], parts[k + 1]))
            elif parts[k] is not None:
                add(k, jnp.where(at < 8 - b, parts[k], 0.0))
            elif parts[k + 1] is not None:
                add(k, jnp.where(at < 8 - b, 0.0, parts[k + 1]))
    zero = jnp.zeros((8, CHUNK), F32)
    return jnp.concatenate([zero if part is None else part for part in sums], axis=0)


def silu_parts(conv, cots):
    gate = 1.0 / (1.0 + jnp.exp(-conv))
    grad = cots * (gate + conv * gate * (1.0 - gate))
    return conv * gate, grad.astype(BF16).astype(F32)


def taps_forward(taps, count, cols):
    return lambda s: taps[s - 1 : s, cols] if 1 <= s <= count else None


def taps_backward(taps, count, cols):
    return lambda s: taps[count - s : count - s + 1, cols] if 1 <= s <= count else None


def conv_chunks(width, cot, cot_other, taps, taps_other):
    for c in range(0, 2 * width, CHUNK):
        own, cols = c < width, slice(c, c + CHUNK)
        local = cols if own else slice(cols.start - width, cols.stop - width)
        yield own, cols, local, cot if own else cot_other, taps if own else taps_other


def conv_inner_body(
    chip, across, cot, cot_other, taps, taps_other, seen, rows_out, edge_rows, edge_conv, part_grad
):
    frames, width = cot.shape
    wide, count = 2 * HALO, taps.shape[0]
    inner = slice(HALO, frames - HALO)
    none = [None] * (wide // 8)
    for own, cols, local, cots_of, tap in conv_chunks(width, cot, cot_other, taps, taps_other):
        rows = summed(chip, across, slice(0, frames), cols, width)
        cots = cots_of[:, local].astype(F32)
        conv = shifted_sum(
            none + tiles_of(rows) + none, taps_forward(tap, count, local), frames + wide
        )
        silu, grad = silu_parts(conv[wide:frames], cots[inner])
        back = shifted_sum(
            none + tiles_of(grad) + none, taps_backward(tap, count, local), frames
        )
        edge_conv[0:wide, cols] = conv[0:wide]
        edge_conv[wide : 2 * wide, cols] = conv[frames : frames + wide]
        if own:
            rows_out[inner, cols] = (rows[inner] + silu).astype(BF16)
            edge_rows[0:HALO, cols] = rows[0:HALO]
            edge_rows[HALO:wide, cols] = rows[frames - HALO :]
        part_grad[:, cols] = cots + back


def conv_edge_body(
    ends, ends_across, rim_near, rim_far, cot, cot_other, taps, taps_other,
    rows_in, edge_rows, edge_conv, part_grad, seen, output, grad_input,
):
    frames, width = cot.shape
    wide, count = 2 * HALO, taps.shape[0]
    even, far = is_even(), far_there()
    low, high = slice(0, HALO), slice(frames - HALO, frames)
    inner = slice(HALO, frames - HALO)
    none = [None] * (wide // 8)
    cots_of = slice(wide, wide + HALO)

    def sides(near, beyond):
        beyond = jnp.where(far, beyond, 0.0)
        return jnp.where(even, beyond, near), jnp.where(even, near, beyond)

    for own, cols, local, block, tap in conv_chunks(width, cot, cot_other, taps, taps_other):
        rows = summed(ends, ends_across, slice(0, 2 * wide), cols, width)
        row_low, row_high = sides(rows[0:wide], rows[wide:])
        cot_low, cot_high = sides(rim_near[cots_of, cols].astype(F32), rim_far[cots_of, cols].astype(F32))
        conv = edge_conv[:, cols] + shifted_sum(
            tiles_of(row_low) + none + tiles_of(row_high), taps_forward(tap, count, local), 2 * wide
        )
        first = block[low, local].astype(F32)
        last = block[high, local].astype(F32)
        cots = jnp.concatenate([cot_low, first, last, cot_high], axis=0)
        silu, grad = silu_parts(conv, cots)
        back = shifted_sum(
            tiles_of(grad[0:wide]) + none + tiles_of(grad[wide:]), taps_backward(tap, count, local), 2 * wide
        )
        part = part_grad[:, cols]
        grad_input[:, cols] = jnp.concatenate(
            [part[0:wide] + back[0:wide], part[wide : frames - wide], part[frames - wide :] + back[wide:]],
            axis=0,
        ).astype(BF16)
        if own:
            output[low, cols] = (edge_rows[0:HALO, cols] + silu[HALO:wide]).astype(BF16)
            output[inner, cols] = rows_in[inner, cols]
            output[high, cols] = (edge_rows[HALO:wide, cols] + silu[wide : wide + HALO]).astype(BF16)


def upstream_part(grads, weight, flips):
    width = weight.shape[0]
    return sum(
        dot_nt(grads[:, k * width : (k + 1) * width], weight_columns(weight, flip))
        for k, flip in enumerate(flips)
    )


def upstream_own_body(own, weight, lse, partial, terms):
    partial[...] = upstream_part(own, weight, (0, 2))
    terms[...] = stat_terms([lse[:, c] for c in columns(lse.shape[1])], 0)


def upstream_body(core, weight, att, partial, terms, message, delta):
    frames, width = att.shape
    heads = columns(width)
    up = (partial[...] + upstream_part(core, weight, (1, 3))).astype(BF16)
    products = [up[:, c].astype(F32) * att[:, c].astype(F32) for c in heads]
    deltas = [jnp.broadcast_to(jnp.sum(p, axis=1, keepdims=True), (frames, HDIM)) for p in products]
    message[0:frames, :] = up
    message[frames : frames + 16, :] = (terms[...] + stat_terms(deltas, 3)).astype(BF16)
    for c, part in zip(heads, deltas):
        delta[:, c] = part


def query_grad_body(
    scale, q, own, near, first, second, relay, message, lse, delta, output_here, grad_here,
    output, grad_input, grad_query, held, sems,
):
    writes = [
        pltpu.make_async_copy(output_here, output, sems.at[0]),
        pltpu.make_async_copy(grad_here.at[:, pl.ds(0, q.shape[1])], grad_input, sems.at[1]),
    ]
    for write in writes:
        write.start()
    frames, width = q.shape
    heads = columns(width)
    blocks = (near, own, first, second, relay)
    biases = (bias_of(near_swapped()), None, None, None, bias_of(far_there()))
    above, below = slice(0, frames), slice(frames, 2 * frames)
    keys = [stacked(blocks, above, c) for c in heads]
    scores = [dot_nt(q[:, c], k) * scale for c, k in zip(heads, keys)]
    dots = [dot_nt(message[0:frames, c], stacked(blocks, below, c)) for c in heads]
    probs = [jnp.exp(by_block(s, biases, [lse[:, c]] * 5)) for c, s in zip(heads, scores)]
    drops = [by_block(d, (None,) * 5, [delta[:, c]] * 5) for c, d in zip(heads, dots)]
    grads = [(p * d * scale).astype(BF16) for p, d in zip(probs, drops)]
    held[...] = jnp.concatenate([dot_nn(g, k).astype(BF16) for g, k in zip(grads, keys)], axis=1)
    writes.append(pltpu.make_async_copy(held, grad_query, sems.at[2]))
    writes[2].start()
    for write in writes:
        write.wait()


def key_part_body(scale, own, *refs):
    queries, late_query, messages, (key_part, value_part, late) = refs[0:4], refs[4], refs[5:9], refs[9:12]
    frames = own.shape[0] // 2
    heads = columns(own.shape[1])
    above, below = slice(0, frames), slice(frames, 2 * frames)
    biases = (None, bias_of(near_swapped()), None, None)
    asks = [stacked(queries, above, c) for c in heads]
    ups = [stacked(messages, above, c) for c in heads]
    scores = [dot_nt(own[above, c], a) * scale for c, a in zip(heads, asks)]
    dots = [dot_nt(own[below, c], u) for c, u in zip(heads, ups)]
    last = [dot_nt(own[above, c], late_query[:, c]) * scale + bias_of(far_there()) for c in heads]
    logs = [[stat_rows(m, frames, 0, c) for m in messages] for c in heads]
    deltas = [[stat_rows(m, frames, 1, c) for m in messages] for c in heads]
    probs = [jnp.exp(by_block(s, biases, n)) for s, n in zip(scores, logs)]
    drops = [by_block(d, (None,) * 4, n) for d, n in zip(dots, deltas)]
    grads = [(p * d * scale).astype(BF16) for p, d in zip(probs, drops)]
    value_sums = [dot_nn(p.astype(BF16), u) for p, u in zip(probs, ups)]
    key_sums = [dot_nn(g, a) for g, a in zip(grads, asks)]
    for c, k, v, s in zip(heads, key_sums, value_sums, last):
        key_part[:, c] = k
        value_part[:, c] = v
        late[:, c] = s


def key_grad_body(
    scale, own, query, message, late, key_part, value_part, grad_key, grad_value, held_key, held_value, sems
):
    frames = own.shape[0] // 2
    heads = columns(own.shape[1])
    above, below = slice(0, frames), slice(frames, 2 * frames)
    ups = [message[above, c] for c in heads]
    probs = [jnp.exp(late[:, c] - stat_rows(message, frames, 0, c)) for c in heads]
    dots = [dot_nt(own[below, c], u) for c, u in zip(heads, ups)]
    values = [value_part[:, c] + dot_nn(p.astype(BF16), u) for c, p, u in zip(heads, probs, ups)]
    held_value[...] = jnp.concatenate([v.astype(BF16) for v in values], axis=1)
    value_write = pltpu.make_async_copy(held_value, grad_value, sems.at[0])
    value_write.start()
    drops = [d - stat_rows(message, frames, 1, c) for c, d in zip(heads, dots)]
    grads = [(p * d * scale).astype(BF16) for p, d in zip(probs, drops)]
    keys = [key_part[:, c] + dot_nn(g, query[:, c]) for c, g in zip(heads, grads)]
    held_key[...] = jnp.concatenate([k.astype(BF16) for k in keys], axis=1)
    key_write = pltpu.make_async_copy(held_key, grad_key, sems.at[1])
    key_write.start()
    value_write.wait()
    key_write.wait()


def per_device(query_rows, key_rows, value_rows, inputs, out_weight, kernel, cotangent):
    frames, width = query_rows.shape
    wide = 2 * HALO
    scale = 1.0 / math.sqrt(HDIM)
    tile = shaped((frames, width), BF16)
    tile32 = shaped((frames, width), F32)
    rim = shaped((wide + HALO, 2 * width), BF16)
    both = shaped((frames, 2 * width), BF16)
    noted = shaped((frames + 16, width), BF16)

    zero = jnp.zeros((), BF16)
    kv = lax.pad(key_rows, zero, ((0, frames, 0), (0, 0, 0))) + lax.pad(
        value_rows, zero, ((frames, 0, 0), (0, 0, 0))
    )
    joined = sum(
        lax.pad(rows, zero, ((k * frames, (2 - k) * frames, 0), (0, 0, 0)))
        for k, rows in enumerate((query_rows, inputs, cotangent))
    )
    near, first, second, relay = window_of(
        kv,
        lambda second: kernel_call(
            turn_body, (shaped(kv.shape, BF16),), (second, joined), 0.1, "turn", 1
        )[0],
    )
    cot_other = pair_swap(cotangent, "mp", 2)
    taps_other = pair_swap(kernel, "mp", 2)
    query, inputs, cotangent = kernel_call(
        split_body, (tile, tile, tile), (joined, second), 0.1, "split", 1
    )
    q_second = ring(query, 1)
    sums, tops, totals = kernel_call(
        functools.partial(forward_body, scale),
        (tile32, tile32, tile32),
        (query, kv, near, first, second),
        1.0, "forward",
    )
    att, lse, send, keep = kernel_call(
        functools.partial(project_body, scale),
        (tile, tile32, both, both),
        (query, relay, sums, tops, totals, out_weight),
        1.0, "project",
    )

    send, q_second = kernel_call(pass_body, (both, tile), (send, q_second, cot_other, taps_other), 0.1, "pass", 2)
    core = pair_swap(send, "mp", 1)
    chip, rim_up, rim_down, q_own = kernel_call(
        join_body,
        (both, rim, rim, tile),
        (keep, core, inputs, cotangent, cot_other, query),
        0.2, "join",
    )
    across = pair_swap(chip, "mp", 2)
    rim_far = outer_swap(rim_down)
    rim_near = pair_swap(rim_up, "ctx", 1)
    ends, q_handed = kernel_call(
        stack_body,
        (shaped((2 * wide, 2 * width), BF16), tile),
        (rim_near, rim_far, q_second),
        0.1, "stack",
    )
    ends_across = pair_swap(ends, "mp", 2)
    q_first = ring(q_own, 0)
    q_near = inner_swap(q_own)
    q_relay = pair_swap(q_handed, "ctx", 1)
    rows_out, edge_rows, edge_conv, part_grad = kernel_call(
        conv_inner_body,
        (
            tile,
            shaped((wide, width), F32),
            shaped((2 * wide, 2 * width), F32),
            shaped((frames, 2 * width), F32),
        ),
        (chip, across, cotangent, cot_other, kernel, taps_other, q_first),
        3.1, "conv_inner", 1,
    )
    output_here, grad_here = kernel_call(
        conv_edge_body,
        (tile, both),
        (ends, ends_across, rim_near, rim_far, cotangent, cot_other, kernel, taps_other)
        + (rows_out, edge_rows, edge_conv, part_grad, q_near),
        1.4, "conv_edge", 1,
    )

    (grad_here,) = kernel_call(turn_body, (both,), (grad_here, q_relay), 0.1, "hand", 1)
    gi_core = pair_swap(grad_here, "mp", 1)
    partial, terms = kernel_call(
        upstream_own_body, (tile32, shaped((16, width), F32)), (grad_here, out_weight, lse), 0.5,
        "upstream_own",
    )
    message, delta = kernel_call(
        upstream_body, (noted, tile32), (gi_core, out_weight, att, partial, terms), 0.6, "upstream"
    )

    m_near, m_first, m_second, m_relay = window_of(message)
    output, grad_input, grad_query = kernel_call(
        functools.partial(query_grad_body, scale),
        (tile, tile, tile),
        (q_own, kv, near, first, second, relay, message, lse, delta, output_here, grad_here),
        1.8, "query_grad", 0,
        [pltpu.VMEM((frames, width), BF16), pltpu.SemaphoreType.DMA((3,))], HBM,
    )
    key_part, value_part, late = kernel_call(
        functools.partial(key_part_body, scale),
        (tile32, tile32, tile32),
        (kv, q_own, q_near, q_first, q_second, q_relay, message, m_near, m_first, m_second),
        1.5, "key_part",
    )
    grad_key, grad_value = kernel_call(
        functools.partial(key_grad_body, scale),
        (tile, tile),
        (kv, q_relay, m_relay, late, key_part, value_part),
        1.0, "key_grad", 0,
        [pltpu.VMEM((frames, width), BF16)] * 2 + [pltpu.SemaphoreType.DMA((2,))], HBM,
    )
    return (output, grad_input, grad_query, grad_key, grad_value)


def solution(mesh):
    rows = P("ctx", "mp")
    return jax.shard_map(
        per_device,
        mesh=mesh,
        in_specs=(rows, rows, rows, rows, P("mp", None), P(None, "mp"), rows),
        out_specs=(rows,) * 5,
        check_vma=False,
    )
```

```python
import functools
import math

import jax
import jax.numpy as jnp
from jax import lax
from jax.experimental import pallas as pl
from jax.experimental.pallas import tpu as pltpu
from jax.sharding import PartitionSpec as P

HDIM = 128
F32 = jnp.float32
BF16 = jnp.bfloat16
CHUNK = 256
HALO = 16
NT = (((1,), (1,)), ((), ()))
NN = (((1,), (0,)), ((), ()))


def dot_nt(a, b):
    return lax.dot_general(a, b, NT, preferred_element_type=F32)


def dot_nn(a, b):
    return lax.dot_general(a, b, NN, preferred_element_type=F32)


def pair_swap(block, axis, bit):
    return lax.ppermute(block, axis, [(i, i ^ bit) for i in range(lax.axis_size(axis))])


def ring_routes(count):
    rise = [(i, i + 2) for i in range(0, count - 2, 2)] + [(count - 2, count - 1)]
    fall = [(i, i - 2) for i in range(count - 1, 2, -2)] + [(1, 0)]
    route = rise + fall
    return route, [(b, a) for a, b in route]


def ring(block, way):
    return lax.ppermute(block, "ctx", ring_routes(lax.axis_size("ctx"))[way])


def total_swap(block, partner_of):
    count, places = lax.axis_size("ctx"), lax.axis_size("mp")
    route = []
    for i in range(count):
        other = partner_of(i, count)
        for m in range(places):
            target = i * places + (m ^ 1) if other is None else other * places + m
            route.append((i * places + m, target))
    return lax.ppermute(block, ("ctx", "mp"), route)


def inner_swap(block):
    return total_swap(block, lambda i, count: i ^ 1 if 2 <= i < count - 2 else None)


def outer_swap(block):
    return total_swap(block, lambda i, count: ((i + 1) ^ 1) - 1 if 0 < i < count - 1 else None)


def window_of(block, before_relay=lambda second: second):
    second = ring(block, 1)
    first = ring(block, 0)
    near = inner_swap(block)
    second = before_relay(second)
    return near, first, second, pair_swap(second, "ctx", 1)


VMEM = pl.BlockSpec(memory_space=pltpu.VMEM)
ANY = pl.BlockSpec(memory_space=pl.ANY)
HBM = pl.BlockSpec(memory_space=pltpu.HBM)


def kernel_call(body, outs, args, micros, name, unread=0, scratch=(), out_space=VMEM):
    return pl.pallas_call(
        body,
        out_shape=outs,
        in_specs=[VMEM] * (len(args) - unread) + [ANY] * unread,
        out_specs=tuple(out_space for _ in outs),
        scratch_shapes=scratch,
        compiler_params=pltpu.CompilerParams(vmem_limit_bytes=24 * 1024 * 1024),
        cost_estimate=pl.CostEstimate(
            flops=0, bytes_accessed=int(micros * 3.69e6), transcendentals=0
        ),
        name=name,
    )(*args)


def shaped(shape, dtype):
    return jax.ShapeDtypeStruct(shape, dtype)


def is_even():
    return lax.axis_index("ctx") % 2 == 0


def near_swapped():
    block = lax.axis_index("ctx")
    return (block >= 2) & (block < lax.axis_size("ctx") - 2)


def far_there():
    block = lax.axis_index("ctx")
    return jnp.where(is_even(), block >= 2, block < lax.axis_size("ctx") - 2)


def bias_of(there):
    return jnp.where(there, jnp.float32(0.0), jnp.float32(-jnp.inf))


def columns(width):
    return [slice(c, c + HDIM) for c in range(0, width, HDIM)]


def stacked(blocks, rows, cols):
    return jnp.concatenate([block[rows, cols] for block in blocks], axis=0)


def with_ones(values):
    return jnp.concatenate([values, jnp.ones_like(values)], axis=1)


def by_block(scores, biases, stats=None):
    parts = []
    for b, bias in enumerate(biases):
        part = scores[:, b * HDIM : (b + 1) * HDIM]
        if stats is not None:
            part = part - stats[b]
        parts.append(part if bias is None else part + bias)
    return jnp.concatenate(parts, axis=1)


def tile_of(wide):
    lane = lax.broadcasted_iota(jnp.int32, (wide[0].shape[0], HDIM), 1)
    tile = jnp.zeros((wide[0].shape[0], HDIM), F32)
    for h, part in enumerate(wide):
        tile = jnp.where(lane == h, part, tile)
    return tile


def term_rows(row, first):
    at = lax.broadcasted_iota(jnp.int32, (16, row.shape[1]), 0)
    block = jnp.zeros((16, row.shape[1]), F32)
    for k in range(3):
        term = row.astype(BF16).astype(F32)
        row = row - term
        block = jnp.where(at == first + k, term, block)
    return block


def stat_terms(wide, first):
    rows = tile_of(wide).T
    return jnp.concatenate([term_rows(rows[h : h + 1], first) for h in range(len(wide))], axis=1)


def stat_rows(message, frames, which, cols):
    terms = message[frames : frames + 16, cols].astype(F32)
    at = 3 * which
    return terms[at : at + 1] + terms[at + 1 : at + 2] + terms[at + 2 : at + 3]


def weight_columns(weight, flip):
    width = weight.shape[0]
    at = (lax.axis_index("mp") ^ flip) * width
    return weight[:, pl.ds(pl.multiple_of(at, 128), width)]


def turn_body(block, seen, copy):
    copy[...] = block[...]


def split_body(joined, seen, *parts):
    frames = parts[0].shape[0]
    for k, part in enumerate(parts):
        part[...] = joined[k * frames : (k + 1) * frames, :]


def forward_body(scale, q, own, near, first, second, *refs):
    sums, tops, totals = refs[-3:]
    frames, width = q.shape
    heads = columns(width)
    blocks = (near, own, first, second)
    biases = (bias_of(near_swapped()), None, None, None)
    keys, values = slice(0, frames), slice(frames, 2 * frames)
    scores = [dot_nt(q[:, c], stacked(blocks, keys, c)) * scale for c in heads]
    scores = [by_block(s, biases) for s in scores]
    top = [jnp.max(s, axis=1, keepdims=True) for s in scores]
    probs = [jnp.exp(s - t).astype(BF16) for s, t in zip(scores, top)]
    summed = [dot_nn(p, with_ones(stacked(blocks, values, c))) for p, c in zip(probs, heads)]
    for c, t, s in zip(heads, top, summed):
        tops[:, c] = jnp.broadcast_to(t, (frames, HDIM))
        sums[:, c] = s[:, 0:HDIM]
        totals[:, c] = s[:, HDIM:]


def project_body(scale, q, relay, sums, tops, totals, weight, att, lse, send, keep):
    frames, width = q.shape
    heads = columns(width)
    bias = bias_of(far_there())
    scores = [dot_nt(q[:, c], relay[0:frames, c]) * scale + bias for c in heads]
    before = [tops[:, c] for c in heads]
    top = [jnp.maximum(b, jnp.max(s, axis=1, keepdims=True)) for b, s in zip(before, scores)]
    shrink = [jnp.exp(b - t) for b, t in zip(before, top)]
    probs = [jnp.exp(s - t).astype(BF16) for s, t in zip(scores, top)]
    late = [dot_nn(p, with_ones(relay[frames : 2 * frames, c])) for p, c in zip(probs, heads)]
    total = [totals[:, c] * k + s[:, HDIM:] for c, k, s in zip(heads, shrink, late)]
    summed = [sums[:, c] * k + s[:, 0:HDIM] for c, k, s in zip(heads, shrink, late)]
    attended = jnp.concatenate([(s * (1.0 / t)).astype(BF16) for s, t in zip(summed, total)], axis=1)
    sent = [dot_nn(attended, weight_columns(weight, flip)).astype(BF16) for flip in (1, 3)]
    kept = [dot_nn(attended, weight_columns(weight, flip)).astype(BF16) for flip in (0, 2)]
    logs = [t + jnp.log(n) for t, n in zip(top, total)]
    att[...] = attended
    send[...] = jnp.concatenate(sent, axis=1)
    keep[...] = jnp.concatenate(kept, axis=1)
    for c, part in zip(heads, logs):
        lse[:, c] = part


def pass_body(send, q_second, seen_a, seen_b, send_copy, second_copy):
    send_copy[...] = send[...]
    second_copy[...] = q_second[...]


def join_body(keep, core, inputs, cot, cot_other, q, chip, rim_near, rim_far, q_copy):
    frames, width = inputs.shape
    wide = 2 * HALO
    even = is_even()
    for cols, rows, cots in (
        (slice(0, width), inputs[...].astype(F32), cot),
        (slice(width, 2 * width), 0.0, cot_other),
    ):
        total = (rows + (keep[:, cols].astype(F32) + core[:, cols].astype(F32))).astype(BF16)
        for at, first, last in (
            (slice(0, wide), total[0:wide], total[frames - wide :]),
            (slice(wide, wide + HALO), cots[0:HALO, :], cots[frames - HALO : frames, :]),
        ):
            first, last = first.astype(F32), last.astype(F32)
            rim_near[at, cols] = jnp.where(even, last, first).astype(BF16)
            rim_far[at, cols] = jnp.where(even, first, last).astype(BF16)
        chip[:, cols] = total
    q_copy[...] = q[...]


def stack_body(rim_near, rim_far, q_second, ends, second_copy):
    wide = 2 * HALO
    ends[0:wide, :] = rim_near[0:wide, :]
    ends[wide : 2 * wide, :] = rim_far[0:wide, :]
    second_copy[...] = q_second[...]


def summed(share, across, rows, cols, width):
    back = slice((cols.start + width) % (2 * width), (cols.stop - 1 + width) % (2 * width) + 1)
    total = share[rows, cols].astype(F32) + across[rows, back].astype(F32)
    return total.astype(BF16).astype(F32)


def tiles_of(rows):
    return [rows[at : at + 8] for at in range(0, rows.shape[0], 8)]


def shifted_sum(tiles, taps_of, count):
    at = lax.broadcasted_iota(jnp.int32, (8, CHUNK), 0)
    sums = [None] * (count // 8)

    def add(k, term):
        sums[k] = term if sums[k] is None else sums[k] + term

    for b in range(8):
        parts = []
        for k in range(count // 8 + (b > 0)):
            part = None
            for a in range(4):
                tap = taps_of(8 * a + b)
                if tap is None or tiles[k + a] is None:
                    continue
                term = tap * tiles[k + a]
                part = term if part is None else part + term
            parts.append(part if part is None or b == 0 else pltpu.roll(part, 8 - b, 0))
        for k in range(count // 8):
            if b == 0:
                if parts[k] is not None:
                    add(k, parts[k])
            elif parts[k] is not None and parts[k + 1] is not None:
                add(k, jnp.where(at < 8 - b, parts[k], parts[k + 1]))
            elif parts[k] is not None:
                add(k, jnp.where(at < 8 - b, parts[k], 0.0))
            elif parts[k + 1] is not None:
                add(k, jnp.where(at < 8 - b, 0.0, parts[k + 1]))
    zero = jnp.zeros((8, CHUNK), F32)
    return jnp.concatenate([zero if part is None else part for part in sums], axis=0)


def silu_parts(conv, cots):
    gate = 1.0 / (1.0 + jnp.exp(-conv))
    grad = cots * (gate + conv * gate * (1.0 - gate))
    return conv * gate, grad.astype(BF16).astype(F32)


def taps_forward(taps, count, cols):
    return lambda s: taps[s - 1 : s, cols] if 1 <= s <= count else None


def taps_backward(taps, count, cols):
    return lambda s: taps[count - s : count - s + 1, cols] if 1 <= s <= count else None


def conv_chunks(width, cot, cot_other, taps, taps_other):
    for c in range(0, 2 * width, CHUNK):
        own, cols = c < width, slice(c, c + CHUNK)
        local = cols if own else slice(cols.start - width, cols.stop - width)
        yield own, cols, local, cot if own else cot_other, taps if own else taps_other


def conv_inner_body(
    chip, across, cot, cot_other, taps, taps_other, seen, rows_out, edge_rows, edge_conv, part_grad
):
    frames, width = cot.shape
    wide, count = 2 * HALO, taps.shape[0]
    inner = slice(HALO, frames - HALO)
    none = [None] * (wide // 8)
    for own, cols, local, cots_of, tap in conv_chunks(width, cot, cot_other, taps, taps_other):
        rows = summed(chip, across, slice(0, frames), cols, width)
        cots = cots_of[:, local].astype(F32)
        conv = shifted_sum(
            none + tiles_of(rows) + none, taps_forward(tap, count, local), frames + wide
        )
        silu, grad = silu_parts(conv[wide:frames], cots[inner])
        back = shifted_sum(
            none + tiles_of(grad) + none, taps_backward(tap, count, local), frames
        )
        edge_conv[0:wide, cols] = conv[0:wide]
        edge_conv[wide : 2 * wide, cols] = conv[frames : frames + wide]
        if own:
            rows_out[inner, cols] = (rows[inner] + silu).astype(BF16)
            edge_rows[0:HALO, cols] = rows[0:HALO]
            edge_rows[HALO:wide, cols] = rows[frames - HALO :]
        part_grad[:, cols] = cots + back


def conv_edge_body(
    ends, ends_across, rim_near, rim_far, cot, cot_other, taps, taps_other,
    rows_in, edge_rows, edge_conv, part_grad, seen, output, grad_input,
):
    frames, width = cot.shape
    wide, count = 2 * HALO, taps.shape[0]
    even, far = is_even(), far_there()
    low, high = slice(0, HALO), slice(frames - HALO, frames)
    inner = slice(HALO, frames - HALO)
    none = [None] * (wide // 8)
    cots_of = slice(wide, wide + HALO)

    def sides(near, beyond):
        beyond = jnp.where(far, beyond, 0.0)
        return jnp.where(even, beyond, near), jnp.where(even, near, beyond)

    for own, cols, local, block, tap in conv_chunks(width, cot, cot_other, taps, taps_other):
        rows = summed(ends, ends_across, slice(0, 2 * wide), cols, width)
        row_low, row_high = sides(rows[0:wide], rows[wide:])
        cot_low, cot_high = sides(rim_near[cots_of, cols].astype(F32), rim_far[cots_of, cols].astype(F32))
        conv = edge_conv[:, cols] + shifted_sum(
            tiles_of(row_low) + none + tiles_of(row_high), taps_forward(tap, count, local), 2 * wide
        )
        first = block[low, local].astype(F32)
        last = block[high, local].astype(F32)
        cots = jnp.concatenate([cot_low, first, last, cot_high], axis=0)
        silu, grad = silu_parts(conv, cots)
        back = shifted_sum(
            tiles_of(grad[0:wide]) + none + tiles_of(grad[wide:]), taps_backward(tap, count, local), 2 * wide
        )
        part = part_grad[:, cols]
        grad_input[:, cols] = jnp.concatenate(
            [part[0:wide] + back[0:wide], part[wide : frames - wide], part[frames - wide :] + back[wide:]],
            axis=0,
        ).astype(BF16)
        if own:
            output[low, cols] = (edge_rows[0:HALO, cols] + silu[HALO:wide]).astype(BF16)
            output[inner, cols] = rows_in[inner, cols]
            output[high, cols] = (edge_rows[HALO:wide, cols] + silu[wide : wide + HALO]).astype(BF16)


def upstream_part(grads, weight, flips):
    width = weight.shape[0]
    return sum(
        dot_nt(grads[:, k * width : (k + 1) * width], weight_columns(weight, flip))
        for k, flip in enumerate(flips)
    )


def upstream_own_body(own, weight, lse, partial, terms):
    partial[...] = upstream_part(own, weight, (0, 2))
    terms[...] = stat_terms([lse[:, c] for c in columns(lse.shape[1])], 0)


def upstream_body(core, weight, att, partial, terms, message, delta):
    frames, width = att.shape
    heads = columns(width)
    up = (partial[...] + upstream_part(core, weight, (1, 3))).astype(BF16)
    products = [up[:, c].astype(F32) * att[:, c].astype(F32) for c in heads]
    deltas = [jnp.broadcast_to(jnp.sum(p, axis=1, keepdims=True), (frames, HDIM)) for p in products]
    message[0:frames, :] = up
    message[frames : frames + 16, :] = (terms[...] + stat_terms(deltas, 3)).astype(BF16)
    for c, part in zip(heads, deltas):
        delta[:, c] = part


def query_grad_body(
    scale, q, own, near, first, second, relay, message, lse, delta, output_here, grad_here,
    output, grad_input, grad_query, held, sems,
):
    writes = [
        pltpu.make_async_copy(output_here, output, sems.at[0]),
        pltpu.make_async_copy(grad_here.at[:, pl.ds(0, q.shape[1])], grad_input, sems.at[1]),
    ]
    for write in writes:
        write.start()
    frames, width = q.shape
    heads = columns(width)
    blocks = (near, own, first, second, relay)
    biases = (bias_of(near_swapped()), None, None, None, bias_of(far_there()))
    above, below = slice(0, frames), slice(frames, 2 * frames)
    keys = [stacked(blocks, above, c) for c in heads]
    scores = [dot_nt(q[:, c], k) * scale for c, k in zip(heads, keys)]
    dots = [dot_nt(message[0:frames, c], stacked(blocks, below, c)) for c in heads]
    probs = [jnp.exp(by_block(s, biases, [lse[:, c]] * 5)) for c, s in zip(heads, scores)]
    drops = [by_block(d, (None,) * 5, [delta[:, c]] * 5) for c, d in zip(heads, dots)]
    grads = [(p * d * scale).astype(BF16) for p, d in zip(probs, drops)]
    held[...] = jnp.concatenate([dot_nn(g, k).astype(BF16) for g, k in zip(grads, keys)], axis=1)
    writes.append(pltpu.make_async_copy(held, grad_query, sems.at[2]))
    writes[2].start()
    for write in writes:
        write.wait()


def key_part_body(scale, own, *refs):
    queries, late_query, messages, (key_part, value_part, late) = refs[0:4], refs[4], refs[5:9], refs[9:12]
    frames = own.shape[0] // 2
    heads = columns(own.shape[1])
    above, below = slice(0, frames), slice(frames, 2 * frames)
    biases = (None, bias_of(near_swapped()), None, None)
    asks = [stacked(queries, above, c) for c in heads]
    ups = [stacked(messages, above, c) for c in heads]
    scores = [dot_nt(own[above, c], a) * scale for c, a in zip(heads, asks)]
    dots = [dot_nt(own[below, c], u) for c, u in zip(heads, ups)]
    last = [dot_nt(own[above, c], late_query[:, c]) * scale + bias_of(far_there()) for c in heads]
    logs = [[stat_rows(m, frames, 0, c) for m in messages] for c in heads]
    deltas = [[stat_rows(m, frames, 1, c) for m in messages] for c in heads]
    probs = [jnp.exp(by_block(s, biases, n)) for s, n in zip(scores, logs)]
    drops = [by_block(d, (None,) * 4, n) for d, n in zip(dots, deltas)]
    grads = [(p * d * scale).astype(BF16) for p, d in zip(probs, drops)]
    value_sums = [dot_nn(p.astype(BF16), u) for p, u in zip(probs, ups)]
    key_sums = [dot_nn(g, a) for g, a in zip(grads, asks)]
    for c, k, v, s in zip(heads, key_sums, value_sums, last):
        key_part[:, c] = k
        value_part[:, c] = v
        late[:, c] = s


def key_grad_body(
    scale, own, query, message, late, key_part, value_part, grad_key, grad_value, held_key, held_value, sems
):
    frames = own.shape[0] // 2
    heads = columns(own.shape[1])
    above, below = slice(0, frames), slice(frames, 2 * frames)
    ups = [message[above, c] for c in heads]
    probs = [jnp.exp(late[:, c] - stat_rows(message, frames, 0, c)) for c in heads]
    dots = [dot_nt(own[below, c], u) for c, u in zip(heads, ups)]
    values = [value_part[:, c] + dot_nn(p.astype(BF16), u) for c, p, u in zip(heads, probs, ups)]
    held_value[...] = jnp.concatenate([v.astype(BF16) for v in values], axis=1)
    value_write = pltpu.make_async_copy(held_value, grad_value, sems.at[0])
    value_write.start()
    drops = [d - stat_rows(message, frames, 1, c) for c, d in zip(heads, dots)]
    grads = [(p * d * scale).astype(BF16) for p, d in zip(probs, drops)]
    keys = [key_part[:, c] + dot_nn(g, query[:, c]) for c, g in zip(heads, grads)]
    held_key[...] = jnp.concatenate([k.astype(BF16) for k in keys], axis=1)
    key_write = pltpu.make_async_copy(held_key, grad_key, sems.at[1])
    key_write.start()
    value_write.wait()
    key_write.wait()


def per_device(query_rows, key_rows, value_rows, inputs, out_weight, kernel, cotangent):
    frames, width = query_rows.shape
    wide = 2 * HALO
    scale = 1.0 / math.sqrt(HDIM)
    tile = shaped((frames, width), BF16)
    tile32 = shaped((frames, width), F32)
    rim = shaped((wide + HALO, 2 * width), BF16)
    both = shaped((frames, 2 * width), BF16)
    noted = shaped((frames + 16, width), BF16)

    zero = jnp.zeros((), BF16)
    kv = lax.pad(key_rows, zero, ((0, frames, 0), (0, 0, 0))) + lax.pad(
        value_rows, zero, ((frames, 0, 0), (0, 0, 0))
    )
    joined = sum(
        lax.pad(rows, zero, ((k * frames, (2 - k) * frames, 0), (0, 0, 0)))
        for k, rows in enumerate((query_rows, inputs, cotangent))
    )
    near, first, second, relay = window_of(
        kv,
        lambda second: kernel_call(
            turn_body, (shaped(kv.shape, BF16),), (second, joined), 0.1, "turn", 1
        )[0],
    )
    cot_other = pair_swap(cotangent, "mp", 2)
    taps_other = pair_swap(kernel, "mp", 2)
    query, inputs, cotangent = kernel_call(
        split_body, (tile, tile, tile), (joined, second), 0.1, "split", 1
    )
    q_second = ring(query, 1)
    sums, tops, totals = kernel_call(
        functools.partial(forward_body, scale),
        (tile32, tile32, tile32),
        (query, kv, near, first, second),
        1.0, "forward",
    )
    att, lse, send, keep = kernel_call(
        functools.partial(project_body, scale),
        (tile, tile32, both, both),
        (query, relay, sums, tops, totals, out_weight),
        1.0, "project",
    )

    send, q_second = kernel_call(pass_body, (both, tile), (send, q_second, cot_other, taps_other), 0.1, "pass", 2)
    core = pair_swap(send, "mp", 1)
    chip, rim_up, rim_down, q_own = kernel_call(
        join_body,
        (both, rim, rim, tile),
        (keep, core, inputs, cotangent, cot_other, query),
        0.2, "join",
    )
    across = pair_swap(chip, "mp", 2)
    rim_far = outer_swap(rim_down)
    rim_near = pair_swap(rim_up, "ctx", 1)
    ends, q_handed = kernel_call(
        stack_body,
        (shaped((2 * wide, 2 * width), BF16), tile),
        (rim_near, rim_far, q_second),
        0.1, "stack",
    )
    ends_across = pair_swap(ends, "mp", 2)
    q_first = ring(q_own, 0)
    q_near = inner_swap(q_own)
    q_relay = pair_swap(q_handed, "ctx", 1)
    rows_out, edge_rows, edge_conv, part_grad = kernel_call(
        conv_inner_body,
        (
            tile,
            shaped((wide, width), F32),
            shaped((2 * wide, 2 * width), F32),
            shaped((frames, 2 * width), F32),
        ),
        (chip, across, cotangent, cot_other, kernel, taps_other, q_first),
        3.1, "conv_inner", 1,
    )
    output_here, grad_here = kernel_call(
        conv_edge_body,
        (tile, both),
        (ends, ends_across, rim_near, rim_far, cotangent, cot_other, kernel, taps_other)
        + (rows_out, edge_rows, edge_conv, part_grad, q_near),
        1.4, "conv_edge", 1,
    )

    (grad_here,) = kernel_call(turn_body, (both,), (grad_here, q_relay), 0.1, "hand", 1)
    gi_core = pair_swap(grad_here, "mp", 1)
    partial, terms = kernel_call(
        upstream_own_body, (tile32, shaped((16, width), F32)), (grad_here, out_weight, lse), 0.5,
        "upstream_own",
    )
    message, delta = kernel_call(
        upstream_body, (noted, tile32), (gi_core, out_weight, att, partial, terms), 0.6, "upstream"
    )

    m_near, m_first, m_second = inner_swap(message), ring(message, 0), ring(message, 1)
    m_relay = outer_swap(message)
    output, grad_input, grad_query = kernel_call(
        functools.partial(query_grad_body, scale),
        (tile, tile, tile),
        (q_own, kv, near, first, second, relay, message, lse, delta, output_here, grad_here),
        1.8, "query_grad", 0,
        [pltpu.VMEM((frames, width), BF16), pltpu.SemaphoreType.DMA((3,))], HBM,
    )
    key_part, value_part, late = kernel_call(
        functools.partial(key_part_body, scale),
        (tile32, tile32, tile32),
        (kv, q_own, q_near, q_first, q_second, q_relay, message, m_near, m_first, m_second),
        1.5, "key_part",
    )
    grad_key, grad_value = kernel_call(
        functools.partial(key_grad_body, scale),
        (tile, tile),
        (kv, q_relay, m_relay, late, key_part, value_part),
        1.0, "key_grad", 0,
        [pltpu.VMEM((frames, width), BF16)] * 2 + [pltpu.SemaphoreType.DMA((2,))], HBM,
    )
    return (output, grad_input, grad_query, grad_key, grad_value)


def solution(mesh):
    rows = P("ctx", "mp")
    return jax.shard_map(
        per_device,
        mesh=mesh,
        in_specs=(rows, rows, rows, rows, P("mp", None), P(None, "mp"), rows),
        out_specs=(rows,) * 5,
        check_vma=False,
    )
```

```python
import functools
import math

import jax
import jax.numpy as jnp
from jax import lax
from jax.experimental import pallas as pl
from jax.experimental.pallas import tpu as pltpu
from jax.sharding import PartitionSpec as P

HDIM = 128
F32 = jnp.float32
BF16 = jnp.bfloat16
CHUNK = 256
HALO = 16
NT = (((1,), (1,)), ((), ()))
NN = (((1,), (0,)), ((), ()))


def dot_nt(a, b):
    return lax.dot_general(a, b, NT, preferred_element_type=F32)


def dot_nn(a, b):
    return lax.dot_general(a, b, NN, preferred_element_type=F32)


def pair_swap(block, axis, bit):
    return lax.ppermute(block, axis, [(i, i ^ bit) for i in range(lax.axis_size(axis))])


def ring_routes(count):
    rise = [(i, i + 2) for i in range(0, count - 2, 2)] + [(count - 2, count - 1)]
    fall = [(i, i - 2) for i in range(count - 1, 2, -2)] + [(1, 0)]
    route = rise + fall
    return route, [(b, a) for a, b in route]


def ring(block, way):
    return lax.ppermute(block, "ctx", ring_routes(lax.axis_size("ctx"))[way])


def total_swap(block, partner_of):
    count, places = lax.axis_size("ctx"), lax.axis_size("mp")
    route = []
    for i in range(count):
        other = partner_of(i, count)
        for m in range(places):
            target = i * places + (m ^ 1) if other is None else other * places + m
            route.append((i * places + m, target))
    return lax.ppermute(block, ("ctx", "mp"), route)


def inner_swap(block):
    return total_swap(block, lambda i, count: i ^ 1 if 2 <= i < count - 2 else None)


def outer_swap(block):
    return total_swap(block, lambda i, count: ((i + 1) ^ 1) - 1 if 0 < i < count - 1 else None)


VMEM = pl.BlockSpec(memory_space=pltpu.VMEM)
ANY = pl.BlockSpec(memory_space=pl.ANY)
HBM = pl.BlockSpec(memory_space=pltpu.HBM)


def kernel_call(body, outs, args, micros, name, unread=0, scratch=(), out_space=VMEM):
    return pl.pallas_call(
        body,
        out_shape=outs,
        in_specs=[VMEM] * (len(args) - unread) + [ANY] * unread,
        out_specs=tuple(out_space for _ in outs),
        scratch_shapes=scratch,
        compiler_params=pltpu.CompilerParams(vmem_limit_bytes=24 * 1024 * 1024),
        cost_estimate=pl.CostEstimate(
            flops=0, bytes_accessed=int(micros * 3.69e6), transcendentals=0
        ),
        name=name,
    )(*args)


def shaped(shape, dtype):
    return jax.ShapeDtypeStruct(shape, dtype)


def is_even():
    return lax.axis_index("ctx") % 2 == 0


def near_swapped():
    block = lax.axis_index("ctx")
    return (block >= 2) & (block < lax.axis_size("ctx") - 2)


def far_there():
    block = lax.axis_index("ctx")
    return jnp.where(is_even(), block >= 2, block < lax.axis_size("ctx") - 2)


def bias_of(there):
    return jnp.where(there, jnp.float32(0.0), jnp.float32(-jnp.inf))


def columns(width):
    return [slice(c, c + HDIM) for c in range(0, width, HDIM)]


def stacked(blocks, rows, cols):
    return jnp.concatenate([block[rows, cols] for block in blocks], axis=0)


def with_ones(values):
    return jnp.concatenate([values, jnp.ones_like(values)], axis=1)


def by_block(scores, biases, stats=None):
    parts = []
    for b, bias in enumerate(biases):
        part = scores[:, b * HDIM : (b + 1) * HDIM]
        if stats is not None:
            part = part - stats[b]
        parts.append(part if bias is None else part + bias)
    return jnp.concatenate(parts, axis=1)


def tile_of(wide):
    lane = lax.broadcasted_iota(jnp.int32, (wide[0].shape[0], HDIM), 1)
    tile = jnp.zeros((wide[0].shape[0], HDIM), F32)
    for h, part in enumerate(wide):
        tile = jnp.where(lane == h, part, tile)
    return tile


def term_rows(row, first):
    at = lax.broadcasted_iota(jnp.int32, (16, row.shape[1]), 0)
    block = jnp.zeros((16, row.shape[1]), F32)
    for k in range(3):
        term = row.astype(BF16).astype(F32)
        row = row - term
        block = jnp.where(at == first + k, term, block)
    return block


def stat_terms(wide, first):
    rows = tile_of(wide).T
    return jnp.concatenate([term_rows(rows[h : h + 1], first) for h in range(len(wide))], axis=1)


def stat_rows(message, frames, which, cols):
    terms = message[frames : frames + 16, cols].astype(F32)
    at = 3 * which
    return terms[at : at + 1] + terms[at + 1 : at + 2] + terms[at + 2 : at + 3]


def weight_columns(weight, flip):
    width = weight.shape[0]
    at = (lax.axis_index("mp") ^ flip) * width
    return weight[:, pl.ds(pl.multiple_of(at, 128), width)]


def turn_body(block, seen, copy):
    copy[...] = block[...]


def split_body(joined, seen, *parts):
    frames = parts[0].shape[0]
    for k, part in enumerate(parts):
        part[...] = joined[k * frames : (k + 1) * frames, :]


def forward_body(scale, q, own, near, first, second, *refs):
    sums, tops, totals = refs[-3:]
    frames, width = q.shape
    heads = columns(width)
    blocks = (near, own, first, second)
    biases = (bias_of(near_swapped()), None, None, None)
    keys, values = slice(0, frames), slice(frames, 2 * frames)
    scores = [dot_nt(q[:, c], stacked(blocks, keys, c)) * scale for c in heads]
    scores = [by_block(s, biases) for s in scores]
    top = [jnp.max(s, axis=1, keepdims=True) for s in scores]
    probs = [jnp.exp(s - t).astype(BF16) for s, t in zip(scores, top)]
    summed = [dot_nn(p, with_ones(stacked(blocks, values, c))) for p, c in zip(probs, heads)]
    for c, t, s in zip(heads, top, summed):
        tops[:, c] = jnp.broadcast_to(t, (frames, HDIM))
        sums[:, c] = s[:, 0:HDIM]
        totals[:, c] = s[:, HDIM:]


def project_body(scale, q, relay, sums, tops, totals, weight, att, lse, send, keep):
    frames, width = q.shape
    heads = columns(width)
    bias = bias_of(far_there())
    scores = [dot_nt(q[:, c], relay[0:frames, c]) * scale + bias for c in heads]
    before = [tops[:, c] for c in heads]
    top = [jnp.maximum(b, jnp.max(s, axis=1, keepdims=True)) for b, s in zip(before, scores)]
    shrink = [jnp.exp(b - t) for b, t in zip(before, top)]
    probs = [jnp.exp(s - t).astype(BF16) for s, t in zip(scores, top)]
    late = [dot_nn(p, with_ones(relay[frames : 2 * frames, c])) for p, c in zip(probs, heads)]
    total = [totals[:, c] * k + s[:, HDIM:] for c, k, s in zip(heads, shrink, late)]
    summed = [sums[:, c] * k + s[:, 0:HDIM] for c, k, s in zip(heads, shrink, late)]
    attended = jnp.concatenate([(s * (1.0 / t)).astype(BF16) for s, t in zip(summed, total)], axis=1)
    sent = [dot_nn(attended, weight_columns(weight, flip)).astype(BF16) for flip in (1, 3)]
    kept = [dot_nn(attended, weight_columns(weight, flip)).astype(BF16) for flip in (0, 2)]
    logs = [t + jnp.log(n) for t, n in zip(top, total)]
    att[...] = attended
    send[...] = jnp.concatenate(sent, axis=1)
    keep[...] = jnp.concatenate(kept, axis=1)
    for c, part in zip(heads, logs):
        lse[:, c] = part


def pass_body(send, q_second, seen_a, seen_b, send_copy, second_copy):
    send_copy[...] = send[...]
    second_copy[...] = q_second[...]


def join_body(keep, core, inputs, cot, cot_other, q, chip, rim_near, rim_far, q_copy):
    frames, width = inputs.shape
    wide = 2 * HALO
    even = is_even()
    for cols, rows, cots in (
        (slice(0, width), inputs[...].astype(F32), cot),
        (slice(width, 2 * width), 0.0, cot_other),
    ):
        total = (rows + (keep[:, cols].astype(F32) + core[:, cols].astype(F32))).astype(BF16)
        for at, first, last in (
            (slice(0, wide), total[0:wide], total[frames - wide :]),
            (slice(wide, wide + HALO), cots[0:HALO, :], cots[frames - HALO : frames, :]),
        ):
            first, last = first.astype(F32), last.astype(F32)
            rim_near[at, cols] = jnp.where(even, last, first).astype(BF16)
            rim_far[at, cols] = jnp.where(even, first, last).astype(BF16)
        chip[:, cols] = total
    q_copy[...] = q[...]


def stack_body(rim_near, rim_far, q_second, ends, second_copy):
    wide = 2 * HALO
    ends[0:wide, :] = rim_near[0:wide, :]
    ends[wide : 2 * wide, :] = rim_far[0:wide, :]
    second_copy[...] = q_second[...]


def summed(share, across, rows, cols, width):
    back = slice((cols.start + width) % (2 * width), (cols.stop - 1 + width) % (2 * width) + 1)
    total = share[rows, cols].astype(F32) + across[rows, back].astype(F32)
    return total.astype(BF16).astype(F32)


def tiles_of(rows):
    return [rows[at : at + 8] for at in range(0, rows.shape[0], 8)]


def shifted_sum(tiles, taps_of, count):
    at = lax.broadcasted_iota(jnp.int32, (8, CHUNK), 0)
    sums = [None] * (count // 8)

    def add(k, term):
        sums[k] = term if sums[k] is None else sums[k] + term

    for b in range(8):
        parts = []
        for k in range(count // 8 + (b > 0)):
            part = None
            for a in range(4):
                tap = taps_of(8 * a + b)
                if tap is None or tiles[k + a] is None:
                    continue
                term = tap * tiles[k + a]
                part = term if part is None else part + term
            parts.append(part if part is None or b == 0 else pltpu.roll(part, 8 - b, 0))
        for k in range(count // 8):
            if b == 0:
                if parts[k] is not None:
                    add(k, parts[k])
            elif parts[k] is not None and parts[k + 1] is not None:
                add(k, jnp.where(at < 8 - b, parts[k], parts[k + 1]))
            elif parts[k] is not None:
                add(k, jnp.where(at < 8 - b, parts[k], 0.0))
            elif parts[k + 1] is not None:
                add(k, jnp.where(at < 8 - b, 0.0, parts[k + 1]))
    zero = jnp.zeros((8, CHUNK), F32)
    return jnp.concatenate([zero if part is None else part for part in sums], axis=0)


def silu_parts(conv, cots):
    gate = 1.0 / (1.0 + jnp.exp(-conv))
    grad = cots * (gate + conv * gate * (1.0 - gate))
    return conv * gate, grad.astype(BF16).astype(F32)


def taps_forward(taps, count, cols):
    return lambda s: taps[s - 1 : s, cols] if 1 <= s <= count else None


def taps_backward(taps, count, cols):
    return lambda s: taps[count - s : count - s + 1, cols] if 1 <= s <= count else None


def conv_chunks(width, cot, cot_other, taps, taps_other):
    for c in range(0, 2 * width, CHUNK):
        own, cols = c < width, slice(c, c + CHUNK)
        local = cols if own else slice(cols.start - width, cols.stop - width)
        yield own, cols, local, cot if own else cot_other, taps if own else taps_other


def conv_inner_body(
    chip, across, cot, cot_other, taps, taps_other, seen, rows_out, edge_rows, edge_conv, part_grad
):
    frames, width = cot.shape
    wide, count = 2 * HALO, taps.shape[0]
    inner = slice(HALO, frames - HALO)
    none = [None] * (wide // 8)
    for own, cols, local, cots_of, tap in conv_chunks(width, cot, cot_other, taps, taps_other):
        rows = summed(chip, across, slice(0, frames), cols, width)
        cots = cots_of[:, local].astype(F32)
        conv = shifted_sum(
            none + tiles_of(rows) + none, taps_forward(tap, count, local), frames + wide
        )
        silu, grad = silu_parts(conv[wide:frames], cots[inner])
        back = shifted_sum(
            none + tiles_of(grad) + none, taps_backward(tap, count, local), frames
        )
        edge_conv[0:wide, cols] = conv[0:wide]
        edge_conv[wide : 2 * wide, cols] = conv[frames : frames + wide]
        if own:
            rows_out[inner, cols] = (rows[inner] + silu).astype(BF16)
            edge_rows[0:HALO, cols] = rows[0:HALO]
            edge_rows[HALO:wide, cols] = rows[frames - HALO :]
        part_grad[:, cols] = cots + back


def conv_edge_body(
    ends, ends_across, rim_near, rim_far, cot, cot_other, taps, taps_other,
    rows_in, edge_rows, edge_conv, part_grad, seen, output, grad_input,
):
    frames, width = cot.shape
    wide, count = 2 * HALO, taps.shape[0]
    even, far = is_even(), far_there()
    low, high = slice(0, HALO), slice(frames - HALO, frames)
    inner = slice(HALO, frames - HALO)
    none = [None] * (wide // 8)
    cots_of = slice(wide, wide + HALO)

    def sides(near, beyond):
        beyond = jnp.where(far, beyond, 0.0)
        return jnp.where(even, beyond, near), jnp.where(even, near, beyond)

    for own, cols, local, block, tap in conv_chunks(width, cot, cot_other, taps, taps_other):
        rows = summed(ends, ends_across, slice(0, 2 * wide), cols, width)
        row_low, row_high = sides(rows[0:wide], rows[wide:])
        cot_low, cot_high = sides(rim_near[cots_of, cols].astype(F32), rim_far[cots_of, cols].astype(F32))
        conv = edge_conv[:, cols] + shifted_sum(
            tiles_of(row_low) + none + tiles_of(row_high), taps_forward(tap, count, local), 2 * wide
        )
        first = block[low, local].astype(F32)
        last = block[high, local].astype(F32)
        cots = jnp.concatenate([cot_low, first, last, cot_high], axis=0)
        silu, grad = silu_parts(conv, cots)
        back = shifted_sum(
            tiles_of(grad[0:wide]) + none + tiles_of(grad[wide:]), taps_backward(tap, count, local), 2 * wide
        )
        part = part_grad[:, cols]
        grad_input[:, cols] = jnp.concatenate(
            [part[0:wide] + back[0:wide], part[wide : frames - wide], part[frames - wide :] + back[wide:]],
            axis=0,
        ).astype(BF16)
        if own:
            output[low, cols] = (edge_rows[0:HALO, cols] + silu[HALO:wide]).astype(BF16)
            output[inner, cols] = rows_in[inner, cols]
            output[high, cols] = (edge_rows[HALO:wide, cols] + silu[wide : wide + HALO]).astype(BF16)


def upstream_part(grads, weight, flips):
    width = weight.shape[0]
    return sum(
        dot_nt(grads[:, k * width : (k + 1) * width], weight_columns(weight, flip))
        for k, flip in enumerate(flips)
    )


def upstream_own_body(own, weight, lse, partial, terms):
    partial[...] = upstream_part(own, weight, (0, 2))
    terms[...] = stat_terms([lse[:, c] for c in columns(lse.shape[1])], 0)


def upstream_body(core, weight, att, partial, terms, message, delta):
    frames, width = att.shape
    heads = columns(width)
    up = (partial[...] + upstream_part(core, weight, (1, 3))).astype(BF16)
    products = [up[:, c].astype(F32) * att[:, c].astype(F32) for c in heads]
    deltas = [jnp.broadcast_to(jnp.sum(p, axis=1, keepdims=True), (frames, HDIM)) for p in products]
    message[0:frames, :] = up
    message[frames : frames + 16, :] = (terms[...] + stat_terms(deltas, 3)).astype(BF16)
    for c, part in zip(heads, deltas):
        delta[:, c] = part


def query_grad_body(
    scale, q, own, near, first, second, relay, message, lse, delta, output_here, grad_here,
    output, grad_input, grad_query, held, sems,
):
    writes = [
        pltpu.make_async_copy(output_here, output, sems.at[0]),
        pltpu.make_async_copy(grad_here.at[:, pl.ds(0, q.shape[1])], grad_input, sems.at[1]),
    ]
    for write in writes:
        write.start()
    frames, width = q.shape
    heads = columns(width)
    blocks = (near, own, first, second, relay)
    biases = (bias_of(near_swapped()), None, None, None, bias_of(far_there()))
    above, below = slice(0, frames), slice(frames, 2 * frames)
    keys = [stacked(blocks, above, c) for c in heads]
    scores = [dot_nt(q[:, c], k) * scale for c, k in zip(heads, keys)]
    dots = [dot_nt(message[0:frames, c], stacked(blocks, below, c)) for c in heads]
    probs = [jnp.exp(by_block(s, biases, [lse[:, c]] * 5)) for c, s in zip(heads, scores)]
    drops = [by_block(d, (None,) * 5, [delta[:, c]] * 5) for c, d in zip(heads, dots)]
    grads = [(p * d * scale).astype(BF16) for p, d in zip(probs, drops)]
    held[...] = jnp.concatenate([dot_nn(g, k).astype(BF16) for g, k in zip(grads, keys)], axis=1)
    writes.append(pltpu.make_async_copy(held, grad_query, sems.at[2]))
    writes[2].start()
    for write in writes:
        write.wait()


def key_part_body(scale, own, *refs):
    queries, late_query, messages, (key_part, value_part, late) = refs[0:4], refs[4], refs[5:9], refs[9:12]
    frames = own.shape[0] // 2
    heads = columns(own.shape[1])
    above, below = slice(0, frames), slice(frames, 2 * frames)
    biases = (None, bias_of(near_swapped()), None, None)
    asks = [stacked(queries, above, c) for c in heads]
    ups = [stacked(messages, above, c) for c in heads]
    scores = [dot_nt(own[above, c], a) * scale for c, a in zip(heads, asks)]
    dots = [dot_nt(own[below, c], u) for c, u in zip(heads, ups)]
    last = [dot_nt(own[above, c], late_query[:, c]) * scale + bias_of(far_there()) for c in heads]
    logs = [[stat_rows(m, frames, 0, c) for m in messages] for c in heads]
    deltas = [[stat_rows(m, frames, 1, c) for m in messages] for c in heads]
    probs = [jnp.exp(by_block(s, biases, n)) for s, n in zip(scores, logs)]
    drops = [by_block(d, (None,) * 4, n) for d, n in zip(dots, deltas)]
    grads = [(p * d * scale).astype(BF16) for p, d in zip(probs, drops)]
    value_sums = [dot_nn(p.astype(BF16), u) for p, u in zip(probs, ups)]
    key_sums = [dot_nn(g, a) for g, a in zip(grads, asks)]
    for c, k, v, s in zip(heads, key_sums, value_sums, last):
        key_part[:, c] = k
        value_part[:, c] = v
        late[:, c] = s


def key_grad_body(
    scale, own, query, message, late, key_part, value_part, grad_key, grad_value, held_key, held_value, sems
):
    frames = own.shape[0] // 2
    heads = columns(own.shape[1])
    above, below = slice(0, frames), slice(frames, 2 * frames)
    ups = [message[above, c] for c in heads]
    probs = [jnp.exp(late[:, c] - stat_rows(message, frames, 0, c)) for c in heads]
    dots = [dot_nt(own[below, c], u) for c, u in zip(heads, ups)]
    values = [value_part[:, c] + dot_nn(p.astype(BF16), u) for c, p, u in zip(heads, probs, ups)]
    held_value[...] = jnp.concatenate([v.astype(BF16) for v in values], axis=1)
    value_write = pltpu.make_async_copy(held_value, grad_value, sems.at[0])
    value_write.start()
    drops = [d - stat_rows(message, frames, 1, c) for c, d in zip(heads, dots)]
    grads = [(p * d * scale).astype(BF16) for p, d in zip(probs, drops)]
    keys = [key_part[:, c] + dot_nn(g, query[:, c]) for c, g in zip(heads, grads)]
    held_key[...] = jnp.concatenate([k.astype(BF16) for k in keys], axis=1)
    key_write = pltpu.make_async_copy(held_key, grad_key, sems.at[1])
    key_write.start()
    value_write.wait()
    key_write.wait()


def per_device(query_rows, key_rows, value_rows, inputs, out_weight, kernel, cotangent):
    frames, width = query_rows.shape
    wide = 2 * HALO
    scale = 1.0 / math.sqrt(HDIM)
    tile = shaped((frames, width), BF16)
    tile32 = shaped((frames, width), F32)
    rim = shaped((wide + HALO, 2 * width), BF16)
    both = shaped((frames, 2 * width), BF16)
    noted = shaped((frames + 16, width), BF16)

    zero = jnp.zeros((), BF16)
    kv = lax.pad(key_rows, zero, ((0, frames, 0), (0, 0, 0))) + lax.pad(
        value_rows, zero, ((frames, 0, 0), (0, 0, 0))
    )
    joined = sum(
        lax.pad(rows, zero, ((k * frames, (2 - k) * frames, 0), (0, 0, 0)))
        for k, rows in enumerate((query_rows, inputs, cotangent))
    )
    near, first, second = inner_swap(kv), ring(kv, 0), ring(kv, 1)
    relay = outer_swap(kv)
    cot_other = pair_swap(cotangent, "mp", 2)
    taps_other = pair_swap(kernel, "mp", 2)
    query, inputs, cotangent = kernel_call(
        split_body, (tile, tile, tile), (joined, second), 0.1, "split", 1
    )
    q_second = ring(query, 1)
    sums, tops, totals = kernel_call(
        functools.partial(forward_body, scale),
        (tile32, tile32, tile32),
        (query, kv, near, first, second),
        1.0, "forward",
    )
    att, lse, send, keep = kernel_call(
        functools.partial(project_body, scale),
        (tile, tile32, both, both),
        (query, relay, sums, tops, totals, out_weight),
        1.0, "project",
    )

    send, q_second = kernel_call(pass_body, (both, tile), (send, q_second, cot_other, taps_other), 0.1, "pass", 2)
    core = pair_swap(send, "mp", 1)
    chip, rim_up, rim_down, q_own = kernel_call(
        join_body,
        (both, rim, rim, tile),
        (keep, core, inputs, cotangent, cot_other, query),
        0.2, "join",
    )
    across = pair_swap(chip, "mp", 2)
    rim_far = outer_swap(rim_down)
    rim_near = pair_swap(rim_up, "ctx", 1)
    ends, q_handed = kernel_call(
        stack_body,
        (shaped((2 * wide, 2 * width), BF16), tile),
        (rim_near, rim_far, q_second),
        0.1, "stack",
    )
    ends_across = pair_swap(ends, "mp", 2)
    q_first = ring(q_own, 0)
    q_near = inner_swap(q_own)
    q_relay = pair_swap(q_handed, "ctx", 1)
    rows_out, edge_rows, edge_conv, part_grad = kernel_call(
        conv_inner_body,
        (
            tile,
            shaped((wide, width), F32),
            shaped((2 * wide, 2 * width), F32),
            shaped((frames, 2 * width), F32),
        ),
        (chip, across, cotangent, cot_other, kernel, taps_other, q_first),
        3.1, "conv_inner", 1,
    )
    output_here, grad_here = kernel_call(
        conv_edge_body,
        (tile, both),
        (ends, ends_across, rim_near, rim_far, cotangent, cot_other, kernel, taps_other)
        + (rows_out, edge_rows, edge_conv, part_grad, q_near),
        1.4, "conv_edge", 1,
    )

    (grad_here,) = kernel_call(turn_body, (both,), (grad_here, q_relay), 0.1, "hand", 1)
    gi_core = pair_swap(grad_here, "mp", 1)
    partial, terms = kernel_call(
        upstream_own_body, (tile32, shaped((16, width), F32)), (grad_here, out_weight, lse), 0.5,
        "upstream_own",
    )
    message, delta = kernel_call(
        upstream_body, (noted, tile32), (gi_core, out_weight, att, partial, terms), 0.6, "upstream"
    )

    m_near, m_first, m_second = inner_swap(message), ring(message, 0), ring(message, 1)
    m_relay = outer_swap(message)
    output, grad_input, grad_query = kernel_call(
        functools.partial(query_grad_body, scale),
        (tile, tile, tile),
        (q_own, kv, near, first, second, relay, message, lse, delta, output_here, grad_here),
        1.8, "query_grad", 0,
        [pltpu.VMEM((frames, width), BF16), pltpu.SemaphoreType.DMA((3,))], HBM,
    )
    key_part, value_part, late = kernel_call(
        functools.partial(key_part_body, scale),
        (tile32, tile32, tile32),
        (kv, q_own, q_near, q_first, q_second, q_relay, message, m_near, m_first, m_second),
        1.5, "key_part",
    )
    grad_key, grad_value = kernel_call(
        functools.partial(key_grad_body, scale),
        (tile, tile),
        (kv, q_relay, m_relay, late, key_part, value_part),
        1.0, "key_grad", 0,
        [pltpu.VMEM((frames, width), BF16)] * 2 + [pltpu.SemaphoreType.DMA((2,))], HBM,
    )
    return (output, grad_input, grad_query, grad_key, grad_value)


def solution(mesh):
    rows = P("ctx", "mp")
    return jax.shard_map(
        per_device,
        mesh=mesh,
        in_specs=(rows, rows, rows, rows, P("mp", None), P(None, "mp"), rows),
        out_specs=(rows,) * 5,
        check_vma=False,
    )
```

```python
import functools
import math

import jax
import jax.numpy as jnp
from jax import lax
from jax.experimental import pallas as pl
from jax.experimental.pallas import tpu as pltpu
from jax.sharding import PartitionSpec as P

HDIM = 128
F32 = jnp.float32
BF16 = jnp.bfloat16
CHUNK = 256
HALO = 16
NT = (((1,), (1,)), ((), ()))
NN = (((1,), (0,)), ((), ()))


def dot_nt(a, b):
    return lax.dot_general(a, b, NT, preferred_element_type=F32)


def dot_nn(a, b):
    return lax.dot_general(a, b, NN, preferred_element_type=F32)


def pair_swap(block, axis, bit):
    return lax.ppermute(block, axis, [(i, i ^ bit) for i in range(lax.axis_size(axis))])


def ring_routes(count):
    rise = [(i, i + 2) for i in range(0, count - 2, 2)] + [(count - 2, count - 1)]
    fall = [(i, i - 2) for i in range(count - 1, 2, -2)] + [(1, 0)]
    route = rise + fall
    return route, [(b, a) for a, b in route]


def ring(block, way):
    return lax.ppermute(block, "ctx", ring_routes(lax.axis_size("ctx"))[way])


def total_swap(block, partner_of):
    count, places = lax.axis_size("ctx"), lax.axis_size("mp")
    route = []
    for i in range(count):
        other = partner_of(i, count)
        for m in range(places):
            target = i * places + (m ^ 1) if other is None else other * places + m
            route.append((i * places + m, target))
    return lax.ppermute(block, ("ctx", "mp"), route)


def inner_swap(block):
    return total_swap(block, lambda i, count: i ^ 1 if 2 <= i < count - 2 else None)


def outer_swap(block):
    return total_swap(block, lambda i, count: ((i + 1) ^ 1) - 1 if 0 < i < count - 1 else None)


def window_of(block, before_relay=lambda second: second):
    second = ring(block, 1)
    first = ring(block, 0)
    near = inner_swap(block)
    second = before_relay(second)
    return near, first, second, pair_swap(second, "ctx", 1)


VMEM = pl.BlockSpec(memory_space=pltpu.VMEM)
ANY = pl.BlockSpec(memory_space=pl.ANY)
HBM = pl.BlockSpec(memory_space=pltpu.HBM)


def kernel_call(body, outs, args, micros, name, unread=0, scratch=(), out_space=VMEM):
    return pl.pallas_call(
        body,
        out_shape=outs,
        in_specs=[VMEM] * (len(args) - unread) + [ANY] * unread,
        out_specs=tuple(out_space for _ in outs),
        scratch_shapes=scratch,
        compiler_params=pltpu.CompilerParams(vmem_limit_bytes=24 * 1024 * 1024),
        cost_estimate=pl.CostEstimate(
            flops=0, bytes_accessed=int(micros * 3.69e6), transcendentals=0
        ),
        name=name,
    )(*args)


def shaped(shape, dtype):
    return jax.ShapeDtypeStruct(shape, dtype)


def is_even():
    return lax.axis_index("ctx") % 2 == 0


def near_swapped():
    block = lax.axis_index("ctx")
    return (block >= 2) & (block < lax.axis_size("ctx") - 2)


def far_there():
    block = lax.axis_index("ctx")
    return jnp.where(is_even(), block >= 2, block < lax.axis_size("ctx") - 2)


def bias_of(there):
    return jnp.where(there, jnp.float32(0.0), jnp.float32(-jnp.inf))


def columns(width):
    return [slice(c, c + HDIM) for c in range(0, width, HDIM)]


def stacked(blocks, rows, cols):
    return jnp.concatenate([block[rows, cols] for block in blocks], axis=0)


def with_ones(values):
    return jnp.concatenate([values, jnp.ones_like(values)], axis=1)


def by_block(scores, biases, stats=None):
    parts = []
    for b, bias in enumerate(biases):
        part = scores[:, b * HDIM : (b + 1) * HDIM]
        if stats is not None:
            part = part - stats[b]
        parts.append(part if bias is None else part + bias)
    return jnp.concatenate(parts, axis=1)


def tile_of(wide):
    lane = lax.broadcasted_iota(jnp.int32, (wide[0].shape[0], HDIM), 1)
    tile = jnp.zeros((wide[0].shape[0], HDIM), F32)
    for h, part in enumerate(wide):
        tile = jnp.where(lane == h, part, tile)
    return tile


def term_rows(row, first):
    at = lax.broadcasted_iota(jnp.int32, (16, row.shape[1]), 0)
    block = jnp.zeros((16, row.shape[1]), F32)
    for k in range(3):
        term = row.astype(BF16).astype(F32)
        row = row - term
        block = jnp.where(at == first + k, term, block)
    return block


def stat_terms(wide, first):
    rows = tile_of(wide).T
    return jnp.concatenate([term_rows(rows[h : h + 1], first) for h in range(len(wide))], axis=1)


def stat_rows(message, frames, which, cols):
    terms = message[frames : frames + 16, cols].astype(F32)
    at = 3 * which
    return terms[at : at + 1] + terms[at + 1 : at + 2] + terms[at + 2 : at + 3]


def weight_columns(weight, flip):
    width = weight.shape[0]
    at = (lax.axis_index("mp") ^ flip) * width
    return weight[:, pl.ds(pl.multiple_of(at, 128), width)]


def turn_body(block, seen, copy):
    copy[...] = block[...]


def split_body(joined, seen, *parts):
    frames = parts[0].shape[0]
    for k, part in enumerate(parts):
        part[...] = joined[k * frames : (k + 1) * frames, :]


def forward_body(scale, q, own, near, first, second, *refs):
    sums, tops, totals = refs[-3:]
    frames, width = q.shape
    heads = columns(width)
    blocks = (near, own, first, second)
    biases = (bias_of(near_swapped()), None, None, None)
    keys, values = slice(0, frames), slice(frames, 2 * frames)
    scores = [dot_nt(q[:, c], stacked(blocks, keys, c)) * scale for c in heads]
    scores = [by_block(s, biases) for s in scores]
    top = [jnp.max(s, axis=1, keepdims=True) for s in scores]
    probs = [jnp.exp(s - t).astype(BF16) for s, t in zip(scores, top)]
    summed = [dot_nn(p, with_ones(stacked(blocks, values, c))) for p, c in zip(probs, heads)]
    for c, t, s in zip(heads, top, summed):
        tops[:, c] = jnp.broadcast_to(t, (frames, HDIM))
        sums[:, c] = s[:, 0:HDIM]
        totals[:, c] = s[:, HDIM:]


def project_body(scale, q, relay, sums, tops, totals, weight, att, lse, send, keep):
    frames, width = q.shape
    heads = columns(width)
    bias = bias_of(far_there())
    scores = [dot_nt(q[:, c], relay[0:frames, c]) * scale + bias for c in heads]
    before = [tops[:, c] for c in heads]
    top = [jnp.maximum(b, jnp.max(s, axis=1, keepdims=True)) for b, s in zip(before, scores)]
    shrink = [jnp.exp(b - t) for b, t in zip(before, top)]
    probs = [jnp.exp(s - t).astype(BF16) for s, t in zip(scores, top)]
    late = [dot_nn(p, with_ones(relay[frames : 2 * frames, c])) for p, c in zip(probs, heads)]
    total = [totals[:, c] * k + s[:, HDIM:] for c, k, s in zip(heads, shrink, late)]
    summed = [sums[:, c] * k + s[:, 0:HDIM] for c, k, s in zip(heads, shrink, late)]
    attended = jnp.concatenate([(s * (1.0 / t)).astype(BF16) for s, t in zip(summed, total)], axis=1)
    sent = [dot_nn(attended, weight_columns(weight, flip)).astype(BF16) for flip in (1, 3)]
    kept = [dot_nn(attended, weight_columns(weight, flip)).astype(BF16) for flip in (0, 2)]
    logs = [t + jnp.log(n) for t, n in zip(top, total)]
    att[...] = attended
    send[...] = jnp.concatenate(sent, axis=1)
    keep[...] = jnp.concatenate(kept, axis=1)
    for c, part in zip(heads, logs):
        lse[:, c] = part


def pass_body(send, q_second, seen_a, seen_b, send_copy, second_copy):
    send_copy[...] = send[...]
    second_copy[...] = q_second[...]


def join_body(keep, core, inputs, cot, cot_other, q, chip, rim_near, rim_far, q_copy):
    frames, width = inputs.shape
    wide = 2 * HALO
    even = is_even()
    for cols, rows, cots in (
        (slice(0, width), inputs[...].astype(F32), cot),
        (slice(width, 2 * width), 0.0, cot_other),
    ):
        total = (rows + (keep[:, cols].astype(F32) + core[:, cols].astype(F32))).astype(BF16)
        for at, first, last in (
            (slice(0, wide), total[0:wide], total[frames - wide :]),
            (slice(wide, wide + HALO), cots[0:HALO, :], cots[frames - HALO : frames, :]),
        ):
            first, last = first.astype(F32), last.astype(F32)
            rim_near[at, cols] = jnp.where(even, last, first).astype(BF16)
            rim_far[at, cols] = jnp.where(even, first, last).astype(BF16)
        chip[:, cols] = total
    q_copy[...] = q[...]


def stack_body(rim_near, rim_far, q_second, ends, second_copy):
    wide = 2 * HALO
    ends[0:wide, :] = rim_near[0:wide, :]
    ends[wide : 2 * wide, :] = rim_far[0:wide, :]
    second_copy[...] = q_second[...]


def summed(share, across, rows, cols, width):
    back = slice((cols.start + width) % (2 * width), (cols.stop - 1 + width) % (2 * width) + 1)
    total = share[rows, cols].astype(F32) + across[rows, back].astype(F32)
    return total.astype(BF16).astype(F32)


def tiles_of(rows):
    return [rows[at : at + 8] for at in range(0, rows.shape[0], 8)]


def shifted_sum(tiles, taps_of, count):
    at = lax.broadcasted_iota(jnp.int32, (8, CHUNK), 0)
    sums = [None] * (count // 8)

    def add(k, term):
        sums[k] = term if sums[k] is None else sums[k] + term

    for b in range(8):
        parts = []
        for k in range(count // 8 + (b > 0)):
            part = None
            for a in range(4):
                tap = taps_of(8 * a + b)
                if tap is None or tiles[k + a] is None:
                    continue
                term = tap * tiles[k + a]
                part = term if part is None else part + term
            parts.append(part if part is None or b == 0 else pltpu.roll(part, 8 - b, 0))
        for k in range(count // 8):
            if b == 0:
                if parts[k] is not None:
                    add(k, parts[k])
            elif parts[k] is not None and parts[k + 1] is not None:
                add(k, jnp.where(at < 8 - b, parts[k], parts[k + 1]))
            elif parts[k] is not None:
                add(k, jnp.where(at < 8 - b, parts[k], 0.0))
            elif parts[k + 1] is not None:
                add(k, jnp.where(at < 8 - b, 0.0, parts[k + 1]))
    zero = jnp.zeros((8, CHUNK), F32)
    return jnp.concatenate([zero if part is None else part for part in sums], axis=0)


def silu_parts(conv, cots):
    gate = 1.0 / (1.0 + jnp.exp(-conv))
    grad = cots * (gate + conv * gate * (1.0 - gate))
    return conv * gate, grad.astype(BF16).astype(F32)


def taps_forward(taps, count, cols):
    return lambda s: taps[s - 1 : s, cols] if 1 <= s <= count else None


def taps_backward(taps, count, cols):
    return lambda s: taps[count - s : count - s + 1, cols] if 1 <= s <= count else None


def conv_chunks(width, cot, cot_other, taps, taps_other):
    for c in range(0, 2 * width, CHUNK):
        own, cols = c < width, slice(c, c + CHUNK)
        local = cols if own else slice(cols.start - width, cols.stop - width)
        yield own, cols, local, cot if own else cot_other, taps if own else taps_other


def conv_inner_body(
    chip, across, cot, cot_other, taps, taps_other, seen, rows_out, edge_rows, edge_conv, part_grad
):
    frames, width = cot.shape
    wide, count = 2 * HALO, taps.shape[0]
    inner = slice(HALO, frames - HALO)
    none = [None] * (wide // 8)
    for own, cols, local, cots_of, tap in conv_chunks(width, cot, cot_other, taps, taps_other):
        rows = summed(chip, across, slice(0, frames), cols, width)
        cots = cots_of[:, local].astype(F32)
        conv = shifted_sum(
            none + tiles_of(rows) + none, taps_forward(tap, count, local), frames + wide
        )
        silu, grad = silu_parts(conv[wide:frames], cots[inner])
        back = shifted_sum(
            none + tiles_of(grad) + none, taps_backward(tap, count, local), frames
        )
        edge_conv[0:wide, cols] = conv[0:wide]
        edge_conv[wide : 2 * wide, cols] = conv[frames : frames + wide]
        if own:
            rows_out[inner, cols] = (rows[inner] + silu).astype(BF16)
            edge_rows[0:HALO, cols] = rows[0:HALO]
            edge_rows[HALO:wide, cols] = rows[frames - HALO :]
        part_grad[:, cols] = cots + back


def conv_edge_body(
    ends, ends_across, rim_near, rim_far, cot, cot_other, taps, taps_other,
    rows_in, edge_rows, edge_conv, part_grad, seen, output, grad_input,
):
    frames, width = cot.shape
    wide, count = 2 * HALO, taps.shape[0]
    even, far = is_even(), far_there()
    low, high = slice(0, HALO), slice(frames - HALO, frames)
    inner = slice(HALO, frames - HALO)
    none = [None] * (wide // 8)
    cots_of = slice(wide, wide + HALO)

    def sides(near, beyond):
        beyond = jnp.where(far, beyond, 0.0)
        return jnp.where(even, beyond, near), jnp.where(even, near, beyond)

    for own, cols, local, block, tap in conv_chunks(width, cot, cot_other, taps, taps_other):
        rows = summed(ends, ends_across, slice(0, 2 * wide), cols, width)
        row_low, row_high = sides(rows[0:wide], rows[wide:])
        cot_low, cot_high = sides(rim_near[cots_of, cols].astype(F32), rim_far[cots_of, cols].astype(F32))
        conv = edge_conv[:, cols] + shifted_sum(
            tiles_of(row_low) + none + tiles_of(row_high), taps_forward(tap, count, local), 2 * wide
        )
        first = block[low, local].astype(F32)
        last = block[high, local].astype(F32)
        cots = jnp.concatenate([cot_low, first, last, cot_high], axis=0)
        silu, grad = silu_parts(conv, cots)
        back = shifted_sum(
            tiles_of(grad[0:wide]) + none + tiles_of(grad[wide:]), taps_backward(tap, count, local), 2 * wide
        )
        part = part_grad[:, cols]
        grad_input[:, cols] = jnp.concatenate(
            [part[0:wide] + back[0:wide], part[wide : frames - wide], part[frames - wide :] + back[wide:]],
            axis=0,
        ).astype(BF16)
        if own:
            output[low, cols] = (edge_rows[0:HALO, cols] + silu[HALO:wide]).astype(BF16)
            output[inner, cols] = rows_in[inner, cols]
            output[high, cols] = (edge_rows[HALO:wide, cols] + silu[wide : wide + HALO]).astype(BF16)


def upstream_part(grads, weight, flips):
    width = weight.shape[0]
    return sum(
        dot_nt(grads[:, k * width : (k + 1) * width], weight_columns(weight, flip))
        for k, flip in enumerate(flips)
    )


def upstream_own_body(own, weight, lse, partial, terms):
    partial[...] = upstream_part(own, weight, (0, 2))
    terms[...] = stat_terms([lse[:, c] for c in columns(lse.shape[1])], 0)


def upstream_body(core, weight, att, partial, terms, message, delta):
    frames, width = att.shape
    heads = columns(width)
    up = (partial[...] + upstream_part(core, weight, (1, 3))).astype(BF16)
    products = [up[:, c].astype(F32) * att[:, c].astype(F32) for c in heads]
    deltas = [jnp.broadcast_to(jnp.sum(p, axis=1, keepdims=True), (frames, HDIM)) for p in products]
    message[0:frames, :] = up
    message[frames : frames + 16, :] = (terms[...] + stat_terms(deltas, 3)).astype(BF16)
    for c, part in zip(heads, deltas):
        delta[:, c] = part


def query_grad_body(
    scale, q, own, near, first, second, relay, message, lse, delta, output_here, grad_here,
    output, grad_input, grad_query, held, sems,
):
    writes = [
        pltpu.make_async_copy(output_here, output, sems.at[0]),
        pltpu.make_async_copy(grad_here.at[:, pl.ds(0, q.shape[1])], grad_input, sems.at[1]),
    ]
    for write in writes:
        write.start()
    frames, width = q.shape
    heads = columns(width)
    blocks = (near, own, first, second, relay)
    biases = (bias_of(near_swapped()), None, None, None, bias_of(far_there()))
    above, below = slice(0, frames), slice(frames, 2 * frames)
    keys = [stacked(blocks, above, c) for c in heads]
    scores = [dot_nt(q[:, c], k) * scale for c, k in zip(heads, keys)]
    dots = [dot_nt(message[0:frames, c], stacked(blocks, below, c)) for c in heads]
    probs = [jnp.exp(by_block(s, biases, [lse[:, c]] * 5)) for c, s in zip(heads, scores)]
    drops = [by_block(d, (None,) * 5, [delta[:, c]] * 5) for c, d in zip(heads, dots)]
    grads = [(p * d * scale).astype(BF16) for p, d in zip(probs, drops)]
    held[...] = jnp.concatenate([dot_nn(g, k).astype(BF16) for g, k in zip(grads, keys)], axis=1)
    writes.append(pltpu.make_async_copy(held, grad_query, sems.at[2]))
    writes[2].start()
    for write in writes:
        write.wait()


def key_part_body(scale, own, *refs):
    queries, late_query, messages, (key_part, value_part, late) = refs[0:4], refs[4], refs[5:9], refs[9:12]
    frames = own.shape[0] // 2
    heads = columns(own.shape[1])
    above, below = slice(0, frames), slice(frames, 2 * frames)
    biases = (None, bias_of(far_there()), bias_of(near_swapped()), None)
    asks = [stacked(queries, above, c) for c in heads]
    ups = [stacked(messages, above, c) for c in heads]
    scores = [dot_nt(own[above, c], a) * scale for c, a in zip(heads, asks)]
    dots = [dot_nt(own[below, c], u) for c, u in zip(heads, ups)]
    last = [dot_nt(own[above, c], late_query[:, c]) * scale for c in heads]
    logs = [[stat_rows(m, frames, 0, c) for m in messages] for c in heads]
    deltas = [[stat_rows(m, frames, 1, c) for m in messages] for c in heads]
    probs = [jnp.exp(by_block(s, biases, n)) for s, n in zip(scores, logs)]
    drops = [by_block(d, (None,) * 4, n) for d, n in zip(dots, deltas)]
    grads = [(p * d * scale).astype(BF16) for p, d in zip(probs, drops)]
    value_sums = [dot_nn(p.astype(BF16), u) for p, u in zip(probs, ups)]
    key_sums = [dot_nn(g, a) for g, a in zip(grads, asks)]
    for c, k, v, s in zip(heads, key_sums, value_sums, last):
        key_part[:, c] = k
        value_part[:, c] = v
        late[:, c] = s


def key_grad_body(
    scale, own, query, message, late, key_part, value_part, grad_key, grad_value, held_key, held_value, sems
):
    frames = own.shape[0] // 2
    heads = columns(own.shape[1])
    above, below = slice(0, frames), slice(frames, 2 * frames)
    ups = [message[above, c] for c in heads]
    probs = [jnp.exp(late[:, c] - stat_rows(message, frames, 0, c)) for c in heads]
    dots = [dot_nt(own[below, c], u) for c, u in zip(heads, ups)]
    values = [value_part[:, c] + dot_nn(p.astype(BF16), u) for c, p, u in zip(heads, probs, ups)]
    held_value[...] = jnp.concatenate([v.astype(BF16) for v in values], axis=1)
    value_write = pltpu.make_async_copy(held_value, grad_value, sems.at[0])
    value_write.start()
    drops = [d - stat_rows(message, frames, 1, c) for c, d in zip(heads, dots)]
    grads = [(p * d * scale).astype(BF16) for p, d in zip(probs, drops)]
    keys = [key_part[:, c] + dot_nn(g, query[:, c]) for c, g in zip(heads, grads)]
    held_key[...] = jnp.concatenate([k.astype(BF16) for k in keys], axis=1)
    key_write = pltpu.make_async_copy(held_key, grad_key, sems.at[1])
    key_write.start()
    value_write.wait()
    key_write.wait()


def per_device(query_rows, key_rows, value_rows, inputs, out_weight, kernel, cotangent):
    frames, width = query_rows.shape
    wide = 2 * HALO
    scale = 1.0 / math.sqrt(HDIM)
    tile = shaped((frames, width), BF16)
    tile32 = shaped((frames, width), F32)
    rim = shaped((wide + HALO, 2 * width), BF16)
    both = shaped((frames, 2 * width), BF16)
    noted = shaped((frames + 16, width), BF16)

    zero = jnp.zeros((), BF16)
    kv = lax.pad(key_rows, zero, ((0, frames, 0), (0, 0, 0))) + lax.pad(
        value_rows, zero, ((frames, 0, 0), (0, 0, 0))
    )
    joined = sum(
        lax.pad(rows, zero, ((k * frames, (2 - k) * frames, 0), (0, 0, 0)))
        for k, rows in enumerate((query_rows, inputs, cotangent))
    )
    near, first, second, relay = window_of(
        kv,
        lambda second: kernel_call(
            turn_body, (shaped(kv.shape, BF16),), (second, joined), 0.1, "turn", 1
        )[0],
    )
    cot_other = pair_swap(cotangent, "mp", 2)
    taps_other = pair_swap(kernel, "mp", 2)
    query, inputs, cotangent = kernel_call(
        split_body, (tile, tile, tile), (joined, second), 0.1, "split", 1
    )
    q_second = ring(query, 1)
    sums, tops, totals = kernel_call(
        functools.partial(forward_body, scale),
        (tile32, tile32, tile32),
        (query, kv, near, first, second),
        1.0, "forward",
    )
    att, lse, send, keep = kernel_call(
        functools.partial(project_body, scale),
        (tile, tile32, both, both),
        (query, relay, sums, tops, totals, out_weight),
        1.0, "project",
    )

    send, q_second = kernel_call(pass_body, (both, tile), (send, q_second, cot_other, taps_other), 0.1, "pass", 2)
    core = pair_swap(send, "mp", 1)
    chip, rim_up, rim_down, q_own = kernel_call(
        join_body,
        (both, rim, rim, tile),
        (keep, core, inputs, cotangent, cot_other, query),
        0.2, "join",
    )
    across = pair_swap(chip, "mp", 2)
    rim_far = outer_swap(rim_down)
    rim_near = pair_swap(rim_up, "ctx", 1)
    ends, q_handed = kernel_call(
        stack_body,
        (shaped((2 * wide, 2 * width), BF16), tile),
        (rim_near, rim_far, q_second),
        0.1, "stack",
    )
    ends_across = pair_swap(ends, "mp", 2)
    q_first = ring(q_own, 0)
    q_near = inner_swap(q_own)
    q_relay = pair_swap(q_handed, "ctx", 1)
    rows_out, edge_rows, edge_conv, part_grad = kernel_call(
        conv_inner_body,
        (
            tile,
            shaped((wide, width), F32),
            shaped((2 * wide, 2 * width), F32),
            shaped((frames, 2 * width), F32),
        ),
        (chip, across, cotangent, cot_other, kernel, taps_other, q_first),
        3.1, "conv_inner", 1,
    )
    output_here, grad_here = kernel_call(
        conv_edge_body,
        (tile, both),
        (ends, ends_across, rim_near, rim_far, cotangent, cot_other, kernel, taps_other)
        + (rows_out, edge_rows, edge_conv, part_grad, q_near),
        1.4, "conv_edge", 1,
    )

    (grad_here,) = kernel_call(turn_body, (both,), (grad_here, q_relay), 0.1, "hand", 1)
    gi_core = pair_swap(grad_here, "mp", 1)
    partial, terms = kernel_call(
        upstream_own_body, (tile32, shaped((16, width), F32)), (grad_here, out_weight, lse), 0.5,
        "upstream_own",
    )
    message, delta = kernel_call(
        upstream_body, (noted, tile32), (gi_core, out_weight, att, partial, terms), 0.6, "upstream"
    )

    m_near, m_first, m_second = inner_swap(message), ring(message, 0), ring(message, 1)
    m_far = outer_swap(message)
    output, grad_input, grad_query = kernel_call(
        functools.partial(query_grad_body, scale),
        (tile, tile, tile),
        (q_own, kv, near, first, second, relay, message, lse, delta, output_here, grad_here),
        1.8, "query_grad", 0,
        [pltpu.VMEM((frames, width), BF16), pltpu.SemaphoreType.DMA((3,))], HBM,
    )
    key_part, value_part, late = kernel_call(
        functools.partial(key_part_body, scale),
        (tile32, tile32, tile32),
        (kv, q_own, q_relay, q_near, q_first, q_second, message, m_far, m_near, m_first),
        1.5, "key_part",
    )
    grad_key, grad_value = kernel_call(
        functools.partial(key_grad_body, scale),
        (tile, tile),
        (kv, q_second, m_second, late, key_part, value_part),
        1.0, "key_grad", 0,
        [pltpu.VMEM((frames, width), BF16)] * 2 + [pltpu.SemaphoreType.DMA((2,))], HBM,
    )
    return (output, grad_input, grad_query, grad_key, grad_value)


def solution(mesh):
    rows = P("ctx", "mp")
    return jax.shard_map(
        per_device,
        mesh=mesh,
        in_specs=(rows, rows, rows, rows, P("mp", None), P(None, "mp"), rows),
        out_specs=(rows,) * 5,
        check_vma=False,
    )
```

```python
import functools
import math

import jax
import jax.numpy as jnp
from jax import lax
from jax.experimental import pallas as pl
from jax.experimental.pallas import tpu as pltpu
from jax.sharding import PartitionSpec as P

HDIM = 128
F32 = jnp.float32
BF16 = jnp.bfloat16
CHUNK = 256
HALO = 16
NT = (((1,), (1,)), ((), ()))
NN = (((1,), (0,)), ((), ()))


def dot_nt(a, b):
    return lax.dot_general(a, b, NT, preferred_element_type=F32)


def dot_nn(a, b):
    return lax.dot_general(a, b, NN, preferred_element_type=F32)


def pair_swap(block, axis, bit):
    return lax.ppermute(block, axis, [(i, i ^ bit) for i in range(lax.axis_size(axis))])


def ring_routes(count):
    rise = [(i, i + 2) for i in range(0, count - 2, 2)] + [(count - 2, count - 1)]
    fall = [(i, i - 2) for i in range(count - 1, 2, -2)] + [(1, 0)]
    route = rise + fall
    return route, [(b, a) for a, b in route]


def ring(block, way):
    return lax.ppermute(block, "ctx", ring_routes(lax.axis_size("ctx"))[way])


def total_swap(block, partner_of):
    count, places = lax.axis_size("ctx"), lax.axis_size("mp")
    route = []
    for i in range(count):
        other = partner_of(i, count)
        for m in range(places):
            target = i * places + (m ^ 1) if other is None else other * places + m
            route.append((i * places + m, target))
    return lax.ppermute(block, ("ctx", "mp"), route)


def inner_swap(block):
    return total_swap(block, lambda i, count: i ^ 1 if 2 <= i < count - 2 else None)


def outer_swap(block):
    return total_swap(block, lambda i, count: ((i + 1) ^ 1) - 1 if 0 < i < count - 1 else None)


VMEM = pl.BlockSpec(memory_space=pltpu.VMEM)
ANY = pl.BlockSpec(memory_space=pl.ANY)
HBM = pl.BlockSpec(memory_space=pltpu.HBM)


def kernel_call(body, outs, args, micros, name, unread=0, scratch=(), out_space=VMEM):
    return pl.pallas_call(
        body,
        out_shape=outs,
        in_specs=[VMEM] * (len(args) - unread) + [ANY] * unread,
        out_specs=tuple(out_space for _ in outs),
        scratch_shapes=scratch,
        compiler_params=pltpu.CompilerParams(vmem_limit_bytes=24 * 1024 * 1024),
        cost_estimate=pl.CostEstimate(
            flops=0, bytes_accessed=int(micros * 3.69e6), transcendentals=0
        ),
        name=name,
    )(*args)


def shaped(shape, dtype):
    return jax.ShapeDtypeStruct(shape, dtype)


def is_even():
    return lax.axis_index("ctx") % 2 == 0


def near_swapped():
    block = lax.axis_index("ctx")
    return (block >= 2) & (block < lax.axis_size("ctx") - 2)


def far_there():
    block = lax.axis_index("ctx")
    return jnp.where(is_even(), block >= 2, block < lax.axis_size("ctx") - 2)


def bias_of(there):
    return jnp.where(there, jnp.float32(0.0), jnp.float32(-jnp.inf))


def columns(width):
    return [slice(c, c + HDIM) for c in range(0, width, HDIM)]


def stacked(blocks, rows, cols):
    return jnp.concatenate([block[rows, cols] for block in blocks], axis=0)


def with_ones(values):
    return jnp.concatenate([values, jnp.ones_like(values)], axis=1)


def by_block(scores, biases, stats=None):
    parts = []
    for b, bias in enumerate(biases):
        part = scores[:, b * HDIM : (b + 1) * HDIM]
        if stats is not None:
            part = part - stats[b]
        parts.append(part if bias is None else part + bias)
    return jnp.concatenate(parts, axis=1)


def tile_of(wide):
    lane = lax.broadcasted_iota(jnp.int32, (wide[0].shape[0], HDIM), 1)
    tile = jnp.zeros((wide[0].shape[0], HDIM), F32)
    for h, part in enumerate(wide):
        tile = jnp.where(lane == h, part, tile)
    return tile


def term_rows(row, first):
    at = lax.broadcasted_iota(jnp.int32, (16, row.shape[1]), 0)
    block = jnp.zeros((16, row.shape[1]), F32)
    for k in range(3):
        term = row.astype(BF16).astype(F32)
        row = row - term
        block = jnp.where(at == first + k, term, block)
    return block


def stat_terms(wide, first):
    rows = tile_of(wide).T
    return jnp.concatenate([term_rows(rows[h : h + 1], first) for h in range(len(wide))], axis=1)


def stat_rows(message, frames, which, cols):
    terms = message[frames : frames + 16, cols].astype(F32)
    at = 3 * which
    return terms[at : at + 1] + terms[at + 1 : at + 2] + terms[at + 2 : at + 3]


def weight_columns(weight, flip):
    width = weight.shape[0]
    at = (lax.axis_index("mp") ^ flip) * width
    return weight[:, pl.ds(pl.multiple_of(at, 128), width)]


def hand_body(block, q, seen, copy, q_copy):
    copy[...] = block[...]
    q_copy[...] = q[...]


def split_body(joined, seen, *parts):
    frames = parts[0].shape[0]
    for k, part in enumerate(parts):
        part[...] = joined[k * frames : (k + 1) * frames, :]


def forward_body(scale, q, own, near, first, second, *refs):
    sums, tops, totals = refs[-3:]
    frames, width = q.shape
    heads = columns(width)
    blocks = (near, own, first, second)
    biases = (bias_of(near_swapped()), None, None, None)
    keys, values = slice(0, frames), slice(frames, 2 * frames)
    scores = [dot_nt(q[:, c], stacked(blocks, keys, c)) * scale for c in heads]
    scores = [by_block(s, biases) for s in scores]
    top = [jnp.max(s, axis=1, keepdims=True) for s in scores]
    probs = [jnp.exp(s - t).astype(BF16) for s, t in zip(scores, top)]
    summed = [dot_nn(p, with_ones(stacked(blocks, values, c))) for p, c in zip(probs, heads)]
    for c, t, s in zip(heads, top, summed):
        tops[:, c] = jnp.broadcast_to(t, (frames, HDIM))
        sums[:, c] = s[:, 0:HDIM]
        totals[:, c] = s[:, HDIM:]


def project_body(scale, q, relay, sums, tops, totals, weight, att, lse, send, keep):
    frames, width = q.shape
    heads = columns(width)
    bias = bias_of(far_there())
    scores = [dot_nt(q[:, c], relay[0:frames, c]) * scale + bias for c in heads]
    before = [tops[:, c] for c in heads]
    top = [jnp.maximum(b, jnp.max(s, axis=1, keepdims=True)) for b, s in zip(before, scores)]
    shrink = [jnp.exp(b - t) for b, t in zip(before, top)]
    probs = [jnp.exp(s - t).astype(BF16) for s, t in zip(scores, top)]
    late = [dot_nn(p, with_ones(relay[frames : 2 * frames, c])) for p, c in zip(probs, heads)]
    total = [totals[:, c] * k + s[:, HDIM:] for c, k, s in zip(heads, shrink, late)]
    summed = [sums[:, c] * k + s[:, 0:HDIM] for c, k, s in zip(heads, shrink, late)]
    attended = jnp.concatenate([(s * (1.0 / t)).astype(BF16) for s, t in zip(summed, total)], axis=1)
    sent = [dot_nn(attended, weight_columns(weight, flip)).astype(BF16) for flip in (1, 3)]
    kept = [dot_nn(attended, weight_columns(weight, flip)).astype(BF16) for flip in (0, 2)]
    logs = [t + jnp.log(n) for t, n in zip(top, total)]
    att[...] = attended
    send[...] = jnp.concatenate(sent, axis=1)
    keep[...] = jnp.concatenate(kept, axis=1)
    for c, part in zip(heads, logs):
        lse[:, c] = part


def pass_body(send, seen_a, seen_b, send_copy):
    send_copy[...] = send[...]


def join_body(keep, core, inputs, cot, cot_other, q, chip, rim_near, rim_far, q_copy):
    frames, width = inputs.shape
    wide = 2 * HALO
    even = is_even()
    for cols, rows, cots in (
        (slice(0, width), inputs[...].astype(F32), cot),
        (slice(width, 2 * width), 0.0, cot_other),
    ):
        total = (rows + (keep[:, cols].astype(F32) + core[:, cols].astype(F32))).astype(BF16)
        for at, first, last in (
            (slice(0, wide), total[0:wide], total[frames - wide :]),
            (slice(wide, wide + HALO), cots[0:HALO, :], cots[frames - HALO : frames, :]),
        ):
            first, last = first.astype(F32), last.astype(F32)
            rim_near[at, cols] = jnp.where(even, last, first).astype(BF16)
            rim_far[at, cols] = jnp.where(even, first, last).astype(BF16)
        chip[:, cols] = total
    q_copy[...] = q[...]


def stack_body(rim_near, rim_far, q, ends, q_copy):
    wide = 2 * HALO
    ends[0:wide, :] = rim_near[0:wide, :]
    ends[wide : 2 * wide, :] = rim_far[0:wide, :]
    q_copy[...] = q[...]


def summed(share, across, rows, cols, width):
    back = slice((cols.start + width) % (2 * width), (cols.stop - 1 + width) % (2 * width) + 1)
    total = share[rows, cols].astype(F32) + across[rows, back].astype(F32)
    return total.astype(BF16).astype(F32)


def tiles_of(rows):
    return [rows[at : at + 8] for at in range(0, rows.shape[0], 8)]


def shifted_sum(tiles, taps_of, count):
    at = lax.broadcasted_iota(jnp.int32, (8, CHUNK), 0)
    sums = [None] * (count // 8)

    def add(k, term):
        sums[k] = term if sums[k] is None else sums[k] + term

    for b in range(8):
        parts = []
        for k in range(count // 8 + (b > 0)):
            part = None
            for a in range(4):
                tap = taps_of(8 * a + b)
                if tap is None or tiles[k + a] is None:
                    continue
                term = tap * tiles[k + a]
                part = term if part is None else part + term
            parts.append(part if part is None or b == 0 else pltpu.roll(part, 8 - b, 0))
        for k in range(count // 8):
            if b == 0:
                if parts[k] is not None:
                    add(k, parts[k])
            elif parts[k] is not None and parts[k + 1] is not None:
                add(k, jnp.where(at < 8 - b, parts[k], parts[k + 1]))
            elif parts[k] is not None:
                add(k, jnp.where(at < 8 - b, parts[k], 0.0))
            elif parts[k + 1] is not None:
                add(k, jnp.where(at < 8 - b, 0.0, parts[k + 1]))
    zero = jnp.zeros((8, CHUNK), F32)
    return jnp.concatenate([zero if part is None else part for part in sums], axis=0)


def silu_parts(conv, cots):
    gate = 1.0 / (1.0 + jnp.exp(-conv))
    grad = cots * (gate + conv * gate * (1.0 - gate))
    return conv * gate, grad.astype(BF16).astype(F32)


def taps_forward(taps, count, cols):
    return lambda s: taps[s - 1 : s, cols] if 1 <= s <= count else None


def taps_backward(taps, count, cols):
    return lambda s: taps[count - s : count - s + 1, cols] if 1 <= s <= count else None


def conv_chunks(width, cot, cot_other, taps, taps_other):
    for c in range(0, 2 * width, CHUNK):
        own, cols = c < width, slice(c, c + CHUNK)
        local = cols if own else slice(cols.start - width, cols.stop - width)
        yield own, cols, local, cot if own else cot_other, taps if own else taps_other


def conv_inner_body(
    chip, across, cot, cot_other, taps, taps_other, seen, rows_out, edge_rows, edge_conv, part_grad
):
    frames, width = cot.shape
    wide, count = 2 * HALO, taps.shape[0]
    inner = slice(HALO, frames - HALO)
    none = [None] * (wide // 8)
    for own, cols, local, cots_of, tap in conv_chunks(width, cot, cot_other, taps, taps_other):
        rows = summed(chip, across, slice(0, frames), cols, width)
        cots = cots_of[:, local].astype(F32)
        conv = shifted_sum(
            none + tiles_of(rows) + none, taps_forward(tap, count, local), frames + wide
        )
        silu, grad = silu_parts(conv[wide:frames], cots[inner])
        back = shifted_sum(
            none + tiles_of(grad) + none, taps_backward(tap, count, local), frames
        )
        edge_conv[0:wide, cols] = conv[0:wide]
        edge_conv[wide : 2 * wide, cols] = conv[frames : frames + wide]
        if own:
            rows_out[inner, cols] = (rows[inner] + silu).astype(BF16)
            edge_rows[0:HALO, cols] = rows[0:HALO]
            edge_rows[HALO:wide, cols] = rows[frames - HALO :]
        part_grad[:, cols] = cots + back


def conv_edge_body(
    ends, ends_across, rim_near, rim_far, cot, cot_other, taps, taps_other,
    rows_in, edge_rows, edge_conv, part_grad, seen, output, grad_input,
):
    frames, width = cot.shape
    wide, count = 2 * HALO, taps.shape[0]
    even, far = is_even(), far_there()
    low, high = slice(0, HALO), slice(frames - HALO, frames)
    inner = slice(HALO, frames - HALO)
    none = [None] * (wide // 8)
    cots_of = slice(wide, wide + HALO)

    def sides(near, beyond):
        beyond = jnp.where(far, beyond, 0.0)
        return jnp.where(even, beyond, near), jnp.where(even, near, beyond)

    for own, cols, local, block, tap in conv_chunks(width, cot, cot_other, taps, taps_other):
        rows = summed(ends, ends_across, slice(0, 2 * wide), cols, width)
        row_low, row_high = sides(rows[0:wide], rows[wide:])
        cot_low, cot_high = sides(rim_near[cots_of, cols].astype(F32), rim_far[cots_of, cols].astype(F32))
        conv = edge_conv[:, cols] + shifted_sum(
            tiles_of(row_low) + none + tiles_of(row_high), taps_forward(tap, count, local), 2 * wide
        )
        first = block[low, local].astype(F32)
        last = block[high, local].astype(F32)
        cots = jnp.concatenate([cot_low, first, last, cot_high], axis=0)
        silu, grad = silu_parts(conv, cots)
        back = shifted_sum(
            tiles_of(grad[0:wide]) + none + tiles_of(grad[wide:]), taps_backward(tap, count, local), 2 * wide
        )
        part = part_grad[:, cols]
        grad_input[:, cols] = jnp.concatenate(
            [part[0:wide] + back[0:wide], part[wide : frames - wide], part[frames - wide :] + back[wide:]],
            axis=0,
        ).astype(BF16)
        if own:
            output[low, cols] = (edge_rows[0:HALO, cols] + silu[HALO:wide]).astype(BF16)
            output[inner, cols] = rows_in[inner, cols]
            output[high, cols] = (edge_rows[HALO:wide, cols] + silu[wide : wide + HALO]).astype(BF16)


def upstream_part(grads, weight, flips):
    width = weight.shape[0]
    return sum(
        dot_nt(grads[:, k * width : (k + 1) * width], weight_columns(weight, flip))
        for k, flip in enumerate(flips)
    )


def upstream_own_body(own, weight, lse, partial, terms):
    partial[...] = upstream_part(own, weight, (0, 2))
    terms[...] = stat_terms([lse[:, c] for c in columns(lse.shape[1])], 0)


def upstream_body(core, weight, att, partial, terms, message, delta):
    frames, width = att.shape
    heads = columns(width)
    up = (partial[...] + upstream_part(core, weight, (1, 3))).astype(BF16)
    products = [up[:, c].astype(F32) * att[:, c].astype(F32) for c in heads]
    deltas = [jnp.broadcast_to(jnp.sum(p, axis=1, keepdims=True), (frames, HDIM)) for p in products]
    message[0:frames, :] = up
    message[frames : frames + 16, :] = (terms[...] + stat_terms(deltas, 3)).astype(BF16)
    for c, part in zip(heads, deltas):
        delta[:, c] = part


def query_grad_body(
    scale, q, own, near, first, second, relay, message, lse, delta, output_here, grad_here,
    output, grad_input, grad_query, held, sems,
):
    writes = [
        pltpu.make_async_copy(output_here, output, sems.at[0]),
        pltpu.make_async_copy(grad_here.at[:, pl.ds(0, q.shape[1])], grad_input, sems.at[1]),
    ]
    for write in writes:
        write.start()
    frames, width = q.shape
    heads = columns(width)
    blocks = (near, own, first, second, relay)
    biases = (bias_of(near_swapped()), None, None, None, bias_of(far_there()))
    above, below = slice(0, frames), slice(frames, 2 * frames)
    keys = [stacked(blocks, above, c) for c in heads]
    scores = [dot_nt(q[:, c], k) * scale for c, k in zip(heads, keys)]
    dots = [dot_nt(message[0:frames, c], stacked(blocks, below, c)) for c in heads]
    probs = [jnp.exp(by_block(s, biases, [lse[:, c]] * 5)) for c, s in zip(heads, scores)]
    drops = [by_block(d, (None,) * 5, [delta[:, c]] * 5) for c, d in zip(heads, dots)]
    grads = [(p * d * scale).astype(BF16) for p, d in zip(probs, drops)]
    held[...] = jnp.concatenate([dot_nn(g, k).astype(BF16) for g, k in zip(grads, keys)], axis=1)
    writes.append(pltpu.make_async_copy(held, grad_query, sems.at[2]))
    writes[2].start()
    for write in writes:
        write.wait()


def key_part_body(scale, own, *refs):
    queries, messages, (key_part, value_part) = refs[0:4], refs[4:8], refs[8:10]
    frames = own.shape[0] // 2
    heads = columns(own.shape[1])
    above, below = slice(0, frames), slice(frames, 2 * frames)
    biases = (None, bias_of(near_swapped()), None, None)
    asks = [stacked(queries, above, c) for c in heads]
    ups = [stacked(messages, above, c) for c in heads]
    scores = [dot_nt(own[above, c], a) * scale for c, a in zip(heads, asks)]
    dots = [dot_nt(own[below, c], u) for c, u in zip(heads, ups)]
    logs = [[stat_rows(m, frames, 0, c) for m in messages] for c in heads]
    deltas = [[stat_rows(m, frames, 1, c) for m in messages] for c in heads]
    probs = [jnp.exp(by_block(s, biases, n)) for s, n in zip(scores, logs)]
    drops = [by_block(d, (None,) * 4, n) for d, n in zip(dots, deltas)]
    grads = [(p * d * scale).astype(BF16) for p, d in zip(probs, drops)]
    value_sums = [dot_nn(p.astype(BF16), u) for p, u in zip(probs, ups)]
    key_sums = [dot_nn(g, a) for g, a in zip(grads, asks)]
    for c, k, v in zip(heads, key_sums, value_sums):
        key_part[:, c] = k
        value_part[:, c] = v


def key_grad_body(
    scale, own, query, message, key_part, value_part, grad_key, grad_value, held_key, held_value, sems
):
    frames = own.shape[0] // 2
    heads = columns(own.shape[1])
    above, below = slice(0, frames), slice(frames, 2 * frames)
    ups = [message[above, c] for c in heads]
    bias = bias_of(far_there())
    scores = [dot_nt(own[above, c], query[:, c]) * scale + bias for c in heads]
    probs = [jnp.exp(s - stat_rows(message, frames, 0, c)) for s, c in zip(scores, heads)]
    dots = [dot_nt(own[below, c], u) for c, u in zip(heads, ups)]
    values = [value_part[:, c] + dot_nn(p.astype(BF16), u) for c, p, u in zip(heads, probs, ups)]
    held_value[...] = jnp.concatenate([v.astype(BF16) for v in values], axis=1)
    value_write = pltpu.make_async_copy(held_value, grad_value, sems.at[0])
    value_write.start()
    drops = [d - stat_rows(message, frames, 1, c) for c, d in zip(heads, dots)]
    grads = [(p * d * scale).astype(BF16) for p, d in zip(probs, drops)]
    keys = [key_part[:, c] + dot_nn(g, query[:, c]) for c, g in zip(heads, grads)]
    held_key[...] = jnp.concatenate([k.astype(BF16) for k in keys], axis=1)
    key_write = pltpu.make_async_copy(held_key, grad_key, sems.at[1])
    key_write.start()
    value_write.wait()
    key_write.wait()


def per_device(query_rows, key_rows, value_rows, inputs, out_weight, kernel, cotangent):
    frames, width = query_rows.shape
    wide = 2 * HALO
    scale = 1.0 / math.sqrt(HDIM)
    tile = shaped((frames, width), BF16)
    tile32 = shaped((frames, width), F32)
    rim = shaped((wide + HALO, 2 * width), BF16)
    both = shaped((frames, 2 * width), BF16)
    noted = shaped((frames + 16, width), BF16)

    zero = jnp.zeros((), BF16)
    kv = lax.pad(key_rows, zero, ((0, frames, 0), (0, 0, 0))) + lax.pad(
        value_rows, zero, ((frames, 0, 0), (0, 0, 0))
    )
    joined = sum(
        lax.pad(rows, zero, ((k * frames, (2 - k) * frames, 0), (0, 0, 0)))
        for k, rows in enumerate((query_rows, inputs, cotangent))
    )
    near, first, second = inner_swap(kv), ring(kv, 0), ring(kv, 1)
    relay = outer_swap(kv)
    cot_other = pair_swap(cotangent, "mp", 2)
    taps_other = pair_swap(kernel, "mp", 2)
    query, inputs, cotangent = kernel_call(
        split_body, (tile, tile, tile), (joined, second), 0.1, "split", 1
    )
    sums, tops, totals = kernel_call(
        functools.partial(forward_body, scale),
        (tile32, tile32, tile32),
        (query, kv, near, first, second),
        1.0, "forward",
    )
    att, lse, send, keep = kernel_call(
        functools.partial(project_body, scale),
        (tile, tile32, both, both),
        (query, relay, sums, tops, totals, out_weight),
        1.0, "project",
    )

    (send,) = kernel_call(pass_body, (both,), (send, cot_other, taps_other), 0.1, "pass", 2)
    core = pair_swap(send, "mp", 1)
    chip, rim_up, rim_down, q_own = kernel_call(
        join_body,
        (both, rim, rim, tile),
        (keep, core, inputs, cotangent, cot_other, query),
        0.2, "join",
    )
    across = pair_swap(chip, "mp", 2)
    rim_far = outer_swap(rim_down)
    rim_near = pair_swap(rim_up, "ctx", 1)
    ends, q_handed = kernel_call(
        stack_body,
        (shaped((2 * wide, 2 * width), BF16), tile),
        (rim_near, rim_far, query),
        0.1, "stack",
    )
    ends_across = pair_swap(ends, "mp", 2)
    q_first = ring(q_own, 0)
    q_near = inner_swap(q_own)
    q_second = ring(q_handed, 1)
    rows_out, edge_rows, edge_conv, part_grad = kernel_call(
        conv_inner_body,
        (
            tile,
            shaped((wide, width), F32),
            shaped((2 * wide, 2 * width), F32),
            shaped((frames, 2 * width), F32),
        ),
        (chip, across, cotangent, cot_other, kernel, taps_other, q_first),
        3.1, "conv_inner", 1,
    )
    output_here, grad_here = kernel_call(
        conv_edge_body,
        (tile, both),
        (ends, ends_across, rim_near, rim_far, cotangent, cot_other, kernel, taps_other)
        + (rows_out, edge_rows, edge_conv, part_grad, q_near),
        1.4, "conv_edge", 1,
    )

    grad_here, q_late = kernel_call(
        hand_body, (both, tile), (grad_here, query, q_second), 0.1, "hand", 1
    )
    q_relay = outer_swap(q_late)
    gi_core = pair_swap(grad_here, "mp", 1)
    partial, terms = kernel_call(
        upstream_own_body, (tile32, shaped((16, width), F32)), (grad_here, out_weight, lse), 0.5,
        "upstream_own",
    )
    message, delta = kernel_call(
        upstream_body, (noted, tile32), (gi_core, out_weight, att, partial, terms), 0.6, "upstream"
    )

    m_near, m_first, m_second = inner_swap(message), ring(message, 0), ring(message, 1)
    m_relay = outer_swap(message)
    output, grad_input, grad_query = kernel_call(
        functools.partial(query_grad_body, scale),
        (tile, tile, tile),
        (q_own, kv, near, first, second, relay, message, lse, delta, output_here, grad_here),
        1.8, "query_grad", 0,
        [pltpu.VMEM((frames, width), BF16), pltpu.SemaphoreType.DMA((3,))], HBM,
    )
    key_part, value_part = kernel_call(
        functools.partial(key_part_body, scale),
        (tile32, tile32),
        (kv, q_own, q_near, q_first, q_second, message, m_near, m_first, m_second),
        1.5, "key_part",
    )
    grad_key, grad_value = kernel_call(
        functools.partial(key_grad_body, scale),
        (tile, tile),
        (kv, q_relay, m_relay, key_part, value_part),
        1.0, "key_grad", 0,
        [pltpu.VMEM((frames, width), BF16)] * 2 + [pltpu.SemaphoreType.DMA((2,))], HBM,
    )
    return (output, grad_input, grad_query, grad_key, grad_value)


def solution(mesh):
    rows = P("ctx", "mp")
    return jax.shard_map(
        per_device,
        mesh=mesh,
        in_specs=(rows, rows, rows, rows, P("mp", None), P(None, "mp"), rows),
        out_specs=(rows,) * 5,
        check_vma=False,
    )
```

```python
import functools
import math

import jax
import jax.numpy as jnp
from jax import lax
from jax.experimental import pallas as pl
from jax.experimental.pallas import tpu as pltpu
from jax.sharding import PartitionSpec as P

HDIM = 128
F32 = jnp.float32
BF16 = jnp.bfloat16
CHUNK = 256
HALO = 16
NT = (((1,), (1,)), ((), ()))
NN = (((1,), (0,)), ((), ()))


def dot_nt(a, b):
    return lax.dot_general(a, b, NT, preferred_element_type=F32)


def dot_nn(a, b):
    return lax.dot_general(a, b, NN, preferred_element_type=F32)


def pair_swap(block, axis, bit):
    return lax.ppermute(block, axis, [(i, i ^ bit) for i in range(lax.axis_size(axis))])


def ring_routes(count):
    rise = [(i, i + 2) for i in range(0, count - 2, 2)] + [(count - 2, count - 1)]
    fall = [(i, i - 2) for i in range(count - 1, 2, -2)] + [(1, 0)]
    route = rise + fall
    return route, [(b, a) for a, b in route]


def ring(block, way):
    return lax.ppermute(block, "ctx", ring_routes(lax.axis_size("ctx"))[way])


def total_swap(block, partner_of):
    count, places = lax.axis_size("ctx"), lax.axis_size("mp")
    route = []
    for i in range(count):
        other = partner_of(i, count)
        for m in range(places):
            target = i * places + (m ^ 1) if other is None else other * places + m
            route.append((i * places + m, target))
    return lax.ppermute(block, ("ctx", "mp"), route)


def inner_swap(block):
    return total_swap(block, lambda i, count: i ^ 1 if 2 <= i < count - 2 else None)


def outer_swap(block):
    return total_swap(block, lambda i, count: ((i + 1) ^ 1) - 1 if 0 < i < count - 1 else None)


def window_of(block, before_relay=lambda second: second):
    second = ring(block, 1)
    first = ring(block, 0)
    near = inner_swap(block)
    second = before_relay(second)
    return near, first, second, pair_swap(second, "ctx", 1)


VMEM = pl.BlockSpec(memory_space=pltpu.VMEM)
ANY = pl.BlockSpec(memory_space=pl.ANY)
HBM = pl.BlockSpec(memory_space=pltpu.HBM)


def kernel_call(body, outs, args, micros, name, unread=0, scratch=(), out_space=VMEM):
    return pl.pallas_call(
        body,
        out_shape=outs,
        in_specs=[VMEM] * (len(args) - unread) + [ANY] * unread,
        out_specs=tuple(out_space for _ in outs),
        scratch_shapes=scratch,
        compiler_params=pltpu.CompilerParams(vmem_limit_bytes=24 * 1024 * 1024),
        cost_estimate=pl.CostEstimate(
            flops=0, bytes_accessed=int(micros * 3.69e6), transcendentals=0
        ),
        name=name,
    )(*args)


def shaped(shape, dtype):
    return jax.ShapeDtypeStruct(shape, dtype)


def is_even():
    return lax.axis_index("ctx") % 2 == 0


def near_swapped():
    block = lax.axis_index("ctx")
    return (block >= 2) & (block < lax.axis_size("ctx") - 2)


def far_there():
    block = lax.axis_index("ctx")
    return jnp.where(is_even(), block >= 2, block < lax.axis_size("ctx") - 2)


def bias_of(there):
    return jnp.where(there, jnp.float32(0.0), jnp.float32(-jnp.inf))


def columns(width):
    return [slice(c, c + HDIM) for c in range(0, width, HDIM)]


def stacked(blocks, rows, cols):
    return jnp.concatenate([block[rows, cols] for block in blocks], axis=0)


def with_ones(values):
    return jnp.concatenate([values, jnp.ones_like(values)], axis=1)


def by_block(scores, biases, stats=None):
    parts = []
    for b, bias in enumerate(biases):
        part = scores[:, b * HDIM : (b + 1) * HDIM]
        if stats is not None:
            part = part - stats[b]
        parts.append(part if bias is None else part + bias)
    return jnp.concatenate(parts, axis=1)


def tile_of(wide):
    lane = lax.broadcasted_iota(jnp.int32, (wide[0].shape[0], HDIM), 1)
    tile = jnp.zeros((wide[0].shape[0], HDIM), F32)
    for h, part in enumerate(wide):
        tile = jnp.where(lane == h, part, tile)
    return tile


def term_rows(row, first):
    at = lax.broadcasted_iota(jnp.int32, (16, row.shape[1]), 0)
    block = jnp.zeros((16, row.shape[1]), F32)
    for k in range(3):
        term = row.astype(BF16).astype(F32)
        row = row - term
        block = jnp.where(at == first + k, term, block)
    return block


def stat_terms(wide, first):
    rows = tile_of(wide).T
    return jnp.concatenate([term_rows(rows[h : h + 1], first) for h in range(len(wide))], axis=1)


def stat_rows(message, frames, which, cols):
    terms = message[frames : frames + 16, cols].astype(F32)
    at = 3 * which
    return terms[at : at + 1] + terms[at + 1 : at + 2] + terms[at + 2 : at + 3]


def weight_columns(weight, flip):
    width = weight.shape[0]
    at = (lax.axis_index("mp") ^ flip) * width
    return weight[:, pl.ds(pl.multiple_of(at, 128), width)]


def turn_body(block, *refs):
    refs[-1][...] = block[...]


def split_body(joined, seen, *parts):
    frames = parts[0].shape[0]
    for k, part in enumerate(parts):
        part[...] = joined[k * frames : (k + 1) * frames, :]


def forward_body(scale, q, own, near, first, second, *refs):
    sums, tops, totals = refs[-3:]
    frames, width = q.shape
    heads = columns(width)
    blocks = (near, own, first, second)
    biases = (bias_of(near_swapped()), None, None, None)
    keys, values = slice(0, frames), slice(frames, 2 * frames)
    scores = [dot_nt(q[:, c], stacked(blocks, keys, c)) * scale for c in heads]
    scores = [by_block(s, biases) for s in scores]
    top = [jnp.max(s, axis=1, keepdims=True) for s in scores]
    probs = [jnp.exp(s - t).astype(BF16) for s, t in zip(scores, top)]
    summed = [dot_nn(p, with_ones(stacked(blocks, values, c))) for p, c in zip(probs, heads)]
    for c, t, s in zip(heads, top, summed):
        tops[:, c] = jnp.broadcast_to(t, (frames, HDIM))
        sums[:, c] = s[:, 0:HDIM]
        totals[:, c] = s[:, HDIM:]


def project_body(scale, q, relay, sums, tops, totals, weight, att, lse, send):
    frames, width = q.shape
    heads = columns(width)
    bias = bias_of(far_there())
    scores = [dot_nt(q[:, c], relay[0:frames, c]) * scale + bias for c in heads]
    before = [tops[:, c] for c in heads]
    top = [jnp.maximum(b, jnp.max(s, axis=1, keepdims=True)) for b, s in zip(before, scores)]
    shrink = [jnp.exp(b - t) for b, t in zip(before, top)]
    probs = [jnp.exp(s - t).astype(BF16) for s, t in zip(scores, top)]
    late = [dot_nn(p, with_ones(relay[frames : 2 * frames, c])) for p, c in zip(probs, heads)]
    total = [totals[:, c] * k + s[:, HDIM:] for c, k, s in zip(heads, shrink, late)]
    summed = [sums[:, c] * k + s[:, 0:HDIM] for c, k, s in zip(heads, shrink, late)]
    attended = jnp.concatenate([(s * (1.0 / t)).astype(BF16) for s, t in zip(summed, total)], axis=1)
    sent = [dot_nn(attended, weight_columns(weight, flip)).astype(BF16) for flip in (1, 3)]
    logs = [t + jnp.log(n) for t, n in zip(top, total)]
    att[...] = attended
    send[...] = jnp.concatenate(sent, axis=1)
    for c, part in zip(heads, logs):
        lse[:, c] = part


def project_own_body(att, weight, keep):
    kept = [dot_nn(att[...], weight_columns(weight, flip)).astype(BF16) for flip in (0, 2)]
    keep[...] = jnp.concatenate(kept, axis=1)


def pass_body(send, seen_a, seen_b, send_copy):
    send_copy[...] = send[...]


def join_body(keep, core, inputs, cot, cot_other, q, chip, rim_near, rim_far, q_copy):
    frames, width = inputs.shape
    wide = 2 * HALO
    even = is_even()
    for cols, rows, cots in (
        (slice(0, width), inputs[...].astype(F32), cot),
        (slice(width, 2 * width), 0.0, cot_other),
    ):
        total = (rows + (keep[:, cols].astype(F32) + core[:, cols].astype(F32))).astype(BF16)
        for at, first, last in (
            (slice(0, wide), total[0:wide], total[frames - wide :]),
            (slice(wide, wide + HALO), cots[0:HALO, :], cots[frames - HALO : frames, :]),
        ):
            first, last = first.astype(F32), last.astype(F32)
            rim_near[at, cols] = jnp.where(even, last, first).astype(BF16)
            rim_far[at, cols] = jnp.where(even, first, last).astype(BF16)
        chip[:, cols] = total
    q_copy[...] = q[...]


def stack_body(rim_near, rim_far, q_second, ends, second_copy):
    wide = 2 * HALO
    ends[0:wide, :] = rim_near[0:wide, :]
    ends[wide : 2 * wide, :] = rim_far[0:wide, :]
    second_copy[...] = q_second[...]


def summed(share, across, rows, cols, width):
    back = slice((cols.start + width) % (2 * width), (cols.stop - 1 + width) % (2 * width) + 1)
    total = share[rows, cols].astype(F32) + across[rows, back].astype(F32)
    return total.astype(BF16).astype(F32)


def tiles_of(rows):
    return [rows[at : at + 8] for at in range(0, rows.shape[0], 8)]


def shifted_sum(tiles, taps_of, count):
    at = lax.broadcasted_iota(jnp.int32, (8, CHUNK), 0)
    sums = [None] * (count // 8)

    def add(k, term):
        sums[k] = term if sums[k] is None else sums[k] + term

    for b in range(8):
        parts = []
        for k in range(count // 8 + (b > 0)):
            part = None
            for a in range(4):
                tap = taps_of(8 * a + b)
                if tap is None or tiles[k + a] is None:
                    continue
                term = tap * tiles[k + a]
                part = term if part is None else part + term
            parts.append(part if part is None or b == 0 else pltpu.roll(part, 8 - b, 0))
        for k in range(count // 8):
            if b == 0:
                if parts[k] is not None:
                    add(k, parts[k])
            elif parts[k] is not None and parts[k + 1] is not None:
                add(k, jnp.where(at < 8 - b, parts[k], parts[k + 1]))
            elif parts[k] is not None:
                add(k, jnp.where(at < 8 - b, parts[k], 0.0))
            elif parts[k + 1] is not None:
                add(k, jnp.where(at < 8 - b, 0.0, parts[k + 1]))
    zero = jnp.zeros((8, CHUNK), F32)
    return jnp.concatenate([zero if part is None else part for part in sums], axis=0)


def silu_parts(conv, cots):
    gate = 1.0 / (1.0 + jnp.exp(-conv))
    grad = cots * (gate + conv * gate * (1.0 - gate))
    return conv * gate, grad.astype(BF16).astype(F32)


def taps_forward(taps, count, cols):
    return lambda s: taps[s - 1 : s, cols] if 1 <= s <= count else None


def taps_backward(taps, count, cols):
    return lambda s: taps[count - s : count - s + 1, cols] if 1 <= s <= count else None


def conv_chunks(width, cot, cot_other, taps, taps_other):
    for c in range(0, 2 * width, CHUNK):
        own, cols = c < width, slice(c, c + CHUNK)
        local = cols if own else slice(cols.start - width, cols.stop - width)
        yield own, cols, local, cot if own else cot_other, taps if own else taps_other


def conv_inner_body(
    chip, across, cot, cot_other, taps, taps_other, seen, rows_out, edge_rows, edge_conv, part_grad
):
    frames, width = cot.shape
    wide, count = 2 * HALO, taps.shape[0]
    inner = slice(HALO, frames - HALO)
    none = [None] * (wide // 8)
    for own, cols, local, cots_of, tap in conv_chunks(width, cot, cot_other, taps, taps_other):
        rows = summed(chip, across, slice(0, frames), cols, width)
        cots = cots_of[:, local].astype(F32)
        conv = shifted_sum(
            none + tiles_of(rows) + none, taps_forward(tap, count, local), frames + wide
        )
        silu, grad = silu_parts(conv[wide:frames], cots[inner])
        back = shifted_sum(
            none + tiles_of(grad) + none, taps_backward(tap, count, local), frames
        )
        edge_conv[0:wide, cols] = conv[0:wide]
        edge_conv[wide : 2 * wide, cols] = conv[frames : frames + wide]
        if own:
            rows_out[inner, cols] = (rows[inner] + silu).astype(BF16)
            edge_rows[0:HALO, cols] = rows[0:HALO]
            edge_rows[HALO:wide, cols] = rows[frames - HALO :]
        part_grad[:, cols] = cots + back


def conv_edge_body(
    ends, ends_across, rim_near, rim_far, cot, cot_other, taps, taps_other,
    rows_in, edge_rows, edge_conv, part_grad, seen, output, grad_input,
):
    frames, width = cot.shape
    wide, count = 2 * HALO, taps.shape[0]
    even, far = is_even(), far_there()
    low, high = slice(0, HALO), slice(frames - HALO, frames)
    inner = slice(HALO, frames - HALO)
    none = [None] * (wide // 8)
    cots_of = slice(wide, wide + HALO)

    def sides(near, beyond):
        beyond = jnp.where(far, beyond, 0.0)
        return jnp.where(even, beyond, near), jnp.where(even, near, beyond)

    for own, cols, local, block, tap in conv_chunks(width, cot, cot_other, taps, taps_other):
        rows = summed(ends, ends_across, slice(0, 2 * wide), cols, width)
        row_low, row_high = sides(rows[0:wide], rows[wide:])
        cot_low, cot_high = sides(rim_near[cots_of, cols].astype(F32), rim_far[cots_of, cols].astype(F32))
        conv = edge_conv[:, cols] + shifted_sum(
            tiles_of(row_low) + none + tiles_of(row_high), taps_forward(tap, count, local), 2 * wide
        )
        first = block[low, local].astype(F32)
        last = block[high, local].astype(F32)
        cots = jnp.concatenate([cot_low, first, last, cot_high], axis=0)
        silu, grad = silu_parts(conv, cots)
        back = shifted_sum(
            tiles_of(grad[0:wide]) + none + tiles_of(grad[wide:]), taps_backward(tap, count, local), 2 * wide
        )
        part = part_grad[:, cols]
        grad_input[:, cols] = jnp.concatenate(
            [part[0:wide] + back[0:wide], part[wide : frames - wide], part[frames - wide :] + back[wide:]],
            axis=0,
        ).astype(BF16)
        if own:
            output[low, cols] = (edge_rows[0:HALO, cols] + silu[HALO:wide]).astype(BF16)
            output[inner, cols] = rows_in[inner, cols]
            output[high, cols] = (edge_rows[HALO:wide, cols] + silu[wide : wide + HALO]).astype(BF16)


def upstream_part(grads, weight, flips):
    width = weight.shape[0]
    return sum(
        dot_nt(grads[:, k * width : (k + 1) * width], weight_columns(weight, flip))
        for k, flip in enumerate(flips)
    )


def upstream_own_body(own, weight, lse, partial, terms):
    partial[...] = upstream_part(own, weight, (0, 2))
    terms[...] = stat_terms([lse[:, c] for c in columns(lse.shape[1])], 0)


def upstream_body(core, weight, att, partial, terms, message, delta):
    frames, width = att.shape
    heads = columns(width)
    up = (partial[...] + upstream_part(core, weight, (1, 3))).astype(BF16)
    products = [up[:, c].astype(F32) * att[:, c].astype(F32) for c in heads]
    deltas = [jnp.broadcast_to(jnp.sum(p, axis=1, keepdims=True), (frames, HDIM)) for p in products]
    message[0:frames, :] = up
    message[frames : frames + 16, :] = (terms[...] + stat_terms(deltas, 3)).astype(BF16)
    for c, part in zip(heads, deltas):
        delta[:, c] = part


def query_grad_body(
    scale, q, own, near, first, second, relay, message, lse, delta, output_here, grad_here,
    output, grad_input, grad_query, held, sems,
):
    writes = [
        pltpu.make_async_copy(output_here, output, sems.at[0]),
        pltpu.make_async_copy(grad_here.at[:, pl.ds(0, q.shape[1])], grad_input, sems.at[1]),
    ]
    for write in writes:
        write.start()
    frames, width = q.shape
    heads = columns(width)
    blocks = (near, own, first, second, relay)
    biases = (bias_of(near_swapped()), None, None, None, bias_of(far_there()))
    above, below = slice(0, frames), slice(frames, 2 * frames)
    keys = [stacked(blocks, above, c) for c in heads]
    scores = [dot_nt(q[:, c], k) * scale for c, k in zip(heads, keys)]
    dots = [dot_nt(message[0:frames, c], stacked(blocks, below, c)) for c in heads]
    probs = [jnp.exp(by_block(s, biases, [lse[:, c]] * 5)) for c, s in zip(heads, scores)]
    drops = [by_block(d, (None,) * 5, [delta[:, c]] * 5) for c, d in zip(heads, dots)]
    grads = [(p * d * scale).astype(BF16) for p, d in zip(probs, drops)]
    held[...] = jnp.concatenate([dot_nn(g, k).astype(BF16) for g, k in zip(grads, keys)], axis=1)
    writes.append(pltpu.make_async_copy(held, grad_query, sems.at[2]))
    writes[2].start()
    for write in writes:
        write.wait()


def key_part_body(scale, own, *refs):
    queries, late_query, messages, (key_part, value_part, late) = refs[0:4], refs[4], refs[5:9], refs[9:12]
    frames = own.shape[0] // 2
    heads = columns(own.shape[1])
    above, below = slice(0, frames), slice(frames, 2 * frames)
    biases = (None, bias_of(near_swapped()), None, None)
    asks = [stacked(queries, above, c) for c in heads]
    ups = [stacked(messages, above, c) for c in heads]
    scores = [dot_nt(own[above, c], a) * scale for c, a in zip(heads, asks)]
    dots = [dot_nt(own[below, c], u) for c, u in zip(heads, ups)]
    last = [dot_nt(own[above, c], late_query[:, c]) * scale + bias_of(far_there()) for c in heads]
    logs = [[stat_rows(m, frames, 0, c) for m in messages] for c in heads]
    deltas = [[stat_rows(m, frames, 1, c) for m in messages] for c in heads]
    probs = [jnp.exp(by_block(s, biases, n)) for s, n in zip(scores, logs)]
    drops = [by_block(d, (None,) * 4, n) for d, n in zip(dots, deltas)]
    grads = [(p * d * scale).astype(BF16) for p, d in zip(probs, drops)]
    value_sums = [dot_nn(p.astype(BF16), u) for p, u in zip(probs, ups)]
    key_sums = [dot_nn(g, a) for g, a in zip(grads, asks)]
    for c, k, v, s in zip(heads, key_sums, value_sums, last):
        key_part[:, c] = k
        value_part[:, c] = v
        late[:, c] = s


def key_grad_body(
    scale, own, query, message, late, key_part, value_part, grad_key, grad_value, held_key, held_value, sems
):
    frames = own.shape[0] // 2
    heads = columns(own.shape[1])
    above, below = slice(0, frames), slice(frames, 2 * frames)
    ups = [message[above, c] for c in heads]
    probs = [jnp.exp(late[:, c] - stat_rows(message, frames, 0, c)) for c in heads]
    dots = [dot_nt(own[below, c], u) for c, u in zip(heads, ups)]
    values = [value_part[:, c] + dot_nn(p.astype(BF16), u) for c, p, u in zip(heads, probs, ups)]
    held_value[...] = jnp.concatenate([v.astype(BF16) for v in values], axis=1)
    value_write = pltpu.make_async_copy(held_value, grad_value, sems.at[0])
    value_write.start()
    drops = [d - stat_rows(message, frames, 1, c) for c, d in zip(heads, dots)]
    grads = [(p * d * scale).astype(BF16) for p, d in zip(probs, drops)]
    keys = [key_part[:, c] + dot_nn(g, query[:, c]) for c, g in zip(heads, grads)]
    held_key[...] = jnp.concatenate([k.astype(BF16) for k in keys], axis=1)
    key_write = pltpu.make_async_copy(held_key, grad_key, sems.at[1])
    key_write.start()
    value_write.wait()
    key_write.wait()


def per_device(query_rows, key_rows, value_rows, inputs, out_weight, kernel, cotangent):
    frames, width = query_rows.shape
    wide = 2 * HALO
    scale = 1.0 / math.sqrt(HDIM)
    tile = shaped((frames, width), BF16)
    tile32 = shaped((frames, width), F32)
    rim = shaped((wide + HALO, 2 * width), BF16)
    both = shaped((frames, 2 * width), BF16)
    noted = shaped((frames + 16, width), BF16)

    zero = jnp.zeros((), BF16)
    kv = lax.pad(key_rows, zero, ((0, frames, 0), (0, 0, 0))) + lax.pad(
        value_rows, zero, ((frames, 0, 0), (0, 0, 0))
    )
    joined = sum(
        lax.pad(rows, zero, ((k * frames, (2 - k) * frames, 0), (0, 0, 0)))
        for k, rows in enumerate((query_rows, inputs, cotangent))
    )
    cot_other = pair_swap(cotangent, "mp", 2)
    near, first, second, relay = window_of(
        kv,
        lambda second: kernel_call(
            turn_body, (shaped(kv.shape, BF16),), (second, joined, cot_other), 0.1, "turn", 2
        )[0],
    )
    taps_other = pair_swap(kernel, "mp", 2)
    query, inputs, cotangent = kernel_call(
        split_body, (tile, tile, tile), (joined, second), 0.1, "split", 1
    )
    q_second = ring(query, 1)
    sums, tops, totals = kernel_call(
        functools.partial(forward_body, scale),
        (tile32, tile32, tile32),
        (query, kv, near, first, second),
        1.0, "forward",
    )
    att, lse, send = kernel_call(
        functools.partial(project_body, scale),
        (tile, tile32, both),
        (query, relay, sums, tops, totals, out_weight),
        1.0, "project",
    )

    (send,) = kernel_call(pass_body, (both,), (send, taps_other, q_second), 0.1, "pass", 2)
    core = pair_swap(send, "mp", 1)
    (keep,) = kernel_call(project_own_body, (both,), (att, out_weight), 0.4, "project_own")
    chip, rim_up, rim_down, q_own = kernel_call(
        join_body,
        (both, rim, rim, tile),
        (keep, core, inputs, cotangent, cot_other, query),
        0.2, "join",
    )
    across = pair_swap(chip, "mp", 2)
    rim_far = outer_swap(rim_down)
    rim_near = pair_swap(rim_up, "ctx", 1)
    ends, q_handed = kernel_call(
        stack_body,
        (shaped((2 * wide, 2 * width), BF16), tile),
        (rim_near, rim_far, q_second),
        0.1, "stack",
    )
    ends_across = pair_swap(ends, "mp", 2)
    q_first = ring(q_own, 0)
    q_near = inner_swap(q_own)
    q_relay = pair_swap(q_handed, "ctx", 1)
    rows_out, edge_rows, edge_conv, part_grad = kernel_call(
        conv_inner_body,
        (
            tile,
            shaped((wide, width), F32),
            shaped((2 * wide, 2 * width), F32),
            shaped((frames, 2 * width), F32),
        ),
        (chip, across, cotangent, cot_other, kernel, taps_other, q_first),
        3.1, "conv_inner", 1,
    )
    output_here, grad_here = kernel_call(
        conv_edge_body,
        (tile, both),
        (ends, ends_across, rim_near, rim_far, cotangent, cot_other, kernel, taps_other)
        + (rows_out, edge_rows, edge_conv, part_grad, q_near),
        1.4, "conv_edge", 1,
    )

    (grad_here,) = kernel_call(turn_body, (both,), (grad_here, q_relay), 0.1, "hand", 1)
    gi_core = pair_swap(grad_here, "mp", 1)
    partial, terms = kernel_call(
        upstream_own_body, (tile32, shaped((16, width), F32)), (grad_here, out_weight, lse), 0.5,
        "upstream_own",
    )
    message, delta = kernel_call(
        upstream_body, (noted, tile32), (gi_core, out_weight, att, partial, terms), 0.6, "upstream"
    )

    m_near, m_first, m_second = inner_swap(message), ring(message, 0), ring(message, 1)
    m_relay = outer_swap(message)
    output, grad_input, grad_query = kernel_call(
        functools.partial(query_grad_body, scale),
        (tile, tile, tile),
        (q_own, kv, near, first, second, relay, message, lse, delta, output_here, grad_here),
        1.8, "query_grad", 0,
        [pltpu.VMEM((frames, width), BF16), pltpu.SemaphoreType.DMA((3,))], HBM,
    )
    key_part, value_part, late = kernel_call(
        functools.partial(key_part_body, scale),
        (tile32, tile32, tile32),
        (kv, q_own, q_near, q_first, q_second, q_relay, message, m_near, m_first, m_second),
        1.5, "key_part",
    )
    grad_key, grad_value = kernel_call(
        functools.partial(key_grad_body, scale),
        (tile, tile),
        (kv, q_relay, m_relay, late, key_part, value_part),
        1.0, "key_grad", 0,
        [pltpu.VMEM((frames, width), BF16)] * 2 + [pltpu.SemaphoreType.DMA((2,))], HBM,
    )
    return (output, grad_input, grad_query, grad_key, grad_value)


def solution(mesh):
    rows = P("ctx", "mp")
    return jax.shard_map(
        per_device,
        mesh=mesh,
        in_specs=(rows, rows, rows, rows, P("mp", None), P(None, "mp"), rows),
        out_specs=(rows,) * 5,
        check_vma=False,
    )
```

```python
import functools
import math

import jax
import jax.numpy as jnp
from jax import lax
from jax.experimental import pallas as pl
from jax.experimental.pallas import tpu as pltpu
from jax.sharding import PartitionSpec as P

HDIM = 128
F32 = jnp.float32
BF16 = jnp.bfloat16
CHUNK = 256
HALO = 16
NT = (((1,), (1,)), ((), ()))
NN = (((1,), (0,)), ((), ()))


def dot_nt(a, b):
    return lax.dot_general(a, b, NT, preferred_element_type=F32)


def dot_nn(a, b):
    return lax.dot_general(a, b, NN, preferred_element_type=F32)


def pair_swap(block, axis, bit):
    return lax.ppermute(block, axis, [(i, i ^ bit) for i in range(lax.axis_size(axis))])


def ring_routes(count):
    rise = [(i, i + 2) for i in range(0, count - 2, 2)] + [(count - 2, count - 1)]
    fall = [(i, i - 2) for i in range(count - 1, 2, -2)] + [(1, 0)]
    route = rise + fall
    return route, [(b, a) for a, b in route]


def ring(block, way):
    return lax.ppermute(block, "ctx", ring_routes(lax.axis_size("ctx"))[way])


def total_swap(block, partner_of):
    count, places = lax.axis_size("ctx"), lax.axis_size("mp")
    route = []
    for i in range(count):
        other = partner_of(i, count)
        for m in range(places):
            target = i * places + (m ^ 1) if other is None else other * places + m
            route.append((i * places + m, target))
    return lax.ppermute(block, ("ctx", "mp"), route)


def inner_swap(block):
    return total_swap(block, lambda i, count: i ^ 1 if 2 <= i < count - 2 else None)


def outer_swap(block):
    return total_swap(block, lambda i, count: ((i + 1) ^ 1) - 1 if 0 < i < count - 1 else None)


def window_of(block, before_relay=lambda second: second):
    second = ring(block, 1)
    first = ring(block, 0)
    near = inner_swap(block)
    second = before_relay(second)
    return near, first, second, pair_swap(second, "ctx", 1)


VMEM = pl.BlockSpec(memory_space=pltpu.VMEM)
ANY = pl.BlockSpec(memory_space=pl.ANY)
HBM = pl.BlockSpec(memory_space=pltpu.HBM)


def kernel_call(body, outs, args, micros, name, unread=0, scratch=(), out_space=VMEM):
    return pl.pallas_call(
        body,
        out_shape=outs,
        in_specs=[VMEM] * (len(args) - unread) + [ANY] * unread,
        out_specs=tuple(out_space for _ in outs),
        scratch_shapes=scratch,
        compiler_params=pltpu.CompilerParams(vmem_limit_bytes=24 * 1024 * 1024),
        cost_estimate=pl.CostEstimate(
            flops=0, bytes_accessed=int(micros * 3.69e6), transcendentals=0
        ),
        name=name,
    )(*args)


def shaped(shape, dtype):
    return jax.ShapeDtypeStruct(shape, dtype)


def is_even():
    return lax.axis_index("ctx") % 2 == 0


def near_swapped():
    block = lax.axis_index("ctx")
    return (block >= 2) & (block < lax.axis_size("ctx") - 2)


def far_there():
    block = lax.axis_index("ctx")
    return jnp.where(is_even(), block >= 2, block < lax.axis_size("ctx") - 2)


def bias_of(there):
    return jnp.where(there, jnp.float32(0.0), jnp.float32(-jnp.inf))


def columns(width):
    return [slice(c, c + HDIM) for c in range(0, width, HDIM)]


def stacked(blocks, rows, cols):
    return jnp.concatenate([block[rows, cols] for block in blocks], axis=0)


def with_ones(values):
    return jnp.concatenate([values, jnp.ones_like(values)], axis=1)


def by_block(scores, biases, stats=None):
    parts = []
    for b, bias in enumerate(biases):
        part = scores[:, b * HDIM : (b + 1) * HDIM]
        if stats is not None:
            part = part - stats[b]
        parts.append(part if bias is None else part + bias)
    return jnp.concatenate(parts, axis=1)


def tile_of(wide):
    lane = lax.broadcasted_iota(jnp.int32, (wide[0].shape[0], HDIM), 1)
    tile = jnp.zeros((wide[0].shape[0], HDIM), F32)
    for h, part in enumerate(wide):
        tile = jnp.where(lane == h, part, tile)
    return tile


def term_rows(row, first):
    at = lax.broadcasted_iota(jnp.int32, (16, row.shape[1]), 0)
    block = jnp.zeros((16, row.shape[1]), F32)
    for k in range(3):
        term = row.astype(BF16).astype(F32)
        row = row - term
        block = jnp.where(at == first + k, term, block)
    return block


def stat_terms(wide, first):
    rows = tile_of(wide).T
    return jnp.concatenate([term_rows(rows[h : h + 1], first) for h in range(len(wide))], axis=1)


def stat_rows(message, frames, which, cols):
    terms = message[frames : frames + 16, cols].astype(F32)
    at = 3 * which
    return terms[at : at + 1] + terms[at + 1 : at + 2] + terms[at + 2 : at + 3]


def weight_columns(weight, flip):
    width = weight.shape[0]
    at = (lax.axis_index("mp") ^ flip) * width
    return weight[:, pl.ds(pl.multiple_of(at, 128), width)]


def turn_body(block, seen, copy):
    copy[...] = block[...]


def split_body(joined, seen, *parts):
    frames = parts[0].shape[0]
    for k, part in enumerate(parts):
        part[...] = joined[k * frames : (k + 1) * frames, :]


def forward_body(scale, q, own, near, first, second, *refs):
    sums, tops, totals = refs[-3:]
    frames, width = q.shape
    heads = columns(width)
    blocks = (near, own, first, second)
    biases = (bias_of(near_swapped()), None, None, None)
    keys, values = slice(0, frames), slice(frames, 2 * frames)
    scores = [dot_nt(q[:, c], stacked(blocks, keys, c)) * scale for c in heads]
    scores = [by_block(s, biases) for s in scores]
    top = [jnp.max(s, axis=1, keepdims=True) for s in scores]
    probs = [jnp.exp(s - t).astype(BF16) for s, t in zip(scores, top)]
    summed = [dot_nn(p, with_ones(stacked(blocks, values, c))) for p, c in zip(probs, heads)]
    for c, t, s in zip(heads, top, summed):
        tops[:, c] = jnp.broadcast_to(t, (frames, HDIM))
        sums[:, c] = s[:, 0:HDIM]
        totals[:, c] = s[:, HDIM:]


def project_body(scale, q, relay, sums, tops, totals, weight, att, lse, send):
    frames, width = q.shape
    heads = columns(width)
    bias = bias_of(far_there())
    scores = [dot_nt(q[:, c], relay[0:frames, c]) * scale + bias for c in heads]
    before = [tops[:, c] for c in heads]
    top = [jnp.maximum(b, jnp.max(s, axis=1, keepdims=True)) for b, s in zip(before, scores)]
    shrink = [jnp.exp(b - t) for b, t in zip(before, top)]
    probs = [jnp.exp(s - t).astype(BF16) for s, t in zip(scores, top)]
    late = [dot_nn(p, with_ones(relay[frames : 2 * frames, c])) for p, c in zip(probs, heads)]
    total = [totals[:, c] * k + s[:, HDIM:] for c, k, s in zip(heads, shrink, late)]
    summed = [sums[:, c] * k + s[:, 0:HDIM] for c, k, s in zip(heads, shrink, late)]
    attended = jnp.concatenate([(s * (1.0 / t)).astype(BF16) for s, t in zip(summed, total)], axis=1)
    sent = [dot_nn(attended, weight_columns(weight, flip)).astype(BF16) for flip in (1, 3)]
    logs = [t + jnp.log(n) for t, n in zip(top, total)]
    att[...] = attended
    send[...] = jnp.concatenate(sent, axis=1)
    for c, part in zip(heads, logs):
        lse[:, c] = part


def project_own_body(att, weight, keep):
    kept = [dot_nn(att[...], weight_columns(weight, flip)).astype(BF16) for flip in (0, 2)]
    keep[...] = jnp.concatenate(kept, axis=1)


def pass_body(send, q_second, seen_a, seen_b, send_copy, second_copy):
    send_copy[...] = send[...]
    second_copy[...] = q_second[...]


def join_body(keep, core, inputs, cot, cot_other, q, chip, rim_near, rim_far, q_copy):
    frames, width = inputs.shape
    wide = 2 * HALO
    even = is_even()
    for cols, rows, cots in (
        (slice(0, width), inputs[...].astype(F32), cot),
        (slice(width, 2 * width), 0.0, cot_other),
    ):
        total = (rows + (keep[:, cols].astype(F32) + core[:, cols].astype(F32))).astype(BF16)
        for at, first, last in (
            (slice(0, wide), total[0:wide], total[frames - wide :]),
            (slice(wide, wide + HALO), cots[0:HALO, :], cots[frames - HALO : frames, :]),
        ):
            first, last = first.astype(F32), last.astype(F32)
            rim_near[at, cols] = jnp.where(even, last, first).astype(BF16)
            rim_far[at, cols] = jnp.where(even, first, last).astype(BF16)
        chip[:, cols] = total
    q_copy[...] = q[...]


def stack_body(rim_near, rim_far, q_second, ends, second_copy):
    wide = 2 * HALO
    ends[0:wide, :] = rim_near[0:wide, :]
    ends[wide : 2 * wide, :] = rim_far[0:wide, :]
    second_copy[...] = q_second[...]


def summed(share, across, rows, cols, width):
    back = slice((cols.start + width) % (2 * width), (cols.stop - 1 + width) % (2 * width) + 1)
    total = share[rows, cols].astype(F32) + across[rows, back].astype(F32)
    return total.astype(BF16).astype(F32)


def tiles_of(rows):
    return [rows[at : at + 8] for at in range(0, rows.shape[0], 8)]


def shifted_sum(tiles, taps_of, count):
    at = lax.broadcasted_iota(jnp.int32, (8, CHUNK), 0)
    sums = [None] * (count // 8)

    def add(k, term):
        sums[k] = term if sums[k] is None else sums[k] + term

    for b in range(8):
        parts = []
        for k in range(count // 8 + (b > 0)):
            part = None
            for a in range(4):
                tap = taps_of(8 * a + b)
                if tap is None or tiles[k + a] is None:
                    continue
                term = tap * tiles[k + a]
                part = term if part is None else part + term
            parts.append(part if part is None or b == 0 else pltpu.roll(part, 8 - b, 0))
        for k in range(count // 8):
            if b == 0:
                if parts[k] is not None:
                    add(k, parts[k])
            elif parts[k] is not None and parts[k + 1] is not None:
                add(k, jnp.where(at < 8 - b, parts[k], parts[k + 1]))
            elif parts[k] is not None:
                add(k, jnp.where(at < 8 - b, parts[k], 0.0))
            elif parts[k + 1] is not None:
                add(k, jnp.where(at < 8 - b, 0.0, parts[k + 1]))
    zero = jnp.zeros((8, CHUNK), F32)
    return jnp.concatenate([zero if part is None else part for part in sums], axis=0)


def silu_parts(conv, cots):
    gate = 1.0 / (1.0 + jnp.exp(-conv))
    grad = cots * (gate + conv * gate * (1.0 - gate))
    return conv * gate, grad.astype(BF16).astype(F32)


def taps_forward(taps, count, cols):
    return lambda s: taps[s - 1 : s, cols] if 1 <= s <= count else None


def taps_backward(taps, count, cols):
    return lambda s: taps[count - s : count - s + 1, cols] if 1 <= s <= count else None


def conv_chunks(width, cot, cot_other, taps, taps_other):
    for c in range(0, 2 * width, CHUNK):
        own, cols = c < width, slice(c, c + CHUNK)
        local = cols if own else slice(cols.start - width, cols.stop - width)
        yield own, cols, local, cot if own else cot_other, taps if own else taps_other


def conv_inner_body(
    chip, across, cot, cot_other, taps, taps_other, seen, rows_out, edge_rows, edge_conv, part_grad
):
    frames, width = cot.shape
    wide, count = 2 * HALO, taps.shape[0]
    inner = slice(HALO, frames - HALO)
    none = [None] * (wide // 8)
    for own, cols, local, cots_of, tap in conv_chunks(width, cot, cot_other, taps, taps_other):
        rows = summed(chip, across, slice(0, frames), cols, width)
        cots = cots_of[:, local].astype(F32)
        conv = shifted_sum(
            none + tiles_of(rows) + none, taps_forward(tap, count, local), frames + wide
        )
        silu, grad = silu_parts(conv[wide:frames], cots[inner])
        back = shifted_sum(
            none + tiles_of(grad) + none, taps_backward(tap, count, local), frames
        )
        edge_conv[0:wide, cols] = conv[0:wide]
        edge_conv[wide : 2 * wide, cols] = conv[frames : frames + wide]
        if own:
            rows_out[inner, cols] = (rows[inner] + silu).astype(BF16)
            edge_rows[0:HALO, cols] = rows[0:HALO]
            edge_rows[HALO:wide, cols] = rows[frames - HALO :]
        part_grad[:, cols] = cots + back


def conv_edge_body(
    ends, ends_across, rim_near, rim_far, cot, cot_other, taps, taps_other,
    rows_in, edge_rows, edge_conv, part_grad, seen, output, grad_input,
):
    frames, width = cot.shape
    wide, count = 2 * HALO, taps.shape[0]
    even, far = is_even(), far_there()
    low, high = slice(0, HALO), slice(frames - HALO, frames)
    inner = slice(HALO, frames - HALO)
    none = [None] * (wide // 8)
    cots_of = slice(wide, wide + HALO)

    def sides(near, beyond):
        beyond = jnp.where(far, beyond, 0.0)
        return jnp.where(even, beyond, near), jnp.where(even, near, beyond)

    for own, cols, local, block, tap in conv_chunks(width, cot, cot_other, taps, taps_other):
        rows = summed(ends, ends_across, slice(0, 2 * wide), cols, width)
        row_low, row_high = sides(rows[0:wide], rows[wide:])
        cot_low, cot_high = sides(rim_near[cots_of, cols].astype(F32), rim_far[cots_of, cols].astype(F32))
        conv = edge_conv[:, cols] + shifted_sum(
            tiles_of(row_low) + none + tiles_of(row_high), taps_forward(tap, count, local), 2 * wide
        )
        first = block[low, local].astype(F32)
        last = block[high, local].astype(F32)
        cots = jnp.concatenate([cot_low, first, last, cot_high], axis=0)
        silu, grad = silu_parts(conv, cots)
        back = shifted_sum(
            tiles_of(grad[0:wide]) + none + tiles_of(grad[wide:]), taps_backward(tap, count, local), 2 * wide
        )
        part = part_grad[:, cols]
        grad_input[:, cols] = jnp.concatenate(
            [part[0:wide] + back[0:wide], part[wide : frames - wide], part[frames - wide :] + back[wide:]],
            axis=0,
        ).astype(BF16)
        if own:
            output[low, cols] = (edge_rows[0:HALO, cols] + silu[HALO:wide]).astype(BF16)
            output[inner, cols] = rows_in[inner, cols]
            output[high, cols] = (edge_rows[HALO:wide, cols] + silu[wide : wide + HALO]).astype(BF16)


def upstream_part(grads, weight, flips):
    width = weight.shape[0]
    return sum(
        dot_nt(grads[:, k * width : (k + 1) * width], weight_columns(weight, flip))
        for k, flip in enumerate(flips)
    )


def upstream_own_body(own, weight, lse, partial, terms):
    partial[...] = upstream_part(own, weight, (0, 2))
    terms[...] = stat_terms([lse[:, c] for c in columns(lse.shape[1])], 0)


def upstream_body(core, weight, att, partial, terms, message, delta):
    frames, width = att.shape
    heads = columns(width)
    up = (partial[...] + upstream_part(core, weight, (1, 3))).astype(BF16)
    products = [up[:, c].astype(F32) * att[:, c].astype(F32) for c in heads]
    deltas = [jnp.broadcast_to(jnp.sum(p, axis=1, keepdims=True), (frames, HDIM)) for p in products]
    message[0:frames, :] = up
    message[frames : frames + 16, :] = (terms[...] + stat_terms(deltas, 3)).astype(BF16)
    for c, part in zip(heads, deltas):
        delta[:, c] = part


def query_grad_body(
    scale, q, own, near, first, second, relay, message, lse, delta, output_here, grad_here,
    output, grad_input, grad_query, held, sems,
):
    writes = [
        pltpu.make_async_copy(output_here, output, sems.at[0]),
        pltpu.make_async_copy(grad_here.at[:, pl.ds(0, q.shape[1])], grad_input, sems.at[1]),
    ]
    for write in writes:
        write.start()
    frames, width = q.shape
    heads = columns(width)
    blocks = (near, own, first, second, relay)
    biases = (bias_of(near_swapped()), None, None, None, bias_of(far_there()))
    above, below = slice(0, frames), slice(frames, 2 * frames)
    keys = [stacked(blocks, above, c) for c in heads]
    scores = [dot_nt(q[:, c], k) * scale for c, k in zip(heads, keys)]
    dots = [dot_nt(message[0:frames, c], stacked(blocks, below, c)) for c in heads]
    probs = [jnp.exp(by_block(s, biases, [lse[:, c]] * 5)) for c, s in zip(heads, scores)]
    drops = [by_block(d, (None,) * 5, [delta[:, c]] * 5) for c, d in zip(heads, dots)]
    grads = [(p * d * scale).astype(BF16) for p, d in zip(probs, drops)]
    held[...] = jnp.concatenate([dot_nn(g, k).astype(BF16) for g, k in zip(grads, keys)], axis=1)
    writes.append(pltpu.make_async_copy(held, grad_query, sems.at[2]))
    writes[2].start()
    for write in writes:
        write.wait()


def key_part_body(scale, own, *refs):
    queries, late_query, messages, (key_part, value_part, late) = refs[0:4], refs[4], refs[5:9], refs[9:12]
    frames = own.shape[0] // 2
    heads = columns(own.shape[1])
    above, below = slice(0, frames), slice(frames, 2 * frames)
    biases = (None, bias_of(near_swapped()), None, None)
    asks = [stacked(queries, above, c) for c in heads]
    ups = [stacked(messages, above, c) for c in heads]
    scores = [dot_nt(own[above, c], a) * scale for c, a in zip(heads, asks)]
    dots = [dot_nt(own[below, c], u) for c, u in zip(heads, ups)]
    last = [dot_nt(own[above, c], late_query[:, c]) * scale + bias_of(far_there()) for c in heads]
    logs = [[stat_rows(m, frames, 0, c) for m in messages] for c in heads]
    deltas = [[stat_rows(m, frames, 1, c) for m in messages] for c in heads]
    probs = [jnp.exp(by_block(s, biases, n)) for s, n in zip(scores, logs)]
    drops = [by_block(d, (None,) * 4, n) for d, n in zip(dots, deltas)]
    grads = [(p * d * scale).astype(BF16) for p, d in zip(probs, drops)]
    value_sums = [dot_nn(p.astype(BF16), u) for p, u in zip(probs, ups)]
    key_sums = [dot_nn(g, a) for g, a in zip(grads, asks)]
    for c, k, v, s in zip(heads, key_sums, value_sums, last):
        key_part[:, c] = k
        value_part[:, c] = v
        late[:, c] = s


def key_grad_body(
    scale, own, query, message, late, key_part, value_part, grad_key, grad_value, held_key, held_value, sems
):
    frames = own.shape[0] // 2
    heads = columns(own.shape[1])
    above, below = slice(0, frames), slice(frames, 2 * frames)
    ups = [message[above, c] for c in heads]
    probs = [jnp.exp(late[:, c] - stat_rows(message, frames, 0, c)) for c in heads]
    dots = [dot_nt(own[below, c], u) for c, u in zip(heads, ups)]
    values = [value_part[:, c] + dot_nn(p.astype(BF16), u) for c, p, u in zip(heads, probs, ups)]
    held_value[...] = jnp.concatenate([v.astype(BF16) for v in values], axis=1)
    value_write = pltpu.make_async_copy(held_value, grad_value, sems.at[0])
    value_write.start()
    drops = [d - stat_rows(message, frames, 1, c) for c, d in zip(heads, dots)]
    grads = [(p * d * scale).astype(BF16) for p, d in zip(probs, drops)]
    keys = [key_part[:, c] + dot_nn(g, query[:, c]) for c, g in zip(heads, grads)]
    held_key[...] = jnp.concatenate([k.astype(BF16) for k in keys], axis=1)
    key_write = pltpu.make_async_copy(held_key, grad_key, sems.at[1])
    key_write.start()
    value_write.wait()
    key_write.wait()


def per_device(query_rows, key_rows, value_rows, inputs, out_weight, kernel, cotangent):
    frames, width = query_rows.shape
    wide = 2 * HALO
    scale = 1.0 / math.sqrt(HDIM)
    tile = shaped((frames, width), BF16)
    tile32 = shaped((frames, width), F32)
    rim = shaped((wide + HALO, 2 * width), BF16)
    both = shaped((frames, 2 * width), BF16)
    noted = shaped((frames + 16, width), BF16)

    zero = jnp.zeros((), BF16)
    kv = lax.pad(key_rows, zero, ((0, frames, 0), (0, 0, 0))) + lax.pad(
        value_rows, zero, ((frames, 0, 0), (0, 0, 0))
    )
    joined = sum(
        lax.pad(rows, zero, ((k * frames, (2 - k) * frames, 0), (0, 0, 0)))
        for k, rows in enumerate((query_rows, inputs, cotangent))
    )
    near, first, second, relay = window_of(
        kv,
        lambda second: kernel_call(
            turn_body, (shaped(kv.shape, BF16),), (second, joined), 0.1, "turn", 1
        )[0],
    )
    cot_other = pair_swap(cotangent, "mp", 2)
    taps_other = pair_swap(kernel, "mp", 2)
    query, inputs, cotangent = kernel_call(
        split_body, (tile, tile, tile), (joined, second), 0.1, "split", 1
    )
    q_second = ring(query, 1)
    sums, tops, totals = kernel_call(
        functools.partial(forward_body, scale),
        (tile32, tile32, tile32),
        (query, kv, near, first, second),
        1.0, "forward",
    )
    att, lse, send = kernel_call(
        functools.partial(project_body, scale),
        (tile, tile32, both),
        (query, relay, sums, tops, totals, out_weight),
        1.0, "project",
    )

    send, q_second = kernel_call(pass_body, (both, tile), (send, q_second, cot_other, taps_other), 0.1, "pass", 2)
    core = pair_swap(send, "mp", 1)
    (keep,) = kernel_call(project_own_body, (both,), (att, out_weight), 0.4, "project_own")
    chip, rim_up, rim_down, q_own = kernel_call(
        join_body,
        (both, rim, rim, tile),
        (keep, core, inputs, cotangent, cot_other, query),
        0.2, "join",
    )
    across = pair_swap(chip, "mp", 2)
    rim_far = outer_swap(rim_down)
    rim_near = pair_swap(rim_up, "ctx", 1)
    ends, q_handed = kernel_call(
        stack_body,
        (shaped((2 * wide, 2 * width), BF16), tile),
        (rim_near, rim_far, q_second),
        0.1, "stack",
    )
    ends_across = pair_swap(ends, "mp", 2)
    q_first = ring(q_own, 0)
    q_near = inner_swap(q_own)
    q_relay = pair_swap(q_handed, "ctx", 1)
    rows_out, edge_rows, edge_conv, part_grad = kernel_call(
        conv_inner_body,
        (
            tile,
            shaped((wide, width), F32),
            shaped((2 * wide, 2 * width), F32),
            shaped((frames, 2 * width), F32),
        ),
        (chip, across, cotangent, cot_other, kernel, taps_other, q_first),
        3.1, "conv_inner", 1,
    )
    output_here, grad_here = kernel_call(
        conv_edge_body,
        (tile, both),
        (ends, ends_across, rim_near, rim_far, cotangent, cot_other, kernel, taps_other)
        + (rows_out, edge_rows, edge_conv, part_grad, q_near),
        1.4, "conv_edge", 1,
    )

    (grad_here,) = kernel_call(turn_body, (both,), (grad_here, q_relay), 0.1, "hand", 1)
    gi_core = pair_swap(grad_here, "mp", 1)
    partial, terms = kernel_call(
        upstream_own_body, (tile32, shaped((16, width), F32)), (grad_here, out_weight, lse), 0.5,
        "upstream_own",
    )
    message, delta = kernel_call(
        upstream_body, (noted, tile32), (gi_core, out_weight, att, partial, terms), 0.6, "upstream"
    )

    m_near, m_first, m_second = inner_swap(message), ring(message, 0), ring(message, 1)
    m_relay = outer_swap(message)
    output, grad_input, grad_query = kernel_call(
        functools.partial(query_grad_body, scale),
        (tile, tile, tile),
        (q_own, kv, near, first, second, relay, message, lse, delta, output_here, grad_here),
        1.8, "query_grad", 0,
        [pltpu.VMEM((frames, width), BF16), pltpu.SemaphoreType.DMA((3,))], HBM,
    )
    key_part, value_part, late = kernel_call(
        functools.partial(key_part_body, scale),
        (tile32, tile32, tile32),
        (kv, q_own, q_near, q_first, q_second, q_relay, message, m_near, m_first, m_second),
        1.5, "key_part",
    )
    grad_key, grad_value = kernel_call(
        functools.partial(key_grad_body, scale),
        (tile, tile),
        (kv, q_relay, m_relay, late, key_part, value_part),
        1.0, "key_grad", 0,
        [pltpu.VMEM((frames, width), BF16)] * 2 + [pltpu.SemaphoreType.DMA((2,))], HBM,
    )
    return (output, grad_input, grad_query, grad_key, grad_value)


def solution(mesh):
    rows = P("ctx", "mp")
    return jax.shard_map(
        per_device,
        mesh=mesh,
        in_specs=(rows, rows, rows, rows, P("mp", None), P(None, "mp"), rows),
        out_specs=(rows,) * 5,
        check_vma=False,
    )
```

```python
import functools
import math

import jax
import jax.numpy as jnp
from jax import lax
from jax.experimental import pallas as pl
from jax.experimental.pallas import tpu as pltpu
from jax.sharding import PartitionSpec as P

HDIM = 128
F32 = jnp.float32
BF16 = jnp.bfloat16
CHUNK = 256
HALO = 16
NT = (((1,), (1,)), ((), ()))
NN = (((1,), (0,)), ((), ()))


def dot_nt(a, b):
    return lax.dot_general(a, b, NT, preferred_element_type=F32)


def dot_nn(a, b):
    return lax.dot_general(a, b, NN, preferred_element_type=F32)


def pair_swap(block, axis, bit):
    return lax.ppermute(block, axis, [(i, i ^ bit) for i in range(lax.axis_size(axis))])


def ring_routes(count):
    rise = [(i, i + 2) for i in range(0, count - 2, 2)] + [(count - 2, count - 1)]
    fall = [(i, i - 2) for i in range(count - 1, 2, -2)] + [(1, 0)]
    route = rise + fall
    return route, [(b, a) for a, b in route]


def ring(block, way):
    return lax.ppermute(block, "ctx", ring_routes(lax.axis_size("ctx"))[way])


def total_swap(block, partner_of):
    count, places = lax.axis_size("ctx"), lax.axis_size("mp")
    route = []
    for i in range(count):
        other = partner_of(i, count)
        for m in range(places):
            target = i * places + (m ^ 1) if other is None else other * places + m
            route.append((i * places + m, target))
    return lax.ppermute(block, ("ctx", "mp"), route)


def inner_swap(block):
    return total_swap(block, lambda i, count: i ^ 1 if 2 <= i < count - 2 else None)


def outer_swap(block):
    return total_swap(block, lambda i, count: ((i + 1) ^ 1) - 1 if 0 < i < count - 1 else None)


def window_of(block, before_relay=lambda second: second):
    second = ring(block, 1)
    first = ring(block, 0)
    near = inner_swap(block)
    second = before_relay(second)
    return near, first, second, pair_swap(second, "ctx", 1)


VMEM = pl.BlockSpec(memory_space=pltpu.VMEM)
ANY = pl.BlockSpec(memory_space=pl.ANY)
HBM = pl.BlockSpec(memory_space=pltpu.HBM)


def kernel_call(body, outs, args, micros, name, unread=0, scratch=(), out_space=VMEM):
    return pl.pallas_call(
        body,
        out_shape=outs,
        in_specs=[VMEM] * (len(args) - unread) + [ANY] * unread,
        out_specs=tuple(out_space for _ in outs),
        scratch_shapes=scratch,
        compiler_params=pltpu.CompilerParams(vmem_limit_bytes=24 * 1024 * 1024),
        cost_estimate=pl.CostEstimate(
            flops=0, bytes_accessed=int(micros * 3.69e6), transcendentals=0
        ),
        name=name,
    )(*args)


def shaped(shape, dtype):
    return jax.ShapeDtypeStruct(shape, dtype)


def is_even():
    return lax.axis_index("ctx") % 2 == 0


def near_swapped():
    block = lax.axis_index("ctx")
    return (block >= 2) & (block < lax.axis_size("ctx") - 2)


def far_there():
    block = lax.axis_index("ctx")
    return jnp.where(is_even(), block >= 2, block < lax.axis_size("ctx") - 2)


def bias_of(there):
    return jnp.where(there, jnp.float32(0.0), jnp.float32(-jnp.inf))


def columns(width):
    return [slice(c, c + HDIM) for c in range(0, width, HDIM)]


def stacked(blocks, rows, cols):
    return jnp.concatenate([block[rows, cols] for block in blocks], axis=0)


def with_ones(values):
    return jnp.concatenate([values, jnp.ones_like(values)], axis=1)


def by_block(scores, biases, stats=None):
    parts = []
    for b, bias in enumerate(biases):
        part = scores[:, b * HDIM : (b + 1) * HDIM]
        if stats is not None:
            part = part - stats[b]
        parts.append(part if bias is None else part + bias)
    return jnp.concatenate(parts, axis=1)


def tile_of(wide):
    lane = lax.broadcasted_iota(jnp.int32, (wide[0].shape[0], HDIM), 1)
    tile = jnp.zeros((wide[0].shape[0], HDIM), F32)
    for h, part in enumerate(wide):
        tile = jnp.where(lane == h, part, tile)
    return tile


def term_rows(row, first):
    at = lax.broadcasted_iota(jnp.int32, (16, row.shape[1]), 0)
    block = jnp.zeros((16, row.shape[1]), F32)
    for k in range(3):
        term = row.astype(BF16).astype(F32)
        row = row - term
        block = jnp.where(at == first + k, term, block)
    return block


def stat_terms(wide, first):
    rows = tile_of(wide).T
    return jnp.concatenate([term_rows(rows[h : h + 1], first) for h in range(len(wide))], axis=1)


def stat_rows(message, frames, which, cols):
    terms = message[frames : frames + 16, cols].astype(F32)
    at = 3 * which
    return terms[at : at + 1] + terms[at + 1 : at + 2] + terms[at + 2 : at + 3]


def weight_columns(weight, flip):
    width = weight.shape[0]
    at = (lax.axis_index("mp") ^ flip) * width
    return weight[:, pl.ds(pl.multiple_of(at, 128), width)]


def turn_body(block, seen, copy):
    copy[...] = block[...]


def split_body(joined, seen, *parts):
    frames = parts[0].shape[0]
    for k, part in enumerate(parts):
        part[...] = joined[k * frames : (k + 1) * frames, :]


def forward_body(scale, q, own, near, first, second, *refs):
    sums, tops, totals = refs[-3:]
    frames, width = q.shape
    heads = columns(width)
    blocks = (near, own, first, second)
    biases = (bias_of(near_swapped()), None, None, None)
    keys, values = slice(0, frames), slice(frames, 2 * frames)
    scores = [dot_nt(q[:, c], stacked(blocks, keys, c)) * scale for c in heads]
    scores = [by_block(s, biases) for s in scores]
    top = [jnp.max(s, axis=1, keepdims=True) for s in scores]
    probs = [jnp.exp(s - t).astype(BF16) for s, t in zip(scores, top)]
    summed = [dot_nn(p, with_ones(stacked(blocks, values, c))) for p, c in zip(probs, heads)]
    for c, t, s in zip(heads, top, summed):
        tops[:, c] = jnp.broadcast_to(t, (frames, HDIM))
        sums[:, c] = s[:, 0:HDIM]
        totals[:, c] = s[:, HDIM:]


def project_body(scale, q, relay, sums, tops, totals, weight, att, lse, send):
    frames, width = q.shape
    heads = columns(width)
    bias = bias_of(far_there())
    scores = [dot_nt(q[:, c], relay[0:frames, c]) * scale + bias for c in heads]
    before = [tops[:, c] for c in heads]
    top = [jnp.maximum(b, jnp.max(s, axis=1, keepdims=True)) for b, s in zip(before, scores)]
    shrink = [jnp.exp(b - t) for b, t in zip(before, top)]
    probs = [jnp.exp(s - t).astype(BF16) for s, t in zip(scores, top)]
    late = [dot_nn(p, with_ones(relay[frames : 2 * frames, c])) for p, c in zip(probs, heads)]
    total = [totals[:, c] * k + s[:, HDIM:] for c, k, s in zip(heads, shrink, late)]
    summed = [sums[:, c] * k + s[:, 0:HDIM] for c, k, s in zip(heads, shrink, late)]
    attended = jnp.concatenate([(s * (1.0 / t)).astype(BF16) for s, t in zip(summed, total)], axis=1)
    sent = [dot_nn(attended, weight_columns(weight, flip)).astype(BF16) for flip in (1, 3)]
    logs = [t + jnp.log(n) for t, n in zip(top, total)]
    att[...] = attended
    send[...] = jnp.concatenate(sent, axis=1)
    for c, part in zip(heads, logs):
        lse[:, c] = part


def project_own_body(att, weight, keep):
    kept = [dot_nn(att[...], weight_columns(weight, flip)).astype(BF16) for flip in (0, 2)]
    keep[...] = jnp.concatenate(kept, axis=1)


def pass_body(send, q_second, seen_a, seen_b, send_copy, second_copy):
    send_copy[...] = send[...]
    second_copy[...] = q_second[...]


def join_body(keep, core, inputs, cot, cot_other, q, chip, rim_near, rim_far, q_copy):
    frames, width = inputs.shape
    wide = 2 * HALO
    even = is_even()
    for cols, rows, cots in (
        (slice(0, width), inputs[...].astype(F32), cot),
        (slice(width, 2 * width), 0.0, cot_other),
    ):
        total = (rows + (keep[:, cols].astype(F32) + core[:, cols].astype(F32))).astype(BF16)
        for at, first, last in (
            (slice(0, wide), total[0:wide], total[frames - wide :]),
            (slice(wide, wide + HALO), cots[0:HALO, :], cots[frames - HALO : frames, :]),
        ):
            first, last = first.astype(F32), last.astype(F32)
            rim_near[at, cols] = jnp.where(even, last, first).astype(BF16)
            rim_far[at, cols] = jnp.where(even, first, last).astype(BF16)
        chip[:, cols] = total
    q_copy[...] = q[...]


def stack_body(rim_near, rim_far, q_second, ends, second_copy):
    wide = 2 * HALO
    ends[0:wide, :] = rim_near[0:wide, :]
    ends[wide : 2 * wide, :] = rim_far[0:wide, :]
    second_copy[...] = q_second[...]


def summed(share, across, rows, cols, width):
    back = slice((cols.start + width) % (2 * width), (cols.stop - 1 + width) % (2 * width) + 1)
    total = share[rows, cols].astype(F32) + across[rows, back].astype(F32)
    return total.astype(BF16).astype(F32)


def tiles_of(rows):
    return [rows[at : at + 8] for at in range(0, rows.shape[0], 8)]


def shifted_sum(tiles, taps_of, count):
    at = lax.broadcasted_iota(jnp.int32, (8, CHUNK), 0)
    sums = [None] * (count // 8)

    def add(k, term):
        sums[k] = term if sums[k] is None else sums[k] + term

    for b in range(8):
        parts = []
        for k in range(count // 8 + (b > 0)):
            part = None
            for a in range(4):
                tap = taps_of(8 * a + b)
                if tap is None or tiles[k + a] is None:
                    continue
                term = tap * tiles[k + a]
                part = term if part is None else part + term
            parts.append(part if part is None or b == 0 else pltpu.roll(part, 8 - b, 0))
        for k in range(count // 8):
            if b == 0:
                if parts[k] is not None:
                    add(k, parts[k])
            elif parts[k] is not None and parts[k + 1] is not None:
                add(k, jnp.where(at < 8 - b, parts[k], parts[k + 1]))
            elif parts[k] is not None:
                add(k, jnp.where(at < 8 - b, parts[k], 0.0))
            elif parts[k + 1] is not None:
                add(k, jnp.where(at < 8 - b, 0.0, parts[k + 1]))
    zero = jnp.zeros((8, CHUNK), F32)
    return jnp.concatenate([zero if part is None else part for part in sums], axis=0)


def silu_parts(conv, cots):
    gate = 1.0 / (1.0 + jnp.exp(-conv))
    grad = cots * (gate + conv * gate * (1.0 - gate))
    return conv * gate, grad.astype(BF16).astype(F32)


def taps_forward(taps, count, cols):
    return lambda s: taps[s - 1 : s, cols] if 1 <= s <= count else None


def taps_backward(taps, count, cols):
    return lambda s: taps[count - s : count - s + 1, cols] if 1 <= s <= count else None


def conv_chunks(width, cot, cot_other, taps, taps_other):
    for c in range(0, 2 * width, CHUNK):
        own, cols = c < width, slice(c, c + CHUNK)
        local = cols if own else slice(cols.start - width, cols.stop - width)
        yield own, cols, local, cot if own else cot_other, taps if own else taps_other


def conv_inner_body(
    chip, across, cot, cot_other, taps, taps_other, seen, rows_out, edge_rows, edge_conv, part_grad
):
    frames, width = cot.shape
    wide, count = 2 * HALO, taps.shape[0]
    inner = slice(HALO, frames - HALO)
    none = [None] * (wide // 8)
    for own, cols, local, cots_of, tap in conv_chunks(width, cot, cot_other, taps, taps_other):
        rows = summed(chip, across, slice(0, frames), cols, width)
        cots = cots_of[:, local].astype(F32)
        conv = shifted_sum(
            none + tiles_of(rows) + none, taps_forward(tap, count, local), frames + wide
        )
        silu, grad = silu_parts(conv[wide:frames], cots[inner])
        back = shifted_sum(
            none + tiles_of(grad) + none, taps_backward(tap, count, local), frames
        )
        edge_conv[0:wide, cols] = conv[0:wide]
        edge_conv[wide : 2 * wide, cols] = conv[frames : frames + wide]
        if own:
            rows_out[inner, cols] = (rows[inner] + silu).astype(BF16)
            edge_rows[0:HALO, cols] = rows[0:HALO]
            edge_rows[HALO:wide, cols] = rows[frames - HALO :]
        part_grad[:, cols] = cots + back


def conv_edge_body(
    ends, ends_across, rim_near, rim_far, cot, cot_other, taps, taps_other,
    rows_in, edge_rows, edge_conv, part_grad, seen, output, grad_input,
):
    frames, width = cot.shape
    wide, count = 2 * HALO, taps.shape[0]
    even, far = is_even(), far_there()
    low, high = slice(0, HALO), slice(frames - HALO, frames)
    inner = slice(HALO, frames - HALO)
    none = [None] * (wide // 8)
    cots_of = slice(wide, wide + HALO)

    def sides(near, beyond):
        beyond = jnp.where(far, beyond, 0.0)
        return jnp.where(even, beyond, near), jnp.where(even, near, beyond)

    for own, cols, local, block, tap in conv_chunks(width, cot, cot_other, taps, taps_other):
        rows = summed(ends, ends_across, slice(0, 2 * wide), cols, width)
        row_low, row_high = sides(rows[0:wide], rows[wide:])
        cot_low, cot_high = sides(rim_near[cots_of, cols].astype(F32), rim_far[cots_of, cols].astype(F32))
        conv = edge_conv[:, cols] + shifted_sum(
            tiles_of(row_low) + none + tiles_of(row_high), taps_forward(tap, count, local), 2 * wide
        )
        first = block[low, local].astype(F32)
        last = block[high, local].astype(F32)
        cots = jnp.concatenate([cot_low, first, last, cot_high], axis=0)
        silu, grad = silu_parts(conv, cots)
        back = shifted_sum(
            tiles_of(grad[0:wide]) + none + tiles_of(grad[wide:]), taps_backward(tap, count, local), 2 * wide
        )
        part = part_grad[:, cols]
        grad_input[:, cols] = jnp.concatenate(
            [part[0:wide] + back[0:wide], part[wide : frames - wide], part[frames - wide :] + back[wide:]],
            axis=0,
        ).astype(BF16)
        if own:
            output[low, cols] = (edge_rows[0:HALO, cols] + silu[HALO:wide]).astype(BF16)
            output[inner, cols] = rows_in[inner, cols]
            output[high, cols] = (edge_rows[HALO:wide, cols] + silu[wide : wide + HALO]).astype(BF16)


def upstream_part(grads, weight, flips):
    width = weight.shape[0]
    return sum(
        dot_nt(grads[:, k * width : (k + 1) * width], weight_columns(weight, flip))
        for k, flip in enumerate(flips)
    )


def upstream_own_body(own, weight, lse, partial, terms):
    partial[...] = upstream_part(own, weight, (0, 2))
    terms[...] = stat_terms([lse[:, c] for c in columns(lse.shape[1])], 0)


def upstream_body(core, weight, att, partial, terms, message, delta):
    frames, width = att.shape
    heads = columns(width)
    up = (partial[...] + upstream_part(core, weight, (1, 3))).astype(BF16)
    products = [up[:, c].astype(F32) * att[:, c].astype(F32) for c in heads]
    deltas = [jnp.broadcast_to(jnp.sum(p, axis=1, keepdims=True), (frames, HDIM)) for p in products]
    message[0:frames, :] = up
    message[frames : frames + 16, :] = (terms[...] + stat_terms(deltas, 3)).astype(BF16)
    for c, part in zip(heads, deltas):
        delta[:, c] = part


def query_grad_body(
    scale, q, own, near, first, second, relay, message, lse, delta, output_here, grad_here,
    output, grad_input, grad_query, held, sems,
):
    writes = [
        pltpu.make_async_copy(output_here, output, sems.at[0]),
        pltpu.make_async_copy(grad_here.at[:, pl.ds(0, q.shape[1])], grad_input, sems.at[1]),
    ]
    for write in writes:
        write.start()
    frames, width = q.shape
    heads = columns(width)
    blocks = (near, own, first, second, relay)
    biases = (bias_of(near_swapped()), None, None, None, bias_of(far_there()))
    above, below = slice(0, frames), slice(frames, 2 * frames)
    keys = [stacked(blocks, above, c) for c in heads]
    scores = [dot_nt(q[:, c], k) * scale for c, k in zip(heads, keys)]
    dots = [dot_nt(message[0:frames, c], stacked(blocks, below, c)) for c in heads]
    probs = [jnp.exp(by_block(s, biases, [lse[:, c]] * 5)) for c, s in zip(heads, scores)]
    drops = [by_block(d, (None,) * 5, [delta[:, c]] * 5) for c, d in zip(heads, dots)]
    grads = [(p * d * scale).astype(BF16) for p, d in zip(probs, drops)]
    held[...] = jnp.concatenate([dot_nn(g, k).astype(BF16) for g, k in zip(grads, keys)], axis=1)
    writes.append(pltpu.make_async_copy(held, grad_query, sems.at[2]))
    writes[2].start()
    for write in writes:
        write.wait()


def key_part_body(scale, own, *refs):
    queries, late_query, messages, (key_part, value_part, late) = refs[0:4], refs[4], refs[5:9], refs[9:12]
    frames = own.shape[0] // 2
    heads = columns(own.shape[1])
    above, below = slice(0, frames), slice(frames, 2 * frames)
    biases = (None, None, None, bias_of(near_swapped()))
    asks = [stacked(queries, above, c) for c in heads]
    ups = [stacked(messages, above, c) for c in heads]
    scores = [dot_nt(own[above, c], a) * scale for c, a in zip(heads, asks)]
    dots = [dot_nt(own[below, c], u) for c, u in zip(heads, ups)]
    last = [dot_nt(own[above, c], late_query[:, c]) * scale + bias_of(far_there()) for c in heads]
    logs = [[stat_rows(m, frames, 0, c) for m in messages] for c in heads]
    deltas = [[stat_rows(m, frames, 1, c) for m in messages] for c in heads]
    probs = [jnp.exp(by_block(s, biases, n)) for s, n in zip(scores, logs)]
    drops = [by_block(d, (None,) * 4, n) for d, n in zip(dots, deltas)]
    grads = [(p * d * scale).astype(BF16) for p, d in zip(probs, drops)]
    value_sums = [dot_nn(p.astype(BF16), u) for p, u in zip(probs, ups)]
    key_sums = [dot_nn(g, a) for g, a in zip(grads, asks)]
    for c, k, v, s in zip(heads, key_sums, value_sums, last):
        key_part[:, c] = k
        value_part[:, c] = v
        late[:, c] = s


def key_grad_body(
    scale, own, query, message, late, key_part, value_part, grad_key, grad_value, held_key, held_value, sems
):
    frames = own.shape[0] // 2
    heads = columns(own.shape[1])
    above, below = slice(0, frames), slice(frames, 2 * frames)
    ups = [message[above, c] for c in heads]
    probs = [jnp.exp(late[:, c] - stat_rows(message, frames, 0, c)) for c in heads]
    dots = [dot_nt(own[below, c], u) for c, u in zip(heads, ups)]
    values = [value_part[:, c] + dot_nn(p.astype(BF16), u) for c, p, u in zip(heads, probs, ups)]
    held_value[...] = jnp.concatenate([v.astype(BF16) for v in values], axis=1)
    value_write = pltpu.make_async_copy(held_value, grad_value, sems.at[0])
    value_write.start()
    drops = [d - stat_rows(message, frames, 1, c) for c, d in zip(heads, dots)]
    grads = [(p * d * scale).astype(BF16) for p, d in zip(probs, drops)]
    keys = [key_part[:, c] + dot_nn(g, query[:, c]) for c, g in zip(heads, grads)]
    held_key[...] = jnp.concatenate([k.astype(BF16) for k in keys], axis=1)
    key_write = pltpu.make_async_copy(held_key, grad_key, sems.at[1])
    key_write.start()
    value_write.wait()
    key_write.wait()


def per_device(query_rows, key_rows, value_rows, inputs, out_weight, kernel, cotangent):
    frames, width = query_rows.shape
    wide = 2 * HALO
    scale = 1.0 / math.sqrt(HDIM)
    tile = shaped((frames, width), BF16)
    tile32 = shaped((frames, width), F32)
    rim = shaped((wide + HALO, 2 * width), BF16)
    both = shaped((frames, 2 * width), BF16)
    noted = shaped((frames + 16, width), BF16)

    zero = jnp.zeros((), BF16)
    kv = lax.pad(key_rows, zero, ((0, frames, 0), (0, 0, 0))) + lax.pad(
        value_rows, zero, ((frames, 0, 0), (0, 0, 0))
    )
    joined = sum(
        lax.pad(rows, zero, ((k * frames, (2 - k) * frames, 0), (0, 0, 0)))
        for k, rows in enumerate((query_rows, inputs, cotangent))
    )
    near, first, second, relay = window_of(
        kv,
        lambda second: kernel_call(
            turn_body, (shaped(kv.shape, BF16),), (second, joined), 0.1, "turn", 1
        )[0],
    )
    cot_other = pair_swap(cotangent, "mp", 2)
    taps_other = pair_swap(kernel, "mp", 2)
    query, inputs, cotangent = kernel_call(
        split_body, (tile, tile, tile), (joined, second), 0.1, "split", 1
    )
    q_second = ring(query, 1)
    sums, tops, totals = kernel_call(
        functools.partial(forward_body, scale),
        (tile32, tile32, tile32),
        (query, kv, near, first, second),
        1.0, "forward",
    )
    att, lse, send = kernel_call(
        functools.partial(project_body, scale),
        (tile, tile32, both),
        (query, relay, sums, tops, totals, out_weight),
        1.0, "project",
    )

    send, q_second = kernel_call(pass_body, (both, tile), (send, q_second, cot_other, taps_other), 0.1, "pass", 2)
    core = pair_swap(send, "mp", 1)
    (keep,) = kernel_call(project_own_body, (both,), (att, out_weight), 0.4, "project_own")
    chip, rim_up, rim_down, q_own = kernel_call(
        join_body,
        (both, rim, rim, tile),
        (keep, core, inputs, cotangent, cot_other, query),
        0.2, "join",
    )
    across = pair_swap(chip, "mp", 2)
    rim_far = outer_swap(rim_down)
    rim_near = pair_swap(rim_up, "ctx", 1)
    ends, q_handed = kernel_call(
        stack_body,
        (shaped((2 * wide, 2 * width), BF16), tile),
        (rim_near, rim_far, q_second),
        0.1, "stack",
    )
    ends_across = pair_swap(ends, "mp", 2)
    q_first = ring(q_own, 0)
    q_near = inner_swap(q_own)
    q_relay = pair_swap(q_handed, "ctx", 1)
    rows_out, edge_rows, edge_conv, part_grad = kernel_call(
        conv_inner_body,
        (
            tile,
            shaped((wide, width), F32),
            shaped((2 * wide, 2 * width), F32),
            shaped((frames, 2 * width), F32),
        ),
        (chip, across, cotangent, cot_other, kernel, taps_other, q_first),
        3.1, "conv_inner", 1,
    )
    output_here, grad_here = kernel_call(
        conv_edge_body,
        (tile, both),
        (ends, ends_across, rim_near, rim_far, cotangent, cot_other, kernel, taps_other)
        + (rows_out, edge_rows, edge_conv, part_grad, q_near),
        1.4, "conv_edge", 1,
    )

    (grad_here,) = kernel_call(turn_body, (both,), (grad_here, q_relay), 0.1, "hand", 1)
    gi_core = pair_swap(grad_here, "mp", 1)
    partial, terms = kernel_call(
        upstream_own_body, (tile32, shaped((16, width), F32)), (grad_here, out_weight, lse), 0.5,
        "upstream_own",
    )
    message, delta = kernel_call(
        upstream_body, (noted, tile32), (gi_core, out_weight, att, partial, terms), 0.6, "upstream"
    )

    m_near, m_first, m_second = inner_swap(message), ring(message, 0), ring(message, 1)
    m_relay = outer_swap(message)
    output, grad_input, grad_query = kernel_call(
        functools.partial(query_grad_body, scale),
        (tile, tile, tile),
        (q_own, kv, near, first, second, relay, message, lse, delta, output_here, grad_here),
        1.8, "query_grad", 0,
        [pltpu.VMEM((frames, width), BF16), pltpu.SemaphoreType.DMA((3,))], HBM,
    )
    key_part, value_part, late = kernel_call(
        functools.partial(key_part_body, scale),
        (tile32, tile32, tile32),
        (kv, q_own, q_first, q_second, q_near, q_relay, message, m_first, m_second, m_near),
        1.5, "key_part",
    )
    grad_key, grad_value = kernel_call(
        functools.partial(key_grad_body, scale),
        (tile, tile),
        (kv, q_relay, m_relay, late, key_part, value_part),
        1.0, "key_grad", 0,
        [pltpu.VMEM((frames, width), BF16)] * 2 + [pltpu.SemaphoreType.DMA((2,))], HBM,
    )
    return (output, grad_input, grad_query, grad_key, grad_value)


def solution(mesh):
    rows = P("ctx", "mp")
    return jax.shard_map(
        per_device,
        mesh=mesh,
        in_specs=(rows, rows, rows, rows, P("mp", None), P(None, "mp"), rows),
        out_specs=(rows,) * 5,
        check_vma=False,
    )
```
